128 devices in a mesh: seq: 32 (over y_lo, x, z), row: 4 (over y_hi, core).
Axes of the slice: x: 4, y: 4 (y_hi: 2, y_lo: 2; y = y_hi * 2 + y_lo), z: 4, core: 2. Of those that a mesh axis runs over, the one named last changes fastest.
Arguments:
- frames: bfloat16 [4, 6144, 1024], P('row', 'seq'), may hold values from -6 to 6
- segment_ids: int32 [4, 6144], P('row', 'seq'), may hold values from 0 to 4, as said below
- norm1_gain: float32 [1024], replicated, may hold values from 0.1 to 1.9
- w_qkv: bfloat16 [1024, 3072], replicated, may hold values from -0.1875 to 0.1875
- w_out: bfloat16 [1024, 1024], replicated, may hold values from -1.5 to 1.5
- norm2_gain: float32 [1024], replicated, may hold values from 0.1 to 1.9
- w_up: bfloat16 [1024, 4096], replicated, may hold values from -0.1875 to 0.1875
- w_down: bfloat16 [4096, 1024], replicated, may hold values from -0.09375 to 0.09375
- out_grad: bfloat16 [4, 6144, 1024], P('row', 'seq'), may hold values from -6 to 6
Outputs:
- block_out: bfloat16 [4, 6144, 1024], P('row', 'seq')
- frames_grad: bfloat16 [4, 6144, 1024], P('row', 'seq')
- norm1_grad: float32 [1024], P(('seq', 'row'))
- qkv_grad: float32 [1024, 3072], P(('seq', 'row'))
- out_w_grad: float32 [1024, 1024], P(('seq', 'row'))
- norm2_grad: float32 [1024], P(('seq', 'row'))
- up_grad: float32 [1024, 4096], P(('seq', 'row'))
- down_grad: float32 [4096, 1024], P(('seq', 'row'))
The draws below stay inside these ranges and needn't reach their ends.
Inputs may be any that keep to these rules, and one draw needn't show every extreme that they name: `segment_ids`: along each row the numbers never fall; each row holds five documents, and one of them begins within the row's first 192 frames and ends within its last 192.
All inputs are finite; a program needn't handle non-finite values.
Results may differ from the reference program's by a relative error of at most 0.025.
Values may be sent and summed in bfloat16 or wider, within the bound.
A program may use at most 192 MiB of HBM per device.

```python
import jax
import jax.numpy as jnp
from jax import lax

D = 1024
H = 16
HD = 64
FF = 4096
FRAME_DEV = 192
FRAMES = 6144
ROWS = 4


def draw_segment_ids(key, part):
    key = jax.random.fold_in(key, 11)
    keys = jax.random.split(key, 4)
    start = jax.random.randint(keys[0], (ROWS, 1), 2, FRAME_DEV)
    first = jax.random.randint(keys[1], (ROWS, 1), 1, start)
    finish = jax.random.randint(keys[2], (ROWS, 1), FRAMES - FRAME_DEV + 1, FRAMES - 2)
    last = jax.random.randint(keys[3], (ROWS, 1), finish + 1, FRAMES)
    pos = jnp.arange(FRAMES, dtype=jnp.int32)[None, :]
    total = (pos >= first).astype(jnp.int32) + (pos >= start).astype(jnp.int32)
    total = total + (pos >= finish).astype(jnp.int32) + (pos >= last).astype(jnp.int32)
    return total.astype(jnp.int32)


def level_of(stream_key, shape, cuts, smallest, high):
    factor_of = 1.0
    for axis_at, blocks in cuts:
        steps = jax.random.uniform(jax.random.fold_in(jax.random.fold_in(stream_key, 6), axis_at), (blocks,), jnp.float32, smallest / len(cuts), high / len(cuts))
        factor_of = factor_of * jnp.repeat(jnp.exp(steps), shape[axis_at] // blocks).reshape((-1,) + (1,) * (len(shape) - 1 - axis_at))
    return factor_of


def scatter_about(key, dims, deviation, limit, cuts=(), held_as=jnp.bfloat16):
    array = jax.random.normal(key, dims, jnp.float32) * deviation
    if len(cuts) > 0:
        array = level_of(key, dims, cuts, -0.22, 0.18) * array
    return jnp.clip(array, min=-limit, max=limit).astype(held_as)


def setup_inputs(seed: int = 0) -> dict:
    streams_of = jax.random.split(jax.random.key(seed), 10)
    frames = scatter_about(streams_of[0], (ROWS, FRAMES, D), 1.0, 6.0, ((0, 4), (1, 32)))
    segment_ids = draw_segment_ids(jax.random.fold_in(streams_of[9], 71), 0)
    norm1_gain = jnp.clip(1.0 + 0.18 * jax.random.normal(streams_of[2], (D,), jnp.float32), 0.1, 1.9)
    w_qkv = scatter_about(streams_of[3], (D, 3 * D), D ** -0.5, 0.1875)
    w_out = scatter_about(streams_of[4], (D, D), (max(D // 64, 1)) ** -0.5, 1.5)
    norm2_gain = jnp.clip(1.0 + 0.18 * jax.random.normal(streams_of[5], (D,), jnp.float32), 0.1, 1.9)
    w_up = scatter_about(streams_of[6], (D, FF), D ** -0.5, 0.1875)
    w_down = scatter_about(streams_of[7], (FF, D), FF ** -0.5, 0.09375)
    out_grad = scatter_about(streams_of[8], (ROWS, FRAMES, D), 1.0, 6.0, ((0, 4), (1, 32)))
    return {"frames": frames, "segment_ids": segment_ids, "norm1_gain": norm1_gain, "w_qkv": w_qkv, "w_out": w_out, "norm2_gain": norm2_gain, "w_up": w_up, "w_down": w_down, "out_grad": out_grad}


@jax.custom_vjp
def low(v):
    return lax.optimization_barrier(v.astype(jnp.bfloat16)).astype(jnp.float32)

@jax.custom_vjp
def low_back(v):
    return v

def low_keep(v):
    return (low(v), None)

def low_pass(kept, grad):
    return (grad,)

def back_keep(v):
    return (v, None)

def back_low(kept, grad):
    return (low(grad),)
low.defvjp(low_keep, low_pass)
low_back.defvjp(back_keep, back_low)
epsilon = 1e-05
highest = lax.Precision.HIGHEST

def rms_scale(value, gain):
    return value * lax.rsqrt(lax.optimization_barrier(jnp.mean(value * value, axis=-1, keepdims=True)) + epsilon) * gain

def query_block(keys, values, key_seg, pieces):
    queries, query_seg, start = pieces
    width = min(512, FRAMES)
    pos_q = start + jnp.arange(width, dtype=jnp.int32)
    pos_k = jnp.arange(FRAMES, dtype=jnp.int32)
    allowed = (query_seg[:, None] == key_seg[None, :]) & (pos_k[None, :] <= pos_q[:, None])
    scores = jnp.einsum('qhd,khd->hqk', queries, keys, precision=highest) * HD ** (-0.5)
    scores = low_back(scores)
    masked = jnp.where(allowed[None], scores, -1e+30)
    top = lax.optimization_barrier(jnp.max(masked, axis=-1, keepdims=True))
    weights = jnp.where(allowed[None], jnp.exp(masked - top), 0.0)
    probs = weights / lax.optimization_barrier(jnp.sum(weights, axis=-1, keepdims=True))
    return jnp.einsum('hqk,khd->qhd', low(probs), values, precision=highest)

def attend_row(pieces):
    queries, keys, values, seg = pieces
    width = min(512, FRAMES)
    blocks = FRAMES // width
    qh = queries.reshape(blocks, width, H, HD)
    kh = keys.reshape(FRAMES, H, HD)
    vh = values.reshape(FRAMES, H, HD)
    segs = seg.reshape(blocks, width)
    starts = (jnp.arange(blocks, dtype=jnp.int32) * width).astype(jnp.int32)
    kept = jax.checkpoint(query_block)
    out = lax.map(lambda p: kept(kh, vh, seg, p), (qh, segs, starts))
    return out.reshape(FRAMES, D)

def make_forward(segment_ids):

    def forward(xf, gain1, wqkv, wout, gain2, wup, wdown):
        h1 = rms_scale(xf, gain1)
        qkv = jnp.einsum('rsd,de->rse', low(h1), wqkv, precision=highest)
        qkv = low(low_back(qkv))
        queries = qkv[..., :D]
        keys = qkv[..., D:2 * D]
        values = qkv[..., 2 * D:]
        attn = lax.map(attend_row, (queries, keys, values, segment_ids))
        attn = low(low_back(attn))
        x1 = xf + low_back(jnp.einsum('rsd,de->rse', attn, wout, precision=highest))
        h2 = rms_scale(x1, gain2)
        hidden = low_back(jnp.einsum('rsd,df->rsf', low(h2), wup, precision=highest))
        act = low(jax.nn.gelu(hidden))
        return x1 + low_back(jnp.einsum('rsf,fd->rsd', act, wdown, precision=highest))
    return forward

def reference(frames, segment_ids, norm1_gain, w_qkv, w_out, norm2_gain, w_up, w_down, out_grad):
    f32 = jnp.float32
    forward = make_forward(segment_ids)
    result, pull = jax.vjp(forward, frames.astype(f32), norm1_gain.astype(f32), w_qkv.astype(f32), w_out.astype(f32), norm2_gain.astype(f32), w_up.astype(f32), w_down.astype(f32))
    grads = pull(out_grad.astype(f32))
    return (result.astype(jnp.bfloat16), grads[0].astype(jnp.bfloat16), grads[1], grads[2], grads[3], grads[4], grads[5], grads[6])
```

```python
import functools
import math

import jax
import jax.numpy as jnp
from jax import lax
from jax.experimental import pallas as pl
from jax.experimental.pallas import tpu as pltpu
from jax.sharding import PartitionSpec as P

MESH = pl.DeviceIdType.MESH
f32 = jnp.float32
bf16 = jnp.bfloat16

D = 1024
H = 16
HD = 64
FF = 4096
T = 192
HT = T // 2
BLOCKS = 32
TILE = 768
TILES = 8
PACK = 304
GRAD = 288
EPS = 1e-05
NEG = -1e30
LOG2E = math.log2(math.e)
LN2 = math.log(2.0)
SCALE = HD**-0.5
VMEM_LIMIT = 60 * 1024 * 1024

ANY = pl.BlockSpec(memory_space=pl.ANY)
VM = pl.BlockSpec(memory_space=pltpu.VMEM)


def dot(a, b):
    return jnp.dot(a, b, preferred_element_type=f32)


def dot_nt(a, b):
    return lax.dot_general(a, b, (((1,), (1,)), ((), ())), preferred_element_type=f32)


def transposed(v):
    return v.astype(f32).T.astype(bf16)


def swap_halves(first, second):
    lane = lax.broadcasted_iota(jnp.int32, first.shape, 1)
    low = lane < HD
    first, second = first.astype(f32), second.astype(f32)
    return (
        jnp.where(low, first, pltpu.roll(second, HD, 1)).astype(bf16),
        jnp.where(low, pltpu.roll(first, HD, 1), second).astype(bf16),
    )


class Place:
    def __init__(self):
        self.s = lax.axis_index("seq")
        self.r = lax.axis_index("row")
        self.y_lo = lax.div(self.s, 16)
        self.head = lax.rem(self.s, 16)
        self.y_hi = lax.div(self.r, 2)
        self.core = lax.rem(self.r, 2)
        tile = lax.div(self.s, 4)
        self.block_core = lax.rem(lax.div(tile + 1, 2), 2)
        self.slot = lax.div(self.s, 8) * 4 + lax.rem(self.s, 4)
        self.partner = (self.s, self.r + 1 - 2 * self.core)
        self.self_served = jnp.logical_and(self.y_lo == self.core, self.block_core == self.core)
        self.self_count = jnp.where(self.self_served, 1, 0)

    def head_device(self, h):
        return (self.core * 16 + h, self.y_hi * 2 + self.block_core)

    def own_tile(self, j, core=None):
        core = self.core if core is None else core
        return 2 * j + lax.rem(j + core, 2)

    def own_block(self, n):
        return self.own_tile(lax.div(n, 4)) * 4 + lax.rem(n, 4)

    def block_device(self, n):
        return (self.own_block(n), self.y_hi * 2 + self.y_lo)

    def is_self(self, device):
        return jnp.logical_and(device[0] == self.s, device[1] == self.r)


def remote(src, dst, send, recv, device):
    return pltpu.make_async_remote_copy(
        src_ref=src, dst_ref=dst, send_sem=send, recv_sem=recv, device_id=device, device_id_type=MESH
    )


def send_to(place, src, dst, send, recv, device):
    own = place.is_self(device)

    @pl.when(own)
    def _():
        pltpu.make_async_copy(src, dst, recv).start()

    @pl.when(jnp.logical_not(own))
    def _():
        remote(src, dst, send, recv, device).start()


def sent_to(place, src, dst, send, recv, device):
    @pl.when(jnp.logical_not(place.is_self(device)))
    def _():
        remote(src, dst, send, recv, device).wait_send()


def arrived(dst, recv):
    pltpu.make_async_copy(dst, dst, recv).wait()


def greet(barrier, device):
    pl.semaphore_signal(barrier, inc=1, device_id=device, device_id_type=MESH)


def greet_all(place, barrier, device_of):
    def one(n, carry):
        device = device_of(n)

        @pl.when(jnp.logical_not(place.is_self(device)))
        def _():
            greet(barrier, device)

        return carry

    lax.fori_loop(0, 16, one, 0)


def loop(count, body):
    def one(n, carry):
        body(n)
        return carry

    lax.fori_loop(0, count, one, 0)


def params(collective_id):
    return pltpu.CompilerParams(
        collective_id=collective_id, has_side_effects=True, vmem_limit_bytes=VMEM_LIMIT
    )


def qkv_kernel(x_ref, seg_ref, gain_ref, w_ref, pk_ref, w_scr, stage, w_sem, send, recv, fsend, frecv):
    place = Place()

    def weight(g, part):
        return pltpu.make_async_copy(
            w_ref.at[:, pl.ds(part * D + g * 256, 256)], w_scr.at[g, part], w_sem.at[g, part]
        )

    for g in range(4):
        for part in range(3):
            weight(g, part).start()
    barrier = pltpu.get_barrier_semaphore()
    greet_all(place, barrier, place.block_device)
    greet(barrier, place.partner)

    x = x_ref[0].astype(f32)
    a = (x * lax.rsqrt(jnp.mean(x * x, axis=-1, keepdims=True) + EPS) * gain_ref[...]).astype(bf16)
    seg = seg_ref[...].astype(f32)
    row = lax.broadcasted_iota(jnp.int32, (16, 128), 0)
    rest = jnp.concatenate([seg[:, 128:T], jnp.zeros((1, 256 - T), f32)], axis=1)
    seg_tile = jnp.where(row == 0, seg[:, :128], jnp.where(row == 1, rest, 0.0)).astype(bf16)
    pl.semaphore_wait(barrier, 17 - place.self_count)

    for g in range(4):
        for part in range(3):
            weight(g, part).wait()
        q = dot(a, w_scr[g, 0]) * (SCALE * LOG2E)
        k = dot(a, w_scr[g, 1])
        v = dot(a, w_scr[g, 2])
        for m in range(2):
            lanes = slice(128 * m, 128 * m + 128)
            h = 4 * g + 2 * m
            kv = swap_halves(k[:, lanes].astype(bf16), v[:, lanes].astype(bf16))
            qq = q[:, lanes].astype(bf16)
            qp = swap_halves(qq[:HT], qq[HT:])
            for e in range(2):
                stage[h + e, 0:T] = kv[e]
                stage[h + e, T : T + HT] = qp[e]
                stage[h + e, T + HT : PACK] = seg_tile
                send_to(
                    place, stage.at[h + e], pk_ref.at[place.s], send.at[h + e], recv.at[place.slot],
                    place.head_device(h + e),
                )

    def forward(n):
        i = place.own_block(n)
        return remote(pk_ref.at[i], pk_ref.at[i], fsend.at[n], frecv.at[n], place.partner)

    def pass_on(n):
        arrived(pk_ref.at[place.own_block(n)], recv.at[n])
        forward(n).start()

    loop(16, pass_on)

    def finish(n):
        sent_to(
            place, stage.at[n], pk_ref.at[place.s], send.at[n], recv.at[place.slot], place.head_device(n)
        )
        forward(n).wait_send()
        forward(n).wait_recv()

    loop(16, finish)


def qkv_call(frames, segment_ids, gain, w_qkv):
    return pl.pallas_call(
        qkv_kernel,
        name="qkv_to_heads",
        out_shape=jax.ShapeDtypeStruct((BLOCKS, PACK, 128), bf16),
        in_specs=[VM, VM, VM, ANY],
        out_specs=ANY,
        scratch_shapes=[
            pltpu.VMEM((4, 3, D, 256), bf16),
            pltpu.VMEM((16, PACK, 128), bf16),
            pltpu.SemaphoreType.DMA((4, 3)),
            pltpu.SemaphoreType.DMA((16,)),
            pltpu.SemaphoreType.DMA((16,)),
            pltpu.SemaphoreType.DMA((16,)),
            pltpu.SemaphoreType.DMA((16,)),
        ],
        compiler_params=params(0),
    )(frames, segment_ids, gain, w_qkv)


def seg_parts(pk_ref, block):
    tile = pk_ref[block, T + HT : PACK].astype(f32)
    first, second = tile[0:1], tile[1:2]
    row = jnp.concatenate([first, second[:, : T - 128]], axis=1)
    column = jnp.concatenate(
        [
            jnp.broadcast_to(first, (128, 128)).T,
            jnp.broadcast_to(second, (128, 128)).T[: T - 128],
        ],
        axis=0,
    )
    return row, column


def fill_segments(pk_ref, seg_row, seg_col):
    row0, col0 = seg_parts(pk_ref, 0)
    row7, col7 = seg_parts(pk_ref, BLOCKS - 1)
    common = row0[:, T - 1 : T]
    common_row = jnp.broadcast_to(common, (1, TILE - T))
    common_col = jnp.broadcast_to(common, (TILE - T, 128))
    seg_row[0, 0:1] = jnp.concatenate([row0, common_row], axis=1)
    seg_row[1, 0:1] = jnp.broadcast_to(common, (1, TILE))
    seg_row[2, 0:1] = jnp.concatenate([common_row, row7], axis=1)
    seg_col[0] = jnp.concatenate([col0, common_col], axis=0)
    seg_col[1] = jnp.broadcast_to(common, (TILE, 128))
    seg_col[2] = jnp.concatenate([common_col, col7], axis=0)


def seg_kind(tile):
    return jnp.where(tile == 0, 0, jnp.where(tile == TILES - 1, 2, 1))


def allowed_pairs(seg_row, seg_col, q_tile, k_tile):
    rows = seg_row[pl.ds(seg_kind(q_tile), 1), 0:1][0]
    columns = seg_col[pl.ds(seg_kind(k_tile), 1)][0][:, 0:1]
    pos_k = k_tile * TILE + lax.broadcasted_iota(jnp.int32, (TILE, TILE), 0)
    pos_q = q_tile * TILE + lax.broadcasted_iota(jnp.int32, (TILE, TILE), 1)
    return jnp.logical_and(columns == rows, pos_k <= pos_q)


def load_queries(pk_ref, tile, qp):
    lane = lax.broadcasted_iota(jnp.int32, (HT, 128), 1)
    for b in range(4):
        packed = pk_ref[tile * 4 + b, T : T + HT].astype(f32)
        qp[b * T : b * T + HT] = jnp.where(lane < HD, packed, 0.0).astype(bf16)
        qp[b * T + HT : b * T + T] = jnp.where(lane < HD, pltpu.roll(packed, HD, 1), 0.0).astype(bf16)


def load_keys(pk_ref, tile):
    return pk_ref[pl.ds(tile * 4, 4), 0:T].reshape(TILE, 128)


def packed_rows(value_t, b):
    twice = jnp.concatenate([value_t, value_t], axis=0)[:, b * T : (b + 1) * T]
    return twice


def pack_transposed(value_t):
    both = jnp.concatenate([value_t, value_t], axis=0).T
    lane = lax.broadcasted_iota(jnp.int32, (HT, 128), 1)
    return [
        jnp.where(lane < HD, both[b * T : b * T + HT], both[b * T + HT : b * T + T]).astype(bf16)
        for b in range(4)
    ]


def forward_kernel(pk_ref, o_in, lse_ref, ot_ref, vt, qp, top, acc, seg_row, seg_col, stage, send, recv):
    place = Place()
    barrier = pltpu.get_barrier_semaphore()
    greet_all(place, barrier, place.head_device)
    fill_segments(pk_ref, seg_row, seg_col)
    one = jnp.where(lax.broadcasted_iota(jnp.int32, (16, TILE), 0) == 0, 1.0, 0.0).astype(bf16)

    def prepare(t):
        vt[t, 0:HD] = transposed(load_keys(pk_ref, t))[HD:]
        vt[t, HD : HD + 16] = one

    loop(TILES, prepare)
    pl.semaphore_wait(barrier, 16 - place.self_count)

    def step(q_tile, k_tile, masked):
        scores = dot_nt(load_keys(pk_ref, k_tile), qp[...])
        if masked:
            scores = jnp.where(allowed_pairs(seg_row, seg_col, q_tile, k_tile), scores, NEG)
        peak = jnp.maximum(top[...], jnp.max(scores, axis=0, keepdims=True))
        fade = jnp.exp2(top[...] - peak)
        top[...] = peak
        weights = jnp.exp2(scores - peak).astype(bf16)
        acc[...] = acc[...] * fade + dot(vt[k_tile], weights)

    def q_loop(n):
        j = 3 - n
        q_tile = place.own_tile(j)
        load_queries(pk_ref, q_tile, qp)
        top[...] = jnp.full((1, TILE), NEG, f32)
        acc[...] = jnp.zeros((HD + 16, TILE), f32)
        step(q_tile, q_tile, True)

        def k_loop(k_tile, carry):
            plain = jnp.logical_and(k_tile > 0, q_tile < TILES - 1)

            @pl.when(plain)
            def _():
                step(q_tile, k_tile, False)

            @pl.when(jnp.logical_not(plain))
            def _():
                step(q_tile, k_tile, True)

            return carry

        lax.fori_loop(0, q_tile, k_loop, 0)
        total = acc[HD : HD + 1]
        out_t = acc[0:HD] / total
        lse_ref[j, 0:1] = top[...] + jnp.log2(total)
        ot_ref[j] = out_t
        packed = pack_transposed(out_t)
        for b in range(4):
            m = j * 4 + b
            stage[m] = packed[b]
            send_to(
                place, stage.at[m], o_in.at[place.head], send.at[m], recv.at[place.head],
                place.block_device(m),
            )

    loop(4, q_loop)

    def finish(n):
        sent_to(
            place, stage.at[n], o_in.at[place.head], send.at[n], recv.at[place.head], place.block_device(n)
        )
        arrived(o_in.at[n], recv.at[n])

    loop(16, finish)


def forward_call(pk):
    return pl.pallas_call(
        forward_kernel,
        name="attention",
        out_shape=(
            jax.ShapeDtypeStruct((16, HT, 128), bf16),
            jax.ShapeDtypeStruct((4, 1, TILE), f32),
            jax.ShapeDtypeStruct((4, HD, TILE), f32),
        ),
        in_specs=[VM],
        out_specs=(ANY, VM, VM),
        scratch_shapes=[
            pltpu.VMEM((TILES, HD + 16, TILE), bf16),
            pltpu.VMEM((TILE, 128), bf16),
            pltpu.VMEM((1, TILE), f32),
            pltpu.VMEM((HD + 16, TILE), f32),
            pltpu.VMEM((3, 1, TILE), f32),
            pltpu.VMEM((3, TILE, 128), f32),
            pltpu.VMEM((16, HT, 128), bf16),
            pltpu.SemaphoreType.DMA((16,)),
            pltpu.SemaphoreType.DMA((16,)),
        ],
        compiler_params=params(1),
    )(pk)


FIRST = lambda c: ((c + 1) // 2) % 2
SECOND = lambda c: c // 2


def chip_bits(x, y, z):
    return [FIRST(x), FIRST(y), FIRST(z), SECOND(x), SECOND(y), SECOND(z)]


def position(part, y_lo, x, z, y_hi):
    bits = chip_bits(x, y_hi * 2 + y_lo, z)
    at = 0
    for k in range(6):
        at = at * 2 + bits[(part + k) % 6]
    return at


class Halving:
    START = [0, 32, 48, 56, 60, 62]

    def __init__(self, place, grads, each, acc, land, keep_sem, send, recv):
        self.place, self.grads, self.each = place, grads, each
        self.acc, self.land, self.keep_sem, self.send, self.recv = acc, land, keep_sem, send, recv
        x, z = lax.div(place.head, 4), lax.rem(place.head, 4)
        y = place.y_hi * 2 + place.y_lo
        self.bits = [
            lax.rem(lax.div(x + 1, 2), 2), lax.rem(lax.div(y + 1, 2), 2), lax.rem(lax.div(z + 1, 2), 2),
            lax.div(x, 2), lax.div(y, 2), lax.div(z, 2),
        ]

        def device(x, y, z):
            return (lax.rem(y, 2) * 16 + x * 4 + z, lax.div(y, 2) * 2 + place.core)

        flip = lambda c: c + 1 - 2 * lax.rem(c, 2)
        self.neighbours = [
            device(flip(x), y, z), device(x, flip(y), z), device(x, y, flip(z)),
            device(3 - x, y, z), device(x, 3 - y, z), device(x, y, 3 - z),
        ]

    def greet(self, barrier):
        for device in self.neighbours:
            greet(barrier, device)

    def bit(self, part, stage):
        return self.bits[(part + stage) % 6]

    def units(self, part):
        return pl.ds(part * self.each, self.each)

    def kept(self, part):
        return pltpu.make_async_copy(
            self.grads.at[self.units(part), pl.ds(self.bit(part, 0) * 32, 32)],
            self.acc.at[self.units(part)],
            self.keep_sem.at[part],
        )

    def hop(self, part, stage):
        half = 32 >> stage
        if stage == 0:
            source = self.grads.at[self.units(part), pl.ds((1 - self.bit(part, 0)) * 32, 32)]
        else:
            base = self.base(part, stage - 1) + (1 - self.bit(part, stage)) * half
            source = self.acc.at[self.units(part), pl.ds(base, half)]
        return remote(
            source,
            self.land.at[self.units(part), pl.ds(self.START[stage], half)],
            self.send.at[part, stage],
            self.recv.at[part, stage],
            self.neighbours[(part + stage) % 6],
        )

    def base(self, part, stage):
        at = 0
        for k in range(1, stage + 1):
            at = at + self.bit(part, k) * (32 >> k)
        return at

    def start(self, part):
        self.hop(part, 0).start()
        self.kept(part).start()

    def add(self, part, base, landed, count):
        group = min(count, 4)

        def body(i):
            here = pl.ds(base + i * group, group)
            there = pl.ds(landed + i * group, group)
            total = self.acc[self.units(part), here].astype(f32) + self.land[self.units(part), there].astype(f32)
            self.acc[self.units(part), here] = total.astype(bf16)

        loop(count // group, body)

    def advance(self, part, stage):
        self.hop(part, stage).wait_recv()
        if stage == 0:
            self.kept(part).wait()
        half = 16 >> stage
        base = self.base(part, stage)
        bit = self.bit(part, stage + 1)
        self.add(part, base + (1 - bit) * half, self.START[stage] + (1 - bit) * half, half)
        self.hop(part, stage + 1).start()
        self.add(part, base + bit * half, self.START[stage] + bit * half, half)

    def last(self, part):
        self.hop(part, 5).wait_recv()
        base = self.base(part, 5)
        return (
            self.acc[self.units(part), pl.ds(base, 1)].astype(f32)
            + self.land[self.units(part), pl.ds(62, 1)].astype(f32)
        )[:, 0]

    def finish(self):
        for part in range(6):
            for stage in range(6):
                self.hop(part, stage).wait_send()


def halving_scratch(units, width):
    return [
        pltpu.VMEM((units, 32, 16, width), bf16),
        pltpu.VMEM((units, 64, 16, width), bf16),
        pltpu.SemaphoreType.DMA((6,)),
        pltpu.SemaphoreType.DMA((6, 6)),
        pltpu.SemaphoreType.DMA((6, 6)),
    ]


class MidSums:
    def __init__(self, place, fin, side, down, sem, up_out, out_out, down_out):
        self.place, self.fin, self.side, self.down, self.sem = place, fin, side, down, sem
        self.up_out, self.out_out, self.down_out = up_out, out_out, down_out

    def targets(self):
        return [(self.place.core * 16 + self.place.head, self.place.y_hi * 2 + k) for k in range(2)]

    def sources(self):
        return [(m * 16 + self.place.head, self.place.y_hi * 2 + self.place.y_lo) for m in range(2)]

    def self_count(self):
        return jnp.where(self.place.y_lo == self.place.core, 1, 0)

    def greet(self, barrier):
        greet(barrier, self.place.partner)
        for device in self.sources():

            @pl.when(jnp.logical_not(self.place.is_self(device)))
            def _(device=device):
                greet(barrier, device)

    def greetings(self):
        return 3 - self.self_count()

    def store(self, part, value):
        for u in range(3):
            self.fin[part * 3 + u] = value[u].reshape(2, 8, 256)

    def aside(self):
        return remote(
            self.fin.at[0:10, 1 - self.place.core], self.side, self.sem.at[0], self.sem.at[1], self.place.partner
        )

    def down_hop(self, k):
        return (
            self.fin.at[10 + 4 * k : 14 + 4 * k],
            self.down.at[self.place.y_lo],
            self.sem.at[2 + k],
            self.sem.at[4 + self.place.y_lo],
            self.targets()[k],
        )

    def run(self):
        place = self.place
        self.aside().start()
        for k in range(2):
            send_to(place, *self.down_hop(k))
        self.aside().wait_recv()
        mine, other = place.core, 1 - place.core
        for u in range(8):
            self.up_out[:, pl.ds(mine * 2048 + u * 256, 256)] = self.fin[u, mine]
            self.up_out[:, pl.ds(other * 2048 + u * 256, 256)] = self.side[u]
        for u in range(2):
            self.out_out[:, pl.ds(mine * 512 + u * 256, 256)] = self.fin[8 + u, mine]
            self.out_out[:, pl.ds(other * 512 + u * 256, 256)] = self.side[8 + u]
        for m in range(2):
            arrived(self.down.at[m], self.sem.at[4 + m])
            for v in range(4):
                group, half = v // 2, v % 2
                self.down_out[group * 16 : group * 16 + 16, m * 512 + half * 256 : m * 512 + half * 256 + 256] = (
                    self.down[m, v].reshape(16, 256)
                )
        self.aside().wait_send()
        for k in range(2):
            sent_to(place, *self.down_hop(k))


def mid_scratch():
    return halving_scratch(18, 256) + [
        pltpu.VMEM((18, 2, 8, 256), f32),
        pltpu.VMEM((10, 8, 256), f32),
        pltpu.VMEM((2, 4, 2, 8, 256), f32),
        pltpu.SemaphoreType.DMA((6,)),
    ]


MID_OUT = (
    jax.ShapeDtypeStruct((8, FF), f32),
    jax.ShapeDtypeStruct((8, D), f32),
    jax.ShapeDtypeStruct((32, D), f32),
)


def mid_sums_kernel(grads, up_out, out_out, down_out, acc, land, keep_sem, hsend, hrecv, fin, side, down, sem):
    place = Place()
    halving = Halving(place, grads, 3, acc, land, keep_sem, hsend, hrecv)
    mid = MidSums(place, fin, side, down, sem, up_out, out_out, down_out)
    barrier = pltpu.get_barrier_semaphore()
    halving.greet(barrier)
    mid.greet(barrier)
    pl.semaphore_wait(barrier, 6 + mid.greetings())
    for part in range(6):
        halving.start(part)
    for stage in range(5):
        for part in range(6):
            halving.advance(part, stage)
    for part in range(6):
        mid.store(part, halving.last(part))
    mid.run()
    halving.finish()


def mid_sums_call(grads):
    return pl.pallas_call(
        mid_sums_kernel,
        name="sum_mid_grads",
        out_shape=MID_OUT,
        in_specs=[ANY],
        out_specs=(VM, VM, VM),
        scratch_shapes=mid_scratch(),
        compiler_params=params(5),
    )(grads)


ROOT = math.sqrt(2.0 / math.pi)
CUBE = 0.044715


def middle_kernel(
    o_in, x_ref, dy_ref, gain_ref, w_out, w_up, w_down,
    y_ref, grads, dx1_ref, gain_grad, da_in,
    wo, wu, wd, o2, b2, dm2, b2t, x1s, ysum, hsum, yside, hside, da_side, outg, gs, stage,
    w_sem, p_send, p_recv, g_sem, send, recv,
):
    place = Place()
    core = place.core

    def up_copy(j):
        at = pl.multiple_of(core * 2048 + j * 512, 512)
        return pltpu.make_async_copy(w_up.at[:, pl.ds(at, 512)], wu.at[j], w_sem.at[1 + j])

    def down_copy(j):
        at = pl.multiple_of(core * 2048 + j * 512, 512)
        return pltpu.make_async_copy(w_down.at[pl.ds(at, 512)], wd.at[j], w_sem.at[5 + j])

    out_copy = pltpu.make_async_copy(w_out, wo, w_sem.at[0])
    out_copy.start()
    for j in range(4):
        up_copy(j).start()
        down_copy(j).start()
    barrier = pltpu.get_barrier_semaphore()
    greet_all(place, barrier, place.block_device)
    greet(barrier, place.partner)

    def across(k, src, dst):
        return remote(src, dst, p_send.at[k], p_recv.at[k], place.partner)

    dm2[0:T] = dy_ref[0]
    for m in range(8):
        lo, hi = swap_halves(o_in[2 * m], o_in[2 * m + 1])
        o2[0:HT, 128 * m : 128 * m + 128] = lo
        o2[HT:T, 128 * m : 128 * m + 128] = hi
    pl.semaphore_wait(barrier, 17 - place.self_count)
    dm_hop = across(0, dm2.at[0:T], dm2.at[T : 2 * T])
    o_hop = across(1, o2.at[0:T], o2.at[T : 2 * T])
    dm_hop.start()
    o_hop.start()
    out_copy.wait()
    x1 = x_ref[0].astype(f32) + dot(o2[0:T], wo[...])
    x1s[...] = x1
    scale1 = lax.rsqrt(jnp.mean(x1 * x1, axis=-1, keepdims=True) + EPS)
    b2[0:T] = (x1 * scale1 * gain_ref[...]).astype(bf16)
    b_hop = across(2, b2.at[0:T], b2.at[T : 2 * T])
    b_hop.start()
    dm_hop.wait_recv()
    b_hop.wait_recv()
    b2t[...] = transposed(b2[...])

    for j in range(4):
        up_copy(j).wait()
        down_copy(j).wait()
        z = dot(b2[...], wu[j])
        zz = z * z
        th = jnp.tanh(ROOT * z * (1.0 + CUBE * zz))
        half = 0.5 * (1.0 + th)
        gz = (z * half).astype(bf16)
        slope = half + 0.5 * z * (1.0 - th * th) * (ROOT * (1.0 + 3.0 * CUBE * zz))
        dz = (dot_nt(dm2[...], wd[j]) * slope).astype(bf16)
        yj = dot(gz, wd[j])
        hj = dot_nt(dz, wu[j])
        if j == 0:
            ysum[...] = yj
            hsum[...] = hj
        else:
            ysum[...] += yj
            hsum[...] += hj
        up = dot(b2t[...], dz).astype(bf16)
        for u in range(2):
            unit = 2 * j + u
            for chip in range(64):
                y_lo, x, z_, y_hi = chip // 32, chip // 8 % 4, chip // 2 % 4, chip % 2
                gs[unit, position(unit // 3, y_lo, x, z_, y_hi)] = up[
                    chip * 16 : chip * 16 + 16, u * 256 : u * 256 + 256
                ]
            pltpu.make_async_copy(gs.at[unit], grads.at[unit], g_sem.at[unit]).start()
        down = dot(transposed(gz), dm2[...]).astype(bf16)
        for chip in range(8):
            for group in range(4):
                rows = slice(chip * 64 + group * 16, chip * 64 + group * 16 + 16)
                for y_lo in range(2):
                    for u in range(2):
                        unit = 10 + group * 2 + u
                        at = y_lo * 512 + u * 256
                        gs[unit, position(unit // 3, y_lo, j, chip // 2, chip % 2)] = down[rows, at : at + 256]
    for unit in range(10, 18):
        pltpu.make_async_copy(gs.at[unit], grads.at[unit], g_sem.at[unit]).start()

    y_hop = across(3, ysum.at[T : 2 * T], yside)
    h_hop = across(4, hsum.at[T : 2 * T], hside)
    h_hop.start()
    y_hop.start()
    h_hop.wait_recv()
    x1 = x1s[...]
    scale1 = lax.rsqrt(jnp.mean(x1 * x1, axis=-1, keepdims=True) + EPS)
    dh2 = hsum[0:T] + hside[...]
    gain_grad[...] = jnp.sum(dh2 * x1 * scale1, axis=0, keepdims=True)
    dn = dh2 * gain_ref[...]
    back = scale1 * dn - x1 * (scale1 * scale1 * scale1) * jnp.mean(dn * x1, axis=-1, keepdims=True)
    dx1 = dy_ref[0].astype(f32) + back
    dx1_ref[...] = dx1
    da = dx1.astype(bf16)
    da_side[0, 0:T] = da[:, 0:512]
    da_side[1, 0:T] = da[:, 512:1024]
    da_hop = across(5, da_side.at[1 - core, 0:T], da_side.at[1 - core, T : 2 * T])
    da_hop.start()
    for g in range(4):
        dattn = dot_nt(da, wo[256 * g : 256 * g + 256]).astype(bf16)
        for m in range(2):
            tile = dattn[:, 128 * m : 128 * m + 128]
            packed = swap_halves(tile[:HT], tile[HT:])
            for e in range(2):
                h = 4 * g + 2 * m + e
                stage[h] = packed[e]
                send_to(
                    place, stage.at[h], da_in.at[place.slot], send.at[h], recv.at[place.slot],
                    place.head_device(h),
                )
    y_hop.wait_recv()
    y_ref[0] = (x1 + ysum[0:T] + yside[...]).astype(bf16)
    o_hop.wait_recv()
    da_hop.wait_recv()
    out = dot(transposed(o2[...]), da_side[core]).astype(bf16)
    for u in range(2):
        unit = 8 + u
        for chip in range(64):
            y_lo, x, z_, y_hi = chip // 32, chip // 8 % 4, chip // 2 % 4, chip % 2
            gs[unit, position(unit // 3, y_lo, x, z_, y_hi)] = out[
                chip * 16 : chip * 16 + 16, u * 256 : u * 256 + 256
            ]
        pltpu.make_async_copy(gs.at[unit], grads.at[unit], g_sem.at[unit]).start()

    def finish(n):
        sent_to(
            place, stage.at[n], da_in.at[place.slot], send.at[n], recv.at[place.slot], place.head_device(n)
        )
        arrived(da_in.at[n], recv.at[n])

    loop(16, finish)
    for unit in range(18):
        pltpu.make_async_copy(gs.at[unit], grads.at[unit], g_sem.at[unit]).wait()
    for hop in (dm_hop, o_hop, b_hop, y_hop, h_hop, da_hop):
        hop.wait_send()


def middle_call(o_in, frames, out_grad, gain, w_out, w_up, w_down):
    return pl.pallas_call(
        middle_kernel,
        name="feed_forward",
        out_shape=(
            jax.ShapeDtypeStruct((1, T, D), bf16),
            jax.ShapeDtypeStruct((18, 64, 16, 256), bf16),
            jax.ShapeDtypeStruct((T, D), f32),
            jax.ShapeDtypeStruct((1, D), f32),
            jax.ShapeDtypeStruct((16, HT, 128), bf16),
        ),
        in_specs=[VM, VM, VM, VM, ANY, ANY, ANY],
        out_specs=(VM, ANY, VM, VM, ANY),
        scratch_shapes=[
            pltpu.VMEM((D, D), bf16),
            pltpu.VMEM((4, D, 512), bf16),
            pltpu.VMEM((4, 512, D), bf16),
            pltpu.VMEM((2 * T, D), bf16),
            pltpu.VMEM((2 * T, D), bf16),
            pltpu.VMEM((2 * T, D), bf16),
            pltpu.VMEM((D, 2 * T), bf16),
            pltpu.VMEM((T, D), f32),
            pltpu.VMEM((2 * T, D), f32),
            pltpu.VMEM((2 * T, D), f32),
            pltpu.VMEM((T, D), f32),
            pltpu.VMEM((T, D), f32),
            pltpu.VMEM((2, 2 * T, 512), bf16),
            pltpu.VMEM((8, 128), f32),
            pltpu.VMEM((18, 64, 16, 256), bf16),
            pltpu.VMEM((16, HT, 128), bf16),
            pltpu.SemaphoreType.DMA((9,)),
            pltpu.SemaphoreType.DMA((6,)),
            pltpu.SemaphoreType.DMA((6,)),
            pltpu.SemaphoreType.DMA((18,)),
            pltpu.SemaphoreType.DMA((16,)),
            pltpu.SemaphoreType.DMA((16,)),
        ],
        compiler_params=params(2),
    )(o_in, frames, out_grad, gain, w_out, w_up, w_down)


def backward_kernel(
    pk_ref, da_ref, lse_ref, ot_ref, dqkv_in,
    kt, qp, gp, delta, lse, dq, dkv, seg_row, seg_col, part, landed, stage,
    p_send, p_recv, send, recv,
):
    place = Place()
    barrier = pltpu.get_barrier_semaphore()
    greet_all(place, barrier, place.head_device)
    greet(barrier, place.partner)
    fill_segments(pk_ref, seg_row, seg_col)

    def prepare(t):
        kt[t] = transposed(load_keys(pk_ref, t))[:HD]
        dkv[t] = jnp.zeros((TILE, 128), f32)

    loop(TILES, prepare)

    def step(q_tile, k_tile, masked):
        keys = load_keys(pk_ref, k_tile)
        scores = dot_nt(keys, qp[...])
        if masked:
            scores = jnp.where(allowed_pairs(seg_row, seg_col, q_tile, k_tile), scores, NEG)
        weights = jnp.exp2(scores - lse[...])
        slopes = (weights * (dot_nt(keys, gp[...]) - delta[...])).astype(bf16)
        weights = weights.astype(bf16)
        dkv[k_tile] += dot(weights, gp[...]) + dot(slopes, qp[...])
        dq[...] += dot(kt[k_tile], slopes)

    def q_loop(n):
        j = 3 - n
        q_tile = place.own_tile(j)
        load_queries(pk_ref, q_tile, qp)
        lane = lax.broadcasted_iota(jnp.int32, (HT, 128), 1)
        for b in range(4):
            packed = da_ref[j * 4 + b].astype(f32)
            gp[b * T : b * T + HT] = jnp.where(lane < HD, 0.0, pltpu.roll(packed, HD, 1)).astype(bf16)
            gp[b * T + HT : b * T + T] = jnp.where(lane < HD, 0.0, packed).astype(bf16)
        delta[...] = jnp.sum(gp[...].astype(f32).T[HD:] * ot_ref[j], axis=0, keepdims=True)
        lse[...] = lse_ref[j, 0:1]
        dq[...] = jnp.zeros((HD, TILE), f32)
        step(q_tile, q_tile, True)

        def k_loop(k_tile, carry):
            plain = jnp.logical_and(k_tile > 0, q_tile < TILES - 1)

            @pl.when(plain)
            def _():
                step(q_tile, k_tile, False)

            @pl.when(jnp.logical_not(plain))
            def _():
                step(q_tile, k_tile, True)

            return carry

        lax.fori_loop(0, q_tile, k_loop, 0)
        packed = pack_transposed(dq[...] * SCALE)
        for b in range(4):
            stage[j * 4 + b, T:GRAD] = packed[b]

    loop(4, q_loop)

    factor = jnp.where(lax.broadcasted_iota(jnp.int32, (1, 128), 1) < HD, LN2, 1.0)
    pl.semaphore_wait(barrier, 17 - place.self_count)

    def part_hop(j):
        return remote(part.at[j], landed.at[j], p_send.at[j], p_recv.at[j], place.partner)

    def give(j):
        part[j] = (dkv[place.own_tile(j, 1 - place.core)] * factor).astype(bf16)
        part_hop(j).start()

    loop(4, give)

    def take(j):
        part_hop(j).wait_recv()
        total = dkv[place.own_tile(j)] * factor + landed[j].astype(f32)
        total = total.astype(bf16)
        for b in range(4):
            m = j * 4 + b
            stage[m, 0:T] = total[b * T : (b + 1) * T]
            send_to(
                place, stage.at[m], dqkv_in.at[place.head], send.at[m], recv.at[place.head],
                place.block_device(m),
            )

    loop(4, take)

    def finish(n):
        sent_to(
            place, stage.at[n], dqkv_in.at[place.head], send.at[n], recv.at[place.head],
            place.block_device(n),
        )
        arrived(dqkv_in.at[n], recv.at[n])

    loop(16, finish)
    loop(4, lambda j: part_hop(j).wait_send())


def backward_call(pk, da_in, lse, ot):
    return pl.pallas_call(
        backward_kernel,
        name="attention_grad",
        out_shape=jax.ShapeDtypeStruct((16, GRAD, 128), bf16),
        in_specs=[VM, VM, VM, VM],
        out_specs=ANY,
        scratch_shapes=[
            pltpu.VMEM((TILES, HD, TILE), bf16),
            pltpu.VMEM((TILE, 128), bf16),
            pltpu.VMEM((TILE, 128), bf16),
            pltpu.VMEM((1, TILE), f32),
            pltpu.VMEM((1, TILE), f32),
            pltpu.VMEM((HD, TILE), f32),
            pltpu.VMEM((TILES, TILE, 128), f32),
            pltpu.VMEM((3, 1, TILE), f32),
            pltpu.VMEM((3, TILE, 128), f32),
            pltpu.VMEM((4, TILE, 128), bf16),
            pltpu.VMEM((4, TILE, 128), bf16),
            pltpu.VMEM((16, GRAD, 128), bf16),
            pltpu.SemaphoreType.DMA((4,)),
            pltpu.SemaphoreType.DMA((4,)),
            pltpu.SemaphoreType.DMA((16,)),
            pltpu.SemaphoreType.DMA((16,)),
        ],
        compiler_params=params(3),
    )(pk, da_in, lse, ot)


def last_kernel(
    dqkv_in, x_ref, dx1_ref, gain_ref, gain2_ref, w_ref,
    dx_ref, qkv_out, gain_out, gain2_out, grads,
    w_scr, a2, dn, dhalf, a2t, fin, side, gstage, gacc, gland,
    acc, land, keep_sem, hsend, hrecv,
    w_sem, p_send, p_recv, g_sem, gs_send, gs_recv,
):
    place = Place()
    core = place.core
    halving = Halving(place, grads, 1, acc, land, keep_sem, hsend, hrecv)
    weight = pltpu.make_async_copy(w_ref, w_scr, w_sem.at[0])
    weight.start()
    barrier = pltpu.get_barrier_semaphore()
    halving.greet(barrier)
    greet(barrier, place.partner)

    def across(k, src, dst):
        return remote(src, dst, p_send.at[k], p_recv.at[k], place.partner)

    x = x_ref[0].astype(f32)
    scale = lax.rsqrt(jnp.mean(x * x, axis=-1, keepdims=True) + EPS)
    a2[0:T] = (x * scale * gain_ref[...]).astype(bf16)
    for m in range(8):
        lo, hi = swap_halves(dqkv_in[2 * m, T:GRAD], dqkv_in[2 * m + 1, T:GRAD])
        dk, dv = swap_halves(dqkv_in[2 * m, 0:T], dqkv_in[2 * m + 1, 0:T])
        dn[0:HT, 128 * m : 128 * m + 128] = lo
        dn[HT:T, 128 * m : 128 * m + 128] = hi
        dn[:, D + 128 * m : D + 128 * m + 128] = dk
        dn[:, 2 * D + 128 * m : 2 * D + 128 * m + 128] = dv
        at = 128 * (m % 4)
        dhalf[m // 4, 0:HT, at : at + 128] = lo
        dhalf[m // 4, HT:T, at : at + 128] = hi
        dhalf[m // 4, 0:T, 512 + at : 512 + at + 128] = dk
        dhalf[m // 4, 0:T, 1024 + at : 1024 + at + 128] = dv
    pl.semaphore_wait(barrier, 7)
    a_hop = across(0, a2.at[0:T], a2.at[T : 2 * T])
    d_hop = across(1, dhalf.at[1 - core, 0:T], dhalf.at[1 - core, T : 2 * T])
    a_hop.start()
    d_hop.start()
    a_hop.wait_recv()
    a2t[...] = transposed(a2[...])
    d_hop.wait_recv()
    for u in range(6):
        block = dot(a2t[...], dhalf[core, :, u * 256 : u * 256 + 256]).astype(bf16)
        for chip in range(64):
            y_lo, cx, z_, y_hi = chip // 32, chip // 8 % 4, chip // 2 % 4, chip % 2
            gstage[u, position(u, y_lo, cx, z_, y_hi)] = block[chip * 16 : chip * 16 + 16]
        pltpu.make_async_copy(gstage.at[u], grads.at[u], g_sem.at[u]).start()
    weight.wait()
    dh1 = dot_nt(dn[...], w_scr[...])
    gain1_grad = jnp.sum(dh1 * x * scale, axis=0, keepdims=True)
    dxn = dh1 * gain_ref[...]
    back = scale * dxn - x * (scale * scale * scale) * jnp.mean(dxn * x, axis=-1, keepdims=True)
    dx_ref[0] = (dx1_ref[...] + back).astype(bf16)

    row = lax.broadcasted_iota(jnp.int32, (128, D), 0)
    both = jnp.where(row == 0, gain1_grad, jnp.where(row == 1, gain2_ref[...], 0.0))
    columns = both.T.astype(bf16)
    for chip in range(64):
        y_lo, cx, z_, y_hi = chip // 32, chip // 8 % 4, chip // 2 % 4, chip % 2
        gacc[position(0, y_lo, cx, z_, y_hi)] = columns[chip * 16 : chip * 16 + 16]

    for u in range(6):
        pltpu.make_async_copy(gstage.at[u], grads.at[u], g_sem.at[u]).wait()
    for p in range(6):
        halving.start(p)

    def gain_hop(stage):
        half = 32 >> stage
        base = 0
        for k in range(stage):
            base = base + halving.bit(0, k) * (32 >> k)
        return base, remote(
            gacc.at[pl.ds(base + (1 - halving.bit(0, stage)) * half, half)],
            gland.at[pl.ds(Halving.START[stage], half)],
            gs_send.at[stage],
            gs_recv.at[stage],
            halving.neighbours[stage],
        )

    def gain_stage(stage):
        base, hop = gain_hop(stage)
        half = 32 >> stage
        hop.wait_recv()
        here = pl.ds(base + halving.bit(0, stage) * half, half)
        there = pl.ds(Halving.START[stage], half)
        gacc[here] = (gacc[here].astype(f32) + gland[there].astype(f32)).astype(bf16)
        if stage < 5:
            gain_hop(stage + 1)[1].start()

    gain_hop(0)[1].start()
    for stage in range(5):
        for p in range(6):
            halving.advance(p, stage)
        gain_stage(stage)
    gain_stage(5)
    for p in range(6):
        fin[p] = halving.last(p)[0].reshape(2, 8, 256)
    base = 0
    for k in range(6):
        base = base + halving.bit(0, k) * (32 >> k)
    gain_rows = gacc[pl.ds(base, 1)][0].astype(f32)
    pair = jnp.concatenate([gain_rows[0:8], gain_rows[8:16]], axis=1)
    fin[6] = jnp.concatenate([gain_rows, jnp.zeros((16, 128), f32)], axis=1).reshape(2, 8, 256)
    del pair
    aside = across(2, fin.at[:, 1 - core], side)
    aside.start()
    aside.wait_recv()
    mine, other = core, 1 - core
    for u in range(6):
        at = (u // 2) * D + (u % 2) * 256
        qkv_out[:, pl.ds(at + mine * 512, 256)] = fin[u, mine]
        qkv_out[:, pl.ds(at + other * 512, 256)] = side[u]
    sums = fin[6, mine][:, 0:128] + side[6][:, 0:128]
    wide = jnp.concatenate([sums] + [jnp.zeros((8, 128), f32)] * 15, axis=0).T
    gain_out[...] = wide[0:1]
    gain2_out[...] = wide[1:2]
    for hop in (a_hop, d_hop, aside):
        hop.wait_send()
    halving.finish()
    for stage in range(6):
        gain_hop(stage)[1].wait_send()


def last_call(dqkv_in, frames, dx1, gain, gain2_grad, w_qkv):
    return pl.pallas_call(
        last_kernel,
        name="input_grad",
        out_shape=(
            jax.ShapeDtypeStruct((1, T, D), bf16),
            jax.ShapeDtypeStruct((8, 3 * D), f32),
            jax.ShapeDtypeStruct((1, 128), f32),
            jax.ShapeDtypeStruct((1, 128), f32),
            jax.ShapeDtypeStruct((6, 64, 16, 256), bf16),
        ),
        in_specs=[VM, VM, VM, VM, VM, ANY],
        out_specs=(VM, VM, VM, VM, ANY),
        scratch_shapes=[
            pltpu.VMEM((D, 3 * D), bf16),
            pltpu.VMEM((2 * T, D), bf16),
            pltpu.VMEM((T, 3 * D), bf16),
            pltpu.VMEM((2, 2 * T, 1536), bf16),
            pltpu.VMEM((D, 2 * T), bf16),
            pltpu.VMEM((7, 2, 8, 256), f32),
            pltpu.VMEM((7, 8, 256), f32),
            pltpu.VMEM((6, 64, 16, 256), bf16),
            pltpu.VMEM((64, 16, 128), bf16),
            pltpu.VMEM((64, 16, 128), bf16),
        ]
        + halving_scratch(6, 256)
        + [
            pltpu.SemaphoreType.DMA((1,)),
            pltpu.SemaphoreType.DMA((3,)),
            pltpu.SemaphoreType.DMA((3,)),
            pltpu.SemaphoreType.DMA((6,)),
            pltpu.SemaphoreType.DMA((6,)),
            pltpu.SemaphoreType.DMA((6,)),
        ],
        compiler_params=params(4),
    )(dqkv_in, frames, dx1, gain, gain2_grad, w_qkv)


def shards(frames, segment_ids, norm1_gain, w_qkv, w_out, norm2_gain, w_up, w_down, out_grad):
    gain1, gain2 = norm1_gain[None], norm2_gain[None]
    pk = qkv_call(frames, segment_ids, gain1, w_qkv)
    o_in, lse, ot = forward_call(pk)
    y, grads, dx1, gain2_grad, da_in = middle_call(o_in, frames, out_grad, gain2, w_out, w_up, w_down)
    dqkv_in = backward_call(pk, da_in, lse, ot)
    up_sum, out_sum, down_sum = mid_sums_call(grads)
    dx, qkv_sum, gain1_sum, gain2_sum, _ = last_call(dqkv_in, frames, dx1, gain1, gain2_grad, w_qkv)
    return (y, dx, gain1_sum[0, 0:8], qkv_sum, out_sum, gain2_sum[0, 0:8], up_sum, down_sum)


def solution(mesh):
    return jax.shard_map(
        shards,
        mesh=mesh,
        in_specs=(
            P("row", "seq", None),
            P("row", "seq"),
            P(),
            P(),
            P(),
            P(),
            P(),
            P(),
            P("row", "seq", None),
        ),
        out_specs=(
            P("row", "seq", None),
            P("row", "seq", None),
            P(("seq", "row")),
            P(("seq", "row"), None),
            P(("seq", "row"), None),
            P(("seq", "row")),
            P(("seq", "row"), None),
            P(("seq", "row"), None),
        ),
        check_vma=False,
    )
```

```python
import functools
import math

import jax
import jax.numpy as jnp
from jax import lax
from jax.experimental import pallas as pl
from jax.experimental.pallas import tpu as pltpu
from jax.sharding import PartitionSpec as P

MESH = pl.DeviceIdType.MESH
f32 = jnp.float32
bf16 = jnp.bfloat16

D = 1024
H = 16
HD = 64
FF = 4096
T = 192
HT = T // 2
BLOCKS = 32
TILE = 768
TILES = 8
PACK = 304
GRAD = 288
EPS = 1e-05
NEG = -1e30
LOG2E = math.log2(math.e)
LN2 = math.log(2.0)
SCALE = HD**-0.5
VMEM_LIMIT = 60 * 1024 * 1024

ANY = pl.BlockSpec(memory_space=pl.ANY)
VM = pl.BlockSpec(memory_space=pltpu.VMEM)


def dot(a, b):
    return jnp.dot(a, b, preferred_element_type=f32)


def dot_nt(a, b):
    return lax.dot_general(a, b, (((1,), (1,)), ((), ())), preferred_element_type=f32)


def transposed(v):
    return v.astype(f32).T.astype(bf16)


def swap_halves(first, second):
    lane = lax.broadcasted_iota(jnp.int32, first.shape, 1)
    low = lane < HD
    first, second = first.astype(f32), second.astype(f32)
    return (
        jnp.where(low, first, pltpu.roll(second, HD, 1)).astype(bf16),
        jnp.where(low, pltpu.roll(first, HD, 1), second).astype(bf16),
    )


class Place:
    def __init__(self):
        self.s = lax.axis_index("seq")
        self.r = lax.axis_index("row")
        self.y_lo = lax.div(self.s, 16)
        self.head = lax.rem(self.s, 16)
        self.y_hi = lax.div(self.r, 2)
        self.core = lax.rem(self.r, 2)
        tile = lax.div(self.s, 4)
        self.block_core = lax.rem(lax.div(tile + 1, 2), 2)
        self.slot = lax.div(self.s, 8) * 4 + lax.rem(self.s, 4)
        self.partner = (self.s, self.r + 1 - 2 * self.core)
        self.self_served = jnp.logical_and(self.y_lo == self.core, self.block_core == self.core)
        self.self_count = jnp.where(self.self_served, 1, 0)

    def head_device(self, h):
        return (self.core * 16 + h, self.y_hi * 2 + self.block_core)

    def own_tile(self, j, core=None):
        core = self.core if core is None else core
        return 2 * j + lax.rem(j + core, 2)

    def own_block(self, n):
        return self.own_tile(lax.div(n, 4)) * 4 + lax.rem(n, 4)

    def block_device(self, n):
        return (self.own_block(n), self.y_hi * 2 + self.y_lo)

    def is_self(self, device):
        return jnp.logical_and(device[0] == self.s, device[1] == self.r)


def remote(src, dst, send, recv, device):
    return pltpu.make_async_remote_copy(
        src_ref=src, dst_ref=dst, send_sem=send, recv_sem=recv, device_id=device, device_id_type=MESH
    )


def send_to(place, src, dst, send, recv, device):
    own = place.is_self(device)

    @pl.when(own)
    def _():
        pltpu.make_async_copy(src, dst, recv).start()

    @pl.when(jnp.logical_not(own))
    def _():
        remote(src, dst, send, recv, device).start()


def sent_to(place, src, dst, send, recv, device):
    @pl.when(jnp.logical_not(place.is_self(device)))
    def _():
        remote(src, dst, send, recv, device).wait_send()


def arrived(dst, recv):
    pltpu.make_async_copy(dst, dst, recv).wait()


def greet(barrier, device):
    pl.semaphore_signal(barrier, inc=1, device_id=device, device_id_type=MESH)


def greet_all(place, barrier, device_of):
    def one(n, carry):
        device = device_of(n)

        @pl.when(jnp.logical_not(place.is_self(device)))
        def _():
            greet(barrier, device)

        return carry

    lax.fori_loop(0, 16, one, 0)


def loop(count, body):
    def one(n, carry):
        body(n)
        return carry

    lax.fori_loop(0, count, one, 0)


def params(collective_id):
    return pltpu.CompilerParams(
        collective_id=collective_id, has_side_effects=True, vmem_limit_bytes=VMEM_LIMIT
    )


def qkv_kernel(x_ref, seg_ref, gain_ref, w_ref, pk_ref, w_scr, stage, w_sem, send, recv, fsend, frecv):
    place = Place()

    def weight(g, part):
        return pltpu.make_async_copy(
            w_ref.at[:, pl.ds(part * D + g * 256, 256)], w_scr.at[g, part], w_sem.at[g, part]
        )

    for g in range(4):
        for part in range(3):
            weight(g, part).start()
    barrier = pltpu.get_barrier_semaphore()
    greet_all(place, barrier, place.block_device)
    greet(barrier, place.partner)

    x = x_ref[0].astype(f32)
    a = (x * lax.rsqrt(jnp.mean(x * x, axis=-1, keepdims=True) + EPS) * gain_ref[...]).astype(bf16)
    seg = seg_ref[...].astype(f32)
    row = lax.broadcasted_iota(jnp.int32, (16, 128), 0)
    rest = jnp.concatenate([seg[:, 128:T], jnp.zeros((1, 256 - T), f32)], axis=1)
    seg_tile = jnp.where(row == 0, seg[:, :128], jnp.where(row == 1, rest, 0.0)).astype(bf16)
    pl.semaphore_wait(barrier, 17 - place.self_count)

    for g in range(4):
        for part in range(3):
            weight(g, part).wait()
        q = dot(a, w_scr[g, 0]) * (SCALE * LOG2E)
        k = dot(a, w_scr[g, 1])
        v = dot(a, w_scr[g, 2])
        for m in range(2):
            lanes = slice(128 * m, 128 * m + 128)
            h = 4 * g + 2 * m
            kv = swap_halves(k[:, lanes].astype(bf16), v[:, lanes].astype(bf16))
            qq = q[:, lanes].astype(bf16)
            qp = swap_halves(qq[:HT], qq[HT:])
            for e in range(2):
                stage[h + e, 0:T] = kv[e]
                stage[h + e, T : T + HT] = qp[e]
                stage[h + e, T + HT : PACK] = seg_tile
                send_to(
                    place, stage.at[h + e], pk_ref.at[place.s], send.at[h + e], recv.at[place.slot],
                    place.head_device(h + e),
                )

    def forward(n):
        i = place.own_block(n)
        return remote(pk_ref.at[i], pk_ref.at[i], fsend.at[n], frecv.at[n], place.partner)

    def pass_on(n):
        arrived(pk_ref.at[place.own_block(n)], recv.at[n])
        forward(n).start()

    loop(16, pass_on)

    def finish(n):
        sent_to(
            place, stage.at[n], pk_ref.at[place.s], send.at[n], recv.at[place.slot], place.head_device(n)
        )
        forward(n).wait_send()
        forward(n).wait_recv()

    loop(16, finish)


def qkv_call(frames, segment_ids, gain, w_qkv):
    return pl.pallas_call(
        qkv_kernel,
        name="qkv_to_heads",
        out_shape=jax.ShapeDtypeStruct((BLOCKS, PACK, 128), bf16),
        in_specs=[VM, VM, VM, ANY],
        out_specs=ANY,
        scratch_shapes=[
            pltpu.VMEM((4, 3, D, 256), bf16),
            pltpu.VMEM((16, PACK, 128), bf16),
            pltpu.SemaphoreType.DMA((4, 3)),
            pltpu.SemaphoreType.DMA((16,)),
            pltpu.SemaphoreType.DMA((16,)),
            pltpu.SemaphoreType.DMA((16,)),
            pltpu.SemaphoreType.DMA((16,)),
        ],
        compiler_params=params(0),
    )(frames, segment_ids, gain, w_qkv)


def seg_column(pk_ref, block):
    tile = pk_ref[block, T + HT : PACK].astype(f32)
    return jnp.concatenate(
        [
            jnp.broadcast_to(tile[0:1], (128, 128)).T,
            jnp.broadcast_to(tile[1:2], (128, 128)).T[: T - 128],
        ],
        axis=0,
    )


def fill_segments(pk_ref, seg):
    first = seg_column(pk_ref, 0)
    last = seg_column(pk_ref, BLOCKS - 1)
    common = jnp.broadcast_to(first[T - 1 : T], (TILE, 128))
    seg[0] = common
    seg[1] = common
    seg[2] = common
    seg[0, 0:T] = first
    seg[2, TILE - T : TILE] = last


def seg_kind(tile):
    return jnp.where(tile == 0, 0, jnp.where(tile == TILES - 1, 2, 1))


def fill_operands(place, pk_ref, seg, keys, queries):
    fill_segments(pk_ref, seg)
    lane = lax.broadcasted_iota(jnp.int32, (TILE, 128), 1)
    number = lane.astype(f32)

    def key_tile(t):
        keys[t, :, 0:128] = load_keys(pk_ref, t)
        keys[t, :, 128:256] = jnp.where(seg[seg_kind(t)] == number, 1.0, 0.0).astype(bf16)

    loop(TILES, key_tile)
    low = lax.broadcasted_iota(jnp.int32, (HT, 128), 1) < HD

    def query_tile(j):
        tile = place.own_tile(j)
        for b in range(4):
            packed = pk_ref[tile * 4 + b, T : T + HT].astype(f32)
            queries[j, b * T : b * T + HT, 0:128] = jnp.where(low, packed, 0.0).astype(bf16)
            queries[j, b * T + HT : b * T + T, 0:128] = jnp.where(low, pltpu.roll(packed, HD, 1), 0.0).astype(bf16)
        other = jnp.logical_and(lane < 8, seg[seg_kind(tile)] != number)
        queries[j, :, 128:256] = jnp.where(other, NEG, 0.0).astype(bf16)

    loop(4, query_tile)


STEPS = 18
HOOKS = (6, 8, 10, 12, 14, 16, 17)


def walk(place, n):
    turn = lax.div(place.head, 4)
    j, start, end = lax.rem(turn, 4), 0, 0
    end = place.own_tile(j) + 1
    for k in range(1, 4):
        past = n >= end
        following = lax.rem(turn + k, 4)
        j = jnp.where(past, following, j)
        start = jnp.where(past, end, start)
        end = jnp.where(past, end + place.own_tile(following) + 1, end)
    at = n - start
    k_tile = jnp.where(at == 0, place.own_tile(j), at - 1)
    return j, k_tile, at == 0, n + 1 == end


def key_order(place, i):
    turn = lax.div(place.head, 4)
    return jnp.where(i == 7, 0, 7 - lax.rem(i + 2 * turn, 7))


def causal(scores):
    k = lax.broadcasted_iota(jnp.int32, scores.shape, 0)
    q = lax.broadcasted_iota(jnp.int32, scores.shape, 1)
    return jnp.where(k <= q, scores, NEG)


def load_keys(pk_ref, tile):
    return pk_ref[pl.ds(tile * 4, 4), 0:T].reshape(TILE, 128)


def pack_transposed(value_t):
    both = jnp.concatenate([value_t, value_t], axis=0).T
    lane = lax.broadcasted_iota(jnp.int32, (HT, 128), 1)
    return [
        jnp.where(lane < HD, both[b * T : b * T + HT], both[b * T + HT : b * T + T]).astype(bf16)
        for b in range(4)
    ]


def forward_kernel(
    pk_ref, o_in, lse_ref, ot_ref, seg, keys, queries, vt, top, acc, even, odd, stage, send, recv
):
    place = Place()
    barrier = pltpu.get_barrier_semaphore()
    greet_all(place, barrier, place.head_device)
    fill_operands(place, pk_ref, seg, keys, queries)
    one = jnp.where(lax.broadcasted_iota(jnp.int32, (16, TILE), 0) == 0, 1.0, 0.0).astype(bf16)

    def prepare(t):
        vt[t, 0:HD] = transposed(keys[t, :, 0:128])[HD:]
        vt[t, HD : HD + 16] = one

    loop(TILES, prepare)
    pl.semaphore_wait(barrier, 16 - place.self_count)

    def score(n, scores):
        j, k_tile, _, _ = walk(place, jnp.minimum(n, STEPS - 1))
        scores[...] = dot_nt(keys[k_tile], queries[j])

    def body(n, now, later):
        j, k_tile, first, last = walk(place, n)

        @pl.when(first)
        def _():
            score(n + 1, later)
            scores = causal(now[...])
            peak = jnp.max(scores, axis=0, keepdims=True)
            top[...] = peak
            acc[...] = dot(vt[k_tile], jnp.exp2(scores - peak).astype(bf16))

        @pl.when(jnp.logical_not(first))
        def _():
            score(n + 1, later)
            scores = now[...]
            peak = jnp.maximum(top[...], jnp.max(scores, axis=0, keepdims=True))
            fade = jnp.exp2(top[...] - peak)
            top[...] = peak
            acc[...] = acc[...] * fade + dot(vt[k_tile], jnp.exp2(scores - peak).astype(bf16))

        @pl.when(last)
        def _():
            total = acc[HD : HD + 1]
            out_t = acc[0:HD] / total
            lse_ref[j] = top[...] + jnp.log2(total)
            ot_ref[j] = out_t
            packed = pack_transposed(out_t)
            for b in range(4):
                m = j * 4 + b
                stage[m] = packed[b]
                send_to(
                    place, stage.at[m], o_in.at[place.head], send.at[m], recv.at[place.head],
                    place.block_device(m),
                )

    score(0, even)

    def pair(i):
        body(2 * i, even, odd)
        body(2 * i + 1, odd, even)

    loop(STEPS // 2, pair)

    def finish(n):
        sent_to(
            place, stage.at[n], o_in.at[place.head], send.at[n], recv.at[place.head], place.block_device(n)
        )
        arrived(o_in.at[n], recv.at[n])

    loop(16, finish)


def forward_call(pk):
    return pl.pallas_call(
        forward_kernel,
        name="attention",
        out_shape=(
            jax.ShapeDtypeStruct((16, HT, 128), bf16),
            jax.ShapeDtypeStruct((4, 1, TILE), f32),
            jax.ShapeDtypeStruct((4, HD, TILE), f32),
        ),
        in_specs=[VM],
        out_specs=(ANY, VM, VM),
        scratch_shapes=[
            pltpu.VMEM((3, TILE, 128), f32),
            pltpu.VMEM((TILES, TILE, 256), bf16),
            pltpu.VMEM((4, TILE, 256), bf16),
            pltpu.VMEM((TILES, HD + 16, TILE), bf16),
            pltpu.VMEM((1, TILE), f32),
            pltpu.VMEM((HD + 16, TILE), f32),
            pltpu.VMEM((TILE, TILE), f32),
            pltpu.VMEM((TILE, TILE), f32),
            pltpu.VMEM((16, HT, 128), bf16),
            pltpu.SemaphoreType.DMA((16,)),
            pltpu.SemaphoreType.DMA((16,)),
        ],
        compiler_params=params(1),
    )(pk)


FIRST = lambda c: ((c + 1) // 2) % 2
SECOND = lambda c: c // 2


def chip_bits(x, y, z):
    return [FIRST(x), FIRST(y), FIRST(z), SECOND(x), SECOND(y), SECOND(z)]


def position(part, y_lo, x, z, y_hi):
    bits = chip_bits(x, y_hi * 2 + y_lo, z)
    at = 0
    for k in range(6):
        at = at * 2 + bits[(part + k) % 6]
    return at


class Part:
    def __init__(self, net, acc, land, at, count, turn, first, send, recv):
        self.net, self.acc, self.land, self.turn, self.first = net, acc, land, turn, first
        self.units = pl.ds(at, count)
        self.count, self.send, self.recv = count, send, recv

    def bit(self, stage):
        return self.net.bits[(self.turn + stage) % 6]

    def base(self, stage):
        at = 0
        for k in range(self.first, stage + 1):
            at = at + self.bit(k) * (32 >> k)
        return at

    def landing(self, stage):
        return sum(32 >> k for k in range(self.first, stage))

    def hop(self, stage):
        half = 32 >> stage
        base = self.base(stage - 1) + (1 - self.bit(stage)) * half
        return remote(
            self.acc.at[self.units, pl.ds(base, half)],
            self.land.at[self.units, pl.ds(self.landing(stage), half)],
            self.send[0].at[self.send[1], stage],
            self.recv[0].at[self.recv[1], stage],
            self.net.neighbours[(self.turn + stage) % 6],
        )

    def start(self):
        self.hop(self.first).start()

    def add(self, base, landed, count):
        group = min(count, 4)

        def body(i):
            here = pl.ds(base + i * group, group)
            there = pl.ds(landed + i * group, group)
            total = self.acc[self.units, here].astype(f32) + self.land[self.units, there].astype(f32)
            self.acc[self.units, here] = total.astype(bf16)

        loop(count // group, body)

    def advance(self, stage):
        self.hop(stage).wait_recv()
        half = 16 >> stage
        base, landed = self.base(stage), self.landing(stage)
        bit = self.bit(stage + 1)
        self.add(base + (1 - bit) * half, landed + (1 - bit) * half, half)
        self.hop(stage + 1).start()
        self.add(base + bit * half, landed + bit * half, half)

    def last(self):
        self.hop(5).wait_recv()
        return (
            self.acc[self.units, pl.ds(self.base(5), 1)].astype(f32)
            + self.land[self.units, pl.ds(self.landing(5), 1)].astype(f32)
        )[:, 0]

    def finish(self):
        for stage in range(self.first, 6):
            self.hop(stage).wait_send()


class Net:
    def __init__(self, place):
        x, z = lax.div(place.head, 4), lax.rem(place.head, 4)
        y = place.y_hi * 2 + place.y_lo
        self.bits = [
            lax.rem(lax.div(x + 1, 2), 2), lax.rem(lax.div(y + 1, 2), 2), lax.rem(lax.div(z + 1, 2), 2),
            lax.div(x, 2), lax.div(y, 2), lax.div(z, 2),
        ]

        def device(x, y, z):
            return (lax.rem(y, 2) * 16 + x * 4 + z, lax.div(y, 2) * 2 + place.core)

        flip = lambda c: c + 1 - 2 * lax.rem(c, 2)
        self.neighbours = [
            device(flip(x), y, z), device(x, flip(y), z), device(x, y, flip(z)),
            device(3 - x, y, z), device(x, 3 - y, z), device(x, y, 3 - z),
        ]

    def greet(self, barrier):
        for device in self.neighbours:
            greet(barrier, device)


TURN = [u % 6 for u in range(18)]
COUNTS = [3, 3, 3, 3, 2, 2]
STARTS = [0, 3, 6, 9, 12, 14]
SLOT = [STARTS[u % 6] + u // 6 for u in range(16)]
FINAL = list(range(8)) + [10 + (v % 4) * 2 + v // 4 for v in range(8)] + [8, 9]


class MidSums:
    def __init__(self, place, fin, side, down, sem, up_out, out_out, down_out):
        self.place, self.fin, self.side, self.down, self.sem = place, fin, side, down, sem
        self.up_out, self.out_out, self.down_out = up_out, out_out, down_out

    def targets(self):
        return [(self.place.core * 16 + self.place.head, self.place.y_hi * 2 + k) for k in range(2)]

    def sources(self):
        return [(m * 16 + self.place.head, self.place.y_hi * 2 + self.place.y_lo) for m in range(2)]

    def self_count(self):
        return jnp.where(self.place.y_lo == self.place.core, 1, 0)

    def greet(self, barrier):
        greet(barrier, self.place.partner)
        for device in self.sources():

            @pl.when(jnp.logical_not(self.place.is_self(device)))
            def _(device=device):
                greet(barrier, device)

    def greetings(self):
        return 3 - self.self_count()

    def store(self, unit, value):
        self.fin[FINAL[unit]] = value.reshape(2, 8, 256)

    def aside(self):
        return remote(
            self.fin.at[0:10, 1 - self.place.core], self.side, self.sem.at[0], self.sem.at[1], self.place.partner
        )

    def down_hop(self, k):
        return (
            self.fin.at[10 + 4 * k : 14 + 4 * k],
            self.down.at[self.place.y_lo],
            self.sem.at[2 + k],
            self.sem.at[4 + self.place.y_lo],
            self.targets()[k],
        )

    def start(self):
        self.aside().start()
        for k in range(2):
            send_to(self.place, *self.down_hop(k))

    def finish(self):
        place = self.place
        self.aside().wait_recv()
        mine, other = place.core, 1 - place.core
        for u in range(8):
            self.up_out[:, pl.ds(mine * 2048 + u * 256, 256)] = self.fin[u, mine]
            self.up_out[:, pl.ds(other * 2048 + u * 256, 256)] = self.side[u]
        for u in range(2):
            self.out_out[:, pl.ds(mine * 512 + u * 256, 256)] = self.fin[8 + u, mine]
            self.out_out[:, pl.ds(other * 512 + u * 256, 256)] = self.side[8 + u]
        for m in range(2):
            arrived(self.down.at[m], self.sem.at[4 + m])
            for v in range(4):
                group, half = v // 2, v % 2
                self.down_out[group * 16 : group * 16 + 16, m * 512 + half * 256 : m * 512 + half * 256 + 256] = (
                    self.down[m, v].reshape(16, 256)
                )
        self.aside().wait_send()
        for k in range(2):
            sent_to(place, *self.down_hop(k))


MID_OUT = (
    jax.ShapeDtypeStruct((8, FF), f32),
    jax.ShapeDtypeStruct((8, D), f32),
    jax.ShapeDtypeStruct((32, D), f32),
)
MID_SCRATCH = [
    pltpu.VMEM((18, 2, 8, 256), f32),
    pltpu.VMEM((10, 8, 256), f32),
    pltpu.VMEM((2, 4, 2, 8, 256), f32),
    pltpu.SemaphoreType.DMA((6,)),
]


def spread(target, unit_slot, turn, block):
    for chip in range(64):
        y_lo, x, z, y_hi = chip // 32, chip // 8 % 4, chip // 2 % 4, chip % 2
        target[unit_slot, position(turn, y_lo, x, z, y_hi)] = block[chip * 16 : chip * 16 + 16]


ROOT = math.sqrt(2.0 / math.pi)
CUBE = 0.044715


def middle_kernel(
    o_in, x_ref, dy_ref, gain_ref, w_out, w_up, w_down,
    y_ref, grads, out_grads, dx1_ref, gain_grad, da_in,
    wo, wu, wd, o2, b2, dm2, b2t, gzt, x1s, ysum, hsum, yside, hside, da_side, gs, land, outg, stage,
    w_sem, p_send, p_recv, g_sem, h_send, h_recv, send, recv,
):
    place = Place()
    core = place.core
    net = Net(place)

    def up_copy(j):
        at = pl.multiple_of(core * 2048 + j * 512, 512)
        return pltpu.make_async_copy(w_up.at[:, pl.ds(at, 512)], wu.at[j], w_sem.at[1 + j])

    def down_copy(j):
        at = pl.multiple_of(core * 2048 + j * 512, 512)
        return pltpu.make_async_copy(w_down.at[pl.ds(at, 512)], wd.at[j], w_sem.at[5 + j])

    out_copy = pltpu.make_async_copy(w_out, wo, w_sem.at[0])
    out_copy.start()
    for j in range(4):
        up_copy(j).start()
        down_copy(j).start()
    barrier = pltpu.get_barrier_semaphore()
    greet_all(place, barrier, place.block_device)
    greet(barrier, place.partner)
    net.greet(barrier)

    def across(k, src, dst):
        return remote(src, dst, p_send.at[k], p_recv.at[k], place.partner)

    def first_hop(unit):
        bit = net.bits[TURN[unit]]
        return remote(
            gs.at[SLOT[unit], pl.ds((1 - bit) * 32, 32)], land.at[SLOT[unit]],
            h_send.at[unit], h_recv.at[unit], net.neighbours[TURN[unit]],
        )

    dm2[0:T] = dy_ref[0]
    for m in range(8):
        lo, hi = swap_halves(o_in[2 * m], o_in[2 * m + 1])
        o2[0:HT, 128 * m : 128 * m + 128] = lo
        o2[HT:T, 128 * m : 128 * m + 128] = hi
    pl.semaphore_wait(barrier, 23 - place.self_count)
    dm_hop = across(0, dm2.at[0:T], dm2.at[T : 2 * T])
    o_hop = across(1, o2.at[0:T], o2.at[T : 2 * T])
    dm_hop.start()
    o_hop.start()
    out_copy.wait()
    x1 = x_ref[0].astype(f32) + dot(o2[0:T], wo[...])
    x1s[...] = x1
    scale1 = lax.rsqrt(jnp.mean(x1 * x1, axis=-1, keepdims=True) + EPS)
    b2[0:T] = (x1 * scale1 * gain_ref[...]).astype(bf16)
    b_hop = across(2, b2.at[0:T], b2.at[T : 2 * T])
    b_hop.start()
    dm_hop.wait_recv()
    b_hop.wait_recv()
    b2t[...] = transposed(b2[...])

    for j in range(4):
        up_copy(j).wait()
        down_copy(j).wait()
        z = dot(b2[...], wu[j])
        zz = z * z
        th = jnp.tanh(ROOT * z * (1.0 + CUBE * zz))
        half = 0.5 * (1.0 + th)
        gz = (z * half).astype(bf16)
        slope = half + 0.5 * z * (1.0 - th * th) * (ROOT * (1.0 + 3.0 * CUBE * zz))
        dz = (dot_nt(dm2[...], wd[j]) * slope).astype(bf16)
        gzt[j * 512 : (j + 1) * 512] = transposed(gz)
        yj = dot(gz, wd[j])
        hj = dot_nt(dz, wu[j])
        if j == 0:
            ysum[...] = yj
            hsum[...] = hj
        else:
            ysum[...] += yj
            hsum[...] += hj
        up = dot(b2t[...], dz).astype(bf16)
        for u in range(2):
            unit = 2 * j + u
            spread(gs, SLOT[unit], TURN[unit], up[:, u * 256 : u * 256 + 256])
            first_hop(unit).start()

    y_hop = across(3, ysum.at[T : 2 * T], yside)
    h_hop = across(4, hsum.at[T : 2 * T], hside)
    h_hop.start()
    y_hop.start()

    def down_units(u):
        for y_lo in range(2):
            at = y_lo * 512 + u * 256
            down = dot(gzt[...], dm2[:, at : at + 256]).astype(bf16)
            for owner in range(32):
                for group in range(4):
                    unit = 8 + u * 4 + group
                    place_at = position(TURN[unit], y_lo, owner // 8, owner // 2 % 4, owner % 2)
                    gs[SLOT[unit], place_at] = down[owner * 64 + group * 16 : owner * 64 + group * 16 + 16]
        for group in range(4):
            first_hop(8 + u * 4 + group).start()

    down_units(0)
    h_hop.wait_recv()
    x1 = x1s[...]
    scale1 = lax.rsqrt(jnp.mean(x1 * x1, axis=-1, keepdims=True) + EPS)
    dh2 = hsum[0:T] + hside[...]
    gain_grad[...] = jnp.sum(dh2 * x1 * scale1, axis=0, keepdims=True)
    dn = dh2 * gain_ref[...]
    back = scale1 * dn - x1 * (scale1 * scale1 * scale1) * jnp.mean(dn * x1, axis=-1, keepdims=True)
    dx1 = dy_ref[0].astype(f32) + back
    dx1_ref[...] = dx1
    da = dx1.astype(bf16)
    da_side[0, 0:T] = da[:, 0:512]
    da_side[1, 0:T] = da[:, 512:1024]
    da_hop = across(5, da_side.at[1 - core, 0:T], da_side.at[1 - core, T : 2 * T])
    da_hop.start()
    for g in range(4):
        dattn = dot_nt(da, wo[256 * g : 256 * g + 256]).astype(bf16)
        for m in range(2):
            tile = dattn[:, 128 * m : 128 * m + 128]
            packed = swap_halves(tile[:HT], tile[HT:])
            for e in range(2):
                h = 4 * g + 2 * m + e
                stage[h] = packed[e]
                send_to(
                    place, stage.at[h], da_in.at[place.slot], send.at[h], recv.at[place.slot],
                    place.head_device(h),
                )
    down_units(1)
    y_hop.wait_recv()
    y_ref[0] = (x1 + ysum[0:T] + yside[...]).astype(bf16)
    o_hop.wait_recv()
    da_hop.wait_recv()
    out = dot(transposed(o2[...]), da_side[core]).astype(bf16)
    for u in range(2):
        spread(outg, u, TURN[16 + u], out[:, u * 256 : u * 256 + 256])
    out_move = pltpu.make_async_copy(outg, out_grads, g_sem.at[16])
    out_move.start()

    def kept(unit):
        return pltpu.make_async_copy(land.at[SLOT[unit]], grads.at[SLOT[unit]], g_sem.at[unit])

    for unit in range(16):
        first_hop(unit).wait_recv()
        bit = net.bits[TURN[unit]]

        def add(i, unit=unit, bit=bit):
            here = pl.ds(i * 4, 4)
            mine = gs[SLOT[unit], pl.ds(bit * 32 + i * 4, 4)].astype(f32)
            land[SLOT[unit], here] = (land[SLOT[unit], here].astype(f32) + mine).astype(bf16)

        loop(8, add)
        kept(unit).start()

    def finish(n):
        sent_to(
            place, stage.at[n], da_in.at[place.slot], send.at[n], recv.at[place.slot], place.head_device(n)
        )
        arrived(da_in.at[n], recv.at[n])

    loop(16, finish)
    out_move.wait()
    for unit in range(16):
        kept(unit).wait()
        first_hop(unit).wait_send()
    for hop in (dm_hop, o_hop, b_hop, y_hop, h_hop, da_hop):
        hop.wait_send()


def middle_call(o_in, frames, out_grad, gain, w_out, w_up, w_down):
    return pl.pallas_call(
        middle_kernel,
        name="feed_forward",
        out_shape=(
            jax.ShapeDtypeStruct((1, T, D), bf16),
            jax.ShapeDtypeStruct((16, 32, 16, 256), bf16),
            jax.ShapeDtypeStruct((2, 64, 16, 256), bf16),
            jax.ShapeDtypeStruct((T, D), f32),
            jax.ShapeDtypeStruct((1, D), f32),
            jax.ShapeDtypeStruct((16, HT, 128), bf16),
        ),
        in_specs=[VM, VM, VM, VM, ANY, ANY, ANY],
        out_specs=(VM, ANY, ANY, VM, VM, ANY),
        scratch_shapes=[
            pltpu.VMEM((D, D), bf16),
            pltpu.VMEM((4, D, 512), bf16),
            pltpu.VMEM((4, 512, D), bf16),
            pltpu.VMEM((2 * T, D), bf16),
            pltpu.VMEM((2 * T, D), bf16),
            pltpu.VMEM((2 * T, D), bf16),
            pltpu.VMEM((D, 2 * T), bf16),
            pltpu.VMEM((2048, 2 * T), bf16),
            pltpu.VMEM((T, D), f32),
            pltpu.VMEM((2 * T, D), f32),
            pltpu.VMEM((2 * T, D), f32),
            pltpu.VMEM((T, D), f32),
            pltpu.VMEM((T, D), f32),
            pltpu.VMEM((2, 2 * T, 512), bf16),
            pltpu.VMEM((16, 64, 16, 256), bf16),
            pltpu.VMEM((16, 32, 16, 256), bf16),
            pltpu.VMEM((2, 64, 16, 256), bf16),
            pltpu.VMEM((16, HT, 128), bf16),
            pltpu.SemaphoreType.DMA((9,)),
            pltpu.SemaphoreType.DMA((6,)),
            pltpu.SemaphoreType.DMA((6,)),
            pltpu.SemaphoreType.DMA((17,)),
            pltpu.SemaphoreType.DMA((16,)),
            pltpu.SemaphoreType.DMA((16,)),
            pltpu.SemaphoreType.DMA((16,)),
            pltpu.SemaphoreType.DMA((16,)),
        ],
        compiler_params=params(2),
    )(o_in, frames, out_grad, gain, w_out, w_up, w_down)


def backward_kernel(
    pk_ref, da_ref, lse_ref, ot_ref, grads, out_grads,
    dqkv_in, up_out, out_out, down_out,
    seg, keys, queries, kt, gp, delta, dq, dkv, part, landed, stage,
    acc, land, acc2, land2, fin, side, down,
    p_send, p_recv, send, recv, l_sem, h_send, h_recv, m_sem,
):
    place = Place()
    core = place.core
    net = Net(place)
    main = [
        Part(net, acc, land, STARTS[p], COUNTS[p], p, 1, (h_send, p), (h_recv, p)) for p in range(6)
    ]
    outs = [Part(net, acc2, land2, u, 1, TURN[16 + u], 0, (h_send, 6 + u), (h_recv, 6 + u)) for u in range(2)]
    mid = MidSums(place, fin, side, down, m_sem, up_out, out_out, down_out)

    def load(p):
        if p < 6:
            return pltpu.make_async_copy(grads.at[main[p].units], acc.at[main[p].units], l_sem.at[p])
        return pltpu.make_async_copy(out_grads.at[p - 6], acc2.at[p - 6], l_sem.at[p])

    for p in range(8):
        load(p).start()
    barrier = pltpu.get_barrier_semaphore()
    greet_all(place, barrier, place.head_device)
    net.greet(barrier)
    mid.greet(barrier)
    pl.semaphore_wait(barrier, 16 - place.self_count + 6 + mid.greetings())
    for p, sums in enumerate(main + outs):
        load(p).wait()
        sums.start()

    fill_operands(place, pk_ref, seg, keys, queries)

    low = lax.broadcasted_iota(jnp.int32, (HT, 128), 1) < HD

    def prepare(t):
        kt[t] = transposed(keys[t, :, 0:128])[:HD]
        dkv[t] = jnp.zeros((TILE, 128), f32)

    loop(TILES, prepare)

    def prepare_query(j):
        for b in range(4):
            packed = da_ref[j * 4 + b].astype(f32)
            gp[j, b * T : b * T + HT] = jnp.where(low, 0.0, pltpu.roll(packed, HD, 1)).astype(bf16)
            gp[j, b * T + HT : b * T + T] = jnp.where(low, 0.0, packed).astype(bf16)
        delta[j] = jnp.sum(gp[j].astype(f32).T[HD:] * ot_ref[j], axis=0, keepdims=True)
        dq[j] = jnp.zeros((HD, TILE), f32)

    loop(4, prepare_query)
    factor = jnp.where(lax.broadcasted_iota(jnp.int32, (1, 128), 1) < HD, LN2, 1.0)

    def part_hop(j):
        return remote(part.at[j], landed.at[j], p_send.at[j], p_recv.at[j], place.partner)

    def give(j):
        part[j] = (dkv[place.own_tile(j, 1 - core)] * factor).astype(bf16)
        part_hop(j).start()

    def key_hop(m):
        return (
            stage.at[m, 0:T], dqkv_in.at[place.head, 0:T], send.at[0, m], recv.at[0, place.head],
            place.block_device(m),
        )

    def query_hop(m):
        return (
            stage.at[m, T:GRAD], dqkv_in.at[place.head, T:GRAD], send.at[1, m], recv.at[1, place.head],
            place.block_device(m),
        )

    def take(j):
        alone = jnp.logical_and(core == 0, j == 3)

        @pl.when(jnp.logical_not(alone))
        def _():
            part_hop(j).wait_recv()

        total = dkv[place.own_tile(j)] * factor
        total = (total + jnp.where(alone, 0.0, landed[j].astype(f32))).astype(bf16)
        for b in range(4):
            m = j * 4 + b
            stage[m, 0:T] = total[b * T : (b + 1) * T]
            send_to(place, *key_hop(m))

    def step(j, k_tile, diagonal):
        rows = keys[k_tile]
        scores = dot_nt(rows, queries[j])
        if diagonal:
            scores = causal(scores)
        weights = jnp.exp2(scores - lse_ref[j])
        slopes = (weights * (dot_nt(rows[:, 0:128], gp[j]) - delta[j])).astype(bf16)
        weights = weights.astype(bf16)
        dkv[k_tile] += dot(weights, gp[j]) + dot(slopes, queries[j, :, 0:128])
        dq[j] += dot(kt[k_tile], slopes)

    def hooks(n):
        @pl.when(n == HOOKS[0])
        def _():
            for sums in main:
                sums.advance(1)
            for sums in outs:
                sums.advance(0)

        @pl.when(n == HOOKS[1])
        def _():
            for sums in main:
                sums.advance(2)
            for sums in outs:
                sums.advance(1)

        @pl.when(n == HOOKS[2])
        def _():
            for sums in main:
                sums.advance(3)
            for sums in outs:
                sums.advance(2)

        @pl.when(n == HOOKS[3])
        def _():
            for sums in main:
                sums.advance(4)
            for sums in outs:
                sums.advance(3)

        @pl.when(n == HOOKS[4])
        def _():
            for p, sums in enumerate(main):
                total = sums.last()
                for k in range(COUNTS[p]):
                    mid.store(p + 6 * k, total[k])
            for sums in outs:
                sums.advance(4)

        @pl.when(n == HOOKS[5])
        def _():
            for u, sums in enumerate(outs):
                mid.store(16 + u, sums.last()[0])
            mid.start()

        @pl.when(n == HOOKS[6])
        def _():
            mid.finish()

    turn = lax.div(place.head, 4)

    def owned(k_tile):
        return lax.rem(lax.div(k_tile + 1, 2), 2) == core

    def key_tile(i, n):
        k_tile = key_order(place, i)
        skip = 0
        for j in range(4):
            skip = skip + jnp.where(place.own_tile(j) < k_tile, 1, 0)

        def query_tile(at, n):
            hooks(n)
            j = jnp.where(k_tile == 0, lax.rem(at + turn, 4), at)
            diagonal = place.own_tile(j) == k_tile

            @pl.when(diagonal)
            def _():
                step(j, k_tile, True)

            @pl.when(jnp.logical_not(diagonal))
            def _():
                step(j, k_tile, False)

            @pl.when(k_tile == 0)
            def _():
                packed = pack_transposed(dq[j] * SCALE)
                for b in range(4):
                    m = j * 4 + b
                    stage[m, T:GRAD] = packed[b]
                    send_to(place, *query_hop(m))

            return n + 1

        n = lax.fori_loop(skip, 4, query_tile, n)
        mine = owned(k_tile)
        before = key_order(place, jnp.maximum(i - 1, 0))

        @pl.when(jnp.logical_and(jnp.logical_not(mine), jnp.logical_not(jnp.logical_and(core == 1, k_tile == 7))))
        def _():
            give(lax.div(k_tile, 2))

        @pl.when(jnp.logical_and(i > 0, owned(before)))
        def _():
            take(lax.div(before, 2))

        return n

    lax.fori_loop(0, TILES, key_tile, 0)

    @pl.when(core == 0)
    def _():
        take(0)

    def finish(n):
        sent_to(place, *key_hop(n))
        sent_to(place, *query_hop(n))
        arrived(dqkv_in.at[n, 0:T], recv.at[0, n])
        arrived(dqkv_in.at[n, T:GRAD], recv.at[1, n])

    loop(16, finish)

    def given(j, carry):
        part_hop(j).wait_send()
        return carry

    lax.fori_loop(0, 4 - core, given, 0)
    for sums in main + outs:
        sums.finish()


def backward_call(pk, da_in, lse, ot, grads, out_grads):
    return pl.pallas_call(
        backward_kernel,
        name="attention_grad",
        out_shape=(jax.ShapeDtypeStruct((16, GRAD, 128), bf16),) + MID_OUT,
        in_specs=[VM, VM, VM, VM, ANY, ANY],
        out_specs=(ANY, VM, VM, VM),
        scratch_shapes=[
            pltpu.VMEM((3, TILE, 128), f32),
            pltpu.VMEM((TILES, TILE, 256), bf16),
            pltpu.VMEM((4, TILE, 256), bf16),
            pltpu.VMEM((TILES, HD, TILE), bf16),
            pltpu.VMEM((4, TILE, 128), bf16),
            pltpu.VMEM((4, 1, TILE), f32),
            pltpu.VMEM((4, HD, TILE), f32),
            pltpu.VMEM((TILES, TILE, 128), f32),
            pltpu.VMEM((4, TILE, 128), bf16),
            pltpu.VMEM((4, TILE, 128), bf16),
            pltpu.VMEM((16, GRAD, 128), bf16),
            pltpu.VMEM((16, 32, 16, 256), bf16),
            pltpu.VMEM((16, 32, 16, 256), bf16),
            pltpu.VMEM((2, 64, 16, 256), bf16),
            pltpu.VMEM((2, 64, 16, 256), bf16),
        ]
        + MID_SCRATCH[:3]
        + [
            pltpu.SemaphoreType.DMA((4,)),
            pltpu.SemaphoreType.DMA((4,)),
            pltpu.SemaphoreType.DMA((2, 16)),
            pltpu.SemaphoreType.DMA((2, 16)),
            pltpu.SemaphoreType.DMA((8,)),
            pltpu.SemaphoreType.DMA((8, 6)),
            pltpu.SemaphoreType.DMA((8, 6)),
        ]
        + MID_SCRATCH[3:],
        compiler_params=params(3),
    )(pk, da_in, lse, ot, grads, out_grads)


def last_kernel(
    dqkv_in, x_ref, dx1_ref, gain_ref, gain2_ref, w_ref,
    dx_ref, qkv_out, gain_out,
    w_scr, a2, dn, dhalf, a2t, fin, side, gs, land, gain_acc, gain_land,
    w_sem, p_send, p_recv, h_send, h_recv,
):
    place = Place()
    core = place.core
    net = Net(place)
    sums = [Part(net, gs, land, u, 1, u, 0, (h_send, u), (h_recv, u)) for u in range(6)]
    gains = Part(net, gain_acc, gain_land, 0, 1, 0, 0, (h_send, 6), (h_recv, 6))
    weight = pltpu.make_async_copy(w_ref, w_scr, w_sem.at[0])
    weight.start()
    barrier = pltpu.get_barrier_semaphore()
    net.greet(barrier)
    greet(barrier, place.partner)

    def across(k, src, dst):
        return remote(src, dst, p_send.at[k], p_recv.at[k], place.partner)

    x = x_ref[0].astype(f32)
    scale = lax.rsqrt(jnp.mean(x * x, axis=-1, keepdims=True) + EPS)
    a2[0:T] = (x * scale * gain_ref[...]).astype(bf16)
    pl.semaphore_wait(barrier, 7)
    a_hop = across(0, a2.at[0:T], a2.at[T : 2 * T])
    a_hop.start()
    for m in range(8):
        lo, hi = swap_halves(dqkv_in[2 * m, T:GRAD], dqkv_in[2 * m + 1, T:GRAD])
        dk, dv = swap_halves(dqkv_in[2 * m, 0:T], dqkv_in[2 * m + 1, 0:T])
        dn[0:HT, 128 * m : 128 * m + 128] = lo
        dn[HT:T, 128 * m : 128 * m + 128] = hi
        dn[:, D + 128 * m : D + 128 * m + 128] = dk
        dn[:, 2 * D + 128 * m : 2 * D + 128 * m + 128] = dv
        at = 128 * (m % 4)
        dhalf[m // 4, 0:HT, at : at + 128] = lo
        dhalf[m // 4, HT:T, at : at + 128] = hi
        dhalf[m // 4, 0:T, 512 + at : 512 + at + 128] = dk
        dhalf[m // 4, 0:T, 1024 + at : 1024 + at + 128] = dv
    d_hop = across(1, dhalf.at[1 - core, 0:T], dhalf.at[1 - core, T : 2 * T])
    d_hop.start()
    a_hop.wait_recv()
    a2t[...] = transposed(a2[...])
    d_hop.wait_recv()
    for u in range(6):
        spread(gs, u, u, dot(a2t[...], dhalf[core, :, u * 256 : u * 256 + 256]).astype(bf16))
        sums[u].start()
    weight.wait()
    dh1 = dot_nt(dn[...], w_scr[...])
    gain1_grad = jnp.sum(dh1 * x * scale, axis=0, keepdims=True)
    row = lax.broadcasted_iota(jnp.int32, (128, D), 0)
    both = jnp.where(row == 0, gain1_grad, jnp.where(row == 1, gain2_ref[...], 0.0))
    columns = both.T.astype(bf16)
    for chip in range(64):
        y_lo, cx, z, y_hi = chip // 32, chip // 8 % 4, chip // 2 % 4, chip % 2
        gain_acc[0, position(0, y_lo, cx, z, y_hi)] = columns[chip * 16 : chip * 16 + 16]
    gains.start()
    dxn = dh1 * gain_ref[...]
    back = scale * dxn - x * (scale * scale * scale) * jnp.mean(dxn * x, axis=-1, keepdims=True)
    dx_ref[0] = (dx1_ref[...] + back).astype(bf16)

    for stage in range(5):
        for part in sums + [gains]:
            part.advance(stage)
    for u in range(6):
        fin[u] = sums[u].last()[0].reshape(2, 8, 256)
    gain_rows = gains.last()[0]
    fin[6] = jnp.concatenate([gain_rows, jnp.zeros((16, 128), f32)], axis=1).reshape(2, 8, 256)
    aside = across(2, fin.at[:, 1 - core], side)
    aside.start()
    aside.wait_recv()
    mine, other = core, 1 - core
    for u in range(6):
        at = (u // 2) * D + (u % 2) * 256
        qkv_out[:, pl.ds(at + mine * 512, 256)] = fin[u, mine]
        qkv_out[:, pl.ds(at + other * 512, 256)] = side[u]
    both = fin[6, mine][:, 0:128] + side[6][:, 0:128]
    wide = jnp.concatenate([both] + [jnp.zeros((8, 128), f32)] * 15, axis=0).T
    gain_out[...] = wide[0:8]
    for hop in (a_hop, d_hop, aside):
        hop.wait_send()
    for part in sums + [gains]:
        part.finish()


def last_call(dqkv_in, frames, dx1, gain, gain2_grad, w_qkv):
    return pl.pallas_call(
        last_kernel,
        name="input_grad",
        out_shape=(
            jax.ShapeDtypeStruct((1, T, D), bf16),
            jax.ShapeDtypeStruct((8, 3 * D), f32),
            jax.ShapeDtypeStruct((8, 128), f32),
        ),
        in_specs=[VM, VM, VM, VM, VM, ANY],
        out_specs=(VM, VM, VM),
        scratch_shapes=[
            pltpu.VMEM((D, 3 * D), bf16),
            pltpu.VMEM((2 * T, D), bf16),
            pltpu.VMEM((T, 3 * D), bf16),
            pltpu.VMEM((2, 2 * T, 1536), bf16),
            pltpu.VMEM((D, 2 * T), bf16),
            pltpu.VMEM((7, 2, 8, 256), f32),
            pltpu.VMEM((7, 8, 256), f32),
            pltpu.VMEM((6, 64, 16, 256), bf16),
            pltpu.VMEM((6, 64, 16, 256), bf16),
            pltpu.VMEM((1, 64, 16, 128), bf16),
            pltpu.VMEM((1, 64, 16, 128), bf16),
            pltpu.SemaphoreType.DMA((1,)),
            pltpu.SemaphoreType.DMA((3,)),
            pltpu.SemaphoreType.DMA((3,)),
            pltpu.SemaphoreType.DMA((7, 6)),
            pltpu.SemaphoreType.DMA((7, 6)),
        ],
        compiler_params=params(4),
    )(dqkv_in, frames, dx1, gain, gain2_grad, w_qkv)


def deliver_kernel(*refs):
    count = len(refs) // 2 - 2
    sources, gains, targets = refs[:count], refs[count], refs[count + 1 : 2 * count + 1]
    gain1, gain2, sem = refs[2 * count + 1 :]
    del sem
    for k in range(count):
        targets[k][...] = sources[k][...]
    gain1[...] = gains[0, 0:8]
    gain2[...] = gains[1, 0:8]


def deliver(arrays, gains):
    count = len(arrays)
    small = jax.ShapeDtypeStruct((8,), f32)
    return pl.pallas_call(
        deliver_kernel,
        name="deliver",
        out_shape=tuple(jax.ShapeDtypeStruct(v.shape, v.dtype) for v in arrays) + (small, small),
        in_specs=[VM] * (count + 1),
        out_specs=(VM,) * (count + 2),
        scratch_shapes=[pltpu.SemaphoreType.DMA((count,))],
    )(*arrays, gains)


def shards(frames, segment_ids, norm1_gain, w_qkv, w_out, norm2_gain, w_up, w_down, out_grad):
    gain1, gain2 = norm1_gain[None], norm2_gain[None]
    pk = qkv_call(frames, segment_ids, gain1, w_qkv)
    o_in, lse, ot = forward_call(pk)
    y, grads, out_grads, dx1, gain2_grad, da_in = middle_call(
        o_in, frames, out_grad, gain2, w_out, w_up, w_down
    )
    dqkv_in, up_sum, out_sum, down_sum = backward_call(pk, da_in, lse, ot, grads, out_grads)
    dx, qkv_sum, gain_sums = last_call(dqkv_in, frames, dx1, gain1, gain2_grad, w_qkv)
    y, dx, qkv_sum, out_sum, up_sum, down_sum, gain1_sum, gain2_sum = deliver(
        (y, dx, qkv_sum, out_sum, up_sum, down_sum), gain_sums
    )
    return (y, dx, gain1_sum, qkv_sum, out_sum, gain2_sum, up_sum, down_sum)


def solution(mesh):
    return jax.shard_map(
        shards,
        mesh=mesh,
        in_specs=(
            P("row", "seq", None),
            P("row", "seq"),
            P(),
            P(),
            P(),
            P(),
            P(),
            P(),
            P("row", "seq", None),
        ),
        out_specs=(
            P("row", "seq", None),
            P("row", "seq", None),
            P(("seq", "row")),
            P(("seq", "row"), None),
            P(("seq", "row"), None),
            P(("seq", "row")),
            P(("seq", "row"), None),
            P(("seq", "row"), None),
        ),
        check_vma=False,
    )
```

```python
import functools
import math

import jax
import jax.numpy as jnp
from jax import lax
from jax.experimental import pallas as pl
from jax.experimental.pallas import tpu as pltpu
from jax.sharding import PartitionSpec as P

MESH = pl.DeviceIdType.MESH
f32 = jnp.float32
bf16 = jnp.bfloat16

D = 1024
H = 16
HD = 64
FF = 4096
T = 192
HT = T // 2
BLOCKS = 32
TILE = 768
TILES = 8
PACK = 304
GRAD = 288
EPS = 1e-05
NEG = -1e30
LOG2E = math.log2(math.e)
LN2 = math.log(2.0)
SCALE = HD**-0.5
VMEM_LIMIT = 60 * 1024 * 1024

ANY = pl.BlockSpec(memory_space=pl.ANY)
VM = pl.BlockSpec(memory_space=pltpu.VMEM)


def dot(a, b):
    return jnp.dot(a, b, preferred_element_type=f32)


def dot_nt(a, b):
    return lax.dot_general(a, b, (((1,), (1,)), ((), ())), preferred_element_type=f32)


def transposed(v):
    return v.astype(f32).T.astype(bf16)


def swap_halves(first, second):
    lane = lax.broadcasted_iota(jnp.int32, first.shape, 1)
    low = lane < HD
    first, second = first.astype(f32), second.astype(f32)
    return (
        jnp.where(low, first, pltpu.roll(second, HD, 1)).astype(bf16),
        jnp.where(low, pltpu.roll(first, HD, 1), second).astype(bf16),
    )


class Place:
    def __init__(self):
        self.s = lax.axis_index("seq")
        self.r = lax.axis_index("row")
        self.y_lo = lax.div(self.s, 16)
        self.head = lax.rem(self.s, 16)
        self.y_hi = lax.div(self.r, 2)
        self.core = lax.rem(self.r, 2)
        tile = lax.div(self.s, 4)
        self.block_core = lax.rem(lax.div(tile + 1, 2), 2)
        self.slot = lax.div(self.s, 8) * 4 + lax.rem(self.s, 4)
        self.partner = (self.s, self.r + 1 - 2 * self.core)
        self.self_served = jnp.logical_and(self.y_lo == self.core, self.block_core == self.core)
        self.self_count = jnp.where(self.self_served, 1, 0)

    def head_device(self, h):
        return (self.core * 16 + h, self.y_hi * 2 + self.block_core)

    def own_tile(self, j, core=None):
        core = self.core if core is None else core
        return 2 * j + lax.rem(j + core, 2)

    def own_block(self, n):
        return self.own_tile(lax.div(n, 4)) * 4 + lax.rem(n, 4)

    def block_device(self, n):
        return (self.own_block(n), self.y_hi * 2 + self.y_lo)

    def is_self(self, device):
        return jnp.logical_and(device[0] == self.s, device[1] == self.r)


def remote(src, dst, send, recv, device):
    return pltpu.make_async_remote_copy(
        src_ref=src, dst_ref=dst, send_sem=send, recv_sem=recv, device_id=device, device_id_type=MESH
    )


def send_to(place, src, dst, send, recv, device):
    own = place.is_self(device)

    @pl.when(own)
    def _():
        pltpu.make_async_copy(src, dst, recv).start()

    @pl.when(jnp.logical_not(own))
    def _():
        remote(src, dst, send, recv, device).start()


def sent_to(place, src, dst, send, recv, device):
    @pl.when(jnp.logical_not(place.is_self(device)))
    def _():
        remote(src, dst, send, recv, device).wait_send()


def arrived(dst, recv):
    pltpu.make_async_copy(dst, dst, recv).wait()


def greet(barrier, device):
    pl.semaphore_signal(barrier, inc=1, device_id=device, device_id_type=MESH)


def greet_all(place, barrier, device_of):
    def one(n, carry):
        device = device_of(n)

        @pl.when(jnp.logical_not(place.is_self(device)))
        def _():
            greet(barrier, device)

        return carry

    lax.fori_loop(0, 16, one, 0)


def loop(count, body):
    def one(n, carry):
        body(n)
        return carry

    lax.fori_loop(0, count, one, 0)


def params(collective_id):
    return pltpu.CompilerParams(
        collective_id=collective_id, has_side_effects=True, vmem_limit_bytes=VMEM_LIMIT
    )


def seg_column(pk_ref, block):
    tile = pk_ref[block, T + HT : PACK].astype(f32)
    return jnp.concatenate(
        [
            jnp.broadcast_to(tile[0:1], (128, 128)).T,
            jnp.broadcast_to(tile[1:2], (128, 128)).T[: T - 128],
        ],
        axis=0,
    )


def fill_segments(pk_ref, seg):
    first = seg_column(pk_ref, 0)
    last = seg_column(pk_ref, BLOCKS - 1)
    common = jnp.broadcast_to(first[T - 1 : T], (TILE, 128))
    seg[0] = common
    seg[1] = common
    seg[2] = common
    seg[0, 0:T] = first
    seg[2, TILE - T : TILE] = last


def seg_kind(tile):
    return jnp.where(tile == 0, 0, jnp.where(tile == TILES - 1, 2, 1))


def fill_operands(place, pk_ref, seg, keys, queries):
    fill_segments(pk_ref, seg)
    lane = lax.broadcasted_iota(jnp.int32, (TILE, 128), 1)
    number = lane.astype(f32)

    def key_tile(t):
        keys[t, :, 0:128] = load_keys(pk_ref, t)
        keys[t, :, 128:256] = jnp.where(seg[seg_kind(t)] == number, 1.0, 0.0).astype(bf16)

    loop(TILES, key_tile)
    low = lax.broadcasted_iota(jnp.int32, (HT, 128), 1) < HD

    def query_tile(j):
        tile = place.own_tile(j)
        for b in range(4):
            packed = pk_ref[tile * 4 + b, T : T + HT].astype(f32)
            queries[j, b * T : b * T + HT, 0:128] = jnp.where(low, packed, 0.0).astype(bf16)
            queries[j, b * T + HT : b * T + T, 0:128] = jnp.where(low, pltpu.roll(packed, HD, 1), 0.0).astype(bf16)
        other = jnp.logical_and(lane < 8, seg[seg_kind(tile)] != number)
        queries[j, :, 128:256] = jnp.where(other, NEG, 0.0).astype(bf16)

    loop(4, query_tile)


STEPS = 18


def walk(place, n):
    turn = lax.div(place.head, 4)
    j, start, end = lax.rem(turn, 4), 0, 0
    end = place.own_tile(j) + 1
    for k in range(1, 4):
        past = n >= end
        following = lax.rem(turn + k, 4)
        j = jnp.where(past, following, j)
        start = jnp.where(past, end, start)
        end = jnp.where(past, end + place.own_tile(following) + 1, end)
    at = n - start
    k_tile = jnp.where(at == 0, place.own_tile(j), at - 1)
    return j, k_tile, at == 0, n + 1 == end


def key_order(place, i):
    turn = lax.div(place.head, 4)
    return jnp.where(i == 7, 0, 7 - lax.rem(i + 2 * turn, 7))


def causal(scores):
    k = lax.broadcasted_iota(jnp.int32, scores.shape, 0)
    q = lax.broadcasted_iota(jnp.int32, scores.shape, 1)
    return jnp.where(k <= q, scores, NEG)


def load_keys(pk_ref, tile):
    return pk_ref[pl.ds(tile * 4, 4), 0:T].reshape(TILE, 128)


def pack_transposed(value_t):
    both = jnp.concatenate([value_t, value_t], axis=0).T
    lane = lax.broadcasted_iota(jnp.int32, (HT, 128), 1)
    return [
        jnp.where(lane < HD, both[b * T : b * T + HT], both[b * T + HT : b * T + T]).astype(bf16)
        for b in range(4)
    ]


def forward_kernel(
    x_ref, seg_ref, gain_ref, w_ref, pk_out, o_in, lse_ref, ot_ref,
    w_scr, packets, pk, seg, keys, queries, vt, top, acc, even, odd, stage,
    w_sem, a_send, a_recv, f_send, f_recv, k_sem, send, recv,
):
    place = Place()

    def weight(g, part):
        return pltpu.make_async_copy(
            w_ref.at[:, pl.ds(part * D + g * 256, 256)], w_scr.at[g, part], w_sem.at[g, part]
        )

    for g in range(4):
        for part in range(3):
            weight(g, part).start()
    barrier = pltpu.get_barrier_semaphore()
    greet_all(place, barrier, place.block_device)
    greet_all(place, barrier, place.head_device)
    greet(barrier, place.partner)

    x = x_ref[0].astype(f32)
    a = (x * lax.rsqrt(jnp.mean(x * x, axis=-1, keepdims=True) + EPS) * gain_ref[...]).astype(bf16)
    numbers = seg_ref[...].astype(f32)
    row = lax.broadcasted_iota(jnp.int32, (16, 128), 0)
    rest = jnp.concatenate([numbers[:, 128:T], jnp.zeros((1, 256 - T), f32)], axis=1)
    seg_tile = jnp.where(row == 0, numbers[:, :128], jnp.where(row == 1, rest, 0.0)).astype(bf16)
    pl.semaphore_wait(barrier, 33 - 2 * place.self_count)

    def packet_hop(h):
        return (
            packets.at[h], pk.at[place.s], a_send.at[h], a_recv.at[place.slot], place.head_device(h),
        )

    for g in range(4):
        for part in range(3):
            weight(g, part).wait()
        q = dot(a, w_scr[g, 0]) * (SCALE * LOG2E)
        k = dot(a, w_scr[g, 1])
        v = dot(a, w_scr[g, 2])
        for m in range(2):
            lanes = slice(128 * m, 128 * m + 128)
            h = 4 * g + 2 * m
            kv = swap_halves(k[:, lanes].astype(bf16), v[:, lanes].astype(bf16))
            qq = q[:, lanes].astype(bf16)
            qp = swap_halves(qq[:HT], qq[HT:])
            for e in range(2):
                packets[h + e, 0:T] = kv[e]
                packets[h + e, T : T + HT] = qp[e]
                packets[h + e, T + HT : PACK] = seg_tile
                send_to(place, *packet_hop(h + e))

    def forward(n):
        i = place.own_block(n)
        return remote(pk.at[i], pk.at[i], f_send.at[n], f_recv.at[n], place.partner)

    def keep(n, core):
        i = place.own_tile(lax.div(n, 4), core) * 4 + lax.rem(n, 4)
        return pltpu.make_async_copy(pk.at[i], pk_out.at[i], k_sem.at[n])

    def pass_on(n):
        arrived(pk.at[place.own_block(n)], a_recv.at[n])
        forward(n).start()
        keep(n, place.core).start()

    loop(16, pass_on)
    one = jnp.where(lax.broadcasted_iota(jnp.int32, (16, TILE), 0) == 0, 1.0, 0.0).astype(bf16)

    def kept_all(n):
        keep(n, place.core).wait()
        forward(n).wait_recv()
        keep(n, 1 - place.core).start()

    loop(16, kept_all)
    fill_operands(place, pk, seg, keys, queries)

    def prepare(t):
        vt[t, 0:HD] = transposed(keys[t, :, 0:128])[HD:]
        vt[t, HD : HD + 16] = one

    loop(TILES, prepare)

    def score(n, scores):
        j, k_tile, _, _ = walk(place, jnp.minimum(n, STEPS - 1))
        scores[...] = dot_nt(keys[k_tile], queries[j])

    def out_hop(m):
        return (
            stage.at[m], o_in.at[place.head], send.at[m], recv.at[place.head], place.block_device(m),
        )

    def body(n, now, later):
        j, k_tile, first, last = walk(place, n)

        @pl.when(first)
        def _():
            score(n + 1, later)
            scores = causal(now[...])
            peak = jnp.max(scores, axis=0, keepdims=True)
            top[...] = peak
            acc[...] = dot(vt[k_tile], jnp.exp2(scores - peak).astype(bf16))

        @pl.when(jnp.logical_not(first))
        def _():
            score(n + 1, later)
            scores = now[...]
            peak = jnp.maximum(top[...], jnp.max(scores, axis=0, keepdims=True))
            fade = jnp.exp2(top[...] - peak)
            top[...] = peak
            acc[...] = acc[...] * fade + dot(vt[k_tile], jnp.exp2(scores - peak).astype(bf16))

        @pl.when(last)
        def _():
            total = acc[HD : HD + 1]
            out_t = acc[0:HD] / total
            lse_ref[j] = top[...] + jnp.log2(total)
            ot_ref[j] = out_t
            packed = pack_transposed(out_t)
            for b in range(4):
                m = j * 4 + b
                stage[m] = packed[b]
                send_to(place, *out_hop(m))

    score(0, even)

    def pair(i):
        body(2 * i, even, odd)
        body(2 * i + 1, odd, even)

    loop(STEPS // 2, pair)

    def finish(n):
        sent_to(place, *packet_hop(n))
        forward(n).wait_send()
        keep(n, 1 - place.core).wait()
        sent_to(place, *out_hop(n))
        arrived(o_in.at[n], recv.at[n])

    loop(16, finish)


def forward_call(frames, segment_ids, gain, w_qkv):
    return pl.pallas_call(
        forward_kernel,
        name="attention",
        out_shape=(
            jax.ShapeDtypeStruct((BLOCKS, PACK, 128), bf16),
            jax.ShapeDtypeStruct((16, HT, 128), bf16),
            jax.ShapeDtypeStruct((4, 1, TILE), f32),
            jax.ShapeDtypeStruct((4, HD, TILE), f32),
        ),
        in_specs=[VM, VM, VM, ANY],
        out_specs=(ANY, ANY, VM, VM),
        scratch_shapes=[
            pltpu.VMEM((4, 3, D, 256), bf16),
            pltpu.VMEM((16, PACK, 128), bf16),
            pltpu.VMEM((BLOCKS, PACK, 128), bf16),
            pltpu.VMEM((3, TILE, 128), f32),
            pltpu.VMEM((TILES, TILE, 256), bf16),
            pltpu.VMEM((4, TILE, 256), bf16),
            pltpu.VMEM((TILES, HD + 16, TILE), bf16),
            pltpu.VMEM((1, TILE), f32),
            pltpu.VMEM((HD + 16, TILE), f32),
            pltpu.VMEM((TILE, TILE), f32),
            pltpu.VMEM((TILE, TILE), f32),
            pltpu.VMEM((16, HT, 128), bf16),
            pltpu.SemaphoreType.DMA((4, 3)),
            pltpu.SemaphoreType.DMA((16,)),
            pltpu.SemaphoreType.DMA((16,)),
            pltpu.SemaphoreType.DMA((16,)),
            pltpu.SemaphoreType.DMA((16,)),
            pltpu.SemaphoreType.DMA((16,)),
            pltpu.SemaphoreType.DMA((16,)),
            pltpu.SemaphoreType.DMA((16,)),
        ],
        compiler_params=params(0),
    )(frames, segment_ids, gain, w_qkv)


FIRST = lambda c: ((c + 1) // 2) % 2
SECOND = lambda c: c // 2


def chip_bits(x, y, z):
    return [FIRST(x), FIRST(y), FIRST(z), SECOND(x), SECOND(y), SECOND(z)]


def position(part, y_lo, x, z, y_hi):
    bits = chip_bits(x, y_hi * 2 + y_lo, z)
    at = 0
    for k in range(6):
        at = at * 2 + bits[(part + k) % 6]
    return at


class Part:
    def __init__(self, net, acc, land, at, count, turn, send, recv, pieces=()):
        self.net, self.acc, self.land, self.turn, self.pieces = net, acc, land, turn, pieces
        self.units = pl.ds(at, count)
        self.count, self.send, self.recv = count, send, recv

    def bit(self, stage):
        return self.net.bits[(self.turn + stage) % 6]

    def base(self, stage):
        at = 0
        for k in range(stage + 1):
            at = at + self.bit(k) * (32 >> k)
        return at

    def landing(self, stage):
        return sum(32 >> k for k in range(stage))

    def hop(self, stage):
        half = 32 >> stage
        base = self.base(stage - 1) + (1 - self.bit(stage)) * half
        return remote(
            self.acc.at[self.units, pl.ds(base, half)],
            self.land.at[self.units, pl.ds(self.landing(stage), half)],
            self.send[0].at[self.send[1], stage],
            self.recv[0].at[self.recv[1], stage],
            self.net.neighbours[(self.turn + stage) % 6],
        )

    def start(self):
        self.hop(0).start()

    def hops(self, stage):
        return list(self.pieces) if stage == 0 and self.pieces else [self.hop(stage)]

    def add(self, base, landed, count):
        group = min(count, 4)

        def body(i):
            here = pl.ds(base + i * group, group)
            there = pl.ds(landed + i * group, group)
            total = self.acc[self.units, here].astype(f32) + self.land[self.units, there].astype(f32)
            self.acc[self.units, here] = total.astype(bf16)

        loop(count // group, body)

    def advance(self, stage):
        for hop in self.hops(stage):
            hop.wait_recv()
        half = 16 >> stage
        base, landed = self.base(stage), self.landing(stage)
        bit = self.bit(stage + 1)
        self.add(base + (1 - bit) * half, landed + (1 - bit) * half, half)
        self.hop(stage + 1).start()
        self.add(base + bit * half, landed + bit * half, half)

    def last(self):
        self.hop(5).wait_recv()
        return (
            self.acc[self.units, pl.ds(self.base(5), 1)].astype(f32)
            + self.land[self.units, pl.ds(self.landing(5), 1)].astype(f32)
        )[:, 0]

    def finish(self):
        for stage in range(6):
            for hop in self.hops(stage):
                hop.wait_send()


class Net:
    def __init__(self, place):
        x, z = lax.div(place.head, 4), lax.rem(place.head, 4)
        y = place.y_hi * 2 + place.y_lo
        self.bits = [
            lax.rem(lax.div(x + 1, 2), 2), lax.rem(lax.div(y + 1, 2), 2), lax.rem(lax.div(z + 1, 2), 2),
            lax.div(x, 2), lax.div(y, 2), lax.div(z, 2),
        ]

        def device(x, y, z):
            return (lax.rem(y, 2) * 16 + x * 4 + z, lax.div(y, 2) * 2 + place.core)

        flip = lambda c: c + 1 - 2 * lax.rem(c, 2)
        self.neighbours = [
            device(flip(x), y, z), device(x, flip(y), z), device(x, y, flip(z)),
            device(3 - x, y, z), device(x, 3 - y, z), device(x, y, 3 - z),
        ]

    def greet(self, barrier):
        for device in self.neighbours:
            greet(barrier, device)


TURN = [u % 6 for u in range(18)]
COUNTS = [3, 3, 3, 3, 2, 2]
STARTS = [0, 3, 6, 9, 12, 14]
SLOT = [STARTS[u % 6] + u // 6 for u in range(16)]
FINAL = list(range(8)) + [10 + (v % 4) * 2 + v // 4 for v in range(8)] + [8, 9]


class MidSums:
    def __init__(self, place, fin, side, down, sem, up_out, out_out, down_out):
        self.place, self.fin, self.side, self.down, self.sem = place, fin, side, down, sem
        self.up_out, self.out_out, self.down_out = up_out, out_out, down_out

    def targets(self):
        return [(self.place.core * 16 + self.place.head, self.place.y_hi * 2 + k) for k in range(2)]

    def sources(self):
        return [(m * 16 + self.place.head, self.place.y_hi * 2 + self.place.y_lo) for m in range(2)]

    def self_count(self):
        return jnp.where(self.place.y_lo == self.place.core, 1, 0)

    def greet(self, barrier):
        greet(barrier, self.place.partner)
        for device in self.sources():

            @pl.when(jnp.logical_not(self.place.is_self(device)))
            def _(device=device):
                greet(barrier, device)

    def greetings(self):
        return 3 - self.self_count()

    def store(self, unit, value):
        self.fin[FINAL[unit]] = value.reshape(2, 8, 256)

    def aside(self):
        return remote(
            self.fin.at[0:10, 1 - self.place.core], self.side, self.sem.at[0], self.sem.at[1], self.place.partner
        )

    def down_hop(self, k):
        return (
            self.fin.at[10 + 4 * k : 14 + 4 * k],
            self.down.at[self.place.y_lo],
            self.sem.at[2 + k],
            self.sem.at[4 + self.place.y_lo],
            self.targets()[k],
        )

    def start(self):
        self.aside().start()
        for k in range(2):
            send_to(self.place, *self.down_hop(k))

    def finish(self):
        place = self.place
        self.aside().wait_recv()
        mine, other = place.core, 1 - place.core
        for u in range(8):
            self.up_out[:, pl.ds(mine * 2048 + u * 256, 256)] = self.fin[u, mine]
            self.up_out[:, pl.ds(other * 2048 + u * 256, 256)] = self.side[u]
        for u in range(2):
            self.out_out[:, pl.ds(mine * 512 + u * 256, 256)] = self.fin[8 + u, mine]
            self.out_out[:, pl.ds(other * 512 + u * 256, 256)] = self.side[8 + u]
        for m in range(2):
            arrived(self.down.at[m], self.sem.at[4 + m])
            for v in range(4):
                group, half = v // 2, v % 2
                self.down_out[group * 16 : group * 16 + 16, m * 512 + half * 256 : m * 512 + half * 256 + 256] = (
                    self.down[m, v].reshape(16, 256)
                )
        self.aside().wait_send()
        for k in range(2):
            sent_to(place, *self.down_hop(k))


MID_OUT = (
    jax.ShapeDtypeStruct((8, FF), f32),
    jax.ShapeDtypeStruct((8, D), f32),
    jax.ShapeDtypeStruct((32, D), f32),
)
MID_SCRATCH = [
    pltpu.VMEM((18, 2, 8, 256), f32),
    pltpu.VMEM((10, 8, 256), f32),
    pltpu.VMEM((2, 4, 2, 8, 256), f32),
    pltpu.SemaphoreType.DMA((6,)),
]


def spread(target, unit_slot, turn, block):
    for chip in range(64):
        y_lo, x, z, y_hi = chip // 32, chip // 8 % 4, chip // 2 % 4, chip % 2
        target[unit_slot, position(turn, y_lo, x, z, y_hi)] = block[chip * 16 : chip * 16 + 16]


ROOT = math.sqrt(2.0 / math.pi)
CUBE = 0.044715


HOOKS = (3, 7, 10, 12, 13, 14, 15, 17)


def rest_kernel(
    o_in, x_ref, dy_ref, gain1_ref, gain2_ref, lse_ref, w_out, w_up, w_down, w_qkv, pk_in, ot_in,
    y_ref, dx_ref, qkv_out, gain_out, up_out, out_out, down_out,
    o2, b2, dm2, yside, hside, da_side, dx1s, gain2_grad, gs, land, outg, land2, da_in, stage1,
    part, landed, dqkv_in, stage2, fin, side, down, a2, dhalf, gs3, land3, gain_acc, gain_land, fin3, side3,
    w_sem, l_sem, p_send, p_recv, q_send, q_recv, h_send, h_recv, a_send, a_recv, b_send, b_recv,
    n_send, n_recv, t_send, t_recv, m_sem,
):
    place = Place()
    core = place.core
    net = Net(place)

    def across(k, src, dst):
        return remote(src, dst, p_send.at[k], p_recv.at[k], place.partner)

    def first_hop(unit):
        bit = net.bits[TURN[unit]]
        return remote(
            gs.at[SLOT[unit], pl.ds((1 - bit) * 32, 32)], land.at[SLOT[unit], 0:32],
            h_send.at[unit], h_recv.at[unit], net.neighbours[TURN[unit]],
        )

    main = [
        Part(
            net, gs, land, STARTS[p], COUNTS[p], p, (n_send, p), (n_recv, p),
            [first_hop(p + 6 * k) for k in range(COUNTS[p])],
        )
        for p in range(6)
    ]
    outs = [Part(net, outg, land2, u, 1, TURN[16 + u], (n_send, 6 + u), (n_recv, 6 + u)) for u in range(2)]
    mid = MidSums(place, fin, side, down, m_sem, up_out, out_out, down_out)
    sums = [Part(net, gs3, land3, u, 1, u, (t_send, u), (t_recv, u)) for u in range(6)]
    gains = Part(net, gain_acc, gain_land, 0, 1, 0, (t_send, 6), (t_recv, 6))

    barrier = pltpu.get_barrier_semaphore()
    greet_all(place, barrier, place.block_device)
    greet_all(place, barrier, place.head_device)
    net.greet(barrier)
    mid.greet(barrier)

    def da_hop(h):
        return (
            stage1.at[h], da_in.at[place.slot], a_send.at[h], a_recv.at[place.slot], place.head_device(h),
        )

    a_hop = across(6, a2.at[0:T], a2.at[T : 2 * T])

    def feed_forward(wo, wu, wd, b2t, gzt, x1s, ysum, hsum):
        def up_copy(j):
            at = pl.multiple_of(core * 2048 + j * 512, 512)
            return pltpu.make_async_copy(w_up.at[:, pl.ds(at, 512)], wu.at[j], w_sem.at[1 + j])

        def down_copy(j):
            at = pl.multiple_of(core * 2048 + j * 512, 512)
            return pltpu.make_async_copy(w_down.at[pl.ds(at, 512)], wd.at[j], w_sem.at[5 + j])

        out_copy = pltpu.make_async_copy(w_out, wo, w_sem.at[0])
        out_copy.start()
        for j in range(4):
            up_copy(j).start()
            down_copy(j).start()
        dm2[0:T] = dy_ref[0]
        for m in range(8):
            lo, hi = swap_halves(o_in[2 * m], o_in[2 * m + 1])
            o2[0:HT, 128 * m : 128 * m + 128] = lo
            o2[HT:T, 128 * m : 128 * m + 128] = hi
        pl.semaphore_wait(barrier, 2 * (16 - place.self_count) + 6 + mid.greetings())
        dm_hop = across(0, dm2.at[0:T], dm2.at[T : 2 * T])
        o_hop = across(1, o2.at[0:T], o2.at[T : 2 * T])
        dm_hop.start()
        o_hop.start()
        out_copy.wait()
        x1 = x_ref[0].astype(f32) + dot(o2[0:T], wo[...])
        x1s[...] = x1
        scale1 = lax.rsqrt(jnp.mean(x1 * x1, axis=-1, keepdims=True) + EPS)
        b2[0:T] = (x1 * scale1 * gain2_ref[...]).astype(bf16)
        b_hop = across(2, b2.at[0:T], b2.at[T : 2 * T])
        b_hop.start()
        x = x_ref[0].astype(f32)
        a2[0:T] = (x * lax.rsqrt(jnp.mean(x * x, axis=-1, keepdims=True) + EPS) * gain1_ref[...]).astype(bf16)
        a_hop.start()
        dm_hop.wait_recv()
        b_hop.wait_recv()
        b2t[...] = transposed(b2[...])

        for j in range(4):
            up_copy(j).wait()
            down_copy(j).wait()
            z = dot(b2[...], wu[j])
            zz = z * z
            th = jnp.tanh(ROOT * z * (1.0 + CUBE * zz))
            half = 0.5 * (1.0 + th)
            gz = (z * half).astype(bf16)
            slope = half + 0.5 * z * (1.0 - th * th) * (ROOT * (1.0 + 3.0 * CUBE * zz))
            dz = (dot_nt(dm2[...], wd[j]) * slope).astype(bf16)
            gzt[j * 512 : (j + 1) * 512] = transposed(gz)
            yj = dot(gz, wd[j])
            hj = dot_nt(dz, wu[j])
            if j == 0:
                ysum[...] = yj
                hsum[...] = hj
            else:
                ysum[...] += yj
                hsum[...] += hj
            up = dot(b2t[...], dz).astype(bf16)
            for u in range(2):
                unit = 2 * j + u
                spread(gs, SLOT[unit], TURN[unit], up[:, u * 256 : u * 256 + 256])
                first_hop(unit).start()

        y_hop = across(3, ysum.at[T : 2 * T], yside)
        h_hop = across(4, hsum.at[T : 2 * T], hside)
        h_hop.start()
        y_hop.start()

        def down_units(u):
            for y_lo in range(2):
                at = y_lo * 512 + u * 256
                grad = dot(gzt[...], dm2[:, at : at + 256]).astype(bf16)
                for owner in range(32):
                    for group in range(4):
                        unit = 8 + u * 4 + group
                        place_at = position(TURN[unit], y_lo, owner // 8, owner // 2 % 4, owner % 2)
                        gs[SLOT[unit], place_at] = grad[owner * 64 + group * 16 : owner * 64 + group * 16 + 16]
            for group in range(4):
                first_hop(8 + u * 4 + group).start()

        down_units(0)
        h_hop.wait_recv()
        x1 = x1s[...]
        scale1 = lax.rsqrt(jnp.mean(x1 * x1, axis=-1, keepdims=True) + EPS)
        dh2 = hsum[0:T] + hside[...]
        gain2_grad[...] = jnp.sum(dh2 * x1 * scale1, axis=0, keepdims=True)
        dn = dh2 * gain2_ref[...]
        back = scale1 * dn - x1 * (scale1 * scale1 * scale1) * jnp.mean(dn * x1, axis=-1, keepdims=True)
        dx1 = dy_ref[0].astype(f32) + back
        dx1s[...] = dx1
        da = dx1.astype(bf16)
        da_side[0, 0:T] = da[:, 0:512]
        da_side[1, 0:T] = da[:, 512:1024]
        side_hop = across(5, da_side.at[1 - core, 0:T], da_side.at[1 - core, T : 2 * T])
        side_hop.start()
        for g in range(4):
            dattn = dot_nt(da, wo[256 * g : 256 * g + 256]).astype(bf16)
            for m in range(2):
                tile = dattn[:, 128 * m : 128 * m + 128]
                packed = swap_halves(tile[:HT], tile[HT:])
                for e in range(2):
                    h = 4 * g + 2 * m + e
                    stage1[h] = packed[e]
                    send_to(place, *da_hop(h))
        down_units(1)
        y_hop.wait_recv()
        y_ref[0] = (x1 + ysum[0:T] + yside[...]).astype(bf16)
        o_hop.wait_recv()
        side_hop.wait_recv()
        out = dot(transposed(o2[...]), da_side[core]).astype(bf16)
        for u in range(2):
            spread(outg, u, TURN[16 + u], out[:, u * 256 : u * 256 + 256])
            outs[u].start()
        for hop in (dm_hop, o_hop, b_hop, y_hop, h_hop, side_hop):
            hop.wait_send()

    pl.run_scoped(
        feed_forward,
        pltpu.VMEM((D, D), bf16),
        pltpu.VMEM((4, D, 512), bf16),
        pltpu.VMEM((4, 512, D), bf16),
        pltpu.VMEM((D, 2 * T), bf16),
        pltpu.VMEM((2048, 2 * T), bf16),
        pltpu.VMEM((T, D), f32),
        pltpu.VMEM((2 * T, D), f32),
        pltpu.VMEM((2 * T, D), f32),
    )

    def key_hop(m):
        return (
            stage2.at[m, 0:T], dqkv_in.at[place.head, 0:T], b_send.at[0, m], b_recv.at[0, place.head],
            place.block_device(m),
        )

    def query_hop(m):
        return (
            stage2.at[m, T:GRAD], dqkv_in.at[place.head, T:GRAD], b_send.at[1, m], b_recv.at[1, place.head],
            place.block_device(m),
        )

    def part_hop(j):
        return remote(part.at[j], landed.at[j], q_send.at[j], q_recv.at[j], place.partner)

    def attention(pk, ot, seg, keys, queries, kt, gp, delta, dq, dkv):
        pk_copy = pltpu.make_async_copy(pk_in, pk, l_sem.at[0])
        ot_copy = pltpu.make_async_copy(ot_in, ot, l_sem.at[1])
        pk_copy.start()
        ot_copy.start()
        pk_copy.wait()
        fill_operands(place, pk, seg, keys, queries)
        low = lax.broadcasted_iota(jnp.int32, (HT, 128), 1) < HD

        def prepare(t):
            kt[t] = transposed(keys[t, :, 0:128])[:HD]
            dkv[t] = jnp.zeros((TILE, 128), f32)

        loop(TILES, prepare)
        ot_copy.wait()

        def prepare_query(j):
            for b in range(4):
                m = j * 4 + b
                arrived(da_in.at[m], a_recv.at[m])
                packed = da_in[m].astype(f32)
                gp[j, b * T : b * T + HT] = jnp.where(low, 0.0, pltpu.roll(packed, HD, 1)).astype(bf16)
                gp[j, b * T + HT : b * T + T] = jnp.where(low, 0.0, packed).astype(bf16)
            delta[j] = jnp.sum(gp[j].astype(f32).T[HD:] * ot[j], axis=0, keepdims=True)
            dq[j] = jnp.zeros((HD, TILE), f32)

        loop(4, prepare_query)
        factor = jnp.where(lax.broadcasted_iota(jnp.int32, (1, 128), 1) < HD, LN2, 1.0)

        def give(j):
            part[j] = (dkv[place.own_tile(j, 1 - core)] * factor).astype(bf16)
            part_hop(j).start()

        def take(j):
            alone = jnp.logical_and(core == 0, j == 3)

            @pl.when(jnp.logical_not(alone))
            def _():
                part_hop(j).wait_recv()

            total = dkv[place.own_tile(j)] * factor
            total = (total + jnp.where(alone, 0.0, landed[j].astype(f32))).astype(bf16)
            for b in range(4):
                m = j * 4 + b
                stage2[m, 0:T] = total[b * T : (b + 1) * T]
                send_to(place, *key_hop(m))

        def step(j, k_tile, diagonal):
            rows = keys[k_tile]
            scores = dot_nt(rows, queries[j])
            if diagonal:
                scores = causal(scores)
            weights = jnp.exp2(scores - lse_ref[j])
            slopes = (weights * (dot_nt(rows[:, 0:128], gp[j]) - delta[j])).astype(bf16)
            weights = weights.astype(bf16)
            dkv[k_tile] += dot(weights, gp[j]) + dot(slopes, queries[j, :, 0:128])
            dq[j] += dot(kt[k_tile], slopes)

        def hooks(n):
            for stage in range(5):

                @pl.when(n == HOOKS[stage])
                def _(stage=stage):
                    for sums_of in main:
                        sums_of.advance(stage)
                    if stage > 0:
                        for sums_of in outs:
                            sums_of.advance(stage - 1)

            @pl.when(n == HOOKS[5])
            def _():
                for p, sums_of in enumerate(main):
                    total = sums_of.last()
                    for k in range(COUNTS[p]):
                        mid.store(p + 6 * k, total[k])
                for sums_of in outs:
                    sums_of.advance(4)

            @pl.when(n == HOOKS[6])
            def _():
                for u, sums_of in enumerate(outs):
                    mid.store(16 + u, sums_of.last()[0])
                mid.start()

            @pl.when(n == HOOKS[7])
            def _():
                mid.finish()

        turn = lax.div(place.head, 4)

        def owned(k_tile):
            return lax.rem(lax.div(k_tile + 1, 2), 2) == core

        def key_tile(i, n):
            k_tile = key_order(place, i)
            skip = 0
            for j in range(4):
                skip = skip + jnp.where(place.own_tile(j) < k_tile, 1, 0)

            def query_tile(at, n):
                hooks(n)
                j = jnp.where(k_tile == 0, lax.rem(at + turn, 4), at)
                diagonal = place.own_tile(j) == k_tile

                @pl.when(diagonal)
                def _():
                    step(j, k_tile, True)

                @pl.when(jnp.logical_not(diagonal))
                def _():
                    step(j, k_tile, False)

                @pl.when(k_tile == 0)
                def _():
                    packed = pack_transposed(dq[j] * SCALE)
                    for b in range(4):
                        m = j * 4 + b
                        stage2[m, T:GRAD] = packed[b]
                        send_to(place, *query_hop(m))

                return n + 1

            n = lax.fori_loop(skip, 4, query_tile, n)
            mine = owned(k_tile)
            before = key_order(place, jnp.maximum(i - 1, 0))

            @pl.when(jnp.logical_and(jnp.logical_not(mine), jnp.logical_not(jnp.logical_and(core == 1, k_tile == 7))))
            def _():
                give(lax.div(k_tile, 2))

            @pl.when(jnp.logical_and(i > 0, owned(before)))
            def _():
                take(lax.div(before, 2))

            return n

        lax.fori_loop(0, TILES, key_tile, 0)

        @pl.when(core == 0)
        def _():
            take(0)

    pl.run_scoped(
        attention,
        pltpu.VMEM((BLOCKS, PACK, 128), bf16),
        pltpu.VMEM((4, HD, TILE), f32),
        pltpu.VMEM((3, TILE, 128), f32),
        pltpu.VMEM((TILES, TILE, 256), bf16),
        pltpu.VMEM((4, TILE, 256), bf16),
        pltpu.VMEM((TILES, HD, TILE), bf16),
        pltpu.VMEM((4, TILE, 128), bf16),
        pltpu.VMEM((4, 1, TILE), f32),
        pltpu.VMEM((4, HD, TILE), f32),
        pltpu.VMEM((TILES, TILE, 128), f32),
    )

    def last(w_scr, dn, a2t):
        weight = pltpu.make_async_copy(w_qkv, w_scr, l_sem.at[2])
        weight.start()
        a_hop.wait_recv()
        a2t[...] = transposed(a2[...])
        for m in range(8):
            for h in (2 * m, 2 * m + 1):
                arrived(dqkv_in.at[h, 0:T], b_recv.at[0, h])
                arrived(dqkv_in.at[h, T:GRAD], b_recv.at[1, h])
            lo, hi = swap_halves(dqkv_in[2 * m, T:GRAD], dqkv_in[2 * m + 1, T:GRAD])
            dk, dv = swap_halves(dqkv_in[2 * m, 0:T], dqkv_in[2 * m + 1, 0:T])
            dn[0:HT, 128 * m : 128 * m + 128] = lo
            dn[HT:T, 128 * m : 128 * m + 128] = hi
            dn[:, D + 128 * m : D + 128 * m + 128] = dk
            dn[:, 2 * D + 128 * m : 2 * D + 128 * m + 128] = dv
            at = 128 * (m % 4)
            dhalf[m // 4, 0:HT, at : at + 128] = lo
            dhalf[m // 4, HT:T, at : at + 128] = hi
            dhalf[m // 4, 0:T, 512 + at : 512 + at + 128] = dk
            dhalf[m // 4, 0:T, 1024 + at : 1024 + at + 128] = dv
        d_hop = across(7, dhalf.at[1 - core, 0:T], dhalf.at[1 - core, T : 2 * T])
        d_hop.start()
        d_hop.wait_recv()
        for u in range(6):
            spread(gs3, u, u, dot(a2t[...], dhalf[core, :, u * 256 : u * 256 + 256]).astype(bf16))
            sums[u].start()
        weight.wait()
        x = x_ref[0].astype(f32)
        scale = lax.rsqrt(jnp.mean(x * x, axis=-1, keepdims=True) + EPS)
        dh1 = dot_nt(dn[...], w_scr[...])
        gain1_grad = jnp.sum(dh1 * x * scale, axis=0, keepdims=True)
        row = lax.broadcasted_iota(jnp.int32, (128, D), 0)
        both = jnp.where(row == 0, gain1_grad, jnp.where(row == 1, gain2_grad[...], 0.0))
        columns = both.T.astype(bf16)
        for chip in range(64):
            y_lo, cx, z, y_hi = chip // 32, chip // 8 % 4, chip // 2 % 4, chip % 2
            gain_acc[0, position(0, y_lo, cx, z, y_hi)] = columns[chip * 16 : chip * 16 + 16]
        gains.start()
        dxn = dh1 * gain1_ref[...]
        back = scale * dxn - x * (scale * scale * scale) * jnp.mean(dxn * x, axis=-1, keepdims=True)
        dx_ref[0] = (dx1s[...] + back).astype(bf16)

        for stage in range(5):
            for sums_of in sums + [gains]:
                sums_of.advance(stage)
        for u in range(6):
            fin3[u] = sums[u].last()[0].reshape(2, 8, 256)
        gain_rows = gains.last()[0]
        fin3[6] = jnp.concatenate([gain_rows, jnp.zeros((16, 128), f32)], axis=1).reshape(2, 8, 256)
        aside = across(8, fin3.at[:, 1 - core], side3)
        aside.start()
        aside.wait_recv()
        mine, other = core, 1 - core
        for u in range(6):
            at = (u // 2) * D + (u % 2) * 256
            qkv_out[:, pl.ds(at + mine * 512, 256)] = fin3[u, mine]
            qkv_out[:, pl.ds(at + other * 512, 256)] = side3[u]
        both = fin3[6, mine][:, 0:128] + side3[6][:, 0:128]
        wide = jnp.concatenate([both] + [jnp.zeros((8, 128), f32)] * 15, axis=0).T
        gain_out[...] = wide[0:8]
        for hop in (a_hop, d_hop, aside):
            hop.wait_send()

    pl.run_scoped(
        last,
        pltpu.VMEM((D, 3 * D), bf16),
        pltpu.VMEM((T, 3 * D), bf16),
        pltpu.VMEM((D, 2 * T), bf16),
    )

    def finish(n):
        sent_to(place, *da_hop(n))
        sent_to(place, *key_hop(n))
        sent_to(place, *query_hop(n))

    loop(16, finish)

    def given(j, carry):
        part_hop(j).wait_send()
        return carry

    lax.fori_loop(0, 4 - core, given, 0)
    for sums_of in main + outs + sums + [gains]:
        sums_of.finish()


def rest_call(o_in, frames, out_grad, gain1, gain2, lse, w_out, w_up, w_down, w_qkv, pk, ot):
    dma = pltpu.SemaphoreType.DMA
    return pl.pallas_call(
        rest_kernel,
        name="feed_forward_and_back",
        out_shape=(
            jax.ShapeDtypeStruct((1, T, D), bf16),
            jax.ShapeDtypeStruct((1, T, D), bf16),
            jax.ShapeDtypeStruct((8, 3 * D), f32),
            jax.ShapeDtypeStruct((8, 128), f32),
            jax.ShapeDtypeStruct((8, FF), f32),
            jax.ShapeDtypeStruct((8, D), f32),
            jax.ShapeDtypeStruct((32, D), f32),
        ),
        in_specs=[VM] * 6 + [ANY] * 6,
        out_specs=(VM,) * 7,
        scratch_shapes=[
            pltpu.VMEM((2 * T, D), bf16),
            pltpu.VMEM((2 * T, D), bf16),
            pltpu.VMEM((2 * T, D), bf16),
            pltpu.VMEM((T, D), f32),
            pltpu.VMEM((T, D), f32),
            pltpu.VMEM((2, 2 * T, 512), bf16),
            pltpu.VMEM((T, D), f32),
            pltpu.VMEM((1, D), f32),
            pltpu.VMEM((16, 64, 16, 256), bf16),
            pltpu.VMEM((16, 64, 16, 256), bf16),
            pltpu.VMEM((2, 64, 16, 256), bf16),
            pltpu.VMEM((2, 64, 16, 256), bf16),
            pltpu.VMEM((16, HT, 128), bf16),
            pltpu.VMEM((16, HT, 128), bf16),
            pltpu.VMEM((4, TILE, 128), bf16),
            pltpu.VMEM((4, TILE, 128), bf16),
            pltpu.VMEM((16, GRAD, 128), bf16),
            pltpu.VMEM((16, GRAD, 128), bf16),
            pltpu.VMEM((18, 2, 8, 256), f32),
            pltpu.VMEM((10, 8, 256), f32),
            pltpu.VMEM((2, 4, 2, 8, 256), f32),
            pltpu.VMEM((2 * T, D), bf16),
            pltpu.VMEM((2, 2 * T, 1536), bf16),
            pltpu.VMEM((6, 64, 16, 256), bf16),
            pltpu.VMEM((6, 64, 16, 256), bf16),
            pltpu.VMEM((1, 64, 16, 128), bf16),
            pltpu.VMEM((1, 64, 16, 128), bf16),
            pltpu.VMEM((7, 2, 8, 256), f32),
            pltpu.VMEM((7, 8, 256), f32),
            dma((9,)), dma((3,)), dma((9,)), dma((9,)), dma((4,)), dma((4,)), dma((16,)), dma((16,)),
            dma((16,)), dma((16,)), dma((2, 16)), dma((2, 16)), dma((8, 6)), dma((8, 6)), dma((7, 6)), dma((7, 6)),
            dma((6,)),
        ],
        compiler_params=params(1),
    )(o_in, frames, out_grad, gain1, gain2, lse, w_out, w_up, w_down, w_qkv, pk, ot)


def deliver_kernel(*refs):
    count = len(refs) // 2 - 2
    sources, gains, targets = refs[:count], refs[count], refs[count + 1 : 2 * count + 1]
    gain1, gain2, sem = refs[2 * count + 1 :]
    del sem
    for k in range(count):
        targets[k][...] = sources[k][...]
    gain1[...] = gains[0, 0:8]
    gain2[...] = gains[1, 0:8]


def deliver(arrays, gains):
    count = len(arrays)
    small = jax.ShapeDtypeStruct((8,), f32)
    return pl.pallas_call(
        deliver_kernel,
        name="deliver",
        out_shape=tuple(jax.ShapeDtypeStruct(v.shape, v.dtype) for v in arrays) + (small, small),
        in_specs=[VM] * (count + 1),
        out_specs=(VM,) * (count + 2),
        scratch_shapes=[pltpu.SemaphoreType.DMA((count,))],
    )(*arrays, gains)


def shards(frames, segment_ids, norm1_gain, w_qkv, w_out, norm2_gain, w_up, w_down, out_grad):
    gain1, gain2 = norm1_gain[None], norm2_gain[None]
    pk, o_in, lse, ot = forward_call(frames, segment_ids, gain1, w_qkv)
    y, dx, qkv_sum, gain_sums, up_sum, out_sum, down_sum = rest_call(
        o_in, frames, out_grad, gain1, gain2, lse, w_out, w_up, w_down, w_qkv, pk, ot
    )
    y, dx, qkv_sum, out_sum, up_sum, down_sum, gain1_sum, gain2_sum = deliver(
        (y, dx, qkv_sum, out_sum, up_sum, down_sum), gain_sums
    )
    return (y, dx, gain1_sum, qkv_sum, out_sum, gain2_sum, up_sum, down_sum)


def solution(mesh):
    return jax.shard_map(
        shards,
        mesh=mesh,
        in_specs=(
            P("row", "seq", None),
            P("row", "seq"),
            P(),
            P(),
            P(),
            P(),
            P(),
            P(),
            P("row", "seq", None),
        ),
        out_specs=(
            P("row", "seq", None),
            P("row", "seq", None),
            P(("seq", "row")),
            P(("seq", "row"), None),
            P(("seq", "row"), None),
            P(("seq", "row")),
            P(("seq", "row"), None),
            P(("seq", "row"), None),
        ),
        check_vma=False,
    )
```

```python
import functools
import math

import jax
import jax.numpy as jnp
from jax import lax
from jax.experimental import pallas as pl
from jax.experimental.pallas import tpu as pltpu
from jax.sharding import PartitionSpec as P

MESH = pl.DeviceIdType.MESH
f32 = jnp.float32
bf16 = jnp.bfloat16

D = 1024
H = 16
HD = 64
FF = 4096
T = 192
HT = T // 2
BLOCKS = 32
TILE = 768
TILES = 8
PACK = 304
GRAD = 288
EPS = 1e-05
NEG = -1e30
LOG2E = math.log2(math.e)
LN2 = math.log(2.0)
SCALE = HD**-0.5
VMEM_LIMIT = 60 * 1024 * 1024

ANY = pl.BlockSpec(memory_space=pl.ANY)
VM = pl.BlockSpec(memory_space=pltpu.VMEM)


def dot(a, b):
    return jnp.dot(a, b, preferred_element_type=f32)


def dot_nt(a, b):
    return lax.dot_general(a, b, (((1,), (1,)), ((), ())), preferred_element_type=f32)


def transposed(v):
    return v.astype(f32).T.astype(bf16)


def swap_halves(first, second):
    lane = lax.broadcasted_iota(jnp.int32, first.shape, 1)
    low = lane < HD
    first, second = first.astype(f32), second.astype(f32)
    return (
        jnp.where(low, first, pltpu.roll(second, HD, 1)).astype(bf16),
        jnp.where(low, pltpu.roll(first, HD, 1), second).astype(bf16),
    )


class Place:
    def __init__(self):
        self.s = lax.axis_index("seq")
        self.r = lax.axis_index("row")
        self.y_lo = lax.div(self.s, 16)
        self.head = lax.rem(self.s, 16)
        self.y_hi = lax.div(self.r, 2)
        self.core = lax.rem(self.r, 2)
        tile = lax.div(self.s, 4)
        self.block_core = lax.rem(lax.div(tile + 1, 2), 2)
        self.slot = lax.div(self.s, 8) * 4 + lax.rem(self.s, 4)
        self.partner = (self.s, self.r + 1 - 2 * self.core)
        self.self_served = jnp.logical_and(self.y_lo == self.core, self.block_core == self.core)
        self.self_count = jnp.where(self.self_served, 1, 0)

    def head_device(self, h):
        return (self.core * 16 + h, self.y_hi * 2 + self.block_core)

    def own_tile(self, j, core=None):
        core = self.core if core is None else core
        return 2 * j + lax.rem(j + core, 2)

    def own_block(self, n):
        return self.own_tile(lax.div(n, 4)) * 4 + lax.rem(n, 4)

    def block_device(self, n):
        return (self.own_block(n), self.y_hi * 2 + self.y_lo)

    def is_self(self, device):
        return jnp.logical_and(device[0] == self.s, device[1] == self.r)


def remote(src, dst, send, recv, device):
    return pltpu.make_async_remote_copy(
        src_ref=src, dst_ref=dst, send_sem=send, recv_sem=recv, device_id=device, device_id_type=MESH
    )


def send_to(place, src, dst, send, recv, device):
    own = place.is_self(device)

    @pl.when(own)
    def _():
        pltpu.make_async_copy(src, dst, recv).start()

    @pl.when(jnp.logical_not(own))
    def _():
        remote(src, dst, send, recv, device).start()


def sent_to(place, src, dst, send, recv, device):
    @pl.when(jnp.logical_not(place.is_self(device)))
    def _():
        remote(src, dst, send, recv, device).wait_send()


def arrived(dst, recv):
    pltpu.make_async_copy(dst, dst, recv).wait()


def greet(barrier, device):
    pl.semaphore_signal(barrier, inc=1, device_id=device, device_id_type=MESH)


def greet_all(place, barrier, device_of):
    def one(n, carry):
        device = device_of(n)

        @pl.when(jnp.logical_not(place.is_self(device)))
        def _():
            greet(barrier, device)

        return carry

    lax.fori_loop(0, 16, one, 0)


def loop(count, body):
    def one(n, carry):
        body(n)
        return carry

    lax.fori_loop(0, count, one, 0)


def params(collective_id):
    return pltpu.CompilerParams(
        collective_id=collective_id, has_side_effects=True, vmem_limit_bytes=VMEM_LIMIT
    )


def seg_column(pk_ref, block):
    tile = pk_ref[block, T + HT : PACK].astype(f32)
    return jnp.concatenate(
        [
            jnp.broadcast_to(tile[0:1], (128, 128)).T,
            jnp.broadcast_to(tile[1:2], (128, 128)).T[: T - 128],
        ],
        axis=0,
    )


def fill_segments(pk_ref, seg):
    first = seg_column(pk_ref, 0)
    last = seg_column(pk_ref, BLOCKS - 1)
    common = jnp.broadcast_to(first[T - 1 : T], (TILE, 128))
    seg[0] = common
    seg[1] = common
    seg[2] = common
    seg[0, 0:T] = first
    seg[2, TILE - T : TILE] = last


def seg_kind(tile):
    return jnp.where(tile == 0, 0, jnp.where(tile == TILES - 1, 2, 1))


def fill_operands(place, pk_ref, seg, keys, queries):
    fill_segments(pk_ref, seg)
    lane = lax.broadcasted_iota(jnp.int32, (TILE, 128), 1)
    number = lane.astype(f32)

    def key_tile(t):
        keys[t, :, 0:128] = load_keys(pk_ref, t)
        keys[t, :, 128:256] = jnp.where(seg[seg_kind(t)] == number, 1.0, 0.0).astype(bf16)

    loop(TILES, key_tile)
    low = lax.broadcasted_iota(jnp.int32, (HT, 128), 1) < HD

    def query_tile(j):
        tile = place.own_tile(j)
        for b in range(4):
            packed = pk_ref[tile * 4 + b, T : T + HT].astype(f32)
            queries[j, b * T : b * T + HT, 0:128] = jnp.where(low, packed, 0.0).astype(bf16)
            queries[j, b * T + HT : b * T + T, 0:128] = jnp.where(low, pltpu.roll(packed, HD, 1), 0.0).astype(bf16)
        other = jnp.logical_and(lane < 8, seg[seg_kind(tile)] != number)
        queries[j, :, 128:256] = jnp.where(other, NEG, 0.0).astype(bf16)

    loop(4, query_tile)


STEPS = 18


def walk(place, n):
    turn = lax.div(place.head, 4)
    j, start, end = lax.rem(turn, 4), 0, 0
    end = place.own_tile(j) + 1
    for k in range(1, 4):
        past = n >= end
        following = lax.rem(turn + k, 4)
        j = jnp.where(past, following, j)
        start = jnp.where(past, end, start)
        end = jnp.where(past, end + place.own_tile(following) + 1, end)
    at = n - start
    k_tile = jnp.where(at == 0, place.own_tile(j), at - 1)
    return j, k_tile, at == 0, n + 1 == end


def key_order(place, i):
    turn = lax.div(place.head, 4)
    return jnp.where(i == 7, 0, 7 - lax.rem(i + 2 * turn, 7))


def causal(scores):
    k = lax.broadcasted_iota(jnp.int32, scores.shape, 0)
    q = lax.broadcasted_iota(jnp.int32, scores.shape, 1)
    return jnp.where(k <= q, scores, NEG)


def load_keys(pk_ref, tile):
    return pk_ref[pl.ds(tile * 4, 4), 0:T].reshape(TILE, 128)


def pack_transposed(value_t):
    both = jnp.concatenate([value_t, value_t], axis=0).T
    lane = lax.broadcasted_iota(jnp.int32, (HT, 128), 1)
    return [
        jnp.where(lane < HD, both[b * T : b * T + HT], both[b * T + HT : b * T + T]).astype(bf16)
        for b in range(4)
    ]


def forward_kernel(
    x_ref, seg_ref, gain_ref, w_ref, pk_out, o_in, lse_ref, ot_ref,
    w_scr, packets, pk, seg, keys, queries, vt, top, acc, even, odd, stage,
    w_sem, a_send, a_recv, f_send, f_recv, k_sem, send, recv,
):
    place = Place()

    def weight(g, part):
        return pltpu.make_async_copy(
            w_ref.at[:, pl.ds(part * D + g * 256, 256)], w_scr.at[g, part], w_sem.at[g, part]
        )

    for g in range(4):
        for part in range(3):
            weight(g, part).start()
    barrier = pltpu.get_barrier_semaphore()
    greet_all(place, barrier, place.block_device)
    greet_all(place, barrier, place.head_device)
    greet(barrier, place.partner)

    x = x_ref[0].astype(f32)
    a = (x * lax.rsqrt(jnp.mean(x * x, axis=-1, keepdims=True) + EPS) * gain_ref[...]).astype(bf16)
    numbers = seg_ref[...].astype(f32)
    row = lax.broadcasted_iota(jnp.int32, (16, 128), 0)
    rest = jnp.concatenate([numbers[:, 128:T], jnp.zeros((1, 256 - T), f32)], axis=1)
    seg_tile = jnp.where(row == 0, numbers[:, :128], jnp.where(row == 1, rest, 0.0)).astype(bf16)
    pl.semaphore_wait(barrier, 33 - 2 * place.self_count)

    def packet_hop(h):
        return (
            packets.at[h], pk.at[place.s], a_send.at[h], a_recv.at[place.slot], place.head_device(h),
        )

    for g in range(4):
        for part in range(3):
            weight(g, part).wait()
        q = dot(a, w_scr[g, 0]) * (SCALE * LOG2E)
        k = dot(a, w_scr[g, 1])
        v = dot(a, w_scr[g, 2])
        for m in range(2):
            lanes = slice(128 * m, 128 * m + 128)
            h = 4 * g + 2 * m
            kv = swap_halves(k[:, lanes].astype(bf16), v[:, lanes].astype(bf16))
            qq = q[:, lanes].astype(bf16)
            qp = swap_halves(qq[:HT], qq[HT:])
            for e in range(2):
                packets[h + e, 0:T] = kv[e]
                packets[h + e, T : T + HT] = qp[e]
                packets[h + e, T + HT : PACK] = seg_tile
                send_to(place, *packet_hop(h + e))

    def forward(n):
        i = place.own_block(n)
        return remote(pk.at[i], pk.at[i], f_send.at[n], f_recv.at[n], place.partner)

    def keep(n, core):
        i = place.own_tile(lax.div(n, 4), core) * 4 + lax.rem(n, 4)
        return pltpu.make_async_copy(pk.at[i], pk_out.at[i], k_sem.at[n])

    def pass_on(n):
        arrived(pk.at[place.own_block(n)], a_recv.at[n])
        forward(n).start()
        keep(n, place.core).start()

    loop(16, pass_on)
    one = jnp.where(lax.broadcasted_iota(jnp.int32, (16, TILE), 0) == 0, 1.0, 0.0).astype(bf16)

    def kept_all(n):
        keep(n, place.core).wait()
        forward(n).wait_recv()
        keep(n, 1 - place.core).start()

    loop(16, kept_all)
    fill_operands(place, pk, seg, keys, queries)

    def prepare(t):
        vt[t, 0:HD] = transposed(keys[t, :, 0:128])[HD:]
        vt[t, HD : HD + 16] = one

    loop(TILES, prepare)

    def score(n, scores):
        j, k_tile, _, _ = walk(place, jnp.minimum(n, STEPS - 1))
        scores[...] = dot_nt(keys[k_tile], queries[j])

    def out_hop(m):
        return (
            stage.at[m], o_in.at[place.head], send.at[m], recv.at[place.head], place.block_device(m),
        )

    def body(n, now, later):
        j, k_tile, first, last = walk(place, n)

        @pl.when(first)
        def _():
            score(n + 1, later)
            scores = causal(now[...])
            peak = jnp.max(scores, axis=0, keepdims=True)
            top[...] = peak
            acc[...] = dot(vt[k_tile], jnp.exp2(scores - peak).astype(bf16))

        @pl.when(jnp.logical_not(first))
        def _():
            score(n + 1, later)
            scores = now[...]
            peak = jnp.maximum(top[...], jnp.max(scores, axis=0, keepdims=True))
            fade = jnp.exp2(top[...] - peak)
            top[...] = peak
            acc[...] = acc[...] * fade + dot(vt[k_tile], jnp.exp2(scores - peak).astype(bf16))

        @pl.when(last)
        def _():
            total = acc[HD : HD + 1]
            out_t = acc[0:HD] / total
            lse_ref[j] = top[...] + jnp.log2(total)
            ot_ref[j] = out_t
            packed = pack_transposed(out_t)
            for b in range(4):
                m = j * 4 + b
                stage[m] = packed[b]
                send_to(place, *out_hop(m))

    score(0, even)

    def pair(i):
        body(2 * i, even, odd)
        body(2 * i + 1, odd, even)

    loop(STEPS // 2, pair)

    def finish(n):
        sent_to(place, *packet_hop(n))
        forward(n).wait_send()
        keep(n, 1 - place.core).wait()
        sent_to(place, *out_hop(n))
        arrived(o_in.at[n], recv.at[n])

    loop(16, finish)


def forward_call(frames, segment_ids, gain, w_qkv):
    return pl.pallas_call(
        forward_kernel,
        name="attention",
        out_shape=(
            jax.ShapeDtypeStruct((BLOCKS, PACK, 128), bf16),
            jax.ShapeDtypeStruct((16, HT, 128), bf16),
            jax.ShapeDtypeStruct((4, 1, TILE), f32),
            jax.ShapeDtypeStruct((4, HD, TILE), f32),
        ),
        in_specs=[VM, VM, VM, ANY],
        out_specs=(ANY, ANY, VM, VM),
        scratch_shapes=[
            pltpu.VMEM((4, 3, D, 256), bf16),
            pltpu.VMEM((16, PACK, 128), bf16),
            pltpu.VMEM((BLOCKS, PACK, 128), bf16),
            pltpu.VMEM((3, TILE, 128), f32),
            pltpu.VMEM((TILES, TILE, 256), bf16),
            pltpu.VMEM((4, TILE, 256), bf16),
            pltpu.VMEM((TILES, HD + 16, TILE), bf16),
            pltpu.VMEM((1, TILE), f32),
            pltpu.VMEM((HD + 16, TILE), f32),
            pltpu.VMEM((TILE, TILE), f32),
            pltpu.VMEM((TILE, TILE), f32),
            pltpu.VMEM((16, HT, 128), bf16),
            pltpu.SemaphoreType.DMA((4, 3)),
            pltpu.SemaphoreType.DMA((16,)),
            pltpu.SemaphoreType.DMA((16,)),
            pltpu.SemaphoreType.DMA((16,)),
            pltpu.SemaphoreType.DMA((16,)),
            pltpu.SemaphoreType.DMA((16,)),
            pltpu.SemaphoreType.DMA((16,)),
            pltpu.SemaphoreType.DMA((16,)),
        ],
        compiler_params=params(0),
    )(frames, segment_ids, gain, w_qkv)


FIRST = lambda c: ((c + 1) // 2) % 2
SECOND = lambda c: c // 2


def chip_bits(x, y, z):
    return [FIRST(x), FIRST(y), FIRST(z), SECOND(x), SECOND(y), SECOND(z)]


ORDER = [[(p + k) % 3 + 3 * (p // 3) for k in range(3)] + [k + 3 * (1 - p // 3) for k in range(3)] for p in range(6)]


def position(part, y_lo, x, z, y_hi):
    bits = chip_bits(x, y_hi * 2 + y_lo, z)
    at = 0
    for k in range(6):
        at = at * 2 + bits[ORDER[part][k]]
    return at


class Net:
    def __init__(self, place):
        self.x, self.z = lax.div(place.head, 4), lax.rem(place.head, 4)
        self.y = place.y_hi * 2 + place.y_lo
        self.core = place.core
        self.bits = [lax.rem(lax.div(c + 1, 2), 2) for c in (self.x, self.y, self.z)]
        self.bits += [lax.div(c, 2) for c in (self.x, self.y, self.z)]

    def across(self, pairing, mask):
        moved = []
        for k, c in enumerate((self.x, self.y, self.z)):
            far = c + 1 - 2 * lax.rem(c, 2) if pairing == 0 else 3 - c
            moved.append(far if mask >> (2 - k) & 1 else c)
        x, y, z = moved
        return (lax.rem(y, 2) * 16 + x * 4 + z, lax.div(y, 2) * 2 + self.core)

    def neighbour(self, dim):
        return self.across(dim // 3, 4 >> dim % 3)

    def greet(self, barrier):
        for pairing in range(2):
            for mask in range(1, 8):
                greet(barrier, self.across(pairing, mask))

    GREETINGS = 14


class Part:
    def __init__(self, net, acc, land, tail, at, tail_at, count, part, send, recv, pieces=()):
        self.net, self.acc, self.land, self.tail, self.part, self.pieces = net, acc, land, tail, part, pieces
        self.units, self.tail_units = pl.ds(at, count), pl.ds(tail_at, count)
        self.count, self.send, self.recv = count, send, recv

    def bit(self, stage):
        return self.net.bits[ORDER[self.part][stage]]

    def base(self, stage):
        at = 0
        for k in range(stage + 1):
            at = at + self.bit(k) * (32 >> k)
        return at

    def landing(self, stage):
        return sum(32 >> k for k in range(stage))

    def hop(self, stage):
        half = 32 >> stage
        base = self.base(stage - 1) + (1 - self.bit(stage)) * half
        return remote(
            self.acc.at[self.units, pl.ds(base, half)],
            self.land.at[self.units, pl.ds(self.landing(stage), half)],
            self.send[0].at[self.send[1], stage],
            self.recv[0].at[self.recv[1], stage],
            self.net.neighbour(ORDER[self.part][stage]),
        )

    def start(self):
        self.hop(0).start()

    def hops(self, stage):
        return list(self.pieces) if stage == 0 and self.pieces else [self.hop(stage)]

    def total(self, base, landed, group):
        mine = self.acc[self.units, pl.ds(base, group)].astype(f32)
        return (mine + self.land[self.units, pl.ds(landed, group)].astype(f32)).astype(bf16)

    def add(self, base, landed, count):
        group = min(count, 4)

        def body(i):
            here = pl.ds(base + i * group, group)
            self.acc[self.units, here] = self.total(base + i * group, landed + i * group, group)

        loop(count // group, body)

    def advance(self, stage):
        for hop in self.hops(stage):
            hop.wait_recv()
        half = 16 >> stage
        base, landed = self.base(stage), self.landing(stage)
        bit = self.bit(stage + 1)
        self.add(base + (1 - bit) * half, landed + (1 - bit) * half, half)
        self.hop(stage + 1).start()
        self.add(base + bit * half, landed + bit * half, half)

    def settle(self):
        self.hop(2).wait_recv()
        for at in range(0, 8, 4):
            self.tail[self.tail_units, at : at + 4] = self.total(self.base(2) + at, self.landing(2) + at, 4)

    def finish(self):
        for stage in range(3):
            for hop in self.hops(stage):
                hop.wait_send()


class Exchange:
    def __init__(self, net, pairing, tail, land, send, recv):
        self.net, self.pairing, self.tail, self.land, self.send, self.recv = net, pairing, tail, land, send, recv

    def row(self, mask):
        at = 0
        for k in range(3):
            bit = self.net.bits[3 * self.pairing + k]
            at = at + (1 - bit if mask >> (2 - k) & 1 else bit) * (4 >> k)
        return at

    def hop(self, mask):
        return remote(
            self.tail.at[:, self.row(mask)], self.land.at[mask - 1],
            self.send.at[mask - 1], self.recv.at[mask - 1], self.net.across(self.pairing, mask),
        )

    def start(self):
        for mask in range(1, 8):
            self.hop(mask).start()

    def result(self, unit):
        total = self.tail[unit, self.row(0)].astype(f32)
        for mask in range(1, 8):
            total = total + self.land[mask - 1, unit].astype(f32)
        return total

    def wait(self):
        for mask in range(1, 8):
            self.hop(mask).wait_recv()

    def finish(self):
        for mask in range(1, 8):
            self.hop(mask).wait_send()


class Shared:
    def __init__(self, net, place, value, land, send, recv):
        self.net, self.place, self.value, self.land, self.send, self.recv = net, place, value, land, send, recv

    def hops(self, pairing):
        if pairing == 2:
            return [
                remote(self.value.at[2], self.land.at[2, 0], self.send.at[2, 0], self.recv.at[2, 0], self.place.partner)
            ]
        return [
            remote(
                self.value.at[pairing], self.land.at[pairing, mask - 1],
                self.send.at[pairing, mask - 1], self.recv.at[pairing, mask - 1], self.net.across(pairing, mask),
            )
            for mask in range(1, 8)
        ]

    def start(self, pairing):
        for hop in self.hops(pairing):
            hop.start()

    def take(self, pairing):
        total = self.value[pairing]
        for k, hop in enumerate(self.hops(pairing)):
            hop.wait_recv()
            total = total + self.land[pairing, k]
        self.value[pairing + 1] = total

    def finish(self):
        for pairing in range(3):
            for hop in self.hops(pairing):
                hop.wait_send()


TURN = [u % 6 for u in range(18)]
COUNTS = [3, 3, 3, 3, 2, 2]
STARTS = [0, 3, 6, 9, 12, 14]
SLOT = [STARTS[u % 6] + u // 6 for u in range(16)]
FINAL = list(range(8)) + [10 + (v % 4) * 2 + v // 4 for v in range(8)] + [8, 9]


class MidSums:
    def __init__(self, place, fin, side, down, sem, up_out, out_out, down_out):
        self.place, self.fin, self.side, self.down, self.sem = place, fin, side, down, sem
        self.up_out, self.out_out, self.down_out = up_out, out_out, down_out

    def targets(self):
        return [(self.place.core * 16 + self.place.head, self.place.y_hi * 2 + k) for k in range(2)]

    def sources(self):
        return [(m * 16 + self.place.head, self.place.y_hi * 2 + self.place.y_lo) for m in range(2)]

    def self_count(self):
        return jnp.where(self.place.y_lo == self.place.core, 1, 0)

    def greet(self, barrier):
        greet(barrier, self.place.partner)
        for device in self.sources():

            @pl.when(jnp.logical_not(self.place.is_self(device)))
            def _(device=device):
                greet(barrier, device)

    def greetings(self):
        return 3 - self.self_count()

    def store(self, unit, value):
        self.fin[FINAL[unit]] = value.reshape(2, 8, 256)

    def aside(self):
        return remote(
            self.fin.at[0:10, 1 - self.place.core], self.side, self.sem.at[0], self.sem.at[1], self.place.partner
        )

    def down_hop(self, k):
        return (
            self.fin.at[10 + 4 * k : 14 + 4 * k],
            self.down.at[self.place.y_lo],
            self.sem.at[2 + k],
            self.sem.at[4 + self.place.y_lo],
            self.targets()[k],
        )

    def start(self):
        self.aside().start()
        for k in range(2):
            send_to(self.place, *self.down_hop(k))

    def finish(self):
        place = self.place
        self.aside().wait_recv()
        mine, other = place.core, 1 - place.core
        for u in range(8):
            self.up_out[:, pl.ds(mine * 2048 + u * 256, 256)] = self.fin[u, mine]
            self.up_out[:, pl.ds(other * 2048 + u * 256, 256)] = self.side[u]
        for u in range(2):
            self.out_out[:, pl.ds(mine * 512 + u * 256, 256)] = self.fin[8 + u, mine]
            self.out_out[:, pl.ds(other * 512 + u * 256, 256)] = self.side[8 + u]
        for m in range(2):
            arrived(self.down.at[m], self.sem.at[4 + m])
            for v in range(4):
                group, half = v // 2, v % 2
                self.down_out[group * 16 : group * 16 + 16, m * 512 + half * 256 : m * 512 + half * 256 + 256] = (
                    self.down[m, v].reshape(16, 256)
                )
        self.aside().wait_send()
        for k in range(2):
            sent_to(place, *self.down_hop(k))


MID_OUT = (
    jax.ShapeDtypeStruct((8, FF), f32),
    jax.ShapeDtypeStruct((8, D), f32),
    jax.ShapeDtypeStruct((32, D), f32),
)
MID_SCRATCH = [
    pltpu.VMEM((18, 2, 8, 256), f32),
    pltpu.VMEM((10, 8, 256), f32),
    pltpu.VMEM((2, 4, 2, 8, 256), f32),
    pltpu.SemaphoreType.DMA((6,)),
]


def spread(target, unit_slot, turn, block):
    for chip in range(64):
        y_lo, x, z, y_hi = chip // 32, chip // 8 % 4, chip // 2 % 4, chip % 2
        target[unit_slot, position(turn, y_lo, x, z, y_hi)] = block[chip * 16 : chip * 16 + 16]


ROOT = math.sqrt(2.0 / math.pi)
CUBE = 0.044715


HOOKS = (1, 7, 18, 19, 20, 22)


def rest_kernel(
    o_in, x_ref, dy_ref, gain1_ref, gain2_ref, lse_ref, w_out, w_up, w_down, w_qkv, pk_in, ot_in,
    y_ref, dx_ref, qkv_out, gain_out, up_out, out_out, down_out,
    o2, b2, dm2, yside, hside, da_side, gain2_grad, gs, land, outg, land2, tail, tail_land, da_in, stage1,
    part, landed, dqkv_in, stage2, fin, side, down, a2, dhalf, gs3, land3, tail3, tail_land3, gain_value, gain_land,
    fin3, side3,
    w_sem, l_sem, p_send, p_recv, q_send, q_recv, h_send, h_recv, a_send, a_recv, b_send, b_recv,
    n_send, n_recv, t_send, t_recv, e_send, e_recv, g_send, g_recv, m_sem,
):
    place = Place()
    core = place.core
    net = Net(place)

    def across(k, src, dst):
        return remote(src, dst, p_send.at[k], p_recv.at[k], place.partner)

    def first_hop(unit):
        bit = net.bits[TURN[unit]]
        return remote(
            gs.at[SLOT[unit], pl.ds((1 - bit) * 32, 32)], land.at[SLOT[unit], 0:32],
            h_send.at[unit], h_recv.at[unit], net.neighbour(TURN[unit]),
        )

    tails = [tail.at[0:9], tail.at[9:18]]
    main = [
        Part(
            net, gs, land, tail, STARTS[p], STARTS[p], COUNTS[p], p, (n_send, p), (n_recv, p),
            [first_hop(p + 6 * k) for k in range(COUNTS[p])],
        )
        for p in range(6)
    ]
    outs = [
        Part(net, outg, land2, tail, u, 16 + u, 1, TURN[16 + u], (n_send, 6 + u), (n_recv, 6 + u))
        for u in range(2)
    ]
    ends = [Exchange(net, 1 - g, tails[g], tail_land.at[g], e_send.at[g], e_recv.at[g]) for g in range(2)]
    mid = MidSums(place, fin, side, down, m_sem, up_out, out_out, down_out)
    sums = [Part(net, gs3, land3, tail3, u, u, 1, u, (t_send, u), (t_recv, u)) for u in range(6)]
    ends3 = [
        Exchange(net, 1 - g, tail3.at[3 * g : 3 * g + 3], tail_land3.at[g], e_send.at[2 + g], e_recv.at[2 + g])
        for g in range(2)
    ]
    gains = Shared(net, place, gain_value, gain_land, g_send, g_recv)

    barrier = pltpu.get_barrier_semaphore()
    greet_all(place, barrier, place.block_device)
    greet_all(place, barrier, place.head_device)
    net.greet(barrier)
    mid.greet(barrier)

    def da_hop(h):
        return (
            stage1.at[h], da_in.at[place.slot], a_send.at[h], a_recv.at[place.slot], place.head_device(h),
        )

    a_hop = across(6, a2.at[0:T], a2.at[T : 2 * T])

    def feed_forward(wo, wu, wd, b2t, gzt, x1s, ysum, hsum):
        def up_copy(j):
            at = pl.multiple_of(core * 2048 + j * 512, 512)
            return pltpu.make_async_copy(w_up.at[:, pl.ds(at, 512)], wu.at[j], w_sem.at[1 + j])

        def down_copy(j):
            at = pl.multiple_of(core * 2048 + j * 512, 512)
            return pltpu.make_async_copy(w_down.at[pl.ds(at, 512)], wd.at[j], w_sem.at[5 + j])

        out_copy = pltpu.make_async_copy(w_out, wo, w_sem.at[0])
        out_copy.start()
        for j in range(4):
            up_copy(j).start()
            down_copy(j).start()
        dm2[0:T] = dy_ref[0]
        for m in range(8):
            lo, hi = swap_halves(o_in[2 * m], o_in[2 * m + 1])
            o2[0:HT, 128 * m : 128 * m + 128] = lo
            o2[HT:T, 128 * m : 128 * m + 128] = hi
        pl.semaphore_wait(barrier, 2 * (16 - place.self_count) + Net.GREETINGS + mid.greetings())
        dm_hop = across(0, dm2.at[0:T], dm2.at[T : 2 * T])
        o_hop = across(1, o2.at[0:T], o2.at[T : 2 * T])
        dm_hop.start()
        o_hop.start()
        out_copy.wait()
        x1 = x_ref[0].astype(f32) + dot(o2[0:T], wo[...])
        x1s[...] = x1
        scale1 = lax.rsqrt(jnp.mean(x1 * x1, axis=-1, keepdims=True) + EPS)
        b2[0:T] = (x1 * scale1 * gain2_ref[...]).astype(bf16)
        b_hop = across(2, b2.at[0:T], b2.at[T : 2 * T])
        b_hop.start()
        x = x_ref[0].astype(f32)
        a2[0:T] = (x * lax.rsqrt(jnp.mean(x * x, axis=-1, keepdims=True) + EPS) * gain1_ref[...]).astype(bf16)
        a_hop.start()
        dm_hop.wait_recv()
        b_hop.wait_recv()
        b2t[...] = transposed(b2[...])

        for j in range(4):
            up_copy(j).wait()
            down_copy(j).wait()
            z = dot(b2[...], wu[j])
            zz = z * z
            th = jnp.tanh(ROOT * z * (1.0 + CUBE * zz))
            half = 0.5 * (1.0 + th)
            gz = (z * half).astype(bf16)
            slope = half + 0.5 * z * (1.0 - th * th) * (ROOT * (1.0 + 3.0 * CUBE * zz))
            dz = (dot_nt(dm2[...], wd[j]) * slope).astype(bf16)
            gzt[j * 512 : (j + 1) * 512] = transposed(gz)
            yj = dot(gz, wd[j])
            hj = dot_nt(dz, wu[j])
            if j == 0:
                ysum[...] = yj
                hsum[...] = hj
            else:
                ysum[...] += yj
                hsum[...] += hj
            up = dot(b2t[...], dz).astype(bf16)
            for u in range(2):
                unit = 2 * j + u
                spread(gs, SLOT[unit], TURN[unit], up[:, u * 256 : u * 256 + 256])
                first_hop(unit).start()

        y_hop = across(3, ysum.at[T : 2 * T], yside)
        h_hop = across(4, hsum.at[T : 2 * T], hside)
        h_hop.start()
        y_hop.start()

        def down_units(u):
            for y_lo in range(2):
                at = y_lo * 512 + u * 256
                grad = dot(gzt[...], dm2[:, at : at + 256]).astype(bf16)
                for owner in range(32):
                    for group in range(4):
                        unit = 8 + u * 4 + group
                        place_at = position(TURN[unit], y_lo, owner // 8, owner // 2 % 4, owner % 2)
                        gs[SLOT[unit], place_at] = grad[owner * 64 + group * 16 : owner * 64 + group * 16 + 16]
            for group in range(4):
                first_hop(8 + u * 4 + group).start()

        down_units(0)
        h_hop.wait_recv()
        x1 = x1s[...]
        scale1 = lax.rsqrt(jnp.mean(x1 * x1, axis=-1, keepdims=True) + EPS)
        dh2 = hsum[0:T] + hside[...]
        gain2_grad[...] = jnp.sum(dh2 * x1 * scale1, axis=0, keepdims=True)
        dn = dh2 * gain2_ref[...]
        back = scale1 * dn - x1 * (scale1 * scale1 * scale1) * jnp.mean(dn * x1, axis=-1, keepdims=True)
        dx1 = dy_ref[0].astype(f32) + back
        hside[...] = dx1
        da = dx1.astype(bf16)
        da_side[0, 0:T] = da[:, 0:512]
        da_side[1, 0:T] = da[:, 512:1024]
        side_hop = across(5, da_side.at[1 - core, 0:T], da_side.at[1 - core, T : 2 * T])
        side_hop.start()
        for g in range(4):
            dattn = dot_nt(da, wo[256 * g : 256 * g + 256]).astype(bf16)
            for m in range(2):
                tile = dattn[:, 128 * m : 128 * m + 128]
                packed = swap_halves(tile[:HT], tile[HT:])
                for e in range(2):
                    h = 4 * g + 2 * m + e
                    stage1[h] = packed[e]
                    send_to(place, *da_hop(h))
        down_units(1)
        y_hop.wait_recv()
        y_ref[0] = (x1 + ysum[0:T] + yside[...]).astype(bf16)
        o_hop.wait_recv()
        side_hop.wait_recv()
        out = dot(transposed(o2[...]), da_side[core]).astype(bf16)
        for u in range(2):
            spread(outg, u, TURN[16 + u], out[:, u * 256 : u * 256 + 256])
            outs[u].start()
        for hop in (dm_hop, o_hop, b_hop, y_hop, h_hop, side_hop):
            hop.wait_send()

    pl.run_scoped(
        feed_forward,
        pltpu.VMEM((D, D), bf16),
        pltpu.VMEM((4, D, 512), bf16),
        pltpu.VMEM((4, 512, D), bf16),
        pltpu.VMEM((D, 2 * T), bf16),
        pltpu.VMEM((2048, 2 * T), bf16),
        pltpu.VMEM((T, D), f32),
        pltpu.VMEM((2 * T, D), f32),
        pltpu.VMEM((2 * T, D), f32),
    )

    def hook(which):
        if which < 2:
            for sums_of in main:
                sums_of.advance(which)
            if which == 1:
                for sums_of in outs:
                    sums_of.advance(0)
        elif which == 2:
            for sums_of in main:
                sums_of.settle()
            ends[0].start()
            for sums_of in outs:
                sums_of.advance(1)
        elif which == 3:
            for sums_of in outs:
                sums_of.settle()
            ends[1].start()
        elif which == 4:
            for end in ends:
                end.wait()
            for unit in range(16):
                group = SLOT[unit] // 9
                mid.store(unit, ends[group].result(SLOT[unit] - 9 * group))
            for u in range(2):
                mid.store(16 + u, ends[1].result(7 + u))
            mid.start()
        else:
            mid.finish()

    def key_hop(m):
        return (
            stage2.at[m, 0:T], dqkv_in.at[place.head, 0:T], b_send.at[0, m], b_recv.at[0, place.head],
            place.block_device(m),
        )

    def query_hop(m):
        return (
            stage2.at[m, T:GRAD], dqkv_in.at[place.head, T:GRAD], b_send.at[1, m], b_recv.at[1, place.head],
            place.block_device(m),
        )

    def part_hop(j):
        return remote(part.at[j], landed.at[j], q_send.at[j], q_recv.at[j], place.partner)

    def attention(pk, ot, seg, keys, queries, kt, gp, delta, dq, dkv):
        pk_copy = pltpu.make_async_copy(pk_in, pk, l_sem.at[0])
        ot_copy = pltpu.make_async_copy(ot_in, ot, l_sem.at[1])
        pk_copy.start()
        ot_copy.start()
        pk_copy.wait()
        fill_operands(place, pk, seg, keys, queries)
        low = lax.broadcasted_iota(jnp.int32, (HT, 128), 1) < HD

        def prepare(t):
            kt[t] = transposed(keys[t, :, 0:128])[:HD]
            dkv[t] = jnp.zeros((TILE, 128), f32)

        loop(TILES, prepare)
        ot_copy.wait()

        def prepare_query(j):
            for b in range(4):
                m = j * 4 + b
                arrived(da_in.at[m], a_recv.at[m])
                packed = da_in[m].astype(f32)
                gp[j, b * T : b * T + HT] = jnp.where(low, 0.0, pltpu.roll(packed, HD, 1)).astype(bf16)
                gp[j, b * T + HT : b * T + T] = jnp.where(low, 0.0, packed).astype(bf16)
            delta[j] = jnp.sum(gp[j].astype(f32).T[HD:] * ot[j], axis=0, keepdims=True)
            dq[j] = jnp.zeros((HD, TILE), f32)

        loop(4, prepare_query)
        factor = jnp.where(lax.broadcasted_iota(jnp.int32, (1, 128), 1) < HD, LN2, 1.0)

        def give(j):
            part[j] = (dkv[place.own_tile(j, 1 - core)] * factor).astype(bf16)
            part_hop(j).start()

        def take(j):
            alone = jnp.logical_and(core == 0, j == 3)

            @pl.when(jnp.logical_not(alone))
            def _():
                part_hop(j).wait_recv()

            total = dkv[place.own_tile(j)] * factor
            total = (total + jnp.where(alone, 0.0, landed[j].astype(f32))).astype(bf16)
            for b in range(4):
                m = j * 4 + b
                stage2[m, 0:T] = total[b * T : (b + 1) * T]
                send_to(place, *key_hop(m))

        def step(j, k_tile, diagonal):
            rows = keys[k_tile]
            scores = dot_nt(rows, queries[j])
            if diagonal:
                scores = causal(scores)
            weights = jnp.exp2(scores - lse_ref[j])
            slopes = (weights * (dot_nt(rows[:, 0:128], gp[j]) - delta[j])).astype(bf16)
            weights = weights.astype(bf16)
            dkv[k_tile] += dot(weights, gp[j]) + dot(slopes, queries[j, :, 0:128])
            dq[j] += dot(kt[k_tile], slopes)

        def hooks(n):
            for which in range(6):
                if HOOKS[which] < STEPS:

                    @pl.when(n == HOOKS[which])
                    def _(which=which):
                        hook(which)

        turn = lax.div(place.head, 4)

        def owned(k_tile):
            return lax.rem(lax.div(k_tile + 1, 2), 2) == core

        def key_tile(i, n):
            k_tile = key_order(place, i)
            skip = 0
            for j in range(4):
                skip = skip + jnp.where(place.own_tile(j) < k_tile, 1, 0)

            def query_tile(at, n):
                hooks(n)
                j = jnp.where(k_tile == 0, lax.rem(at + turn, 4), at)
                diagonal = place.own_tile(j) == k_tile

                @pl.when(diagonal)
                def _():
                    step(j, k_tile, True)

                @pl.when(jnp.logical_not(diagonal))
                def _():
                    step(j, k_tile, False)

                @pl.when(k_tile == 0)
                def _():
                    packed = pack_transposed(dq[j] * SCALE)
                    for b in range(4):
                        m = j * 4 + b
                        stage2[m, T:GRAD] = packed[b]
                        send_to(place, *query_hop(m))

                return n + 1

            n = lax.fori_loop(skip, 4, query_tile, n)
            mine = owned(k_tile)
            before = key_order(place, jnp.maximum(i - 1, 0))

            @pl.when(jnp.logical_and(jnp.logical_not(mine), jnp.logical_not(jnp.logical_and(core == 1, k_tile == 7))))
            def _():
                give(lax.div(k_tile, 2))

            @pl.when(jnp.logical_and(i > 0, owned(before)))
            def _():
                take(lax.div(before, 2))

            return n

        lax.fori_loop(0, TILES, key_tile, 0)

        @pl.when(core == 0)
        def _():
            take(0)

        for which in range(6):
            if HOOKS[which] == STEPS:
                hook(which)

    pl.run_scoped(
        attention,
        pltpu.VMEM((BLOCKS, PACK, 128), bf16),
        pltpu.VMEM((4, HD, TILE), f32),
        pltpu.VMEM((3, TILE, 128), f32),
        pltpu.VMEM((TILES, TILE, 256), bf16),
        pltpu.VMEM((4, TILE, 256), bf16),
        pltpu.VMEM((TILES, HD, TILE), bf16),
        pltpu.VMEM((4, TILE, 128), bf16),
        pltpu.VMEM((4, 1, TILE), f32),
        pltpu.VMEM((4, HD, TILE), f32),
        pltpu.VMEM((TILES, TILE, 128), f32),
    )

    def last(w_scr, dn, a2t):
        weight = pltpu.make_async_copy(w_qkv, w_scr, l_sem.at[2])
        weight.start()
        a_hop.wait_recv()
        a2t[...] = transposed(a2[...])
        for m in range(8):
            for h in (2 * m, 2 * m + 1):
                arrived(dqkv_in.at[h, 0:T], b_recv.at[0, h])
                arrived(dqkv_in.at[h, T:GRAD], b_recv.at[1, h])
            lo, hi = swap_halves(dqkv_in[2 * m, T:GRAD], dqkv_in[2 * m + 1, T:GRAD])
            dk, dv = swap_halves(dqkv_in[2 * m, 0:T], dqkv_in[2 * m + 1, 0:T])
            dn[0:HT, 128 * m : 128 * m + 128] = lo
            dn[HT:T, 128 * m : 128 * m + 128] = hi
            dn[:, D + 128 * m : D + 128 * m + 128] = dk
            dn[:, 2 * D + 128 * m : 2 * D + 128 * m + 128] = dv
            at = 128 * (m % 4)
            dhalf[m // 4, 0:HT, at : at + 128] = lo
            dhalf[m // 4, HT:T, at : at + 128] = hi
            dhalf[m // 4, 0:T, 512 + at : 512 + at + 128] = dk
            dhalf[m // 4, 0:T, 1024 + at : 1024 + at + 128] = dv
        d_hop = across(7, dhalf.at[1 - core, 0:T], dhalf.at[1 - core, T : 2 * T])
        d_hop.start()
        d_hop.wait_recv()
        for u in range(6):
            spread(gs3, u, u, dot(a2t[...], dhalf[core, :, u * 256 : u * 256 + 256]).astype(bf16))
            sums[u].start()
        weight.wait()
        x = x_ref[0].astype(f32)
        scale = lax.rsqrt(jnp.mean(x * x, axis=-1, keepdims=True) + EPS)
        dh1 = dot_nt(dn[...], w_scr[...])
        gain1_grad = jnp.sum(dh1 * x * scale, axis=0, keepdims=True)
        both = [gain1_grad[:, 128 * k : 128 * k + 128] for k in range(8)]
        both += [gain2_grad[:, 128 * k : 128 * k + 128] for k in range(8)]
        gain_value[0] = jnp.concatenate(both, axis=0)
        gains.start(0)
        dxn = dh1 * gain1_ref[...]
        back = scale * dxn - x * (scale * scale * scale) * jnp.mean(dxn * x, axis=-1, keepdims=True)
        dx_ref[0] = (hside[...] + back).astype(bf16)

        for stage in range(2):
            for sums_of in sums:
                sums_of.advance(stage)
            gains.take(stage)
            gains.start(stage + 1)
            for which in range(6):
                if HOOKS[which] == STEPS + 1 + stage:
                    hook(which)
        for g in range(2):
            for sums_of in sums[3 * g : 3 * g + 3]:
                sums_of.settle()
            ends3[g].start()
        gains.take(2)
        for which in range(6):
            if HOOKS[which] == STEPS + 3:
                hook(which)
        for g in range(2):
            ends3[g].wait()
            for u in range(3):
                fin3[3 * g + u] = ends3[g].result(u).reshape(2, 8, 256)
        aside = across(8, fin3.at[:, 1 - core], side3)
        aside.start()
        for which in range(6):
            if HOOKS[which] == STEPS + 4:
                hook(which)
        shard = place.s * 4 + place.r
        turn = lax.rem(128 - lax.rem(shard, 16) * 8, 128)
        for k in range(2):
            row = gain_value[3, pl.ds(8 * k + lax.div(shard, 16), 1)]
            gain_out[k : k + 1] = pltpu.roll(row, turn, 1)
        aside.wait_recv()
        mine, other = core, 1 - core
        for u in range(6):
            at = (u // 2) * D + (u % 2) * 256
            qkv_out[:, pl.ds(at + mine * 512, 256)] = fin3[u, mine]
            qkv_out[:, pl.ds(at + other * 512, 256)] = side3[u]
        for hop in (a_hop, d_hop, aside):
            hop.wait_send()

    pl.run_scoped(
        last,
        pltpu.VMEM((D, 3 * D), bf16),
        pltpu.VMEM((T, 3 * D), bf16),
        pltpu.VMEM((D, 2 * T), bf16),
    )

    def finish(n):
        sent_to(place, *da_hop(n))
        sent_to(place, *key_hop(n))
        sent_to(place, *query_hop(n))

    loop(16, finish)

    def given(j, carry):
        part_hop(j).wait_send()
        return carry

    lax.fori_loop(0, 4 - core, given, 0)
    for sums_of in main + outs + sums + ends + ends3 + [gains]:
        sums_of.finish()


def rest_call(o_in, frames, out_grad, gain1, gain2, lse, w_out, w_up, w_down, w_qkv, pk, ot):
    dma = pltpu.SemaphoreType.DMA
    return pl.pallas_call(
        rest_kernel,
        name="feed_forward_and_back",
        out_shape=(
            jax.ShapeDtypeStruct((1, T, D), bf16),
            jax.ShapeDtypeStruct((1, T, D), bf16),
            jax.ShapeDtypeStruct((8, 3 * D), f32),
            jax.ShapeDtypeStruct((8, 128), f32),
            jax.ShapeDtypeStruct((8, FF), f32),
            jax.ShapeDtypeStruct((8, D), f32),
            jax.ShapeDtypeStruct((32, D), f32),
        ),
        in_specs=[VM] * 6 + [ANY] * 6,
        out_specs=(VM,) * 7,
        scratch_shapes=[
            pltpu.VMEM((2 * T, D), bf16),
            pltpu.VMEM((2 * T, D), bf16),
            pltpu.VMEM((2 * T, D), bf16),
            pltpu.VMEM((T, D), f32),
            pltpu.VMEM((T, D), f32),
            pltpu.VMEM((2, 2 * T, 512), bf16),
            pltpu.VMEM((1, D), f32),
            pltpu.VMEM((16, 64, 16, 256), bf16),
            pltpu.VMEM((16, 56, 16, 256), bf16),
            pltpu.VMEM((2, 64, 16, 256), bf16),
            pltpu.VMEM((2, 56, 16, 256), bf16),
            pltpu.VMEM((18, 8, 16, 256), bf16),
            pltpu.VMEM((2, 7, 9, 16, 256), bf16),
            pltpu.VMEM((16, HT, 128), bf16),
            pltpu.VMEM((16, HT, 128), bf16),
            pltpu.VMEM((4, TILE, 128), bf16),
            pltpu.VMEM((4, TILE, 128), bf16),
            pltpu.VMEM((16, GRAD, 128), bf16),
            pltpu.VMEM((16, GRAD, 128), bf16),
            pltpu.VMEM((18, 2, 8, 256), f32),
            pltpu.VMEM((10, 8, 256), f32),
            pltpu.VMEM((2, 4, 2, 8, 256), f32),
            pltpu.VMEM((2 * T, D), bf16),
            pltpu.VMEM((2, 2 * T, 1536), bf16),
            pltpu.VMEM((6, 64, 16, 256), bf16),
            pltpu.VMEM((6, 56, 16, 256), bf16),
            pltpu.VMEM((6, 8, 16, 256), bf16),
            pltpu.VMEM((2, 7, 3, 16, 256), bf16),
            pltpu.VMEM((4, 16, 128), f32),
            pltpu.VMEM((3, 7, 16, 128), f32),
            pltpu.VMEM((6, 2, 8, 256), f32),
            pltpu.VMEM((6, 8, 256), f32),
            dma((9,)), dma((3,)), dma((9,)), dma((9,)), dma((4,)), dma((4,)), dma((16,)), dma((16,)),
            dma((16,)), dma((16,)), dma((2, 16)), dma((2, 16)), dma((8, 3)), dma((8, 3)), dma((6, 3)), dma((6, 3)),
            dma((4, 7)), dma((4, 7)), dma((3, 7)), dma((3, 7)), dma((6,)),
        ],
        compiler_params=params(1),
    )(o_in, frames, out_grad, gain1, gain2, lse, w_out, w_up, w_down, w_qkv, pk, ot)


def deliver_kernel(*refs):
    count = len(refs) // 2 - 2
    sources, gains, targets = refs[:count], refs[count], refs[count + 1 : 2 * count + 1]
    gain1, gain2, sem = refs[2 * count + 1 :]
    del sem
    for k in range(count):
        targets[k][...] = sources[k][...]
    gain1[...] = gains[0, 0:8]
    gain2[...] = gains[1, 0:8]


def deliver(arrays, gains):
    count = len(arrays)
    small = jax.ShapeDtypeStruct((8,), f32)
    return pl.pallas_call(
        deliver_kernel,
        name="deliver",
        out_shape=tuple(jax.ShapeDtypeStruct(v.shape, v.dtype) for v in arrays) + (small, small),
        in_specs=[VM] * (count + 1),
        out_specs=(VM,) * (count + 2),
        scratch_shapes=[pltpu.SemaphoreType.DMA((count,))],
    )(*arrays, gains)


def shards(frames, segment_ids, norm1_gain, w_qkv, w_out, norm2_gain, w_up, w_down, out_grad):
    gain1, gain2 = norm1_gain[None], norm2_gain[None]
    pk, o_in, lse, ot = forward_call(frames, segment_ids, gain1, w_qkv)
    y, dx, qkv_sum, gain_sums, up_sum, out_sum, down_sum = rest_call(
        o_in, frames, out_grad, gain1, gain2, lse, w_out, w_up, w_down, w_qkv, pk, ot
    )
    y, dx, qkv_sum, out_sum, up_sum, down_sum, gain1_sum, gain2_sum = deliver(
        (y, dx, qkv_sum, out_sum, up_sum, down_sum), gain_sums
    )
    return (y, dx, gain1_sum, qkv_sum, out_sum, gain2_sum, up_sum, down_sum)


def solution(mesh):
    return jax.shard_map(
        shards,
        mesh=mesh,
        in_specs=(
            P("row", "seq", None),
            P("row", "seq"),
            P(),
            P(),
            P(),
            P(),
            P(),
            P(),
            P("row", "seq", None),
        ),
        out_specs=(
            P("row", "seq", None),
            P("row", "seq", None),
            P(("seq", "row")),
            P(("seq", "row"), None),
            P(("seq", "row"), None),
            P(("seq", "row")),
            P(("seq", "row"), None),
            P(("seq", "row"), None),
        ),
        check_vma=False,
    )
```

```python
import functools
import math

import jax
import jax.numpy as jnp
from jax import lax
from jax.experimental import pallas as pl
from jax.experimental.pallas import tpu as pltpu
from jax.sharding import PartitionSpec as P

MESH = pl.DeviceIdType.MESH
f32 = jnp.float32
bf16 = jnp.bfloat16

D = 1024
H = 16
HD = 64
FF = 4096
T = 192
HT = T // 2
BLOCKS = 32
TILE = 768
TILES = 8
PACK = 304
GRAD = 288
EPS = 1e-05
NEG = -1e30
LOG2E = math.log2(math.e)
LN2 = math.log(2.0)
SCALE = HD**-0.5
VMEM_LIMIT = 60 * 1024 * 1024

ANY = pl.BlockSpec(memory_space=pl.ANY)
VM = pl.BlockSpec(memory_space=pltpu.VMEM)


def dot(a, b):
    return jnp.dot(a, b, preferred_element_type=f32)


def dot_nt(a, b):
    return lax.dot_general(a, b, (((1,), (1,)), ((), ())), preferred_element_type=f32)


def transposed(v):
    return v.astype(f32).T.astype(bf16)


def swap_halves(first, second):
    lane = lax.broadcasted_iota(jnp.int32, first.shape, 1)
    low = lane < HD
    first, second = first.astype(f32), second.astype(f32)
    return (
        jnp.where(low, first, pltpu.roll(second, HD, 1)).astype(bf16),
        jnp.where(low, pltpu.roll(first, HD, 1), second).astype(bf16),
    )


class Place:
    def __init__(self):
        self.s = lax.axis_index("seq")
        self.r = lax.axis_index("row")
        self.y_lo = lax.div(self.s, 16)
        self.head = lax.rem(self.s, 16)
        self.y_hi = lax.div(self.r, 2)
        self.core = lax.rem(self.r, 2)
        tile = lax.div(self.s, 4)
        self.block_core = lax.rem(lax.div(tile + 1, 2), 2)
        self.slot = lax.div(self.s, 8) * 4 + lax.rem(self.s, 4)
        self.partner = (self.s, self.r + 1 - 2 * self.core)
        self.self_served = jnp.logical_and(self.y_lo == self.core, self.block_core == self.core)
        self.self_count = jnp.where(self.self_served, 1, 0)

    def head_device(self, h):
        return (self.core * 16 + h, self.y_hi * 2 + self.block_core)

    def own_tile(self, j, core=None):
        core = self.core if core is None else core
        return 2 * j + lax.rem(j + core, 2)

    def own_block(self, n):
        return self.own_tile(lax.div(n, 4)) * 4 + lax.rem(n, 4)

    def block_device(self, n):
        return (self.own_block(n), self.y_hi * 2 + self.y_lo)

    def is_self(self, device):
        return jnp.logical_and(device[0] == self.s, device[1] == self.r)


def remote(src, dst, send, recv, device):
    return pltpu.make_async_remote_copy(
        src_ref=src, dst_ref=dst, send_sem=send, recv_sem=recv, device_id=device, device_id_type=MESH
    )


def send_to(place, src, dst, send, recv, device):
    own = place.is_self(device)

    @pl.when(own)
    def _():
        pltpu.make_async_copy(src, dst, recv).start()

    @pl.when(jnp.logical_not(own))
    def _():
        remote(src, dst, send, recv, device).start()


def sent_to(place, src, dst, send, recv, device):
    @pl.when(jnp.logical_not(place.is_self(device)))
    def _():
        remote(src, dst, send, recv, device).wait_send()


def arrived(dst, recv):
    pltpu.make_async_copy(dst, dst, recv).wait()


def greet(barrier, device):
    pl.semaphore_signal(barrier, inc=1, device_id=device, device_id_type=MESH)


def greet_all(place, barrier, device_of):
    def one(n, carry):
        device = device_of(n)

        @pl.when(jnp.logical_not(place.is_self(device)))
        def _():
            greet(barrier, device)

        return carry

    lax.fori_loop(0, 16, one, 0)


def loop(count, body):
    def one(n, carry):
        body(n)
        return carry

    lax.fori_loop(0, count, one, 0)


def params(collective_id):
    return pltpu.CompilerParams(
        collective_id=collective_id, has_side_effects=True, vmem_limit_bytes=VMEM_LIMIT
    )


def seg_column(pk_ref, block):
    tile = pk_ref[block, T + HT : PACK].astype(f32)
    return jnp.concatenate(
        [
            jnp.broadcast_to(tile[0:1], (128, 128)).T,
            jnp.broadcast_to(tile[1:2], (128, 128)).T[: T - 128],
        ],
        axis=0,
    )


def fill_segments(pk_ref, seg):
    first = seg_column(pk_ref, 0)
    last = seg_column(pk_ref, BLOCKS - 1)
    common = jnp.broadcast_to(first[T - 1 : T], (TILE, 128))
    seg[0] = common
    seg[1] = common
    seg[2] = common
    seg[0, 0:T] = first
    seg[2, TILE - T : TILE] = last


def seg_kind(tile):
    return jnp.where(tile == 0, 0, jnp.where(tile == TILES - 1, 2, 1))


def key_marks(seg, tile):
    number = lax.broadcasted_iota(jnp.int32, (TILE, 128), 1).astype(f32)
    return jnp.where(seg[seg_kind(tile)] == number, 1.0, 0.0).astype(bf16)


def query_marks(seg, tile):
    lane = lax.broadcasted_iota(jnp.int32, (TILE, 128), 1)
    other = jnp.logical_and(lane < 8, seg[seg_kind(tile)] != lane.astype(f32))
    return jnp.where(other, NEG, 0.0).astype(bf16)


def put_unpacked(packed, high, target):
    low = lax.broadcasted_iota(jnp.int32, (HT, 128), 1) < HD
    packed = packed.astype(f32)
    turned = pltpu.roll(packed, HD, 1)
    if high:
        target[0:HT] = jnp.where(low, 0.0, turned).astype(bf16)
        target[HT:T] = jnp.where(low, 0.0, packed).astype(bf16)
    else:
        target[0:HT] = jnp.where(low, packed, 0.0).astype(bf16)
        target[HT:T] = jnp.where(low, turned, 0.0).astype(bf16)


STEPS = 18


def walk(place, n):
    turn = lax.div(place.head, 4)
    j, start, end = lax.rem(turn, 4), 0, 0
    end = place.own_tile(j) + 1
    for k in range(1, 4):
        past = n >= end
        following = lax.rem(turn + k, 4)
        j = jnp.where(past, following, j)
        start = jnp.where(past, end, start)
        end = jnp.where(past, end + place.own_tile(following) + 1, end)
    at = n - start
    k_tile = jnp.where(at == 0, place.own_tile(j), at - 1)
    return j, k_tile, at == 0, n + 1 == end


def key_order(place, i):
    turn = lax.div(place.head, 4)
    return jnp.where(i == 7, 0, 7 - lax.rem(i + 2 * turn, 7))


def causal(scores):
    k = lax.broadcasted_iota(jnp.int32, scores.shape, 0)
    q = lax.broadcasted_iota(jnp.int32, scores.shape, 1)
    return jnp.where(k <= q, scores, NEG)


def load_keys(pk_ref, tile):
    return pk_ref[pl.ds(tile * 4, 4), 0:T].reshape(TILE, 128)


def pack_transposed(value_t):
    both = jnp.concatenate([value_t, value_t], axis=0).T
    lane = lax.broadcasted_iota(jnp.int32, (HT, 128), 1)
    return [
        jnp.where(lane < HD, both[b * T : b * T + HT], both[b * T + HT : b * T + T]).astype(bf16)
        for b in range(4)
    ]


FIRST = lambda c: ((c + 1) // 2) % 2
SECOND = lambda c: c // 2


def chip_bits(x, y, z):
    return [FIRST(x), FIRST(y), FIRST(z), SECOND(x), SECOND(y), SECOND(z)]


ORDER = [[(p + k) % 3 + 3 * (p // 3) for k in range(3)] + [k + 3 * (1 - p // 3) for k in range(3)] for p in range(6)]


def position(part, y_lo, x, z, y_hi):
    bits = chip_bits(x, y_hi * 2 + y_lo, z)
    at = 0
    for k in range(6):
        at = at * 2 + bits[ORDER[part][k]]
    return at


class Net:
    def __init__(self, place):
        self.x, self.z = lax.div(place.head, 4), lax.rem(place.head, 4)
        self.y = place.y_hi * 2 + place.y_lo
        self.core = place.core
        self.bits = [lax.rem(lax.div(c + 1, 2), 2) for c in (self.x, self.y, self.z)]
        self.bits += [lax.div(c, 2) for c in (self.x, self.y, self.z)]

    def across(self, pairing, mask):
        moved = []
        for k, c in enumerate((self.x, self.y, self.z)):
            far = c + 1 - 2 * lax.rem(c, 2) if pairing == 0 else 3 - c
            moved.append(far if mask >> (2 - k) & 1 else c)
        x, y, z = moved
        return (lax.rem(y, 2) * 16 + x * 4 + z, lax.div(y, 2) * 2 + self.core)

    def neighbour(self, dim):
        return self.across(dim // 3, 4 >> dim % 3)

    def greet(self, barrier):
        for pairing in range(2):
            for mask in range(1, 8):
                greet(barrier, self.across(pairing, mask))

    GREETINGS = 14


class Part:
    def __init__(self, net, acc, land, tail, at, tail_at, count, part, send, recv, pieces=()):
        self.net, self.acc, self.land, self.tail, self.part, self.pieces = net, acc, land, tail, part, pieces
        self.units, self.tail_units = pl.ds(at, count), pl.ds(tail_at, count)
        self.count, self.send, self.recv = count, send, recv

    def bit(self, stage):
        return self.net.bits[ORDER[self.part][stage]]

    def base(self, stage):
        at = 0
        for k in range(stage + 1):
            at = at + self.bit(k) * (32 >> k)
        return at

    def landing(self, stage):
        return sum(32 >> k for k in range(stage))

    def hop(self, stage):
        half = 32 >> stage
        base = self.base(stage - 1) + (1 - self.bit(stage)) * half
        return remote(
            self.acc.at[self.units, pl.ds(base, half)],
            self.land.at[self.units, pl.ds(self.landing(stage), half)],
            self.send[0].at[self.send[1], stage],
            self.recv[0].at[self.recv[1], stage],
            self.net.neighbour(ORDER[self.part][stage]),
        )

    def start(self):
        self.hop(0).start()

    def hops(self, stage):
        return list(self.pieces) if stage == 0 and self.pieces else [self.hop(stage)]

    def total(self, base, landed, group):
        mine = self.acc[self.units, pl.ds(base, group)].astype(f32)
        return (mine + self.land[self.units, pl.ds(landed, group)].astype(f32)).astype(bf16)

    def add(self, base, landed, count):
        group = min(count, 4)

        def body(i):
            here = pl.ds(base + i * group, group)
            self.acc[self.units, here] = self.total(base + i * group, landed + i * group, group)

        loop(count // group, body)

    def advance(self, stage):
        for hop in self.hops(stage):
            hop.wait_recv()
        half = 16 >> stage
        base, landed = self.base(stage), self.landing(stage)
        bit = self.bit(stage + 1)
        self.add(base + (1 - bit) * half, landed + (1 - bit) * half, half)
        self.hop(stage + 1).start()
        self.add(base + bit * half, landed + bit * half, half)

    def settle(self):
        self.hop(2).wait_recv()
        for at in range(0, 8, 4):
            self.tail[self.tail_units, at : at + 4] = self.total(self.base(2) + at, self.landing(2) + at, 4)

    def finish(self):
        for stage in range(3):
            for hop in self.hops(stage):
                hop.wait_send()


class Exchange:
    def __init__(self, net, pairing, tail, land, send, recv):
        self.net, self.pairing, self.tail, self.land, self.send, self.recv = net, pairing, tail, land, send, recv

    def row(self, mask):
        at = 0
        for k in range(3):
            bit = self.net.bits[3 * self.pairing + k]
            at = at + (1 - bit if mask >> (2 - k) & 1 else bit) * (4 >> k)
        return at

    def hop(self, mask):
        return remote(
            self.tail.at[:, self.row(mask)], self.land.at[mask - 1],
            self.send.at[mask - 1], self.recv.at[mask - 1], self.net.across(self.pairing, mask),
        )

    def start(self):
        for mask in range(1, 8):
            self.hop(mask).start()

    def result(self, unit):
        total = self.tail[unit, self.row(0)].astype(f32)
        for mask in range(1, 8):
            total = total + self.land[mask - 1, unit].astype(f32)
        return total

    def wait(self):
        for mask in range(1, 8):
            self.hop(mask).wait_recv()

    def finish(self):
        for mask in range(1, 8):
            self.hop(mask).wait_send()


class Shared:
    def __init__(self, net, place, value, land, send, recv):
        self.net, self.place, self.value, self.land, self.send, self.recv = net, place, value, land, send, recv

    def hops(self, pairing):
        if pairing == 2:
            return [
                remote(self.value.at[2], self.land.at[2, 0], self.send.at[2, 0], self.recv.at[2, 0], self.place.partner)
            ]
        return [
            remote(
                self.value.at[pairing], self.land.at[pairing, mask - 1],
                self.send.at[pairing, mask - 1], self.recv.at[pairing, mask - 1], self.net.across(pairing, mask),
            )
            for mask in range(1, 8)
        ]

    def start(self, pairing):
        for hop in self.hops(pairing):
            hop.start()

    def take(self, pairing):
        total = self.value[pairing]
        for k, hop in enumerate(self.hops(pairing)):
            hop.wait_recv()
            total = total + self.land[pairing, k]
        self.value[pairing + 1] = total

    def finish(self):
        for pairing in range(3):
            for hop in self.hops(pairing):
                hop.wait_send()


TURN = [u % 6 for u in range(18)]
COUNTS = [3, 3, 3, 3, 2, 2]
STARTS = [0, 3, 6, 9, 12, 14]
SLOT = [STARTS[u % 6] + u // 6 for u in range(16)]
FINAL = list(range(8)) + [10 + (v % 4) * 2 + v // 4 for v in range(8)] + [8, 9]


class MidSums:
    def __init__(self, place, fin, side, down, sem, up_out, out_out, down_out):
        self.place, self.fin, self.side, self.down, self.sem = place, fin, side, down, sem
        self.up_out, self.out_out, self.down_out = up_out, out_out, down_out

    def targets(self):
        return [(self.place.core * 16 + self.place.head, self.place.y_hi * 2 + k) for k in range(2)]

    def sources(self):
        return [(m * 16 + self.place.head, self.place.y_hi * 2 + self.place.y_lo) for m in range(2)]

    def self_count(self):
        return jnp.where(self.place.y_lo == self.place.core, 1, 0)

    def greet(self, barrier):
        greet(barrier, self.place.partner)
        for device in self.sources():

            @pl.when(jnp.logical_not(self.place.is_self(device)))
            def _(device=device):
                greet(barrier, device)

    def greetings(self):
        return 3 - self.self_count()

    def store(self, unit, value):
        self.fin[FINAL[unit]] = value.reshape(2, 8, 256)

    def aside(self):
        return remote(
            self.fin.at[0:10, 1 - self.place.core], self.side, self.sem.at[0], self.sem.at[1], self.place.partner
        )

    def down_hop(self, k):
        return (
            self.fin.at[10 + 4 * k : 14 + 4 * k],
            self.down.at[self.place.y_lo],
            self.sem.at[2 + k],
            self.sem.at[4 + self.place.y_lo],
            self.targets()[k],
        )

    def start(self):
        self.aside().start()
        for k in range(2):
            send_to(self.place, *self.down_hop(k))

    def finish(self):
        place = self.place
        self.aside().wait_recv()
        mine, other = place.core, 1 - place.core
        for u in range(8):
            self.up_out[:, pl.ds(mine * 2048 + u * 256, 256)] = self.fin[u, mine]
            self.up_out[:, pl.ds(other * 2048 + u * 256, 256)] = self.side[u]
        for u in range(2):
            self.out_out[:, pl.ds(mine * 512 + u * 256, 256)] = self.fin[8 + u, mine]
            self.out_out[:, pl.ds(other * 512 + u * 256, 256)] = self.side[8 + u]
        for m in range(2):
            arrived(self.down.at[m], self.sem.at[4 + m])
            for v in range(4):
                group, half = v // 2, v % 2
                self.down_out[group * 16 : group * 16 + 16, m * 512 + half * 256 : m * 512 + half * 256 + 256] = (
                    self.down[m, v].reshape(16, 256)
                )
        self.aside().wait_send()
        for k in range(2):
            sent_to(place, *self.down_hop(k))


MID_OUT = (
    jax.ShapeDtypeStruct((8, FF), f32),
    jax.ShapeDtypeStruct((8, D), f32),
    jax.ShapeDtypeStruct((32, D), f32),
)
MID_SCRATCH = [
    pltpu.VMEM((18, 2, 8, 256), f32),
    pltpu.VMEM((10, 8, 256), f32),
    pltpu.VMEM((2, 4, 2, 8, 256), f32),
    pltpu.SemaphoreType.DMA((6,)),
]


def spread(target, unit_slot, turn, block):
    for chip in range(64):
        y_lo, x, z, y_hi = chip // 32, chip // 8 % 4, chip // 2 % 4, chip % 2
        target[unit_slot, position(turn, y_lo, x, z, y_hi)] = block[chip * 16 : chip * 16 + 16]


ROOT = math.sqrt(2.0 / math.pi)
CUBE = 0.044715


HOOKS = (1, 7, 18, 19, 20, 22)


def block_kernel(
    x_ref, seg_ref, dy_ref, gain1_ref, gain2_ref, w_qkv, w_out, w_up, w_down,
    y_ref, dx_ref, qkv_out, gain_out, up_out, out_out, down_out, probs,
    pk, o_in, ot, lse, peaks, o2, b2, dm2, yside, hside, das, da_side, gain2_grad,
    gs, land, outg, land2, tail, tail_land, da_in, stage1,
    part, landed, dqkv_in, stage2, fin, side, down, a2, d_side, land3, tail3, tail_land3, gain_value, gain_land,
    fin3, side3,
    w_sem, l_sem, p_send, p_recv, q_send, q_recv, h_send, h_recv, a_send, a_recv, b_send, b_recv,
    n_send, n_recv, t_send, t_recv, e_send, e_recv, g_send, g_recv, m_sem,
    k_sem, x_send, x_recv, f_send, f_recv, c_send, c_recv, s_sem,
):
    place = Place()
    core = place.core
    net = Net(place)
    turn = lax.rem(lax.div(place.s, 4), 4)

    def across(k, src, dst):
        return remote(src, dst, p_send.at[k], p_recv.at[k], place.partner)

    def first_hop(unit):
        bit = net.bits[TURN[unit]]
        return remote(
            gs.at[SLOT[unit], pl.ds((1 - bit) * 32, 32)], land.at[SLOT[unit], 0:32],
            h_send.at[unit], h_recv.at[unit], net.neighbour(TURN[unit]),
        )

    tails = [tail.at[0:9], tail.at[9:18]]
    main = [
        Part(
            net, gs, land, tail, STARTS[p], STARTS[p], COUNTS[p], p, (n_send, p), (n_recv, p),
            [first_hop(p + 6 * k) for k in range(COUNTS[p])],
        )
        for p in range(6)
    ]
    outs = [
        Part(net, outg, land2, tail, u, 16 + u, 1, TURN[16 + u], (n_send, 6 + u), (n_recv, 6 + u))
        for u in range(2)
    ]
    ends = [Exchange(net, 1 - g, tails[g], tail_land.at[g], e_send.at[g], e_recv.at[g]) for g in range(2)]
    mid = MidSums(place, fin, side, down, m_sem, up_out, out_out, down_out)
    ends3 = [
        Exchange(net, 1 - g, tail3.at[3 * g : 3 * g + 3], tail_land3.at[g], e_send.at[2 + g], e_recv.at[2 + g])
        for g in range(2)
    ]
    gains = Shared(net, place, gain_value, gain_land, g_send, g_recv)

    barrier = pltpu.get_barrier_semaphore()
    greet_all(place, barrier, place.block_device)
    greet_all(place, barrier, place.head_device)
    net.greet(barrier)
    mid.greet(barrier)
    a_hop = across(6, a2.at[0:T], a2.at[T : 2 * T])

    def packet_hop(h):
        return (stage2.at[h], pk.at[place.s], x_send.at[h], x_recv.at[place.slot], place.head_device(h))

    def qkv(w_scr):
        def weight(g, section):
            at = pl.multiple_of(section * D + lax.rem(g + turn, 4) * 256, 256)
            return pltpu.make_async_copy(w_qkv.at[:, pl.ds(at, 256)], w_scr.at[g, section], k_sem.at[g, section])

        for g in range(4):
            for section in range(3):
                weight(g, section).start()
        x = x_ref[0].astype(f32)
        a = (x * lax.rsqrt(jnp.mean(x * x, axis=-1, keepdims=True) + EPS) * gain1_ref[...]).astype(bf16)
        a2[0:T] = a
        numbers = seg_ref[...].astype(f32)
        row = lax.broadcasted_iota(jnp.int32, (16, 128), 0)
        rest = jnp.concatenate([numbers[:, 128:T], jnp.zeros((1, 256 - T), f32)], axis=1)
        seg_tile = jnp.where(row == 0, numbers[:, :128], jnp.where(row == 1, rest, 0.0)).astype(bf16)
        pl.semaphore_wait(barrier, 2 * (16 - place.self_count) + Net.GREETINGS + mid.greetings())
        for g in range(4):
            for section in range(3):
                weight(g, section).wait()
            q = dot(a, w_scr[g, 0]) * (SCALE * LOG2E)
            k = dot(a, w_scr[g, 1])
            v = dot(a, w_scr[g, 2])
            for m in range(2):
                lanes = slice(128 * m, 128 * m + 128)
                h = 4 * lax.rem(g + turn, 4) + 2 * m
                kv = swap_halves(k[:, lanes].astype(bf16), v[:, lanes].astype(bf16))
                qq = q[:, lanes].astype(bf16)
                qp = swap_halves(qq[:HT], qq[HT:])
                for e in range(2):
                    stage2[h + e, 0:T] = kv[e]
                    stage2[h + e, T : T + HT] = qp[e]
                    stage2[h + e, T + HT : PACK] = seg_tile
                    send_to(place, *packet_hop(h + e))
        a_hop.start()

    pl.run_scoped(qkv, pltpu.VMEM((4, 3, D, 256), bf16))

    def out_hop(m):
        return (stage1.at[m], o_in.at[place.head], c_send.at[m], c_recv.at[place.head], place.block_device(m))

    def attention(seg, keys, queries, vt, top, acc, even, odd, even_p, odd_p):
        one = jnp.where(lax.broadcasted_iota(jnp.int32, (16, TILE), 0) == 0, 1.0, 0.0).astype(bf16)

        def forward(n):
            i = place.own_block(n)
            return remote(pk.at[i], pk.at[i], f_send.at[n], f_recv.at[n], place.partner)

        def key_tile(t):
            rows = load_keys(pk, t)
            keys[t, :, 0:128] = rows
            vt[t, 0:HD] = transposed(rows)[HD:]
            vt[t, HD : HD + 16] = one

        def own(j):
            for b in range(4):
                n = j * 4 + b
                arrived(pk.at[place.own_block(n)], x_recv.at[n])
                forward(n).start()
            t = place.own_tile(j)
            key_tile(t)
            for b in range(4):
                put_unpacked(pk[t * 4 + b, T : T + HT], False, queries.at[j, b * T : (b + 1) * T, 0:128])

        loop(4, own)

        def others(j):
            for b in range(4):
                forward(j * 4 + b).wait_recv()
            key_tile(place.own_tile(j, 1 - core))

        loop(4, others)
        fill_segments(pk, seg)

        def key_mark(t):
            keys[t, :, 128:256] = key_marks(seg, t)

        def query_mark(j):
            queries[j, :, 128:256] = query_marks(seg, place.own_tile(j))

        loop(TILES, key_mark)
        loop(4, query_mark)

        def score(n, scores):
            j, k_tile, _, _ = walk(place, jnp.minimum(n, STEPS - 1))
            scores[...] = dot_nt(keys[k_tile], queries[j])

        def keep(j, k_tile, weights, which):
            return pltpu.make_async_copy(weights, probs.at[j, k_tile], s_sem.at[which])

        def body(n, now, later, weights, which):
            j, k_tile, first, last = walk(place, n)

            @pl.when(n >= 2)
            def _():
                keep(j, k_tile, weights, which).wait()

            @pl.when(first)
            def _():
                score(n + 1, later)
                scores = causal(now[...])
                peak = jnp.max(scores, axis=0, keepdims=True)
                top[...] = peak
                value = jnp.exp2(scores - peak).astype(bf16)
                weights[...] = value
                acc[...] = dot(vt[k_tile], value)

            @pl.when(jnp.logical_not(first))
            def _():
                score(n + 1, later)
                scores = now[...]
                peak = jnp.maximum(top[...], jnp.max(scores, axis=0, keepdims=True))
                fade = jnp.exp2(top[...] - peak)
                top[...] = peak
                value = jnp.exp2(scores - peak).astype(bf16)
                weights[...] = value
                acc[...] = acc[...] * fade + dot(vt[k_tile], value)

            keep(j, k_tile, weights, which).start()
            peaks[j, k_tile] = top[...]

            @pl.when(last)
            def _():
                total = acc[HD : HD + 1]
                out_t = acc[0:HD] / total
                lse[j] = top[...] + jnp.log2(total)
                ot[j] = out_t
                packed = pack_transposed(out_t)
                for b in range(4):
                    m = j * 4 + b
                    stage1[m] = packed[b]
                    send_to(place, *out_hop(m))

        score(0, even)

        def pair(i):
            body(2 * i, even, odd, even_p, 0)
            body(2 * i + 1, odd, even, odd_p, 1)

        loop(STEPS // 2, pair)
        keep(0, 0, even_p, 0).wait()
        keep(0, 0, odd_p, 1).wait()

        def finish(n):
            sent_to(place, *packet_hop(n))
            forward(n).wait_send()
            sent_to(place, *out_hop(n))

        loop(16, finish)

    pl.run_scoped(
        attention,
        pltpu.VMEM((3, TILE, 128), f32),
        pltpu.VMEM((TILES, TILE, 256), bf16),
        pltpu.VMEM((4, TILE, 256), bf16),
        pltpu.VMEM((TILES, HD + 16, TILE), bf16),
        pltpu.VMEM((1, TILE), f32),
        pltpu.VMEM((HD + 16, TILE), f32),
        pltpu.VMEM((TILE, TILE), f32),
        pltpu.VMEM((TILE, TILE), f32),
        pltpu.VMEM((TILE, TILE), bf16),
        pltpu.VMEM((TILE, TILE), bf16),
    )

    def da_hop(h):
        return (
            stage1.at[h], da_in.at[place.slot], a_send.at[h], a_recv.at[place.slot], place.head_device(h),
        )

    def feed_forward(wo, wu, wd, b2t, gzt, x1s, ysum, hsum):
        def up_copy(j):
            at = pl.multiple_of(core * 2048 + j * 512, 512)
            return pltpu.make_async_copy(w_up.at[:, pl.ds(at, 512)], wu.at[j], w_sem.at[1 + j])

        def down_copy(j):
            at = pl.multiple_of(core * 2048 + j * 512, 512)
            return pltpu.make_async_copy(w_down.at[pl.ds(at, 512)], wd.at[j], w_sem.at[5 + j])

        out_copy = pltpu.make_async_copy(w_out, wo, w_sem.at[0])
        out_copy.start()
        for j in range(4):
            up_copy(j).start()
            down_copy(j).start()
        dm2[0:T] = dy_ref[0]
        dm_hop = across(0, dm2.at[0:T], dm2.at[T : 2 * T])
        dm_hop.start()
        for m in range(8):
            for h in (2 * m, 2 * m + 1):
                arrived(o_in.at[h], c_recv.at[h])
            lo, hi = swap_halves(o_in[2 * m], o_in[2 * m + 1])
            o2[0:HT, 128 * m : 128 * m + 128] = lo
            o2[HT:T, 128 * m : 128 * m + 128] = hi
        o_hop = across(1, o2.at[0:T], o2.at[T : 2 * T])
        o_hop.start()
        out_copy.wait()
        x1 = x_ref[0].astype(f32) + dot(o2[0:T], wo[...])
        x1s[...] = x1
        scale1 = lax.rsqrt(jnp.mean(x1 * x1, axis=-1, keepdims=True) + EPS)
        b2[0:T] = (x1 * scale1 * gain2_ref[...]).astype(bf16)
        b_hop = across(2, b2.at[0:T], b2.at[T : 2 * T])
        b_hop.start()
        dm_hop.wait_recv()
        b_hop.wait_recv()
        b2t[...] = transposed(b2[...])

        for j in range(4):
            up_copy(j).wait()
            down_copy(j).wait()
            z = dot(b2[...], wu[j])
            zz = z * z
            th = jnp.tanh(ROOT * z * (1.0 + CUBE * zz))
            half = 0.5 * (1.0 + th)
            gz = (z * half).astype(bf16)
            slope = half + 0.5 * z * (1.0 - th * th) * (ROOT * (1.0 + 3.0 * CUBE * zz))
            dz = (dot_nt(dm2[...], wd[j]) * slope).astype(bf16)
            gzt[j * 512 : (j + 1) * 512] = transposed(gz)
            yj = dot(gz, wd[j])
            hj = dot_nt(dz, wu[j])
            if j == 0:
                ysum[...] = yj
                hsum[...] = hj
            else:
                ysum[...] += yj
                hsum[...] += hj
            up = dot(b2t[...], dz).astype(bf16)
            for u in range(2):
                unit = 2 * j + u
                spread(gs, SLOT[unit], TURN[unit], up[:, u * 256 : u * 256 + 256])
                first_hop(unit).start()

        y_hop = across(3, ysum.at[T : 2 * T], yside)
        h_hop = across(4, hsum.at[T : 2 * T], hside)
        h_hop.start()
        y_hop.start()

        def down_units(u):
            for y_lo in range(2):
                at = y_lo * 512 + u * 256
                grad = dot(gzt[...], dm2[:, at : at + 256]).astype(bf16)
                for owner in range(32):
                    for group in range(4):
                        unit = 8 + u * 4 + group
                        place_at = position(TURN[unit], y_lo, owner // 8, owner // 2 % 4, owner % 2)
                        gs[SLOT[unit], place_at] = grad[owner * 64 + group * 16 : owner * 64 + group * 16 + 16]
            for group in range(4):
                first_hop(8 + u * 4 + group).start()

        down_units(0)
        h_hop.wait_recv()
        x1 = x1s[...]
        scale1 = lax.rsqrt(jnp.mean(x1 * x1, axis=-1, keepdims=True) + EPS)
        dh2 = hsum[0:T] + hside[...]
        gain2_grad[...] = jnp.sum(dh2 * x1 * scale1, axis=0, keepdims=True)
        dn = dh2 * gain2_ref[...]
        back = scale1 * dn - x1 * (scale1 * scale1 * scale1) * jnp.mean(dn * x1, axis=-1, keepdims=True)
        dx1 = dy_ref[0].astype(f32) + back
        hside[...] = dx1
        da = dx1.astype(bf16)
        das[...] = da
        side_hop = across(5, das.at[:, pl.ds(pl.multiple_of((1 - core) * 512, 512), 512)], da_side)
        side_hop.start()
        for g in range(4):
            group = lax.rem(g + lax.rem(lax.div(place.s, 4), 4), 4)
            dattn = dot_nt(da, wo[pl.ds(pl.multiple_of(group * 256, 256), 256)]).astype(bf16)
            for m in range(2):
                tile = dattn[:, 128 * m : 128 * m + 128]
                packed = swap_halves(tile[:HT], tile[HT:])
                for e in range(2):
                    h = 4 * group + 2 * m + e
                    stage1[h] = packed[e]
                    send_to(place, *da_hop(h))
        down_units(1)
        y_hop.wait_recv()
        y_ref[0] = (x1 + ysum[0:T] + yside[...]).astype(bf16)
        o_hop.wait_recv()
        side_hop.wait_recv()
        o2t = transposed(o2[...])
        mine = das[:, pl.ds(pl.multiple_of(core * 512, 512), 512)]
        out = (dot(o2t[:, 0:T], mine) + dot(o2t[:, T:], da_side[...])).astype(bf16)
        for u in range(2):
            spread(outg, u, TURN[16 + u], out[:, u * 256 : u * 256 + 256])
            outs[u].start()
        for hop in (dm_hop, o_hop, b_hop, y_hop, h_hop, side_hop):
            hop.wait_send()

    pl.run_scoped(
        feed_forward,
        pltpu.VMEM((D, D), bf16),
        pltpu.VMEM((4, D, 512), bf16),
        pltpu.VMEM((4, 512, D), bf16),
        pltpu.VMEM((D, 2 * T), bf16),
        pltpu.VMEM((2048, 2 * T), bf16),
        pltpu.VMEM((T, D), f32),
        pltpu.VMEM((2 * T, D), f32),
        pltpu.VMEM((2 * T, D), f32),
    )

    def hook(which):
        if which < 2:
            for sums_of in main:
                sums_of.advance(which)
            if which == 1:
                for sums_of in outs:
                    sums_of.advance(0)
        elif which == 2:
            for sums_of in main:
                sums_of.settle()
            ends[0].start()
            for sums_of in outs:
                sums_of.advance(1)
        elif which == 3:
            for sums_of in outs:
                sums_of.settle()
            ends[1].start()
        elif which == 4:
            for end in ends:
                end.wait()
            for unit in range(16):
                group = SLOT[unit] // 9
                mid.store(unit, ends[group].result(SLOT[unit] - 9 * group))
            for u in range(2):
                mid.store(16 + u, ends[1].result(7 + u))
            mid.start()
        else:
            mid.finish()

    def key_hop(m):
        return (
            stage2.at[m, 0:T], dqkv_in.at[place.head, 0:T], b_send.at[0, m], b_recv.at[0, place.head],
            place.block_device(m),
        )

    def query_hop(m):
        return (
            stage2.at[m, T:GRAD], dqkv_in.at[place.head, T:GRAD], b_send.at[1, m], b_recv.at[1, place.head],
            place.block_device(m),
        )

    def part_hop(j):
        return remote(part.at[j], landed.at[j], q_send.at[j], q_recv.at[j], place.partner)

    def attention_back(queries, kt, gp, delta, dq, dkv, weights):
        def prepare(t):
            kt[t] = transposed(load_keys(pk, t))[:HD]
            dkv[t] = jnp.zeros((TILE, 128), f32)

        loop(TILES, prepare)

        def prepare_query(j):
            for b in range(4):
                m = j * 4 + b
                put_unpacked(pk[place.own_block(m), T : T + HT], False, queries.at[j, b * T : (b + 1) * T])
                arrived(da_in.at[m], a_recv.at[m])
                put_unpacked(da_in[m], True, gp.at[j, b * T : (b + 1) * T])
            delta[j] = jnp.sum(gp[j].astype(f32).T[HD:] * ot[j], axis=0, keepdims=True)
            dq[j] = jnp.zeros((HD, TILE), f32)

        loop(4, prepare_query)
        factor = jnp.where(lax.broadcasted_iota(jnp.int32, (1, 128), 1) < HD, LN2, 1.0)

        def give(j):
            part[j] = (dkv[place.own_tile(j, 1 - core)] * factor).astype(bf16)
            part_hop(j).start()

        def take(j):
            alone = jnp.logical_and(core == 0, j == 3)

            @pl.when(jnp.logical_not(alone))
            def _():
                part_hop(j).wait_recv()

            total = dkv[place.own_tile(j)] * factor
            total = (total + jnp.where(alone, 0.0, landed[j].astype(f32))).astype(bf16)
            for b in range(4):
                m = j * 4 + b
                stage2[m, 0:T] = total[b * T : (b + 1) * T]
                send_to(place, *key_hop(m))

        def fetch(j, k_tile, n):
            which = lax.rem(n, 2)
            return pltpu.make_async_copy(probs.at[j, k_tile], weights.at[which], s_sem.at[2 + which])

        def step(j, k_tile, n):
            rows = load_keys(pk, k_tile)
            value = weights[lax.rem(n, 2)].astype(f32) * jnp.exp2(peaks[j, k_tile] - lse[j])
            slopes = (value * (dot_nt(rows, gp[j]) - delta[j])).astype(bf16)
            value = value.astype(bf16)
            dkv[k_tile] += dot(value, gp[j]) + dot(slopes, queries[j])
            dq[j] += dot(kt[k_tile], slopes)

        def hooks(n):
            for which in range(6):
                if HOOKS[which] < STEPS:

                    @pl.when(n == HOOKS[which])
                    def _(which=which):
                        hook(which)

        def owned(k_tile):
            return lax.rem(lax.div(k_tile + 1, 2), 2) == core

        def skipped(k_tile):
            skip = 0
            for j in range(4):
                skip = skip + jnp.where(place.own_tile(j) < k_tile, 1, 0)
            return skip

        def query_of(at, k_tile):
            return jnp.where(k_tile == 0, lax.rem(at + turn, 4), at)

        def later(i):
            k_tile = key_order(place, i)
            return jnp.where(jnp.logical_and(core == 1, k_tile == 7), key_order(place, i + 1), k_tile)

        first = later(0)
        fetch(query_of(skipped(first), first), first, 0).start()

        def key_tile(i, n):
            k_tile = key_order(place, i)
            following = later(jnp.minimum(i + 1, 7))

            def query_tile(at, n):
                hooks(n)
                j = query_of(at, k_tile)
                fetch(j, k_tile, n).wait()

                @pl.when(at < 3)
                def _():
                    fetch(query_of(at + 1, k_tile), k_tile, n + 1).start()

                @pl.when(jnp.logical_and(at == 3, i < 7))
                def _():
                    fetch(query_of(skipped(following), following), following, n + 1).start()

                step(j, k_tile, n)

                @pl.when(k_tile == 0)
                def _():
                    packed = pack_transposed(dq[j] * SCALE)
                    for b in range(4):
                        m = j * 4 + b
                        stage2[m, T:GRAD] = packed[b]
                        send_to(place, *query_hop(m))

                return n + 1

            n = lax.fori_loop(skipped(k_tile), 4, query_tile, n)
            mine = owned(k_tile)
            before = key_order(place, jnp.maximum(i - 1, 0))

            @pl.when(jnp.logical_and(jnp.logical_not(mine), jnp.logical_not(jnp.logical_and(core == 1, k_tile == 7))))
            def _():
                give(lax.div(k_tile, 2))

            @pl.when(jnp.logical_and(i > 0, owned(before)))
            def _():
                take(lax.div(before, 2))

            return n

        lax.fori_loop(0, TILES, key_tile, 0)

        @pl.when(core == 0)
        def _():
            take(0)

        for which in range(6):
            if HOOKS[which] == STEPS:
                hook(which)

    def back(w_scr, a2t):
        weight = pltpu.make_async_copy(w_qkv, w_scr, l_sem.at[0])
        weight.start()
        a_hop.wait_recv()
        a2t[...] = transposed(a2[...])
        pl.run_scoped(
            attention_back,
            pltpu.VMEM((4, TILE, 128), bf16),
            pltpu.VMEM((TILES, HD, TILE), bf16),
            pltpu.VMEM((4, TILE, 128), bf16),
            pltpu.VMEM((4, 1, TILE), f32),
            pltpu.VMEM((4, HD, TILE), f32),
            pltpu.VMEM((TILES, TILE, 128), f32),
            pltpu.VMEM((2, TILE, TILE), bf16),
        )
        pl.run_scoped(
            functools.partial(last, weight, w_scr, a2t),
            pltpu.VMEM((T, 3 * D), bf16),
            pltpu.VMEM((6, 64, 16, 256), bf16),
        )

    def last(weight, w_scr, a2t, dn, gs3):
        sums = [Part(net, gs3, land3, tail3, u, u, 1, u, (t_send, u), (t_recv, u)) for u in range(6)]
        for m in range(8):
            for h in (2 * m, 2 * m + 1):
                arrived(dqkv_in.at[h, 0:T], b_recv.at[0, h])
                arrived(dqkv_in.at[h, T:GRAD], b_recv.at[1, h])
            lo, hi = swap_halves(dqkv_in[2 * m, T:GRAD], dqkv_in[2 * m + 1, T:GRAD])
            dk, dv = swap_halves(dqkv_in[2 * m, 0:T], dqkv_in[2 * m + 1, 0:T])
            dn[0:HT, 128 * m : 128 * m + 128] = lo
            dn[HT:T, 128 * m : 128 * m + 128] = hi
            dn[:, D + 128 * m : D + 128 * m + 128] = dk
            dn[:, 2 * D + 128 * m : 2 * D + 128 * m + 128] = dv
        d_hops = []
        for section in range(3):
            at = pl.multiple_of(section * D + (1 - core) * 512, 512)
            d_hops.append(
                across(9 + section, dn.at[:, pl.ds(at, 512)], d_side.at[:, section * 512 : section * 512 + 512])
            )
            d_hops[section].start()
        for u in range(6):
            section, half = u // 2, u % 2
            if half == 0:
                d_hops[section].wait_recv()
            at = pl.multiple_of(section * D + core * 512 + half * 256, 256)
            grad = dot(a2t[:, 0:T], dn[:, pl.ds(at, 256)]) + dot(a2t[:, T:], d_side[:, u * 256 : u * 256 + 256])
            spread(gs3, u, u, grad.astype(bf16))
            sums[u].start()
        weight.wait()
        x = x_ref[0].astype(f32)
        scale = lax.rsqrt(jnp.mean(x * x, axis=-1, keepdims=True) + EPS)
        dh1 = dot_nt(dn[...], w_scr[...])
        gain1_grad = jnp.sum(dh1 * x * scale, axis=0, keepdims=True)
        both = [gain1_grad[:, 128 * k : 128 * k + 128] for k in range(8)]
        both += [gain2_grad[:, 128 * k : 128 * k + 128] for k in range(8)]
        gain_value[0] = jnp.concatenate(both, axis=0)
        gains.start(0)
        dxn = dh1 * gain1_ref[...]
        back = scale * dxn - x * (scale * scale * scale) * jnp.mean(dxn * x, axis=-1, keepdims=True)
        dx_ref[0] = (hside[...] + back).astype(bf16)

        for stage in range(2):
            for sums_of in sums:
                sums_of.advance(stage)
            gains.take(stage)
            gains.start(stage + 1)
            for which in range(6):
                if HOOKS[which] == STEPS + 1 + stage:
                    hook(which)
        for g in range(2):
            for sums_of in sums[3 * g : 3 * g + 3]:
                sums_of.settle()
            ends3[g].start()
        gains.take(2)
        for which in range(6):
            if HOOKS[which] == STEPS + 3:
                hook(which)
        for g in range(2):
            ends3[g].wait()
            for u in range(3):
                fin3[3 * g + u] = ends3[g].result(u).reshape(2, 8, 256)
        aside = across(8, fin3.at[:, 1 - core], side3)
        aside.start()
        for which in range(6):
            if HOOKS[which] == STEPS + 4:
                hook(which)
        shard = place.s * 4 + place.r
        turn = lax.rem(128 - lax.rem(shard, 16) * 8, 128)
        for k in range(2):
            row = gain_value[3, pl.ds(8 * k + lax.div(shard, 16), 1)]
            gain_out[k : k + 1] = pltpu.roll(row, turn, 1)
        aside.wait_recv()
        mine, other = core, 1 - core
        for u in range(6):
            at = (u // 2) * D + (u % 2) * 256
            qkv_out[:, pl.ds(at + mine * 512, 256)] = fin3[u, mine]
            qkv_out[:, pl.ds(at + other * 512, 256)] = side3[u]
        for hop in [a_hop, aside] + d_hops:
            hop.wait_send()
        for sums_of in sums:
            sums_of.finish()

    pl.run_scoped(back, pltpu.VMEM((D, 3 * D), bf16), pltpu.VMEM((D, 2 * T), bf16))

    def finish(n):
        sent_to(place, *da_hop(n))
        sent_to(place, *key_hop(n))
        sent_to(place, *query_hop(n))

    loop(16, finish)

    def given(j, carry):
        part_hop(j).wait_send()
        return carry

    lax.fori_loop(0, 4 - core, given, 0)
    for sums_of in main + outs + ends + ends3 + [gains]:
        sums_of.finish()


def block_call(frames, segment_ids, out_grad, gain1, gain2, w_qkv, w_out, w_up, w_down):
    dma = pltpu.SemaphoreType.DMA
    return pl.pallas_call(
        block_kernel,
        name="block",
        out_shape=(
            jax.ShapeDtypeStruct((1, T, D), bf16),
            jax.ShapeDtypeStruct((1, T, D), bf16),
            jax.ShapeDtypeStruct((8, 3 * D), f32),
            jax.ShapeDtypeStruct((8, 128), f32),
            jax.ShapeDtypeStruct((8, FF), f32),
            jax.ShapeDtypeStruct((8, D), f32),
            jax.ShapeDtypeStruct((32, D), f32),
            jax.ShapeDtypeStruct((4, TILES, TILE, TILE), bf16),
        ),
        in_specs=[VM] * 5 + [ANY] * 4,
        out_specs=(VM,) * 7 + (ANY,),
        scratch_shapes=[
            pltpu.VMEM((BLOCKS, PACK, 128), bf16),
            pltpu.VMEM((16, HT, 128), bf16),
            pltpu.VMEM((4, HD, TILE), f32),
            pltpu.VMEM((4, 1, TILE), f32),
            pltpu.VMEM((4, TILES, 1, TILE), f32),
            pltpu.VMEM((2 * T, D), bf16),
            pltpu.VMEM((2 * T, D), bf16),
            pltpu.VMEM((2 * T, D), bf16),
            pltpu.VMEM((T, D), f32),
            pltpu.VMEM((T, D), f32),
            pltpu.VMEM((T, D), bf16),
            pltpu.VMEM((T, 512), bf16),
            pltpu.VMEM((1, D), f32),
            pltpu.VMEM((16, 64, 16, 256), bf16),
            pltpu.VMEM((16, 56, 16, 256), bf16),
            pltpu.VMEM((2, 64, 16, 256), bf16),
            pltpu.VMEM((2, 56, 16, 256), bf16),
            pltpu.VMEM((18, 8, 16, 256), bf16),
            pltpu.VMEM((2, 7, 9, 16, 256), bf16),
            pltpu.VMEM((16, HT, 128), bf16),
            pltpu.VMEM((16, HT, 128), bf16),
            pltpu.VMEM((4, TILE, 128), bf16),
            pltpu.VMEM((4, TILE, 128), bf16),
            pltpu.VMEM((16, GRAD, 128), bf16),
            pltpu.VMEM((16, PACK, 128), bf16),
            pltpu.VMEM((18, 2, 8, 256), f32),
            pltpu.VMEM((10, 8, 256), f32),
            pltpu.VMEM((2, 4, 2, 8, 256), f32),
            pltpu.VMEM((2 * T, D), bf16),
            pltpu.VMEM((T, 1536), bf16),
            pltpu.VMEM((6, 56, 16, 256), bf16),
            pltpu.VMEM((6, 8, 16, 256), bf16),
            pltpu.VMEM((2, 7, 3, 16, 256), bf16),
            pltpu.VMEM((4, 16, 128), f32),
            pltpu.VMEM((3, 7, 16, 128), f32),
            pltpu.VMEM((6, 2, 8, 256), f32),
            pltpu.VMEM((6, 8, 256), f32),
            dma((9,)), dma((1,)), dma((12,)), dma((12,)), dma((4,)), dma((4,)), dma((16,)), dma((16,)),
            dma((16,)), dma((16,)), dma((2, 16)), dma((2, 16)), dma((8, 3)), dma((8, 3)), dma((6, 3)), dma((6, 3)),
            dma((4, 7)), dma((4, 7)), dma((3, 7)), dma((3, 7)), dma((6,)),
            dma((4, 3)), dma((16,)), dma((16,)), dma((16,)), dma((16,)), dma((16,)), dma((16,)), dma((4,)),
        ],
        compiler_params=params(0),
    )(frames, segment_ids, out_grad, gain1, gain2, w_qkv, w_out, w_up, w_down)


def deliver_kernel(*refs):
    count = len(refs) // 2 - 2
    sources, gains, targets = refs[:count], refs[count], refs[count + 1 : 2 * count + 1]
    gain1, gain2, sem = refs[2 * count + 1 :]
    del sem
    for k in range(count):
        targets[k][...] = sources[k][...]
    gain1[...] = gains[0, 0:8]
    gain2[...] = gains[1, 0:8]


def deliver(arrays, gains):
    count = len(arrays)
    small = jax.ShapeDtypeStruct((8,), f32)
    return pl.pallas_call(
        deliver_kernel,
        name="deliver",
        out_shape=tuple(jax.ShapeDtypeStruct(v.shape, v.dtype) for v in arrays) + (small, small),
        in_specs=[VM] * (count + 1),
        out_specs=(VM,) * (count + 2),
        scratch_shapes=[pltpu.SemaphoreType.DMA((count,))],
    )(*arrays, gains)


def shards(frames, segment_ids, norm1_gain, w_qkv, w_out, norm2_gain, w_up, w_down, out_grad):
    gain1, gain2 = norm1_gain[None], norm2_gain[None]
    y, dx, qkv_sum, gain_sums, up_sum, out_sum, down_sum, _ = block_call(
        frames, segment_ids, out_grad, gain1, gain2, w_qkv, w_out, w_up, w_down
    )
    y, dx, qkv_sum, out_sum, up_sum, down_sum, gain1_sum, gain2_sum = deliver(
        (y, dx, qkv_sum, out_sum, up_sum, down_sum), gain_sums
    )
    return (y, dx, gain1_sum, qkv_sum, out_sum, gain2_sum, up_sum, down_sum)


def solution(mesh):
    return jax.shard_map(
        shards,
        mesh=mesh,
        in_specs=(
            P("row", "seq", None),
            P("row", "seq"),
            P(),
            P(),
            P(),
            P(),
            P(),
            P(),
            P("row", "seq", None),
        ),
        out_specs=(
            P("row", "seq", None),
            P("row", "seq", None),
            P(("seq", "row")),
            P(("seq", "row"), None),
            P(("seq", "row"), None),
            P(("seq", "row")),
            P(("seq", "row"), None),
            P(("seq", "row"), None),
        ),
        check_vma=False,
    )
```

```python
import functools
import math

import jax
import jax.numpy as jnp
from jax import lax
from jax.experimental import pallas as pl
from jax.experimental.pallas import tpu as pltpu
from jax.sharding import PartitionSpec as P

MESH = pl.DeviceIdType.MESH
f32 = jnp.float32
bf16 = jnp.bfloat16

D = 1024
H = 16
HD = 64
FF = 4096
T = 192
HT = T // 2
BLOCKS = 32
TILE = 768
TILES = 8
PACK = 304
GRAD = 288
EPS = 1e-05
NEG = -1e30
LOG2E = math.log2(math.e)
LN2 = math.log(2.0)
SCALE = HD**-0.5
VMEM_LIMIT = 60 * 1024 * 1024

ANY = pl.BlockSpec(memory_space=pl.ANY)
VM = pl.BlockSpec(memory_space=pltpu.VMEM)


def dot(a, b):
    return jnp.dot(a, b, preferred_element_type=f32)


def dot_nt(a, b):
    return lax.dot_general(a, b, (((1,), (1,)), ((), ())), preferred_element_type=f32)


def transposed(v):
    return v.astype(f32).T.astype(bf16)


def swap_halves(first, second):
    lane = lax.broadcasted_iota(jnp.int32, first.shape, 1)
    low = lane < HD
    first, second = first.astype(f32), second.astype(f32)
    return (
        jnp.where(low, first, pltpu.roll(second, HD, 1)).astype(bf16),
        jnp.where(low, pltpu.roll(first, HD, 1), second).astype(bf16),
    )


class Place:
    def __init__(self):
        self.s = lax.axis_index("seq")
        self.r = lax.axis_index("row")
        self.y_lo = lax.div(self.s, 16)
        self.head = lax.rem(self.s, 16)
        self.y_hi = lax.div(self.r, 2)
        self.core = lax.rem(self.r, 2)
        tile = lax.div(self.s, 4)
        self.block_core = lax.rem(lax.div(tile + 1, 2), 2)
        self.slot = lax.div(self.s, 8) * 4 + lax.rem(self.s, 4)
        self.partner = (self.s, self.r + 1 - 2 * self.core)
        self.self_served = jnp.logical_and(self.y_lo == self.core, self.block_core == self.core)
        self.self_count = jnp.where(self.self_served, 1, 0)

    def head_device(self, h):
        return (self.core * 16 + h, self.y_hi * 2 + self.block_core)

    def own_tile(self, j, core=None):
        core = self.core if core is None else core
        return 2 * j + lax.rem(j + core, 2)

    def own_block(self, n):
        return self.own_tile(lax.div(n, 4)) * 4 + lax.rem(n, 4)

    def block_device(self, n):
        return (self.own_block(n), self.y_hi * 2 + self.y_lo)

    def is_self(self, device):
        return jnp.logical_and(device[0] == self.s, device[1] == self.r)


def remote(src, dst, send, recv, device):
    return pltpu.make_async_remote_copy(
        src_ref=src, dst_ref=dst, send_sem=send, recv_sem=recv, device_id=device, device_id_type=MESH
    )


def send_to(place, src, dst, send, recv, device):
    own = place.is_self(device)

    @pl.when(own)
    def _():
        pltpu.make_async_copy(src, dst, recv).start()

    @pl.when(jnp.logical_not(own))
    def _():
        remote(src, dst, send, recv, device).start()


def sent_to(place, src, dst, send, recv, device):
    @pl.when(jnp.logical_not(place.is_self(device)))
    def _():
        remote(src, dst, send, recv, device).wait_send()


def arrived(dst, recv):
    pltpu.make_async_copy(dst, dst, recv).wait()


def greet(barrier, device):
    pl.semaphore_signal(barrier, inc=1, device_id=device, device_id_type=MESH)


def greet_all(place, barrier, device_of):
    def one(n, carry):
        device = device_of(n)

        @pl.when(jnp.logical_not(place.is_self(device)))
        def _():
            greet(barrier, device)

        return carry

    lax.fori_loop(0, 16, one, 0)


def loop(count, body):
    def one(n, carry):
        body(n)
        return carry

    lax.fori_loop(0, count, one, 0)


def params(collective_id):
    return pltpu.CompilerParams(
        collective_id=collective_id, has_side_effects=True, vmem_limit_bytes=VMEM_LIMIT
    )


def seg_column(pk_ref, block):
    tile = pk_ref[block, T + HT : PACK].astype(f32)
    return jnp.concatenate(
        [
            jnp.broadcast_to(tile[0:1], (128, 128)).T,
            jnp.broadcast_to(tile[1:2], (128, 128)).T[: T - 128],
        ],
        axis=0,
    )


MIDDLE = 4


def put_marks(pk_ref, tile, put):
    lane = lax.broadcasted_iota(jnp.int32, (TILE, 128), 1).astype(f32)
    put(slice(0, TILE), lane, jnp.full((TILE, 128), MIDDLE, f32))
    for special, block, rows in ((0, 0, slice(0, T)), (TILES - 1, BLOCKS - 1, slice(TILE - T, TILE))):

        @pl.when(tile == special)
        def _(block=block, rows=rows):
            put(rows, lane[:T], seg_column(pk_ref, block) + MIDDLE)


def put_unpacked(packed, high, target):
    low = lax.broadcasted_iota(jnp.int32, (HT, 128), 1) < HD
    packed = packed.astype(f32)
    turned = pltpu.roll(packed, HD, 1)
    if high:
        target[0:HT] = jnp.where(low, 0.0, turned).astype(bf16)
        target[HT:T] = jnp.where(low, 0.0, packed).astype(bf16)
    else:
        target[0:HT] = jnp.where(low, packed, 0.0).astype(bf16)
        target[HT:T] = jnp.where(low, turned, 0.0).astype(bf16)


STEPS = 18


OFF = STEPS - 4


def walk(place, n):
    turn = lax.div(place.head, 4)
    j, start = turn, 0
    end = place.own_tile(j)
    for k in range(1, 4):
        past = n >= end
        following = lax.rem(turn + k, 4)
        j = jnp.where(past, following, j)
        start = jnp.where(past, end, start)
        end = jnp.where(past, end + place.own_tile(following), end)
    return j, n - start, n + 1 == end


def key_order(place, i):
    turn = lax.div(place.head, 4)
    k_tile = 7 - lax.rem(i + 2 * turn, 7)
    k_tile = jnp.where(jnp.logical_and(place.core == 1, k_tile == 1), 0, k_tile)
    return jnp.where(i == 7, place.core, k_tile)


def causal(scores):
    k = lax.broadcasted_iota(jnp.int32, scores.shape, 0)
    q = lax.broadcasted_iota(jnp.int32, scores.shape, 1)
    return jnp.where(k <= q, scores, NEG)


def load_keys(pk_ref, tile):
    return pk_ref[pl.ds(tile * 4, 4), 0:T].reshape(TILE, 128)


def pack_transposed(value_t):
    both = jnp.concatenate([value_t, value_t], axis=0).T
    lane = lax.broadcasted_iota(jnp.int32, (HT, 128), 1)
    return [
        jnp.where(lane < HD, both[b * T : b * T + HT], both[b * T + HT : b * T + T]).astype(bf16)
        for b in range(4)
    ]


FIRST = lambda c: ((c + 1) // 2) % 2
SECOND = lambda c: c // 2


def chip_bits(x, y, z):
    return [FIRST(x), FIRST(y), FIRST(z), SECOND(x), SECOND(y), SECOND(z)]


SHORT = [[(p + k) % 3 + 3 * (p // 3) for k in range(3)] + [k + 3 * (1 - p // 3) for k in range(3)] for p in range(6)]
LONG = [[(p + k) % 3 + 3 * ((p // 3 + k // 3) % 2) for k in range(6)] for p in range(6)]


def position(order, y_lo, x, z, y_hi):
    bits = chip_bits(x, y_hi * 2 + y_lo, z)
    at = 0
    for dim in order:
        at = at * 2 + bits[dim]
    return at


class Net:
    def __init__(self, place):
        self.x, self.z = lax.div(place.head, 4), lax.rem(place.head, 4)
        self.y = place.y_hi * 2 + place.y_lo
        self.core = place.core
        self.bits = [lax.rem(lax.div(c + 1, 2), 2) for c in (self.x, self.y, self.z)]
        self.bits += [lax.div(c, 2) for c in (self.x, self.y, self.z)]

    def across(self, pairing, mask):
        moved = []
        for k, c in enumerate((self.x, self.y, self.z)):
            far = c + 1 - 2 * lax.rem(c, 2) if pairing == 0 else 3 - c
            moved.append(far if mask >> (2 - k) & 1 else c)
        x, y, z = moved
        return (lax.rem(y, 2) * 16 + x * 4 + z, lax.div(y, 2) * 2 + self.core)

    def neighbour(self, dim):
        return self.across(dim // 3, 4 >> dim % 3)

    def greet(self, barrier):
        for pairing in range(2):
            for mask in range(1, 8):
                greet(barrier, self.across(pairing, mask))

    GREETINGS = 14


class Part:
    def __init__(self, net, acc, land, at, count, order, send, recv, pieces=(), tail=None):
        self.net, self.acc, self.land, self.order, self.pieces, self.tail = net, acc, land, order, pieces, tail
        self.units = pl.ds(at, count)
        self.send, self.recv = send, recv

    def bit(self, stage):
        return self.net.bits[self.order[stage]]

    def base(self, stage):
        at = 0
        for k in range(stage + 1):
            at = at + self.bit(k) * (32 >> k)
        return at

    def landing(self, stage):
        return sum(32 >> k for k in range(stage))

    def hop(self, stage):
        half = 32 >> stage
        base = self.base(stage - 1) + (1 - self.bit(stage)) * half
        return remote(
            self.acc.at[self.units, pl.ds(base, half)],
            self.land.at[self.units, pl.ds(self.landing(stage), half)],
            self.send[0].at[self.send[1], stage],
            self.recv[0].at[self.recv[1], stage],
            self.net.neighbour(self.order[stage]),
        )

    def start(self):
        self.hop(0).start()

    def hops(self, stage):
        return list(self.pieces) if stage == 0 and self.pieces else [self.hop(stage)]

    def total(self, base, landed, group):
        mine = self.acc[self.units, pl.ds(base, group)].astype(f32)
        return (mine + self.land[self.units, pl.ds(landed, group)].astype(f32)).astype(bf16)

    def add(self, base, landed, count):
        group = min(count, 4)

        def body(i):
            here = pl.ds(base + i * group, group)
            self.acc[self.units, here] = self.total(base + i * group, landed + i * group, group)

        loop(count // group, body)

    def advance(self, stage):
        for hop in self.hops(stage):
            hop.wait_recv()
        half = 16 >> stage
        base, landed = self.base(stage), self.landing(stage)
        bit = self.bit(stage + 1)
        self.add(base + (1 - bit) * half, landed + (1 - bit) * half, half)
        self.hop(stage + 1).start()
        self.add(base + bit * half, landed + bit * half, half)

    def settle(self):
        self.hop(2).wait_recv()
        for at in range(0, 8, 4):
            self.tail[self.units, at : at + 4] = self.total(self.base(2) + at, self.landing(2) + at, 4)

    def last(self):
        self.hop(5).wait_recv()
        mine = self.acc[self.units, pl.ds(self.base(5), 1)].astype(f32)
        return (mine + self.land[self.units, pl.ds(self.landing(5), 1)].astype(f32))[:, 0]

    def finish(self):
        for stage in range(6 if self.tail is None else 3):
            for hop in self.hops(stage):
                hop.wait_send()


class Exchange:
    def __init__(self, net, pairing, tail, land, send, recv):
        self.net, self.pairing, self.tail, self.land, self.send, self.recv = net, pairing, tail, land, send, recv

    def row(self, mask):
        at = 0
        for k in range(3):
            bit = self.net.bits[3 * self.pairing + k]
            at = at + (1 - bit if mask >> (2 - k) & 1 else bit) * (4 >> k)
        return at

    def hop(self, mask):
        return remote(
            self.tail.at[:, self.row(mask)], self.land.at[mask - 1],
            self.send.at[mask - 1], self.recv.at[mask - 1], self.net.across(self.pairing, mask),
        )

    def start(self):
        for mask in range(1, 8):
            self.hop(mask).start()

    def result(self, unit):
        total = self.tail[unit, self.row(0)].astype(f32)
        for mask in range(1, 8):
            total = total + self.land[mask - 1, unit].astype(f32)
        return total

    def wait(self):
        for mask in range(1, 8):
            self.hop(mask).wait_recv()

    def finish(self):
        for mask in range(1, 8):
            self.hop(mask).wait_send()


class Shared:
    def __init__(self, net, place, value, land, send, recv):
        self.net, self.place, self.value, self.land, self.send, self.recv = net, place, value, land, send, recv

    def hops(self, pairing):
        if pairing == 2:
            return [
                remote(self.value.at[2], self.land.at[2, 0], self.send.at[2, 0], self.recv.at[2, 0], self.place.partner)
            ]
        return [
            remote(
                self.value.at[pairing], self.land.at[pairing, mask - 1],
                self.send.at[pairing, mask - 1], self.recv.at[pairing, mask - 1], self.net.across(pairing, mask),
            )
            for mask in range(1, 8)
        ]

    def start(self, pairing):
        for hop in self.hops(pairing):
            hop.start()

    def take(self, pairing):
        total = self.value[pairing]
        for k, hop in enumerate(self.hops(pairing)):
            hop.wait_recv()
            total = total + self.land[pairing, k]
        self.value[pairing + 1] = total

    def finish(self):
        for pairing in range(3):
            for hop in self.hops(pairing):
                hop.wait_send()


TURN = [u % 6 for u in range(18)]
COUNTS = [3, 3, 3, 3, 2, 2]
STARTS = [0, 3, 6, 9, 12, 14]
SLOT = [STARTS[u % 6] + u // 6 for u in range(16)]
FINAL = list(range(8)) + [10 + (v % 4) * 2 + v // 4 for v in range(8)] + [8, 9]


class MidSums:
    def __init__(self, place, fin, side, down, sem, up_out, out_out, down_out):
        self.place, self.fin, self.side, self.down, self.sem = place, fin, side, down, sem
        self.up_out, self.out_out, self.down_out = up_out, out_out, down_out

    def targets(self):
        return [(self.place.core * 16 + self.place.head, self.place.y_hi * 2 + k) for k in range(2)]

    def sources(self):
        return [(m * 16 + self.place.head, self.place.y_hi * 2 + self.place.y_lo) for m in range(2)]

    def self_count(self):
        return jnp.where(self.place.y_lo == self.place.core, 1, 0)

    def greet(self, barrier):
        greet(barrier, self.place.partner)
        for device in self.sources():

            @pl.when(jnp.logical_not(self.place.is_self(device)))
            def _(device=device):
                greet(barrier, device)

    def greetings(self):
        return 3 - self.self_count()

    def store(self, unit, value):
        self.fin[FINAL[unit]] = value.reshape(2, 8, 256)

    def aside(self):
        return remote(
            self.fin.at[0:10, 1 - self.place.core], self.side, self.sem.at[0], self.sem.at[1], self.place.partner
        )

    def down_hop(self, k):
        return (
            self.fin.at[10 + 4 * k : 14 + 4 * k],
            self.down.at[self.place.y_lo],
            self.sem.at[2 + k],
            self.sem.at[4 + self.place.y_lo],
            self.targets()[k],
        )

    def start(self):
        self.aside().start()
        for k in range(2):
            send_to(self.place, *self.down_hop(k))

    def finish(self):
        place = self.place
        self.aside().wait_recv()
        mine, other = place.core, 1 - place.core
        for u in range(8):
            self.up_out[:, pl.ds(mine * 2048 + u * 256, 256)] = self.fin[u, mine]
            self.up_out[:, pl.ds(other * 2048 + u * 256, 256)] = self.side[u]
        for u in range(2):
            self.out_out[:, pl.ds(mine * 512 + u * 256, 256)] = self.fin[8 + u, mine]
            self.out_out[:, pl.ds(other * 512 + u * 256, 256)] = self.side[8 + u]
        for m in range(2):
            arrived(self.down.at[m], self.sem.at[4 + m])
            for v in range(4):
                group, half = v // 2, v % 2
                self.down_out[group * 16 : group * 16 + 16, m * 512 + half * 256 : m * 512 + half * 256 + 256] = (
                    self.down[m, v].reshape(16, 256)
                )
        self.aside().wait_send()
        for k in range(2):
            sent_to(place, *self.down_hop(k))


MID_OUT = (
    jax.ShapeDtypeStruct((8, FF), f32),
    jax.ShapeDtypeStruct((8, D), f32),
    jax.ShapeDtypeStruct((32, D), f32),
)
MID_SCRATCH = [
    pltpu.VMEM((18, 2, 8, 256), f32),
    pltpu.VMEM((10, 8, 256), f32),
    pltpu.VMEM((2, 4, 2, 8, 256), f32),
    pltpu.SemaphoreType.DMA((6,)),
]


def spread(target, unit_slot, order, block):
    for chip in range(64):
        y_lo, x, z, y_hi = chip // 32, chip // 8 % 4, chip // 2 % 4, chip % 2
        target[unit_slot, position(order, y_lo, x, z, y_hi)] = block[chip * 16 : chip * 16 + 16]


ROOT = math.sqrt(2.0 / math.pi)
CUBE = 0.044715


HOOKS = (1, 5, 11, 18, 19, 20, 21, 22)


def block_kernel(
    x_ref, seg_ref, dy_ref, gain1_ref, gain2_ref, w_qkv, w_out, w_up, w_down,
    y_ref, dx_ref, qkv_out, gain_out, up_out, out_out, down_out, probs,
    pk, kt, o_in, ot, lse, peaks, o2, b2, dm2, yside, hside, das, da_side, gain2_grad,
    gs, land, outg, land2, da_in, stage1,
    part, landed, dqkv_in, stage2, fin, side, down, a2, d_side, land3, tail3, tail_land3, gain_value, gain_land,
    fin3, side3,
    w_sem, l_sem, p_send, p_recv, q_send, q_recv, h_send, h_recv, a_send, a_recv, b_send, b_recv,
    n_send, n_recv, t_send, t_recv, e_send, e_recv, g_send, g_recv, m_sem,
    k_sem, x_send, x_recv, f_send, f_recv, c_send, c_recv, s_sem,
):
    place = Place()
    core = place.core
    net = Net(place)
    turn = lax.rem(lax.div(place.s, 4), 4)

    def across(k, src, dst):
        return remote(src, dst, p_send.at[k], p_recv.at[k], place.partner)

    def first_hop(unit):
        bit = net.bits[TURN[unit]]
        return remote(
            gs.at[SLOT[unit], pl.ds((1 - bit) * 32, 32)], land.at[SLOT[unit], 0:32],
            h_send.at[unit], h_recv.at[unit], net.neighbour(TURN[unit]),
        )

    main = [
        Part(
            net, gs, land, STARTS[p], COUNTS[p], LONG[p], (n_send, p), (n_recv, p),
            [first_hop(p + 6 * k) for k in range(COUNTS[p])],
        )
        for p in range(6)
    ]
    outs = [
        Part(net, outg, land2, u, 1, LONG[TURN[16 + u]], (n_send, 6 + u), (n_recv, 6 + u)) for u in range(2)
    ]
    mid = MidSums(place, fin, side, down, m_sem, up_out, out_out, down_out)
    ends3 = [
        Exchange(net, 1 - g, tail3.at[3 * g : 3 * g + 3], tail_land3.at[g], e_send.at[g], e_recv.at[g])
        for g in range(2)
    ]
    gains = Shared(net, place, gain_value, gain_land, g_send, g_recv)

    barrier = pltpu.get_barrier_semaphore()
    greet_all(place, barrier, place.block_device)
    greet_all(place, barrier, place.head_device)
    net.greet(barrier)
    mid.greet(barrier)
    a_hop = across(6, a2.at[0:T], a2.at[T : 2 * T])
    dm_hop = across(0, dm2.at[0:T], dm2.at[T : 2 * T])

    def packet_hop(h):
        return (stage2.at[h], pk.at[place.s], x_send.at[h], x_recv.at[place.slot], place.head_device(h))

    def qkv(w_scr):
        def weight(g, section):
            at = pl.multiple_of(section * D + lax.rem(g + turn, 4) * 256, 256)
            return pltpu.make_async_copy(w_qkv.at[:, pl.ds(at, 256)], w_scr.at[g, section], k_sem.at[g, section])

        for g in range(4):
            for section in range(3):
                weight(g, section).start()
        x = x_ref[0].astype(f32)
        a = (x * lax.rsqrt(jnp.mean(x * x, axis=-1, keepdims=True) + EPS) * gain1_ref[...]).astype(bf16)
        a2[0:T] = a
        dm2[0:T] = dy_ref[0]
        numbers = seg_ref[...].astype(f32)
        numbers = numbers - jnp.where(place.s == BLOCKS - 1, numbers[:, 0:1], numbers[:, T - 1 : T])
        row = lax.broadcasted_iota(jnp.int32, (16, 128), 0)
        rest = jnp.concatenate([numbers[:, 128:T], jnp.zeros((1, 256 - T), f32)], axis=1)
        seg_tile = jnp.where(row == 0, numbers[:, :128], jnp.where(row == 1, rest, 0.0)).astype(bf16)
        pl.semaphore_wait(barrier, 2 * (16 - place.self_count) + Net.GREETINGS + mid.greetings())
        for g in range(4):
            for section in range(3):
                weight(g, section).wait()
            q = dot(a, w_scr[g, 0]) * (SCALE * LOG2E)
            k = dot(a, w_scr[g, 1])
            v = dot(a, w_scr[g, 2])
            for m in range(2):
                lanes = slice(128 * m, 128 * m + 128)
                h = 4 * lax.rem(g + turn, 4) + 2 * m
                kv = swap_halves(k[:, lanes].astype(bf16), v[:, lanes].astype(bf16))
                qq = q[:, lanes].astype(bf16)
                qp = swap_halves(qq[:HT], qq[HT:])
                for e in range(2):
                    stage2[h + e, 0:T] = kv[e]
                    stage2[h + e, T : T + HT] = qp[e]
                    stage2[h + e, T + HT : PACK] = seg_tile
                    send_to(place, *packet_hop(h + e))
        a_hop.start()
        dm_hop.start()

    pl.run_scoped(qkv, pltpu.VMEM((4, 3, D, 256), bf16))

    def out_hop(m):
        return (stage1.at[m], o_in.at[place.head], c_send.at[m], c_recv.at[place.head], place.block_device(m))

    def attention(keys, queries, vt, top, acc, even, odd, even_p, odd_p):
        one = jnp.where(lax.broadcasted_iota(jnp.int32, (16, TILE), 0) == 0, 1.0, 0.0).astype(bf16)

        def forward(n):
            i = place.own_block(n)
            return remote(pk.at[i], pk.at[i], f_send.at[n], f_recv.at[n], place.partner)

        def key_tile(t):
            rows = load_keys(pk, t)
            keys[t, :, 0:128] = rows

            def put(rows, lane, number):
                keys[t, rows, 128:256] = jnp.where(lane == number, 1.0, 0.0).astype(bf16)

            put_marks(pk, t, put)
            turned = transposed(rows)
            kt[t] = turned[:HD]
            vt[t, 0:HD] = turned[HD:]
            vt[t, HD : HD + 16] = one

        def query_tile(j):
            t = place.own_tile(j)
            for b in range(4):
                put_unpacked(pk[t * 4 + b, T : T + HT], False, queries.at[j, b * T : (b + 1) * T, 0:128])

            def put(rows, lane, number):
                other = jnp.logical_and(lane < 2 * MIDDLE + 1, lane != number)
                queries[j, rows, 128:256] = jnp.where(other, NEG, 0.0).astype(bf16)

            put_marks(pk, t, put)

        def keep(j, k_tile, weights, which):
            for half in (slice(0, TILE // 2), slice(TILE // 2, TILE)):
                pltpu.make_async_copy(weights.at[half], probs.at[j, k_tile, half], s_sem.at[which]).start()

        def kept(weights, which):
            pltpu.make_async_copy(weights, probs.at[0, 0], s_sem.at[which]).wait()

        def finish_tile(j):
            total = acc[j, HD : HD + 1]
            out_t = acc[j, 0:HD] / total
            lse[j] = top[j] + jnp.log2(total)
            ot[j] = out_t
            packed = pack_transposed(out_t)
            for b in range(4):
                m = j * 4 + b
                stage1[m] = packed[b]
                send_to(place, *out_hop(m))

        def diagonal(j, weights, which, again):
            for b in range(4):
                n = j * 4 + b
                arrived(pk.at[place.own_block(n)], x_recv.at[n])
                forward(n).start()
            t = place.own_tile(j)
            key_tile(t)
            query_tile(j)
            scores = causal(dot_nt(keys[t], queries[j]))
            peak = jnp.max(scores, axis=0, keepdims=True)
            top[j] = peak
            peaks[j, t] = peak
            value = jnp.exp2(scores - peak).astype(bf16)

            @pl.when(again)
            def _():
                kept(weights, which)

            weights[...] = value
            keep(j, t, weights, which)
            acc[j] = dot(vt[t], value)

        def diagonals(i):
            diagonal(2 * i, even_p, 0, i > 0)
            diagonal(2 * i + 1, odd_p, 1, i > 0)

        loop(2, diagonals)

        @pl.when(core == 0)
        def _():
            finish_tile(0)

        def others(j):
            for b in range(4):
                forward(j * 4 + b).wait_recv()
            key_tile(place.own_tile(j, 1 - core))

        loop(4, others)

        def score(n, scores):
            j, k_tile, _ = walk(place, jnp.minimum(n, OFF - 1))
            scores[...] = dot_nt(keys[k_tile], queries[j])

        def body(n, now, later, weights, which):
            j, k_tile, last = walk(place, n)
            kept(weights, which)
            score(n + 1, later)
            scores = now[...]
            peak = jnp.maximum(top[j], jnp.max(scores, axis=0, keepdims=True))
            fade = jnp.exp2(top[j] - peak)
            top[j] = peak
            peaks[j, k_tile] = peak
            value = jnp.exp2(scores - peak).astype(bf16)
            weights[...] = value
            acc[j] = acc[j] * fade + dot(vt[k_tile], value)
            keep(j, k_tile, weights, which)

            @pl.when(last)
            def _():
                finish_tile(j)

        score(0, even)

        def pair(i):
            body(2 * i, even, odd, even_p, 0)
            body(2 * i + 1, odd, even, odd_p, 1)

        loop(OFF // 2, pair)
        kept(even_p, 0)
        kept(odd_p, 1)

        def finish(n):
            sent_to(place, *packet_hop(n))
            forward(n).wait_send()
            sent_to(place, *out_hop(n))

        loop(16, finish)

    pl.run_scoped(
        attention,
        pltpu.VMEM((TILES, TILE, 256), bf16),
        pltpu.VMEM((4, TILE, 256), bf16),
        pltpu.VMEM((TILES, HD + 16, TILE), bf16),
        pltpu.VMEM((4, 1, TILE), f32),
        pltpu.VMEM((4, HD + 16, TILE), f32),
        pltpu.VMEM((TILE, TILE), f32),
        pltpu.VMEM((TILE, TILE), f32),
        pltpu.VMEM((TILE, TILE), bf16),
        pltpu.VMEM((TILE, TILE), bf16),
    )

    def da_hop(h):
        return (
            stage1.at[h], da_in.at[place.slot], a_send.at[h], a_recv.at[place.slot], place.head_device(h),
        )

    def feed_forward(wo, wu, wd, b2t, gzt, x1s, ysum, hsum, dgz):
        def up_copy(j):
            at = pl.multiple_of(core * 2048 + j * 512, 512)
            return pltpu.make_async_copy(w_up.at[:, pl.ds(at, 512)], wu.at[j], w_sem.at[1 + j])

        def down_copy(j):
            at = pl.multiple_of(core * 2048 + j * 512, 512)
            return pltpu.make_async_copy(w_down.at[pl.ds(at, 512)], wd.at[j], w_sem.at[5 + j])

        out_copy = pltpu.make_async_copy(w_out, wo, w_sem.at[0])
        for j in range(4):
            down_copy(j).start()
        out_copy.start()
        for j in range(4):
            up_copy(j).start()
        dm_hop.wait_recv()
        for j in range(4):
            down_copy(j).wait()
            dgz[j] = dot_nt(dm2[...], wd[j]).astype(bf16)
        for m in range(8):
            for h in (2 * m, 2 * m + 1):
                arrived(o_in.at[h], c_recv.at[h])
            lo, hi = swap_halves(o_in[2 * m], o_in[2 * m + 1])
            o2[0:HT, 128 * m : 128 * m + 128] = lo
            o2[HT:T, 128 * m : 128 * m + 128] = hi
        o_hop = across(1, o2.at[0:T], o2.at[T : 2 * T])
        o_hop.start()
        out_copy.wait()
        x1 = x_ref[0].astype(f32) + dot(o2[0:T], wo[...])
        x1s[...] = x1
        scale1 = lax.rsqrt(jnp.mean(x1 * x1, axis=-1, keepdims=True) + EPS)
        b2[0:T] = (x1 * scale1 * gain2_ref[...]).astype(bf16)
        b_hop = across(2, b2.at[0:T], b2.at[T : 2 * T])
        b_hop.start()
        b_hop.wait_recv()
        b2t[...] = transposed(b2[...])

        for j in range(4):
            up_copy(j).wait()
            z = dot(b2[...], wu[j])
            zz = z * z
            th = jnp.tanh(ROOT * z * (1.0 + CUBE * zz))
            half = 0.5 * (1.0 + th)
            gz = (z * half).astype(bf16)
            slope = half + 0.5 * z * (1.0 - th * th) * (ROOT * (1.0 + 3.0 * CUBE * zz))
            dz = (dgz[j].astype(f32) * slope).astype(bf16)
            gzt[j * 512 : (j + 1) * 512] = transposed(gz)
            yj = dot(gz, wd[j])
            hj = dot_nt(dz, wu[j])
            if j == 0:
                ysum[...] = yj
                hsum[...] = hj
            else:
                ysum[...] += yj
                hsum[...] += hj
            up = dot(b2t[...], dz).astype(bf16)
            for u in range(2):
                unit = 2 * j + u
                spread(gs, SLOT[unit], LONG[TURN[unit]], up[:, u * 256 : u * 256 + 256])
                first_hop(unit).start()

        y_hop = across(3, ysum.at[T : 2 * T], yside)
        h_hop = across(4, hsum.at[T : 2 * T], hside)
        h_hop.start()
        y_hop.start()

        def down_units(u):
            for y_lo in range(2):
                at = y_lo * 512 + u * 256
                grad = dot(gzt[...], dm2[:, at : at + 256]).astype(bf16)
                for owner in range(32):
                    for group in range(4):
                        unit = 8 + u * 4 + group
                        place_at = position(LONG[TURN[unit]], y_lo, owner // 8, owner // 2 % 4, owner % 2)
                        gs[SLOT[unit], place_at] = grad[owner * 64 + group * 16 : owner * 64 + group * 16 + 16]
            for group in range(4):
                first_hop(8 + u * 4 + group).start()

        down_units(0)
        h_hop.wait_recv()
        x1 = x1s[...]
        scale1 = lax.rsqrt(jnp.mean(x1 * x1, axis=-1, keepdims=True) + EPS)
        dh2 = hsum[0:T] + hside[...]
        gain2_grad[...] = jnp.sum(dh2 * x1 * scale1, axis=0, keepdims=True)
        dn = dh2 * gain2_ref[...]
        back = scale1 * dn - x1 * (scale1 * scale1 * scale1) * jnp.mean(dn * x1, axis=-1, keepdims=True)
        dx1 = dy_ref[0].astype(f32) + back
        hside[...] = dx1
        da = dx1.astype(bf16)
        das[...] = da
        side_hop = across(5, das.at[:, pl.ds(pl.multiple_of((1 - core) * 512, 512), 512)], da_side)
        side_hop.start()
        for g in range(4):
            group = lax.rem(g + lax.rem(lax.div(place.s, 4), 4), 4)
            dattn = dot_nt(da, wo[pl.ds(pl.multiple_of(group * 256, 256), 256)]).astype(bf16)
            for m in range(2):
                tile = dattn[:, 128 * m : 128 * m + 128]
                packed = swap_halves(tile[:HT], tile[HT:])
                for e in range(2):
                    h = 4 * group + 2 * m + e
                    stage1[h] = packed[e]
                    send_to(place, *da_hop(h))
        down_units(1)
        y_hop.wait_recv()
        y_ref[0] = (x1 + ysum[0:T] + yside[...]).astype(bf16)
        o_hop.wait_recv()
        side_hop.wait_recv()
        o2t = transposed(o2[...])
        mine = das[:, pl.ds(pl.multiple_of(core * 512, 512), 512)]
        out = (dot(o2t[:, 0:T], mine) + dot(o2t[:, T:], da_side[...])).astype(bf16)
        for u in range(2):
            spread(outg, u, LONG[TURN[16 + u]], out[:, u * 256 : u * 256 + 256])
            outs[u].start()
        for hop in (dm_hop, o_hop, b_hop, y_hop, h_hop, side_hop):
            hop.wait_send()

    pl.run_scoped(
        feed_forward,
        pltpu.VMEM((D, D), bf16),
        pltpu.VMEM((4, D, 512), bf16),
        pltpu.VMEM((4, 512, D), bf16),
        pltpu.VMEM((D, 2 * T), bf16),
        pltpu.VMEM((2048, 2 * T), bf16),
        pltpu.VMEM((T, D), f32),
        pltpu.VMEM((2 * T, D), f32),
        pltpu.VMEM((2 * T, D), f32),
        pltpu.VMEM((4, 2 * T, 512), bf16),
    )

    def hook(which):
        if which == 0:
            for sums_of in main:
                sums_of.advance(0)
        elif which == 1:
            for sums_of in outs:
                sums_of.advance(0)
        elif which < 6:
            for sums_of in main + outs:
                sums_of.advance(which - 1)
        elif which == 6:
            for p, sums_of in enumerate(main):
                total = sums_of.last()
                for k in range(COUNTS[p]):
                    mid.store(p + 6 * k, total[k])
            for u, sums_of in enumerate(outs):
                mid.store(16 + u, sums_of.last()[0])
            mid.start()
        else:
            mid.finish()

    def hooks_at(slot):
        for which in range(8):
            if HOOKS[which] == slot:
                hook(which)

    def key_hop(m):
        return (
            stage2.at[m, 0:T], dqkv_in.at[place.head, 0:T], b_send.at[0, m], b_recv.at[0, place.head],
            place.block_device(m),
        )

    def query_hop(m):
        return (
            stage2.at[m, T:GRAD], dqkv_in.at[place.head, T:GRAD], b_send.at[1, m], b_recv.at[1, place.head],
            place.block_device(m),
        )

    def part_hop(j):
        return remote(part.at[j], landed.at[j], q_send.at[j], q_recv.at[j], place.partner)

    def attention_back(queries, gp, delta, dq, dkv, weights):
        hooks_at(-1)

        def prepare(t):
            dkv[t] = jnp.zeros((TILE, 128), f32)

        loop(TILES, prepare)

        def prepare_query(j):
            for b in range(4):
                m = j * 4 + b
                put_unpacked(pk[place.own_block(m), T : T + HT], False, queries.at[j, b * T : (b + 1) * T])
                arrived(da_in.at[m], a_recv.at[m])
                put_unpacked(da_in[m], True, gp.at[j, b * T : (b + 1) * T])
            delta[j] = jnp.sum(gp[j].astype(f32).T[HD:] * ot[j], axis=0, keepdims=True)
            dq[j] = jnp.zeros((HD, TILE), f32)

        loop(4, prepare_query)
        factor = jnp.where(lax.broadcasted_iota(jnp.int32, (1, 128), 1) < HD, LN2, 1.0)

        def give(j):
            part[j] = (dkv[place.own_tile(j, 1 - core)] * factor).astype(bf16)
            part_hop(j).start()

        def take(j):
            alone = jnp.logical_and(core == 0, j == 3)

            @pl.when(jnp.logical_not(alone))
            def _():
                part_hop(j).wait_recv()

            total = dkv[place.own_tile(j)] * factor
            total = (total + jnp.where(alone, 0.0, landed[j].astype(f32))).astype(bf16)
            for b in range(4):
                m = j * 4 + b
                stage2[m, 0:T] = total[b * T : (b + 1) * T]
                send_to(place, *key_hop(m))

        def fetch(j, k_tile, n):
            which = lax.rem(n, 2)
            for half in (slice(0, TILE // 2), slice(TILE // 2, TILE)):
                pltpu.make_async_copy(
                    probs.at[j, k_tile, half], weights.at[which, half], s_sem.at[2 + which]
                ).start()

        def fetched(n):
            which = lax.rem(n, 2)
            pltpu.make_async_copy(probs.at[0, 0], weights.at[which], s_sem.at[2 + which]).wait()

        def step(j, k_tile, n, pieces):
            size = TILE // len(pieces)
            which = lax.rem(n, 2)
            shift = jnp.exp2(peaks[j, k_tile] - lse[j])
            for at, begin in pieces:
                ks, qs = slice(at, at + size), slice(begin, TILE)
                value = weights[which, ks, qs].astype(f32) * shift[:, qs]
                rows = load_keys(pk, k_tile)[ks]
                slopes = (value * (dot_nt(rows, gp[j, qs]) - delta[j][:, qs])).astype(bf16)
                value = value.astype(bf16)
                dkv[k_tile, ks] += dot(value, gp[j, qs]) + dot(slopes, queries[j, qs])
                dq[j, :, qs] += dot(kt[k_tile][:, ks], slopes)

        def hooks(n):
            for which in range(8):
                if 0 <= HOOKS[which] < STEPS:

                    @pl.when(n == HOOKS[which])
                    def _(which=which):
                        hook(which)

        def owned(k_tile):
            return lax.rem(lax.div(k_tile + 1, 2), 2) == core

        def skipped(k_tile):
            skip = 0
            for j in range(4):
                skip = skip + jnp.where(place.own_tile(j) < k_tile, 1, 0)
            return skip

        def query_of(at, i):
            return jnp.where(i == 7, lax.rem(at + turn, 4), at)

        def later(i):
            empty = jnp.logical_and(core == 1, key_order(place, i) == 7)
            i = jnp.where(empty, i + 1, i)
            k_tile = key_order(place, i)
            return query_of(skipped(k_tile), i), k_tile

        fetch(*later(0), 0)

        def key_tile(i, n):
            k_tile = key_order(place, i)

            def query_tile(at, n):
                hooks(n)
                j = query_of(at, i)
                fetched(n)

                @pl.when(at < 3)
                def _():
                    fetch(query_of(at + 1, i), k_tile, n + 1)

                @pl.when(jnp.logical_and(at == 3, i < 7))
                def _():
                    fetch(*later(jnp.minimum(i + 1, 7)), n + 1)

                diagonal = place.own_tile(j) == k_tile

                @pl.when(diagonal)
                def _():
                    step(j, k_tile, n, [(at, at) for at in range(0, TILE, 256)])

                @pl.when(jnp.logical_not(diagonal))
                def _():
                    step(j, k_tile, n, [(0, 0)])

                @pl.when(i == 7)
                def _():
                    packed = pack_transposed(dq[j] * SCALE)
                    for b in range(4):
                        m = j * 4 + b
                        stage2[m, T:GRAD] = packed[b]
                        send_to(place, *query_hop(m))

                return n + 1

            n = lax.fori_loop(skipped(k_tile), 4, query_tile, n)
            mine = owned(k_tile)
            before = key_order(place, jnp.maximum(i - 1, 0))

            @pl.when(jnp.logical_and(jnp.logical_not(mine), jnp.logical_not(jnp.logical_and(core == 1, k_tile == 7))))
            def _():
                give(lax.div(k_tile, 2))

            @pl.when(jnp.logical_and(i > 0, owned(before)))
            def _():
                take(lax.div(before, 2))

            return n

        lax.fori_loop(0, TILES, key_tile, 0)
        take(0)

        hooks_at(STEPS)

    def back(w_scr, a2t):
        weight = pltpu.make_async_copy(w_qkv, w_scr, l_sem.at[0])
        weight.start()
        a_hop.wait_recv()
        a2t[...] = transposed(a2[...])
        pl.run_scoped(
            attention_back,
            pltpu.VMEM((4, TILE, 128), bf16),
            pltpu.VMEM((4, TILE, 128), bf16),
            pltpu.VMEM((4, 1, TILE), f32),
            pltpu.VMEM((4, HD, TILE), f32),
            pltpu.VMEM((TILES, TILE, 128), f32),
            pltpu.VMEM((2, TILE, TILE), bf16),
        )
        pl.run_scoped(
            functools.partial(last, weight, w_scr, a2t),
            pltpu.VMEM((T, 3 * D), bf16),
            pltpu.VMEM((6, 64, 16, 256), bf16),
        )

    def last(weight, w_scr, a2t, dn, gs3):
        sums = [Part(net, gs3, land3, u, 1, SHORT[u], (t_send, u), (t_recv, u), (), tail3) for u in range(6)]
        for m in range(8):
            for h in (2 * m, 2 * m + 1):
                arrived(dqkv_in.at[h, 0:T], b_recv.at[0, h])
                arrived(dqkv_in.at[h, T:GRAD], b_recv.at[1, h])
            lo, hi = swap_halves(dqkv_in[2 * m, T:GRAD], dqkv_in[2 * m + 1, T:GRAD])
            dk, dv = swap_halves(dqkv_in[2 * m, 0:T], dqkv_in[2 * m + 1, 0:T])
            dn[0:HT, 128 * m : 128 * m + 128] = lo
            dn[HT:T, 128 * m : 128 * m + 128] = hi
            dn[:, D + 128 * m : D + 128 * m + 128] = dk
            dn[:, 2 * D + 128 * m : 2 * D + 128 * m + 128] = dv
        d_hops = []
        for section in range(3):
            at = pl.multiple_of(section * D + (1 - core) * 512, 512)
            d_hops.append(
                across(9 + section, dn.at[:, pl.ds(at, 512)], d_side.at[:, section * 512 : section * 512 + 512])
            )
            d_hops[section].start()
        for u in range(6):
            section, half = u // 2, u % 2
            if half == 0:
                d_hops[section].wait_recv()
            at = pl.multiple_of(section * D + core * 512 + half * 256, 256)
            grad = dot(a2t[:, 0:T], dn[:, pl.ds(at, 256)]) + dot(a2t[:, T:], d_side[:, u * 256 : u * 256 + 256])
            spread(gs3, u, SHORT[u], grad.astype(bf16))
            sums[u].start()
        weight.wait()
        x = x_ref[0].astype(f32)
        scale = lax.rsqrt(jnp.mean(x * x, axis=-1, keepdims=True) + EPS)
        dh1 = dot_nt(dn[...], w_scr[...])
        gain1_grad = jnp.sum(dh1 * x * scale, axis=0, keepdims=True)
        both = [gain1_grad[:, 128 * k : 128 * k + 128] for k in range(8)]
        both += [gain2_grad[:, 128 * k : 128 * k + 128] for k in range(8)]
        gain_value[0] = jnp.concatenate(both, axis=0)
        gains.start(0)
        dxn = dh1 * gain1_ref[...]
        back = scale * dxn - x * (scale * scale * scale) * jnp.mean(dxn * x, axis=-1, keepdims=True)
        dx_ref[0] = (hside[...] + back).astype(bf16)

        for stage in range(2):
            for sums_of in sums:
                sums_of.advance(stage)
            gains.take(stage)
            gains.start(stage + 1)
            hooks_at(STEPS + 1 + stage)
        for g in range(2):
            for sums_of in sums[3 * g : 3 * g + 3]:
                sums_of.settle()
            ends3[g].start()
        gains.take(2)
        hooks_at(STEPS + 3)
        for g in range(2):
            ends3[g].wait()
            for u in range(3):
                fin3[3 * g + u] = ends3[g].result(u).reshape(2, 8, 256)
        aside = across(8, fin3.at[:, 1 - core], side3)
        aside.start()
        hooks_at(STEPS + 4)
        shard = place.s * 4 + place.r
        turn = lax.rem(128 - lax.rem(shard, 16) * 8, 128)
        for k in range(2):
            row = gain_value[3, pl.ds(8 * k + lax.div(shard, 16), 1)]
            gain_out[k : k + 1] = pltpu.roll(row, turn, 1)
        aside.wait_recv()
        mine, other = core, 1 - core
        for u in range(6):
            at = (u // 2) * D + (u % 2) * 256
            qkv_out[:, pl.ds(at + mine * 512, 256)] = fin3[u, mine]
            qkv_out[:, pl.ds(at + other * 512, 256)] = side3[u]
        for hop in [a_hop, aside] + d_hops:
            hop.wait_send()
        for sums_of in sums:
            sums_of.finish()

    pl.run_scoped(back, pltpu.VMEM((D, 3 * D), bf16), pltpu.VMEM((D, 2 * T), bf16))

    def finish(n):
        sent_to(place, *da_hop(n))
        sent_to(place, *key_hop(n))
        sent_to(place, *query_hop(n))

    loop(16, finish)

    def given(j, carry):
        part_hop(j).wait_send()
        return carry

    lax.fori_loop(0, 4 - core, given, 0)
    for sums_of in main + outs + ends3 + [gains]:
        sums_of.finish()


def block_call(frames, segment_ids, out_grad, gain1, gain2, w_qkv, w_out, w_up, w_down):
    dma = pltpu.SemaphoreType.DMA
    return pl.pallas_call(
        block_kernel,
        name="block",
        out_shape=(
            jax.ShapeDtypeStruct((1, T, D), bf16),
            jax.ShapeDtypeStruct((1, T, D), bf16),
            jax.ShapeDtypeStruct((8, 3 * D), f32),
            jax.ShapeDtypeStruct((8, 128), f32),
            jax.ShapeDtypeStruct((8, FF), f32),
            jax.ShapeDtypeStruct((8, D), f32),
            jax.ShapeDtypeStruct((32, D), f32),
            jax.ShapeDtypeStruct((4, TILES, TILE, TILE), bf16),
        ),
        in_specs=[VM] * 5 + [ANY] * 4,
        out_specs=(VM,) * 7 + (ANY,),
        scratch_shapes=[
            pltpu.VMEM((BLOCKS, PACK, 128), bf16),
            pltpu.VMEM((TILES, HD, TILE), bf16),
            pltpu.VMEM((16, HT, 128), bf16),
            pltpu.VMEM((4, HD, TILE), f32),
            pltpu.VMEM((4, 1, TILE), f32),
            pltpu.VMEM((4, TILES, 1, TILE), f32),
            pltpu.VMEM((2 * T, D), bf16),
            pltpu.VMEM((2 * T, D), bf16),
            pltpu.VMEM((2 * T, D), bf16),
            pltpu.VMEM((T, D), f32),
            pltpu.VMEM((T, D), f32),
            pltpu.VMEM((T, D), bf16),
            pltpu.VMEM((T, 512), bf16),
            pltpu.VMEM((1, D), f32),
            pltpu.VMEM((16, 64, 16, 256), bf16),
            pltpu.VMEM((16, 63, 16, 256), bf16),
            pltpu.VMEM((2, 64, 16, 256), bf16),
            pltpu.VMEM((2, 63, 16, 256), bf16),
            pltpu.VMEM((16, HT, 128), bf16),
            pltpu.VMEM((16, HT, 128), bf16),
            pltpu.VMEM((4, TILE, 128), bf16),
            pltpu.VMEM((4, TILE, 128), bf16),
            pltpu.VMEM((16, GRAD, 128), bf16),
            pltpu.VMEM((16, PACK, 128), bf16),
            pltpu.VMEM((18, 2, 8, 256), f32),
            pltpu.VMEM((10, 8, 256), f32),
            pltpu.VMEM((2, 4, 2, 8, 256), f32),
            pltpu.VMEM((2 * T, D), bf16),
            pltpu.VMEM((T, 1536), bf16),
            pltpu.VMEM((6, 56, 16, 256), bf16),
            pltpu.VMEM((6, 8, 16, 256), bf16),
            pltpu.VMEM((2, 7, 3, 16, 256), bf16),
            pltpu.VMEM((4, 16, 128), f32),
            pltpu.VMEM((3, 7, 16, 128), f32),
            pltpu.VMEM((6, 2, 8, 256), f32),
            pltpu.VMEM((6, 8, 256), f32),
            dma((9,)), dma((1,)), dma((12,)), dma((12,)), dma((4,)), dma((4,)), dma((16,)), dma((16,)),
            dma((16,)), dma((16,)), dma((2, 16)), dma((2, 16)), dma((8, 6)), dma((8, 6)), dma((6, 3)), dma((6, 3)),
            dma((2, 7)), dma((2, 7)), dma((3, 7)), dma((3, 7)), dma((6,)),
            dma((4, 3)), dma((16,)), dma((16,)), dma((16,)), dma((16,)), dma((16,)), dma((16,)), dma((4,)),
        ],
        compiler_params=params(0),
    )(frames, segment_ids, out_grad, gain1, gain2, w_qkv, w_out, w_up, w_down)


def deliver_kernel(*refs):
    count = len(refs) // 2 - 2
    sources, gains, targets = refs[:count], refs[count], refs[count + 1 : 2 * count + 1]
    gain1, gain2, sem = refs[2 * count + 1 :]
    del sem
    for k in range(count):
        targets[k][...] = sources[k][...]
    gain1[...] = gains[0, 0:8]
    gain2[...] = gains[1, 0:8]


def deliver(arrays, gains):
    count = len(arrays)
    small = jax.ShapeDtypeStruct((8,), f32)
    return pl.pallas_call(
        deliver_kernel,
        name="deliver",
        out_shape=tuple(jax.ShapeDtypeStruct(v.shape, v.dtype) for v in arrays) + (small, small),
        in_specs=[VM] * (count + 1),
        out_specs=(VM,) * (count + 2),
        scratch_shapes=[pltpu.SemaphoreType.DMA((count,))],
    )(*arrays, gains)


def shards(frames, segment_ids, norm1_gain, w_qkv, w_out, norm2_gain, w_up, w_down, out_grad):
    gain1, gain2 = norm1_gain[None], norm2_gain[None]
    y, dx, qkv_sum, gain_sums, up_sum, out_sum, down_sum, _ = block_call(
        frames, segment_ids, out_grad, gain1, gain2, w_qkv, w_out, w_up, w_down
    )
    y, dx, qkv_sum, out_sum, up_sum, down_sum, gain1_sum, gain2_sum = deliver(
        (y, dx, qkv_sum, out_sum, up_sum, down_sum), gain_sums
    )
    return (y, dx, gain1_sum, qkv_sum, out_sum, gain2_sum, up_sum, down_sum)


def solution(mesh):
    return jax.shard_map(
        shards,
        mesh=mesh,
        in_specs=(
            P("row", "seq", None),
            P("row", "seq"),
            P(),
            P(),
            P(),
            P(),
            P(),
            P(),
            P("row", "seq", None),
        ),
        out_specs=(
            P("row", "seq", None),
            P("row", "seq", None),
            P(("seq", "row")),
            P(("seq", "row"), None),
            P(("seq", "row"), None),
            P(("seq", "row")),
            P(("seq", "row"), None),
            P(("seq", "row"), None),
        ),
        check_vma=False,
    )
```

```python
import functools
import math

import jax
import jax.numpy as jnp
from jax import lax
from jax.experimental import pallas as pl
from jax.experimental.pallas import tpu as pltpu
from jax.sharding import PartitionSpec as P

MESH = pl.DeviceIdType.MESH
f32 = jnp.float32
bf16 = jnp.bfloat16

D = 1024
H = 16
HD = 64
FF = 4096
T = 192
HT = T // 2
BLOCKS = 32
TILE = 768
TILES = 8
PACK = 288
EPS = 1e-05
NEG = -1e30
LOG2E = math.log2(math.e)
LN2 = math.log(2.0)
SCALE = HD**-0.5
VMEM_LIMIT = 60 * 1024 * 1024

ANY = pl.BlockSpec(memory_space=pl.ANY)
VM = pl.BlockSpec(memory_space=pltpu.VMEM)


def dot(a, b):
    return jnp.dot(a, b, preferred_element_type=f32)


def dot_nt(a, b):
    return lax.dot_general(a, b, (((1,), (1,)), ((), ())), preferred_element_type=f32)


def transposed(v):
    return v.astype(f32).T.astype(bf16)


def swap_halves(first, second):
    lane = lax.broadcasted_iota(jnp.int32, first.shape, 1)
    low = lane < HD
    first, second = first.astype(f32), second.astype(f32)
    return (
        jnp.where(low, first, pltpu.roll(second, HD, 1)).astype(bf16),
        jnp.where(low, pltpu.roll(first, HD, 1), second).astype(bf16),
    )


class Place:
    def __init__(self):
        self.s = lax.axis_index("seq")
        self.r = lax.axis_index("row")
        self.y_lo = lax.div(self.s, 16)
        self.head = lax.rem(self.s, 16)
        self.y_hi = lax.div(self.r, 2)
        self.core = lax.rem(self.r, 2)
        tile = lax.div(self.s, 4)
        self.block_core = lax.rem(lax.div(tile + 1, 2), 2)
        self.slot = lax.div(self.s, 8) * 4 + lax.rem(self.s, 4)
        self.partner = (self.s, self.r + 1 - 2 * self.core)
        self.self_served = jnp.logical_and(self.y_lo == self.core, self.block_core == self.core)
        self.self_count = jnp.where(self.self_served, 1, 0)

    def head_device(self, h):
        return (self.core * 16 + h, self.y_hi * 2 + self.block_core)

    def own_tile(self, j, core=None):
        core = self.core if core is None else core
        return 2 * j + lax.rem(j + core, 2)

    def own_block(self, n):
        return self.own_tile(lax.div(n, 4)) * 4 + lax.rem(n, 4)

    def block_device(self, n):
        return (self.own_block(n), self.y_hi * 2 + self.y_lo)

    def is_self(self, device):
        return jnp.logical_and(device[0] == self.s, device[1] == self.r)


def remote(src, dst, send, recv, device):
    return pltpu.make_async_remote_copy(
        src_ref=src, dst_ref=dst, send_sem=send, recv_sem=recv, device_id=device, device_id_type=MESH
    )


def send_to(place, src, dst, send, recv, device):
    own = place.is_self(device)

    @pl.when(own)
    def _():
        pltpu.make_async_copy(src, dst, recv).start()

    @pl.when(jnp.logical_not(own))
    def _():
        remote(src, dst, send, recv, device).start()


def sent_to(place, src, dst, send, recv, device):
    @pl.when(jnp.logical_not(place.is_self(device)))
    def _():
        remote(src, dst, send, recv, device).wait_send()


def arrived(dst, recv):
    pltpu.make_async_copy(dst, dst, recv).wait()


def greet(barrier, device):
    pl.semaphore_signal(barrier, inc=1, device_id=device, device_id_type=MESH)


def greet_all(place, barrier, device_of):
    def one(n, carry):
        device = device_of(n)

        @pl.when(jnp.logical_not(place.is_self(device)))
        def _():
            greet(barrier, device)

        return carry

    lax.fori_loop(0, 16, one, 0)


def loop(count, body):
    def one(n, carry):
        body(n)
        return carry

    lax.fori_loop(0, count, one, 0)


def params(collective_id):
    return pltpu.CompilerParams(
        collective_id=collective_id, has_side_effects=True, vmem_limit_bytes=VMEM_LIMIT
    )


def seg_column(tile):
    tile = tile.astype(f32)
    return jnp.concatenate(
        [
            jnp.broadcast_to(tile[0:1], (128, 128)).T,
            jnp.broadcast_to(tile[1:2], (128, 128)).T[: T - 128],
        ],
        axis=0,
    )


MIDDLE = 4


def put_marks(segs, tile, put):
    lane = lax.broadcasted_iota(jnp.int32, (TILE, 128), 1).astype(f32)
    put(slice(0, TILE), lane, jnp.full((TILE, 128), MIDDLE, f32))
    for which, special, rows in ((0, 0, slice(0, T)), (1, TILES - 1, slice(TILE - T, TILE))):

        @pl.when(tile == special)
        def _(which=which, rows=rows):
            put(rows, lane[:T], seg_column(segs[which]) + MIDDLE)


def put_unpacked(packed, high, target):
    low = lax.broadcasted_iota(jnp.int32, (HT, 128), 1) < HD
    packed = packed.astype(f32)
    turned = pltpu.roll(packed, HD, 1)
    if high:
        target[0:HT] = jnp.where(low, 0.0, turned).astype(bf16)
        target[HT:T] = jnp.where(low, 0.0, packed).astype(bf16)
    else:
        target[0:HT] = jnp.where(low, packed, 0.0).astype(bf16)
        target[HT:T] = jnp.where(low, turned, 0.0).astype(bf16)


STEPS = 18
AHEAD = 4


OFF = STEPS - 4


def walk(place, n):
    turn = lax.div(place.head, 4)
    j, start = turn, 0
    end = place.own_tile(j)
    for k in range(1, 4):
        past = n >= end
        following = lax.rem(turn + k, 4)
        j = jnp.where(past, following, j)
        start = jnp.where(past, end, start)
        end = jnp.where(past, end + place.own_tile(following), end)
    return j, n - start, n + 1 == end


def key_order(place, i):
    turn = lax.div(place.head, 4)
    k_tile = 7 - lax.rem(i + 2 * turn, 7)
    k_tile = jnp.where(jnp.logical_and(place.core == 1, k_tile == 1), 0, k_tile)
    return jnp.where(i == 7, place.core, k_tile)


def causal(scores):
    k = lax.broadcasted_iota(jnp.int32, scores.shape, 0)
    q = lax.broadcasted_iota(jnp.int32, scores.shape, 1)
    return jnp.where(k <= q, scores, NEG)


def load_keys(pk_ref, tile):
    return pk_ref[pl.ds(tile * 4, 4), 0:T].reshape(TILE, 128)


def pack_transposed(value_t):
    both = jnp.concatenate([value_t, value_t], axis=0).T
    lane = lax.broadcasted_iota(jnp.int32, (HT, 128), 1)
    return [
        jnp.where(lane < HD, both[b * T : b * T + HT], both[b * T + HT : b * T + T]).astype(bf16)
        for b in range(4)
    ]


FIRST = lambda c: ((c + 1) // 2) % 2
SECOND = lambda c: c // 2


def chip_bits(x, y, z):
    return [FIRST(x), FIRST(y), FIRST(z), SECOND(x), SECOND(y), SECOND(z)]


SHORT = [[(p + k) % 3 + 3 * (p // 3) for k in range(3)] + [k + 3 * (1 - p // 3) for k in range(3)] for p in range(6)]
LONG = [[(p + k) % 3 + 3 * ((p // 3 + k // 3) % 2) for k in range(6)] for p in range(6)]


def position(order, y_lo, x, z, y_hi):
    bits = chip_bits(x, y_hi * 2 + y_lo, z)
    at = 0
    for dim in order:
        at = at * 2 + bits[dim]
    return at


class Net:
    def __init__(self, place):
        self.x, self.z = lax.div(place.head, 4), lax.rem(place.head, 4)
        self.y = place.y_hi * 2 + place.y_lo
        self.core = place.core
        self.bits = [lax.rem(lax.div(c + 1, 2), 2) for c in (self.x, self.y, self.z)]
        self.bits += [lax.div(c, 2) for c in (self.x, self.y, self.z)]

    def across(self, pairing, mask):
        moved = []
        for k, c in enumerate((self.x, self.y, self.z)):
            far = c + 1 - 2 * lax.rem(c, 2) if pairing == 0 else 3 - c
            moved.append(far if mask >> (2 - k) & 1 else c)
        x, y, z = moved
        return (lax.rem(y, 2) * 16 + x * 4 + z, lax.div(y, 2) * 2 + self.core)

    def neighbour(self, dim):
        return self.across(dim // 3, 4 >> dim % 3)

    def greet(self, barrier):
        for pairing in range(2):
            for mask in range(1, 8):
                greet(barrier, self.across(pairing, mask))

    GREETINGS = 14


class Part:
    def __init__(self, net, acc, land, at, count, order, send, recv, pieces=(), tail=None):
        self.net, self.acc, self.land, self.order, self.pieces, self.tail = net, acc, land, order, pieces, tail
        self.units = pl.ds(at, count)
        self.send, self.recv = send, recv

    def bit(self, stage):
        return self.net.bits[self.order[stage]]

    def base(self, stage):
        at = 0
        for k in range(stage + 1):
            at = at + self.bit(k) * (32 >> k)
        return at

    def landing(self, stage):
        return sum(32 >> k for k in range(stage))

    def hop(self, stage):
        half = 32 >> stage
        base = self.base(stage - 1) + (1 - self.bit(stage)) * half
        return remote(
            self.acc.at[self.units, pl.ds(base, half)],
            self.land.at[self.units, pl.ds(self.landing(stage), half)],
            self.send[0].at[self.send[1], stage],
            self.recv[0].at[self.recv[1], stage],
            self.net.neighbour(self.order[stage]),
        )

    def start(self):
        self.hop(0).start()

    def hops(self, stage):
        return list(self.pieces) if stage == 0 and self.pieces else [self.hop(stage)]

    def total(self, base, landed, group):
        mine = self.acc[self.units, pl.ds(base, group)].astype(f32)
        return (mine + self.land[self.units, pl.ds(landed, group)].astype(f32)).astype(bf16)

    def add(self, base, landed, count):
        group = min(count, 4)

        def body(i):
            here = pl.ds(base + i * group, group)
            self.acc[self.units, here] = self.total(base + i * group, landed + i * group, group)

        loop(count // group, body)

    def advance(self, stage):
        for hop in self.hops(stage):
            hop.wait_recv()
        half = 16 >> stage
        base, landed = self.base(stage), self.landing(stage)
        bit = self.bit(stage + 1)
        self.add(base + (1 - bit) * half, landed + (1 - bit) * half, half)
        self.hop(stage + 1).start()
        self.add(base + bit * half, landed + bit * half, half)

    def settle(self):
        self.hop(2).wait_recv()
        for at in range(0, 8, 4):
            self.tail[self.units, at : at + 4] = self.total(self.base(2) + at, self.landing(2) + at, 4)

    def last(self):
        self.hop(5).wait_recv()
        mine = self.acc[self.units, pl.ds(self.base(5), 1)].astype(f32)
        return (mine + self.land[self.units, pl.ds(self.landing(5), 1)].astype(f32))[:, 0]

    def finish(self):
        for stage in range(6 if self.tail is None else 3):
            for hop in self.hops(stage):
                hop.wait_send()


class Exchange:
    def __init__(self, net, pairing, tail, land, send, recv):
        self.net, self.pairing, self.tail, self.land, self.send, self.recv = net, pairing, tail, land, send, recv

    def row(self, mask):
        at = 0
        for k in range(3):
            bit = self.net.bits[3 * self.pairing + k]
            at = at + (1 - bit if mask >> (2 - k) & 1 else bit) * (4 >> k)
        return at

    def hop(self, mask):
        return remote(
            self.tail.at[:, self.row(mask)], self.land.at[mask - 1],
            self.send.at[mask - 1], self.recv.at[mask - 1], self.net.across(self.pairing, mask),
        )

    def start(self):
        for mask in range(1, 8):
            self.hop(mask).start()

    def result(self, unit):
        total = self.tail[unit, self.row(0)].astype(f32)
        for mask in range(1, 8):
            total = total + self.land[mask - 1, unit].astype(f32)
        return total

    def wait(self):
        for mask in range(1, 8):
            self.hop(mask).wait_recv()

    def finish(self):
        for mask in range(1, 8):
            self.hop(mask).wait_send()


class Shared:
    def __init__(self, net, place, value, land, send, recv):
        self.net, self.place, self.value, self.land, self.send, self.recv = net, place, value, land, send, recv

    def hops(self, pairing):
        if pairing == 2:
            return [
                remote(self.value.at[2], self.land.at[2, 0], self.send.at[2, 0], self.recv.at[2, 0], self.place.partner)
            ]
        return [
            remote(
                self.value.at[pairing], self.land.at[pairing, mask - 1],
                self.send.at[pairing, mask - 1], self.recv.at[pairing, mask - 1], self.net.across(pairing, mask),
            )
            for mask in range(1, 8)
        ]

    def start(self, pairing):
        for hop in self.hops(pairing):
            hop.start()

    def take(self, pairing):
        total = self.value[pairing]
        for k, hop in enumerate(self.hops(pairing)):
            hop.wait_recv()
            total = total + self.land[pairing, k]
        self.value[pairing + 1] = total

    def finish(self):
        for pairing in range(3):
            for hop in self.hops(pairing):
                hop.wait_send()


TURN = [u % 6 for u in range(18)]
COUNTS = [3, 3, 3, 3, 2, 2]
STARTS = [0, 3, 6, 9, 12, 14]
SLOT = [STARTS[u % 6] + u // 6 for u in range(16)]
FINAL = list(range(8)) + [10 + (v % 4) * 2 + v // 4 for v in range(8)] + [8, 9]


class MidSums:
    def __init__(self, place, fin, side, down, sem, up_out, out_out, down_out):
        self.place, self.fin, self.side, self.down, self.sem = place, fin, side, down, sem
        self.up_out, self.out_out, self.down_out = up_out, out_out, down_out

    def targets(self):
        return [(self.place.core * 16 + self.place.head, self.place.y_hi * 2 + k) for k in range(2)]

    def sources(self):
        return [(m * 16 + self.place.head, self.place.y_hi * 2 + self.place.y_lo) for m in range(2)]

    def self_count(self):
        return jnp.where(self.place.y_lo == self.place.core, 1, 0)

    def greet(self, barrier):
        greet(barrier, self.place.partner)
        for device in self.sources():

            @pl.when(jnp.logical_not(self.place.is_self(device)))
            def _(device=device):
                greet(barrier, device)

    def greetings(self):
        return 3 - self.self_count()

    def store(self, unit, value):
        self.fin[FINAL[unit]] = value.reshape(2, 8, 256)

    def aside(self):
        return remote(
            self.fin.at[0:10, 1 - self.place.core], self.side, self.sem.at[0], self.sem.at[1], self.place.partner
        )

    def down_hop(self, k):
        return (
            self.fin.at[10 + 4 * k : 14 + 4 * k],
            self.down.at[self.place.y_lo],
            self.sem.at[2 + k],
            self.sem.at[4 + self.place.y_lo],
            self.targets()[k],
        )

    def start(self):
        self.aside().start()
        for k in range(2):
            send_to(self.place, *self.down_hop(k))

    def finish(self):
        place = self.place
        self.aside().wait_recv()
        mine, other = place.core, 1 - place.core
        for u in range(8):
            self.up_out[:, pl.ds(mine * 2048 + u * 256, 256)] = self.fin[u, mine]
            self.up_out[:, pl.ds(other * 2048 + u * 256, 256)] = self.side[u]
        for u in range(2):
            self.out_out[:, pl.ds(mine * 512 + u * 256, 256)] = self.fin[8 + u, mine]
            self.out_out[:, pl.ds(other * 512 + u * 256, 256)] = self.side[8 + u]
        for m in range(2):
            arrived(self.down.at[m], self.sem.at[4 + m])
            for v in range(4):
                group, half = v // 2, v % 2
                self.down_out[group * 16 : group * 16 + 16, m * 512 + half * 256 : m * 512 + half * 256 + 256] = (
                    self.down[m, v].reshape(16, 256)
                )
        self.aside().wait_send()
        for k in range(2):
            sent_to(place, *self.down_hop(k))


MID_OUT = (
    jax.ShapeDtypeStruct((8, FF), f32),
    jax.ShapeDtypeStruct((8, D), f32),
    jax.ShapeDtypeStruct((32, D), f32),
)
MID_SCRATCH = [
    pltpu.VMEM((18, 2, 8, 256), f32),
    pltpu.VMEM((10, 8, 256), f32),
    pltpu.VMEM((2, 4, 2, 8, 256), f32),
    pltpu.SemaphoreType.DMA((6,)),
]


def spread(target, unit_slot, order, block):
    for chip in range(64):
        y_lo, x, z, y_hi = chip // 32, chip // 8 % 4, chip // 2 % 4, chip % 2
        target[unit_slot, position(order, y_lo, x, z, y_hi)] = block[chip * 16 : chip * 16 + 16]


ROOT = math.sqrt(2.0 / math.pi)
CUBE = 0.044715


HOOKS = (1, 5, 11, 18, 19, 20, 21, 22)


def block_kernel(
    x_ref, seg_ref, dy_ref, gain1_ref, gain2_ref, w_qkv, w_out, w_up, w_down,
    y_ref, dx_ref, qkv_out, gain_out, up_out, out_out, down_out, probs,
    pk, segs, seg_tile, kt, o_in, ot, lse, peaks, o2, b2, dm2, yside, hside, das, da_side, gain2_grad,
    gs, land, outg, land2, da_in, stage1,
    part, landed, dqkv_in, stage2, fin, side, down, a2, d_side, land3, tail3, tail_land3, gain_value, gain_land,
    fin3, side3,
    w_sem, l_sem, p_send, p_recv, q_send, q_recv, h_send, h_recv, a_send, a_recv, b_send, b_recv,
    n_send, n_recv, t_send, t_recv, e_send, e_recv, g_send, g_recv, m_sem,
    k_sem, x_send, x_recv, f_send, f_recv, c_send, c_recv, s_sem, y_send, y_recv,
):
    place = Place()
    core = place.core
    net = Net(place)
    turn = lax.rem(lax.div(place.s, 4), 4)

    def across(k, src, dst):
        return remote(src, dst, p_send.at[k], p_recv.at[k], place.partner)

    def first_hop(unit):
        bit = net.bits[TURN[unit]]
        return remote(
            gs.at[SLOT[unit], pl.ds((1 - bit) * 32, 32)], land.at[SLOT[unit], 0:32],
            h_send.at[unit], h_recv.at[unit], net.neighbour(TURN[unit]),
        )

    main = [
        Part(
            net, gs, land, STARTS[p], COUNTS[p], LONG[p], (n_send, p), (n_recv, p),
            [first_hop(p + 6 * k) for k in range(COUNTS[p])],
        )
        for p in range(6)
    ]
    outs = [
        Part(net, outg, land2, u, 1, LONG[TURN[16 + u]], (n_send, 6 + u), (n_recv, 6 + u)) for u in range(2)
    ]
    mid = MidSums(place, fin, side, down, m_sem, up_out, out_out, down_out)
    ends3 = [
        Exchange(net, 1 - g, tail3.at[3 * g : 3 * g + 3], tail_land3.at[g], e_send.at[g], e_recv.at[g])
        for g in range(2)
    ]
    gains = Shared(net, place, gain_value, gain_land, g_send, g_recv)

    barrier = pltpu.get_barrier_semaphore()
    greet_all(place, barrier, place.block_device)
    greet_all(place, barrier, place.head_device)
    net.greet(barrier)
    mid.greet(barrier)
    a_hop = across(6, a2.at[0:T], a2.at[T : 2 * T])
    dm_hop = across(0, dm2.at[0:T], dm2.at[T : 2 * T])

    edge = jnp.logical_or(place.s == 0, place.s == BLOCKS - 1)
    which_edge = lax.div(place.s, BLOCKS - 1)

    def seg_hop(h):
        return (seg_tile, segs.at[which_edge], y_send.at[h], y_recv.at[which_edge], place.head_device(h))

    def packet_hop(h):
        return (stage2.at[h], pk.at[place.s], x_send.at[h], x_recv.at[place.slot], place.head_device(h))

    def qkv(w_scr):
        def weight(g, section):
            at = pl.multiple_of(section * D + lax.rem(g + turn, 4) * 256, 256)
            return pltpu.make_async_copy(w_qkv.at[:, pl.ds(at, 256)], w_scr.at[g, section], k_sem.at[g, section])

        for g in range(4):
            for section in range(3):
                weight(g, section).start()
        x = x_ref[0].astype(f32)
        a = (x * lax.rsqrt(jnp.mean(x * x, axis=-1, keepdims=True) + EPS) * gain1_ref[...]).astype(bf16)
        a2[0:T] = a
        dm2[0:T] = dy_ref[0]
        numbers = seg_ref[...].astype(f32)
        numbers = numbers - jnp.where(place.s == BLOCKS - 1, numbers[:, 0:1], numbers[:, T - 1 : T])
        row = lax.broadcasted_iota(jnp.int32, (16, 128), 0)
        rest = jnp.concatenate([numbers[:, 128:T], jnp.zeros((1, 256 - T), f32)], axis=1)
        seg_tile[...] = jnp.where(row == 0, numbers[:, :128], jnp.where(row == 1, rest, 0.0)).astype(bf16)
        for g in range(4):
            for section in range(3):
                weight(g, section).wait()
            q = dot(a, w_scr[g, 0]) * (SCALE * LOG2E)
            k = dot(a, w_scr[g, 1])
            v = dot(a, w_scr[g, 2])
            if g == 0:
                pl.semaphore_wait(barrier, 2 * (16 - place.self_count) + Net.GREETINGS + mid.greetings())

                @pl.when(edge)
                def _():
                    loop(16, lambda h: send_to(place, *seg_hop(h)))

            for m in range(2):
                lanes = slice(128 * m, 128 * m + 128)
                h = 4 * lax.rem(g + turn, 4) + 2 * m
                kv = swap_halves(k[:, lanes].astype(bf16), v[:, lanes].astype(bf16))
                qq = q[:, lanes].astype(bf16)
                qp = swap_halves(qq[:HT], qq[HT:])
                for e in range(2):
                    stage2[h + e, 0:T] = kv[e]
                    stage2[h + e, T:PACK] = qp[e]
                    send_to(place, *packet_hop(h + e))
        a_hop.start()
        dm_hop.start()

    pl.run_scoped(qkv, pltpu.VMEM((4, 3, D, 256), bf16))

    def out_hop(m):
        return (stage1.at[m], o_in.at[place.head], c_send.at[m], c_recv.at[place.head], place.block_device(m))

    def attention(keys, queries, vt, top, acc, even, odd, even_p, odd_p):
        one = jnp.where(lax.broadcasted_iota(jnp.int32, (16, TILE), 0) == 0, 1.0, 0.0).astype(bf16)

        def forward(n):
            i = place.own_block(n)
            return remote(pk.at[i, 0:T], pk.at[i, 0:T], f_send.at[n], f_recv.at[n], place.partner)

        def seg_forward(k):
            return remote(segs.at[k], segs.at[k], f_send.at[16 + k], f_recv.at[16 + k], place.partner)

        def key_tile(t):
            rows = load_keys(pk, t)
            keys[t, :, 0:128] = rows

            def put(rows, lane, number):
                keys[t, rows, 128:256] = jnp.where(lane == number, 1.0, 0.0).astype(bf16)

            put_marks(segs, t, put)
            turned = transposed(rows)
            kt[t] = turned[:HD]
            vt[t, 0:HD] = turned[HD:]
            vt[t, HD : HD + 16] = one

        def query_tile(j):
            t = place.own_tile(j)
            for b in range(4):
                put_unpacked(pk[t * 4 + b, T : T + HT], False, queries.at[j, b * T : (b + 1) * T, 0:128])

            def put(rows, lane, number):
                other = jnp.logical_and(lane < 2 * MIDDLE + 1, lane != number)
                queries[j, rows, 128:256] = jnp.where(other, NEG, 0.0).astype(bf16)

            put_marks(segs, t, put)

        def keep(j, k_tile, weights, which):
            for half in (slice(0, TILE // 2), slice(TILE // 2, TILE)):
                pltpu.make_async_copy(weights.at[half], probs.at[j, k_tile, half], s_sem.at[which]).start()

        def kept(weights, which):
            pltpu.make_async_copy(weights, probs.at[0, 0], s_sem.at[which]).wait()

        def finish_tile(j):
            total = acc[j, HD : HD + 1]
            out_t = acc[j, 0:HD] / total
            lse[j] = top[j] + jnp.log2(total)
            ot[j] = out_t
            packed = pack_transposed(out_t)
            for b in range(4):
                m = j * 4 + b
                stage1[m] = packed[b]
                send_to(place, *out_hop(m))

        def diagonal(j, weights, which, again):
            for b in range(4):
                n = j * 4 + b
                arrived(pk.at[place.own_block(n)], x_recv.at[n])
                forward(n).start()
            t = place.own_tile(j)
            for k, special in ((0, 0), (1, TILES - 1)):

                @pl.when(t == special)
                def _(k=k):
                    arrived(segs.at[k], y_recv.at[k])
                    seg_forward(k).start()

            key_tile(t)
            query_tile(j)
            scores = causal(dot_nt(keys[t], queries[j]))
            peak = jnp.max(scores, axis=0, keepdims=True)
            top[j] = peak
            peaks[j, t] = peak
            value = jnp.exp2(scores - peak).astype(bf16)

            @pl.when(again)
            def _():
                kept(weights, which)

            weights[...] = value
            keep(j, t, weights, which)
            acc[j] = dot(vt[t], value)

        def diagonals(i):
            diagonal(2 * i, even_p, 0, i > 0)
            diagonal(2 * i + 1, odd_p, 1, i > 0)

        loop(2, diagonals)

        @pl.when(core == 0)
        def _():
            finish_tile(0)

        def others(j):
            for b in range(4):
                forward(j * 4 + b).wait_recv()
            other = place.own_tile(j, 1 - core)
            for k, special in ((0, 0), (1, TILES - 1)):

                @pl.when(other == special)
                def _(k=k):
                    seg_forward(k).wait_recv()

            key_tile(place.own_tile(j, 1 - core))

        loop(4, others)

        def score(n, scores):
            j, k_tile, _ = walk(place, jnp.minimum(n, OFF - 1))
            scores[...] = dot_nt(keys[k_tile], queries[j])

        def body(n, now, later, weights, which):
            j, k_tile, last = walk(place, n)
            kept(weights, which)
            score(n + 1, later)
            scores = now[...]
            peak = jnp.maximum(top[j], jnp.max(scores, axis=0, keepdims=True))
            fade = jnp.exp2(top[j] - peak)
            top[j] = peak
            peaks[j, k_tile] = peak
            value = jnp.exp2(scores - peak).astype(bf16)
            weights[...] = value
            acc[j] = acc[j] * fade + dot(vt[k_tile], value)
            keep(j, k_tile, weights, which)

            @pl.when(last)
            def _():
                finish_tile(j)

        score(0, even)

        def pair(i):
            body(2 * i, even, odd, even_p, 0)
            body(2 * i + 1, odd, even, odd_p, 1)

        loop(OFF // 2, pair)
        kept(even_p, 0)
        kept(odd_p, 1)

        @pl.when(core == 0)
        def _():
            for k in range(2):
                seg_forward(k).wait_send()


        def finish(n):
            sent_to(place, *packet_hop(n))

            @pl.when(edge)
            def _():
                sent_to(place, *seg_hop(n))

            forward(n).wait_send()

        loop(16, finish)

    pl.run_scoped(
        attention,
        pltpu.VMEM((TILES, TILE, 256), bf16),
        pltpu.VMEM((4, TILE, 256), bf16),
        pltpu.VMEM((TILES, HD + 16, TILE), bf16),
        pltpu.VMEM((4, 1, TILE), f32),
        pltpu.VMEM((4, HD + 16, TILE), f32),
        pltpu.VMEM((TILE, TILE), f32),
        pltpu.VMEM((TILE, TILE), f32),
        pltpu.VMEM((TILE, TILE), bf16),
        pltpu.VMEM((TILE, TILE), bf16),
    )

    def da_hop(h):
        return (
            stage1.at[h], da_in.at[place.slot], a_send.at[h], a_recv.at[place.slot], place.head_device(h),
        )

    def feed_forward(wo, wu, wd, b2t, gzt, x1s, ysum, hsum, dgz):
        def up_copy(j):
            at = pl.multiple_of(core * 2048 + j * 512, 512)
            return pltpu.make_async_copy(w_up.at[:, pl.ds(at, 512)], wu.at[j], w_sem.at[1 + j])

        def down_copy(j):
            at = pl.multiple_of(core * 2048 + j * 512, 512)
            return pltpu.make_async_copy(w_down.at[pl.ds(at, 512)], wd.at[j], w_sem.at[5 + j])

        out_copy = pltpu.make_async_copy(w_out, wo, w_sem.at[0])
        for j in range(4):
            down_copy(j).start()
        out_copy.start()
        for j in range(4):
            up_copy(j).start()
        dm_hop.wait_recv()
        for j in range(4):
            down_copy(j).wait()
            dgz[j] = dot_nt(dm2[...], wd[j]).astype(bf16)
        for m in range(8):
            for h in (2 * m, 2 * m + 1):
                arrived(o_in.at[h], c_recv.at[h])
            lo, hi = swap_halves(o_in[2 * m], o_in[2 * m + 1])
            o2[0:HT, 128 * m : 128 * m + 128] = lo
            o2[HT:T, 128 * m : 128 * m + 128] = hi
        o_hop = across(1, o2.at[0:T], o2.at[T : 2 * T])
        o_hop.start()
        out_copy.wait()
        x1 = x_ref[0].astype(f32) + dot(o2[0:T], wo[...])
        x1s[...] = x1
        scale1 = lax.rsqrt(jnp.mean(x1 * x1, axis=-1, keepdims=True) + EPS)
        b2[0:T] = (x1 * scale1 * gain2_ref[...]).astype(bf16)
        b_hop = across(2, b2.at[0:T], b2.at[T : 2 * T])
        b_hop.start()
        b_hop.wait_recv()
        b2t[...] = transposed(b2[...])

        for j in range(4):
            up_copy(j).wait()
            z = dot(b2[...], wu[j])
            zz = z * z
            th = jnp.tanh(ROOT * z * (1.0 + CUBE * zz))
            half = 0.5 * (1.0 + th)
            gz = (z * half).astype(bf16)
            slope = half + 0.5 * z * (1.0 - th * th) * (ROOT * (1.0 + 3.0 * CUBE * zz))
            dz = (dgz[j].astype(f32) * slope).astype(bf16)
            gzt[j * 512 : (j + 1) * 512] = transposed(gz)
            yj = dot(gz, wd[j])
            hj = dot_nt(dz, wu[j])
            if j == 0:
                ysum[...] = yj
                hsum[...] = hj
            else:
                ysum[...] += yj
                hsum[...] += hj
            up = dot(b2t[...], dz).astype(bf16)
            for u in range(2):
                unit = 2 * j + u
                spread(gs, SLOT[unit], LONG[TURN[unit]], up[:, u * 256 : u * 256 + 256])
                first_hop(unit).start()

        y_hop = across(3, ysum.at[T : 2 * T], yside)
        h_hop = across(4, hsum.at[T : 2 * T], hside)
        h_hop.start()
        y_hop.start()

        def down_units(u):
            for y_lo in range(2):
                at = y_lo * 512 + u * 256
                grad = dot(gzt[...], dm2[:, at : at + 256]).astype(bf16)
                for owner in range(32):
                    for group in range(4):
                        unit = 8 + u * 4 + group
                        place_at = position(LONG[TURN[unit]], y_lo, owner // 8, owner // 2 % 4, owner % 2)
                        gs[SLOT[unit], place_at] = grad[owner * 64 + group * 16 : owner * 64 + group * 16 + 16]
            for group in range(4):
                first_hop(8 + u * 4 + group).start()

        down_units(0)
        h_hop.wait_recv()
        x1 = x1s[...]
        scale1 = lax.rsqrt(jnp.mean(x1 * x1, axis=-1, keepdims=True) + EPS)
        dh2 = hsum[0:T] + hside[...]
        gain2_grad[...] = jnp.sum(dh2 * x1 * scale1, axis=0, keepdims=True)
        dn = dh2 * gain2_ref[...]
        back = scale1 * dn - x1 * (scale1 * scale1 * scale1) * jnp.mean(dn * x1, axis=-1, keepdims=True)
        dx1 = dy_ref[0].astype(f32) + back
        hside[...] = dx1
        da = dx1.astype(bf16)
        das[...] = da
        side_hop = across(5, das.at[:, pl.ds(pl.multiple_of((1 - core) * 512, 512), 512)], da_side)
        side_hop.start()
        loop(16, lambda n: sent_to(place, *out_hop(n)))
        for g in range(4):
            group = lax.rem(g + lax.rem(lax.div(place.s, 4), 4), 4)
            dattn = dot_nt(da, wo[pl.ds(pl.multiple_of(group * 256, 256), 256)]).astype(bf16)
            for m in range(2):
                tile = dattn[:, 128 * m : 128 * m + 128]
                packed = swap_halves(tile[:HT], tile[HT:])
                for e in range(2):
                    h = 4 * group + 2 * m + e
                    stage1[h] = packed[e]
                    send_to(place, *da_hop(h))
        down_units(1)
        y_hop.wait_recv()
        y_ref[0] = (x1 + ysum[0:T] + yside[...]).astype(bf16)
        o_hop.wait_recv()
        side_hop.wait_recv()
        o2t = transposed(o2[...])
        mine = das[:, pl.ds(pl.multiple_of(core * 512, 512), 512)]
        out = (dot(o2t[:, 0:T], mine) + dot(o2t[:, T:], da_side[...])).astype(bf16)
        for u in range(2):
            spread(outg, u, LONG[TURN[16 + u]], out[:, u * 256 : u * 256 + 256])
            outs[u].start()
        for hop in (dm_hop, o_hop, b_hop, y_hop, h_hop, side_hop):
            hop.wait_send()

    pl.run_scoped(
        feed_forward,
        pltpu.VMEM((D, D), bf16),
        pltpu.VMEM((4, D, 512), bf16),
        pltpu.VMEM((4, 512, D), bf16),
        pltpu.VMEM((D, 2 * T), bf16),
        pltpu.VMEM((2048, 2 * T), bf16),
        pltpu.VMEM((T, D), f32),
        pltpu.VMEM((2 * T, D), f32),
        pltpu.VMEM((2 * T, D), f32),
        pltpu.VMEM((4, 2 * T, 512), bf16),
    )

    def hook(which):
        if which == 0:
            for sums_of in main:
                sums_of.advance(0)
        elif which == 1:
            for sums_of in outs:
                sums_of.advance(0)
        elif which < 6:
            for sums_of in main + outs:
                sums_of.advance(which - 1)
        elif which == 6:
            for p, sums_of in enumerate(main):
                total = sums_of.last()
                for k in range(COUNTS[p]):
                    mid.store(p + 6 * k, total[k])
            for u, sums_of in enumerate(outs):
                mid.store(16 + u, sums_of.last()[0])
            mid.start()
        else:
            mid.finish()

    def hooks_at(slot):
        for which in range(8):
            if HOOKS[which] == slot:
                hook(which)

    def key_hop(m):
        return (
            stage2.at[m, 0:T], dqkv_in.at[place.head, 0:T], b_send.at[0, m], b_recv.at[0, place.head],
            place.block_device(m),
        )

    def query_hop(m):
        return (
            stage2.at[m, T:PACK], dqkv_in.at[place.head, T:PACK], b_send.at[1, m], b_recv.at[1, place.head],
            place.block_device(m),
        )

    def part_hop(j):
        return remote(part.at[j], landed.at[j], q_send.at[j], q_recv.at[j], place.partner)

    def attention_back(queries, gp, delta, dq, dkv, weights):
        hooks_at(-1)

        def prepare(t):
            dkv[t] = jnp.zeros((TILE, 128), f32)

        loop(TILES, prepare)

        def prepare_query(j):
            for b in range(4):
                m = j * 4 + b
                put_unpacked(pk[place.own_block(m), T : T + HT], False, queries.at[j, b * T : (b + 1) * T])
                arrived(da_in.at[m], a_recv.at[m])
                put_unpacked(da_in[m], True, gp.at[j, b * T : (b + 1) * T])
            delta[j] = jnp.sum(gp[j].astype(f32).T[HD:] * ot[j], axis=0, keepdims=True)
            dq[j] = jnp.zeros((HD, TILE), f32)

        loop(4, prepare_query)
        factor = jnp.where(lax.broadcasted_iota(jnp.int32, (1, 128), 1) < HD, LN2, 1.0)

        def give(j):
            part[j] = (dkv[place.own_tile(j, 1 - core)] * factor).astype(bf16)
            part_hop(j).start()

        def take(j):
            alone = jnp.logical_and(core == 0, j == 3)

            @pl.when(jnp.logical_not(alone))
            def _():
                part_hop(j).wait_recv()

            total = dkv[place.own_tile(j)] * factor
            total = (total + jnp.where(alone, 0.0, landed[j].astype(f32))).astype(bf16)
            for b in range(4):
                m = j * 4 + b
                stage2[m, 0:T] = total[b * T : (b + 1) * T]
                send_to(place, *key_hop(m))

        def fetch(i, at, n):
            which = lax.rem(n, AHEAD)
            j, k_tile = query_of(at, i), key_order(place, i)
            for half in (slice(0, TILE // 2), slice(TILE // 2, TILE)):
                pltpu.make_async_copy(
                    probs.at[j, k_tile, half], weights.at[which, half], s_sem.at[2 + which]
                ).start()

        def fetched(n):
            which = lax.rem(n, AHEAD)
            pltpu.make_async_copy(probs.at[0, 0], weights.at[which], s_sem.at[2 + which]).wait()

        def step(j, k_tile, n, pieces):
            size = TILE // len(pieces)
            which = lax.rem(n, AHEAD)
            shift = jnp.exp2(peaks[j, k_tile] - lse[j])
            for at, begin in pieces:
                ks, qs = slice(at, at + size), slice(begin, TILE)
                value = weights[which, ks, qs].astype(f32) * shift[:, qs]
                rows = load_keys(pk, k_tile)[ks]
                slopes = (value * (dot_nt(rows, gp[j, qs]) - delta[j][:, qs])).astype(bf16)
                value = value.astype(bf16)
                dkv[k_tile, ks] += dot(value, gp[j, qs]) + dot(slopes, queries[j, qs])
                dq[j, :, qs] += dot(kt[k_tile][:, ks], slopes)

        def hooks(n):
            for which in range(8):
                if 0 <= HOOKS[which] < STEPS:

                    @pl.when(n == HOOKS[which])
                    def _(which=which):
                        hook(which)

        def owned(k_tile):
            return lax.rem(lax.div(k_tile + 1, 2), 2) == core

        def skipped(k_tile):
            skip = 0
            for j in range(4):
                skip = skip + jnp.where(place.own_tile(j) < k_tile, 1, 0)
            return skip

        def query_of(at, i):
            return jnp.where(i == 7, lax.rem(at + turn, 4), at)

        def first_of(i):
            i = jnp.where(jnp.logical_and(core == 1, key_order(place, i) == 7), i + 1, i)
            return i, skipped(key_order(place, i))

        def following(i, at):
            next_i, next_at = first_of(jnp.minimum(i + 1, 7))
            return jnp.where(at < 3, i, next_i), jnp.where(at < 3, at + 1, next_at)

        ahead = first_of(0)
        for n in range(AHEAD - 1):
            fetch(*ahead, n)
            ahead = following(*ahead)

        def key_tile(i, carry):
            k_tile = key_order(place, i)

            def query_tile(at, carry):
                n, ahead = carry[0], carry[1:]
                hooks(n)
                j = query_of(at, i)
                fetched(n)

                @pl.when(n + AHEAD - 1 < STEPS)
                def _():
                    fetch(*ahead, n + AHEAD - 1)

                diagonal = place.own_tile(j) == k_tile

                @pl.when(diagonal)
                def _():
                    step(j, k_tile, n, [(at, at) for at in range(0, TILE, 256)])

                @pl.when(jnp.logical_not(diagonal))
                def _():
                    step(j, k_tile, n, [(0, 0)])

                @pl.when(i == 7)
                def _():
                    packed = pack_transposed(dq[j] * SCALE)
                    for b in range(4):
                        m = j * 4 + b
                        stage2[m, T:PACK] = packed[b]
                        send_to(place, *query_hop(m))

                return (n + 1,) + following(*ahead)

            carry = lax.fori_loop(skipped(k_tile), 4, query_tile, carry)
            mine = owned(k_tile)
            before = key_order(place, jnp.maximum(i - 1, 0))

            @pl.when(jnp.logical_and(jnp.logical_not(mine), jnp.logical_not(jnp.logical_and(core == 1, k_tile == 7))))
            def _():
                give(lax.div(k_tile, 2))

            @pl.when(jnp.logical_and(i > 0, owned(before)))
            def _():
                take(lax.div(before, 2))

            return carry

        lax.fori_loop(0, TILES, key_tile, (0,) + ahead)
        take(0)

        hooks_at(STEPS)

    def back(w_scr, a2t):
        weight = pltpu.make_async_copy(w_qkv, w_scr, l_sem.at[0])
        weight.start()
        a_hop.wait_recv()
        a2t[...] = transposed(a2[...])
        pl.run_scoped(
            attention_back,
            pltpu.VMEM((4, TILE, 128), bf16),
            pltpu.VMEM((4, TILE, 128), bf16),
            pltpu.VMEM((4, 1, TILE), f32),
            pltpu.VMEM((4, HD, TILE), f32),
            pltpu.VMEM((TILES, TILE, 128), f32),
            pltpu.VMEM((AHEAD, TILE, TILE), bf16),
        )
        pl.run_scoped(
            functools.partial(last, weight, w_scr, a2t),
            pltpu.VMEM((T, 3 * D), bf16),
            pltpu.VMEM((6, 64, 16, 256), bf16),
        )

    def last(weight, w_scr, a2t, dn, gs3):
        sums = [Part(net, gs3, land3, u, 1, SHORT[u], (t_send, u), (t_recv, u), (), tail3) for u in range(6)]
        for m in range(8):
            for h in (2 * m, 2 * m + 1):
                arrived(dqkv_in.at[h, 0:T], b_recv.at[0, h])
                arrived(dqkv_in.at[h, T:PACK], b_recv.at[1, h])
            lo, hi = swap_halves(dqkv_in[2 * m, T:PACK], dqkv_in[2 * m + 1, T:PACK])
            dk, dv = swap_halves(dqkv_in[2 * m, 0:T], dqkv_in[2 * m + 1, 0:T])
            dn[0:HT, 128 * m : 128 * m + 128] = lo
            dn[HT:T, 128 * m : 128 * m + 128] = hi
            dn[:, D + 128 * m : D + 128 * m + 128] = dk
            dn[:, 2 * D + 128 * m : 2 * D + 128 * m + 128] = dv
        d_hops = []
        for section in range(3):
            at = pl.multiple_of(section * D + (1 - core) * 512, 512)
            d_hops.append(
                across(9 + section, dn.at[:, pl.ds(at, 512)], d_side.at[:, section * 512 : section * 512 + 512])
            )
            d_hops[section].start()
        for u in range(6):
            section, half = u // 2, u % 2
            if half == 0:
                d_hops[section].wait_recv()
            at = pl.multiple_of(section * D + core * 512 + half * 256, 256)
            grad = dot(a2t[:, 0:T], dn[:, pl.ds(at, 256)]) + dot(a2t[:, T:], d_side[:, u * 256 : u * 256 + 256])
            spread(gs3, u, SHORT[u], grad.astype(bf16))
            sums[u].start()
        weight.wait()
        x = x_ref[0].astype(f32)
        scale = lax.rsqrt(jnp.mean(x * x, axis=-1, keepdims=True) + EPS)
        dh1 = dot_nt(dn[...], w_scr[...])
        gain1_grad = jnp.sum(dh1 * x * scale, axis=0, keepdims=True)
        both = [gain1_grad[:, 128 * k : 128 * k + 128] for k in range(8)]
        both += [gain2_grad[:, 128 * k : 128 * k + 128] for k in range(8)]
        gain_value[0] = jnp.concatenate(both, axis=0)
        gains.start(0)
        dxn = dh1 * gain1_ref[...]
        back = scale * dxn - x * (scale * scale * scale) * jnp.mean(dxn * x, axis=-1, keepdims=True)
        dx_ref[0] = (hside[...] + back).astype(bf16)

        for stage in range(2):
            for sums_of in sums:
                sums_of.advance(stage)
            gains.take(stage)
            gains.start(stage + 1)
            hooks_at(STEPS + 1 + stage)
        for g in range(2):
            for sums_of in sums[3 * g : 3 * g + 3]:
                sums_of.settle()
            ends3[g].start()
        gains.take(2)
        hooks_at(STEPS + 3)
        for g in range(2):
            ends3[g].wait()
            for u in range(3):
                fin3[3 * g + u] = ends3[g].result(u).reshape(2, 8, 256)
        aside = across(8, fin3.at[:, 1 - core], side3)
        aside.start()
        hooks_at(STEPS + 4)
        shard = place.s * 4 + place.r
        turn = lax.rem(128 - lax.rem(shard, 16) * 8, 128)
        for k in range(2):
            row = gain_value[3, pl.ds(8 * k + lax.div(shard, 16), 1)]
            gain_out[k : k + 1] = pltpu.roll(row, turn, 1)
        aside.wait_recv()
        mine, other = core, 1 - core
        for u in range(6):
            at = (u // 2) * D + (u % 2) * 256
            qkv_out[:, pl.ds(at + mine * 512, 256)] = fin3[u, mine]
            qkv_out[:, pl.ds(at + other * 512, 256)] = side3[u]
        for hop in [a_hop, aside] + d_hops:
            hop.wait_send()
        for sums_of in sums:
            sums_of.finish()

    pl.run_scoped(back, pltpu.VMEM((D, 3 * D), bf16), pltpu.VMEM((D, 2 * T), bf16))

    def finish(n):
        sent_to(place, *da_hop(n))
        sent_to(place, *key_hop(n))
        sent_to(place, *query_hop(n))

    loop(16, finish)

    def given(j, carry):
        part_hop(j).wait_send()
        return carry

    lax.fori_loop(0, 4 - core, given, 0)
    for sums_of in main + outs + ends3 + [gains]:
        sums_of.finish()


def block_call(frames, segment_ids, out_grad, gain1, gain2, w_qkv, w_out, w_up, w_down):
    dma = pltpu.SemaphoreType.DMA
    return pl.pallas_call(
        block_kernel,
        name="block",
        out_shape=(
            jax.ShapeDtypeStruct((1, T, D), bf16),
            jax.ShapeDtypeStruct((1, T, D), bf16),
            jax.ShapeDtypeStruct((8, 3 * D), f32),
            jax.ShapeDtypeStruct((8, 128), f32),
            jax.ShapeDtypeStruct((8, FF), f32),
            jax.ShapeDtypeStruct((8, D), f32),
            jax.ShapeDtypeStruct((32, D), f32),
            jax.ShapeDtypeStruct((4, TILES, TILE, TILE), bf16),
        ),
        in_specs=[VM] * 5 + [ANY] * 4,
        out_specs=(VM,) * 7 + (ANY,),
        scratch_shapes=[
            pltpu.VMEM((BLOCKS, PACK, 128), bf16),
            pltpu.VMEM((2, 16, 128), bf16),
            pltpu.VMEM((16, 128), bf16),
            pltpu.VMEM((TILES, HD, TILE), bf16),
            pltpu.VMEM((16, HT, 128), bf16),
            pltpu.VMEM((4, HD, TILE), f32),
            pltpu.VMEM((4, 1, TILE), f32),
            pltpu.VMEM((4, TILES, 1, TILE), f32),
            pltpu.VMEM((2 * T, D), bf16),
            pltpu.VMEM((2 * T, D), bf16),
            pltpu.VMEM((2 * T, D), bf16),
            pltpu.VMEM((T, D), f32),
            pltpu.VMEM((T, D), f32),
            pltpu.VMEM((T, D), bf16),
            pltpu.VMEM((T, 512), bf16),
            pltpu.VMEM((1, D), f32),
            pltpu.VMEM((16, 64, 16, 256), bf16),
            pltpu.VMEM((16, 63, 16, 256), bf16),
            pltpu.VMEM((2, 64, 16, 256), bf16),
            pltpu.VMEM((2, 63, 16, 256), bf16),
            pltpu.VMEM((16, HT, 128), bf16),
            pltpu.VMEM((16, HT, 128), bf16),
            pltpu.VMEM((4, TILE, 128), bf16),
            pltpu.VMEM((4, TILE, 128), bf16),
            pltpu.VMEM((16, PACK, 128), bf16),
            pltpu.VMEM((16, PACK, 128), bf16),
            pltpu.VMEM((18, 2, 8, 256), f32),
            pltpu.VMEM((10, 8, 256), f32),
            pltpu.VMEM((2, 4, 2, 8, 256), f32),
            pltpu.VMEM((2 * T, D), bf16),
            pltpu.VMEM((T, 1536), bf16),
            pltpu.VMEM((6, 56, 16, 256), bf16),
            pltpu.VMEM((6, 8, 16, 256), bf16),
            pltpu.VMEM((2, 7, 3, 16, 256), bf16),
            pltpu.VMEM((4, 16, 128), f32),
            pltpu.VMEM((3, 7, 16, 128), f32),
            pltpu.VMEM((6, 2, 8, 256), f32),
            pltpu.VMEM((6, 8, 256), f32),
            dma((9,)), dma((1,)), dma((12,)), dma((12,)), dma((4,)), dma((4,)), dma((16,)), dma((16,)),
            dma((16,)), dma((16,)), dma((2, 16)), dma((2, 16)), dma((8, 6)), dma((8, 6)), dma((6, 3)), dma((6, 3)),
            dma((2, 7)), dma((2, 7)), dma((3, 7)), dma((3, 7)), dma((6,)),
            dma((4, 3)), dma((16,)), dma((16,)), dma((18,)), dma((18,)), dma((16,)), dma((16,)), dma((2 + AHEAD,)),
            dma((16,)), dma((2,)),
        ],
        compiler_params=params(0),
    )(frames, segment_ids, out_grad, gain1, gain2, w_qkv, w_out, w_up, w_down)


def deliver_kernel(*refs):
    count = len(refs) // 2 - 2
    sources, gains, targets = refs[:count], refs[count], refs[count + 1 : 2 * count + 1]
    gain1, gain2, sem = refs[2 * count + 1 :]
    del sem
    for k in range(count):
        targets[k][...] = sources[k][...]
    gain1[...] = gains[0, 0:8]
    gain2[...] = gains[1, 0:8]


def deliver(arrays, gains):
    count = len(arrays)
    small = jax.ShapeDtypeStruct((8,), f32)
    return pl.pallas_call(
        deliver_kernel,
        name="deliver",
        out_shape=tuple(jax.ShapeDtypeStruct(v.shape, v.dtype) for v in arrays) + (small, small),
        in_specs=[VM] * (count + 1),
        out_specs=(VM,) * (count + 2),
        scratch_shapes=[pltpu.SemaphoreType.DMA((count,))],
    )(*arrays, gains)


def shards(frames, segment_ids, norm1_gain, w_qkv, w_out, norm2_gain, w_up, w_down, out_grad):
    gain1, gain2 = norm1_gain[None], norm2_gain[None]
    y, dx, qkv_sum, gain_sums, up_sum, out_sum, down_sum, _ = block_call(
        frames, segment_ids, out_grad, gain1, gain2, w_qkv, w_out, w_up, w_down
    )
    y, dx, qkv_sum, out_sum, up_sum, down_sum, gain1_sum, gain2_sum = deliver(
        (y, dx, qkv_sum, out_sum, up_sum, down_sum), gain_sums
    )
    return (y, dx, gain1_sum, qkv_sum, out_sum, gain2_sum, up_sum, down_sum)


def solution(mesh):
    return jax.shard_map(
        shards,
        mesh=mesh,
        in_specs=(
            P("row", "seq", None),
            P("row", "seq"),
            P(),
            P(),
            P(),
            P(),
            P(),
            P(),
            P("row", "seq", None),
        ),
        out_specs=(
            P("row", "seq", None),
            P("row", "seq", None),
            P(("seq", "row")),
            P(("seq", "row"), None),
            P(("seq", "row"), None),
            P(("seq", "row")),
            P(("seq", "row"), None),
            P(("seq", "row"), None),
        ),
        check_vma=False,
    )
```

```python
import functools
import math

import jax
import jax.numpy as jnp
from jax import lax
from jax.experimental import pallas as pl
from jax.experimental.pallas import tpu as pltpu
from jax.sharding import PartitionSpec as P

MESH = pl.DeviceIdType.MESH
f32 = jnp.float32
bf16 = jnp.bfloat16

D = 1024
H = 16
HD = 64
FF = 4096
T = 192
HT = T // 2
BLOCKS = 32
TILE = 768
TILES = 8
PACK = 288
EPS = 1e-05
NEG = -1e30
LOG2E = math.log2(math.e)
LN2 = math.log(2.0)
SCALE = HD**-0.5
VMEM_LIMIT = 60 * 1024 * 1024

ANY = pl.BlockSpec(memory_space=pl.ANY)
VM = pl.BlockSpec(memory_space=pltpu.VMEM)


def dot(a, b):
    return jnp.dot(a, b, preferred_element_type=f32)


def dot_nt(a, b):
    return lax.dot_general(a, b, (((1,), (1,)), ((), ())), preferred_element_type=f32)


def transposed(v):
    return v.astype(f32).T.astype(bf16)


def swap_halves(first, second):
    lane = lax.broadcasted_iota(jnp.int32, first.shape, 1)
    low = lane < HD
    first, second = first.astype(f32), second.astype(f32)
    return (
        jnp.where(low, first, pltpu.roll(second, HD, 1)).astype(bf16),
        jnp.where(low, pltpu.roll(first, HD, 1), second).astype(bf16),
    )


class Place:
    def __init__(self):
        self.s = lax.axis_index("seq")
        self.r = lax.axis_index("row")
        self.y_lo = lax.div(self.s, 16)
        self.head = lax.rem(self.s, 16)
        self.y_hi = lax.div(self.r, 2)
        self.core = lax.rem(self.r, 2)
        tile = lax.div(self.s, 4)
        self.block_core = lax.rem(lax.div(tile + 1, 2), 2)
        self.slot = lax.div(self.s, 8) * 4 + lax.rem(self.s, 4)
        self.partner = (self.s, self.r + 1 - 2 * self.core)
        self.self_served = jnp.logical_and(self.y_lo == self.core, self.block_core == self.core)
        self.self_count = jnp.where(self.self_served, 1, 0)

    def head_device(self, h):
        return (self.core * 16 + h, self.y_hi * 2 + self.block_core)

    def own_tile(self, j, core=None):
        core = self.core if core is None else core
        return 2 * j + lax.rem(j + core, 2)

    def own_block(self, n):
        return self.own_tile(lax.div(n, 4)) * 4 + lax.rem(n, 4)

    def block_device(self, n):
        return (self.own_block(n), self.y_hi * 2 + self.y_lo)

    def is_self(self, device):
        return jnp.logical_and(device[0] == self.s, device[1] == self.r)


def remote(src, dst, send, recv, device):
    return pltpu.make_async_remote_copy(
        src_ref=src, dst_ref=dst, send_sem=send, recv_sem=recv, device_id=device, device_id_type=MESH
    )


def send_to(place, src, dst, send, recv, device):
    own = place.is_self(device)

    @pl.when(own)
    def _():
        pltpu.make_async_copy(src, dst, recv).start()

    @pl.when(jnp.logical_not(own))
    def _():
        remote(src, dst, send, recv, device).start()


def sent_to(place, src, dst, send, recv, device):
    @pl.when(jnp.logical_not(place.is_self(device)))
    def _():
        remote(src, dst, send, recv, device).wait_send()


def arrived(dst, recv):
    pltpu.make_async_copy(dst, dst, recv).wait()


def greet(barrier, device):
    pl.semaphore_signal(barrier, inc=1, device_id=device, device_id_type=MESH)


def greet_all(place, barrier, device_of):
    def one(n, carry):
        device = device_of(n)

        @pl.when(jnp.logical_not(place.is_self(device)))
        def _():
            greet(barrier, device)

        return carry

    lax.fori_loop(0, 16, one, 0)


def loop(count, body):
    def one(n, carry):
        body(n)
        return carry

    lax.fori_loop(0, count, one, 0)


def params(collective_id):
    return pltpu.CompilerParams(
        collective_id=collective_id, has_side_effects=True, vmem_limit_bytes=VMEM_LIMIT
    )


def seg_column(tile):
    tile = tile.astype(f32)
    return jnp.concatenate(
        [
            jnp.broadcast_to(tile[0:1], (128, 128)).T,
            jnp.broadcast_to(tile[1:2], (128, 128)).T[: T - 128],
        ],
        axis=0,
    )


MIDDLE = 4


def put_marks(segs, tile, put):
    lane = lax.broadcasted_iota(jnp.int32, (TILE, 128), 1).astype(f32)
    put(slice(0, TILE), lane, jnp.full((TILE, 128), MIDDLE, f32))
    for which, special, rows in ((0, 0, slice(0, T)), (1, TILES - 1, slice(TILE - T, TILE))):

        @pl.when(tile == special)
        def _(which=which, rows=rows):
            put(rows, lane[:T], seg_column(segs[which]) + MIDDLE)


def put_unpacked(packed, high, target):
    low = lax.broadcasted_iota(jnp.int32, (HT, 128), 1) < HD
    packed = packed.astype(f32)
    turned = pltpu.roll(packed, HD, 1)
    if high:
        target[0:HT] = jnp.where(low, 0.0, turned).astype(bf16)
        target[HT:T] = jnp.where(low, 0.0, packed).astype(bf16)
    else:
        target[0:HT] = jnp.where(low, packed, 0.0).astype(bf16)
        target[HT:T] = jnp.where(low, turned, 0.0).astype(bf16)


STEPS = 18
AHEAD = 4


OFF = STEPS - 4


def walk(place, n):
    turn = lax.div(place.head, 4)
    j, start = turn, 0
    end = place.own_tile(j)
    for k in range(1, 4):
        past = n >= end
        following = lax.rem(turn + k, 4)
        j = jnp.where(past, following, j)
        start = jnp.where(past, end, start)
        end = jnp.where(past, end + place.own_tile(following), end)
    return j, n - start, n + 1 == end


def key_order(place, i):
    turn = lax.div(place.head, 4)
    k_tile = 7 - lax.rem(i + 2 * turn, 7)
    k_tile = jnp.where(jnp.logical_and(place.core == 1, k_tile == 1), 0, k_tile)
    return jnp.where(i == 7, place.core, k_tile)


def causal(scores):
    k = lax.broadcasted_iota(jnp.int32, scores.shape, 0)
    q = lax.broadcasted_iota(jnp.int32, scores.shape, 1)
    return jnp.where(k <= q, scores, NEG)


def load_keys(pk_ref, tile):
    return pk_ref[pl.ds(tile * 4, 4), 0:T].reshape(TILE, 128)


def pack_transposed(value_t):
    both = jnp.concatenate([value_t, value_t], axis=0).T
    lane = lax.broadcasted_iota(jnp.int32, (HT, 128), 1)
    return [
        jnp.where(lane < HD, both[b * T : b * T + HT], both[b * T + HT : b * T + T]).astype(bf16)
        for b in range(4)
    ]


FIRST = lambda c: ((c + 1) // 2) % 2
SECOND = lambda c: c // 2


def chip_bits(x, y, z):
    return [FIRST(x), FIRST(y), FIRST(z), SECOND(x), SECOND(y), SECOND(z)]


SHORT = [[(p + k) % 3 + 3 * (p // 3) for k in range(3)] + [k + 3 * (1 - p // 3) for k in range(3)] for p in range(6)]
LONG = [[(p + k) % 3 + 3 * ((p // 3 + k // 3) % 2) for k in range(6)] for p in range(6)]


def position(order, y_lo, x, z, y_hi):
    bits = chip_bits(x, y_hi * 2 + y_lo, z)
    at = 0
    for dim in order:
        at = at * 2 + bits[dim]
    return at


class Net:
    def __init__(self, place):
        self.x, self.z = lax.div(place.head, 4), lax.rem(place.head, 4)
        self.y = place.y_hi * 2 + place.y_lo
        self.core = place.core
        self.bits = [lax.rem(lax.div(c + 1, 2), 2) for c in (self.x, self.y, self.z)]
        self.bits += [lax.div(c, 2) for c in (self.x, self.y, self.z)]

    def across(self, pairing, mask):
        moved = []
        for k, c in enumerate((self.x, self.y, self.z)):
            far = c + 1 - 2 * lax.rem(c, 2) if pairing == 0 else 3 - c
            moved.append(far if mask >> (2 - k) & 1 else c)
        x, y, z = moved
        return (lax.rem(y, 2) * 16 + x * 4 + z, lax.div(y, 2) * 2 + self.core)

    def neighbour(self, dim):
        return self.across(dim // 3, 4 >> dim % 3)

    def greet(self, barrier):
        for pairing in range(2):
            for mask in range(1, 8):
                greet(barrier, self.across(pairing, mask))

    GREETINGS = 14


class Part:
    def __init__(self, net, acc, land, at, count, order, send, recv, pieces=(), tail=None):
        self.net, self.acc, self.land, self.order, self.pieces, self.tail = net, acc, land, order, pieces, tail
        self.units = pl.ds(at, count)
        self.send, self.recv = send, recv

    def bit(self, stage):
        return self.net.bits[self.order[stage]]

    def base(self, stage):
        at = 0
        for k in range(stage + 1):
            at = at + self.bit(k) * (32 >> k)
        return at

    def landing(self, stage):
        return sum(32 >> k for k in range(stage))

    def hop(self, stage):
        half = 32 >> stage
        base = self.base(stage - 1) + (1 - self.bit(stage)) * half
        return remote(
            self.acc.at[self.units, pl.ds(base, half)],
            self.land.at[self.units, pl.ds(self.landing(stage), half)],
            self.send[0].at[self.send[1], stage],
            self.recv[0].at[self.recv[1], stage],
            self.net.neighbour(self.order[stage]),
        )

    def start(self):
        self.hop(0).start()

    def hops(self, stage):
        return list(self.pieces) if stage == 0 and self.pieces else [self.hop(stage)]

    def total(self, base, landed, group):
        mine = self.acc[self.units, pl.ds(base, group)].astype(f32)
        return (mine + self.land[self.units, pl.ds(landed, group)].astype(f32)).astype(bf16)

    def add(self, base, landed, count):
        group = min(count, 4)

        def body(i):
            here = pl.ds(base + i * group, group)
            self.acc[self.units, here] = self.total(base + i * group, landed + i * group, group)

        loop(count // group, body)

    def advance(self, stage):
        for hop in self.hops(stage):
            hop.wait_recv()
        half = 16 >> stage
        base, landed = self.base(stage), self.landing(stage)
        bit = self.bit(stage + 1)
        self.add(base + (1 - bit) * half, landed + (1 - bit) * half, half)
        self.hop(stage + 1).start()
        self.add(base + bit * half, landed + bit * half, half)

    def settle(self):
        self.hop(2).wait_recv()
        for at in range(0, 8, 4):
            self.tail[self.units, at : at + 4] = self.total(self.base(2) + at, self.landing(2) + at, 4)

    def last(self):
        self.hop(5).wait_recv()
        mine = self.acc[self.units, pl.ds(self.base(5), 1)].astype(f32)
        return (mine + self.land[self.units, pl.ds(self.landing(5), 1)].astype(f32))[:, 0]

    def finish(self):
        for stage in range(6 if self.tail is None else 3):
            for hop in self.hops(stage):
                hop.wait_send()


class Exchange:
    def __init__(self, net, pairing, tail, land, send, recv):
        self.net, self.pairing, self.tail, self.land, self.send, self.recv = net, pairing, tail, land, send, recv

    def row(self, mask):
        at = 0
        for k in range(3):
            bit = self.net.bits[3 * self.pairing + k]
            at = at + (1 - bit if mask >> (2 - k) & 1 else bit) * (4 >> k)
        return at

    def hop(self, mask):
        return remote(
            self.tail.at[:, self.row(mask)], self.land.at[mask - 1],
            self.send.at[mask - 1], self.recv.at[mask - 1], self.net.across(self.pairing, mask),
        )

    def start(self):
        for mask in range(1, 8):
            self.hop(mask).start()

    def result(self, unit):
        total = self.tail[unit, self.row(0)].astype(f32)
        for mask in range(1, 8):
            total = total + self.land[mask - 1, unit].astype(f32)
        return total

    def wait(self):
        for mask in range(1, 8):
            self.hop(mask).wait_recv()

    def finish(self):
        for mask in range(1, 8):
            self.hop(mask).wait_send()


class Shared:
    def __init__(self, net, place, value, land, send, recv):
        self.net, self.place, self.value, self.land, self.send, self.recv = net, place, value, land, send, recv

    def hops(self, pairing):
        if pairing == 2:
            return [
                remote(self.value.at[2], self.land.at[2, 0], self.send.at[2, 0], self.recv.at[2, 0], self.place.partner)
            ]
        return [
            remote(
                self.value.at[pairing], self.land.at[pairing, mask - 1],
                self.send.at[pairing, mask - 1], self.recv.at[pairing, mask - 1], self.net.across(pairing, mask),
            )
            for mask in range(1, 8)
        ]

    def start(self, pairing):
        for hop in self.hops(pairing):
            hop.start()

    def take(self, pairing):
        total = self.value[pairing]
        for k, hop in enumerate(self.hops(pairing)):
            hop.wait_recv()
            total = total + self.land[pairing, k]
        self.value[pairing + 1] = total

    def finish(self):
        for pairing in range(3):
            for hop in self.hops(pairing):
                hop.wait_send()


TURN = [u % 6 for u in range(18)]
COUNTS = [3, 3, 3, 3, 2, 2]
STARTS = [0, 3, 6, 9, 12, 14]
SLOT = [STARTS[u % 6] + u // 6 for u in range(16)]
FINAL = list(range(8)) + [10 + (v % 4) * 2 + v // 4 for v in range(8)] + [8, 9]


class MidSums:
    def __init__(self, place, fin, side, down, sem, up_out, out_out, down_out):
        self.place, self.fin, self.side, self.down, self.sem = place, fin, side, down, sem
        self.up_out, self.out_out, self.down_out = up_out, out_out, down_out

    def targets(self):
        return [(self.place.core * 16 + self.place.head, self.place.y_hi * 2 + k) for k in range(2)]

    def sources(self):
        return [(m * 16 + self.place.head, self.place.y_hi * 2 + self.place.y_lo) for m in range(2)]

    def self_count(self):
        return jnp.where(self.place.y_lo == self.place.core, 1, 0)

    def greet(self, barrier):
        greet(barrier, self.place.partner)
        for device in self.sources():

            @pl.when(jnp.logical_not(self.place.is_self(device)))
            def _(device=device):
                greet(barrier, device)

    def greetings(self):
        return 3 - self.self_count()

    def store(self, unit, value):
        self.fin[FINAL[unit]] = value.reshape(2, 8, 256)

    def aside(self):
        return remote(
            self.fin.at[0:10, 1 - self.place.core], self.side, self.sem.at[0], self.sem.at[1], self.place.partner
        )

    def down_hop(self, k):
        return (
            self.fin.at[10 + 4 * k : 14 + 4 * k],
            self.down.at[self.place.y_lo],
            self.sem.at[2 + k],
            self.sem.at[4 + self.place.y_lo],
            self.targets()[k],
        )

    def start(self):
        self.aside().start()
        for k in range(2):
            send_to(self.place, *self.down_hop(k))

    def finish(self):
        place = self.place
        self.aside().wait_recv()
        mine, other = place.core, 1 - place.core
        for u in range(8):
            self.up_out[:, pl.ds(mine * 2048 + u * 256, 256)] = self.fin[u, mine]
            self.up_out[:, pl.ds(other * 2048 + u * 256, 256)] = self.side[u]
        for u in range(2):
            self.out_out[:, pl.ds(mine * 512 + u * 256, 256)] = self.fin[8 + u, mine]
            self.out_out[:, pl.ds(other * 512 + u * 256, 256)] = self.side[8 + u]
        for m in range(2):
            arrived(self.down.at[m], self.sem.at[4 + m])
            for v in range(4):
                group, half = v // 2, v % 2
                self.down_out[group * 16 : group * 16 + 16, m * 512 + half * 256 : m * 512 + half * 256 + 256] = (
                    self.down[m, v].reshape(16, 256)
                )
        self.aside().wait_send()
        for k in range(2):
            sent_to(place, *self.down_hop(k))


MID_OUT = (
    jax.ShapeDtypeStruct((8, FF), f32),
    jax.ShapeDtypeStruct((8, D), f32),
    jax.ShapeDtypeStruct((32, D), f32),
)
MID_SCRATCH = [
    pltpu.VMEM((18, 2, 8, 256), f32),
    pltpu.VMEM((10, 8, 256), f32),
    pltpu.VMEM((2, 4, 2, 8, 256), f32),
    pltpu.SemaphoreType.DMA((6,)),
]


def spread(target, unit_slot, order, block):
    for chip in range(64):
        y_lo, x, z, y_hi = chip // 32, chip // 8 % 4, chip // 2 % 4, chip % 2
        target[unit_slot, position(order, y_lo, x, z, y_hi)] = block[chip * 16 : chip * 16 + 16]


ROOT = math.sqrt(2.0 / math.pi)
CUBE = 0.044715


HOOKS = (1, 5, 11, 18, 19, 20, 21, 22)


def block_kernel(
    x_ref, seg_ref, dy_ref, gain1_ref, gain2_ref, w_qkv, w_out, w_up, w_down,
    y_ref, dx_ref, qkv_out, gain_out, up_out, out_out, down_out, probs,
    pk, segs, seg_tile, kt, o_in, ot, lse, peaks, o2, b2, dm2, yside, hside, das, da_side, gain2_grad,
    gs, land, outg, land2, da_in, stage1,
    part, landed, dqkv_in, stage2, fin, side, down, a2, d_side, land3, tail3, tail_land3, gain_value, gain_land,
    fin3, side3,
    w_sem, l_sem, p_send, p_recv, q_send, q_recv, h_send, h_recv, a_send, a_recv, b_send, b_recv,
    n_send, n_recv, t_send, t_recv, e_send, e_recv, g_send, g_recv, m_sem,
    k_sem, x_send, x_recv, f_send, f_recv, c_send, c_recv, s_sem, y_send, y_recv,
):
    place = Place()
    core = place.core
    net = Net(place)
    turn = lax.rem(lax.div(place.s, 4), 4)

    def across(k, src, dst):
        return remote(src, dst, p_send.at[k], p_recv.at[k], place.partner)

    def first_hop(unit):
        bit = net.bits[TURN[unit]]
        return remote(
            gs.at[SLOT[unit], pl.ds((1 - bit) * 32, 32)], land.at[SLOT[unit], 0:32],
            h_send.at[unit], h_recv.at[unit], net.neighbour(TURN[unit]),
        )

    main = [
        Part(
            net, gs, land, STARTS[p], COUNTS[p], LONG[p], (n_send, p), (n_recv, p),
            [first_hop(p + 6 * k) for k in range(COUNTS[p])],
        )
        for p in range(6)
    ]
    outs = [
        Part(net, outg, land2, u, 1, LONG[TURN[16 + u]], (n_send, 6 + u), (n_recv, 6 + u)) for u in range(2)
    ]
    mid = MidSums(place, fin, side, down, m_sem, up_out, out_out, down_out)
    ends3 = [
        Exchange(net, 1 - g, tail3.at[3 * g : 3 * g + 3], tail_land3.at[g], e_send.at[g], e_recv.at[g])
        for g in range(2)
    ]
    gains = Shared(net, place, gain_value, gain_land, g_send, g_recv)

    barrier = pltpu.get_barrier_semaphore()
    greet_all(place, barrier, place.block_device)
    greet_all(place, barrier, place.head_device)
    net.greet(barrier)
    mid.greet(barrier)
    a_hop = across(6, a2.at[0:T], a2.at[T : 2 * T])
    dm_hop = across(0, dm2.at[0:T], dm2.at[T : 2 * T])

    edge = jnp.logical_or(place.s == 0, place.s == BLOCKS - 1)
    which_edge = lax.div(place.s, BLOCKS - 1)

    def seg_hop(h):
        return (seg_tile, segs.at[which_edge], y_send.at[h], y_recv.at[which_edge], place.head_device(h))

    def packet_hop(h):
        return (stage2.at[h], pk.at[place.s], x_send.at[h], x_recv.at[place.slot], place.head_device(h))

    def qkv(w_scr):
        def weight(g, section):
            at = pl.multiple_of(section * D + lax.rem(g + turn, 4) * 256, 256)
            return pltpu.make_async_copy(w_qkv.at[:, pl.ds(at, 256)], w_scr.at[g, section], k_sem.at[g, section])

        for g in range(4):
            for section in range(3):
                weight(g, section).start()
        x = x_ref[0].astype(f32)
        a = (x * lax.rsqrt(jnp.mean(x * x, axis=-1, keepdims=True) + EPS) * gain1_ref[...]).astype(bf16)
        a2[0:T] = a
        dm2[0:T] = dy_ref[0]
        numbers = seg_ref[...].astype(f32)
        numbers = numbers - jnp.where(place.s == BLOCKS - 1, numbers[:, 0:1], numbers[:, T - 1 : T])
        row = lax.broadcasted_iota(jnp.int32, (16, 128), 0)
        rest = jnp.concatenate([numbers[:, 128:T], jnp.zeros((1, 256 - T), f32)], axis=1)
        seg_tile[...] = jnp.where(row == 0, numbers[:, :128], jnp.where(row == 1, rest, 0.0)).astype(bf16)
        for g in range(4):
            for section in range(3):
                weight(g, section).wait()
            q = dot(a, w_scr[g, 0]) * (SCALE * LOG2E)
            k = dot(a, w_scr[g, 1])
            v = dot(a, w_scr[g, 2])
            if g == 0:
                pl.semaphore_wait(barrier, 2 * (16 - place.self_count) + Net.GREETINGS + mid.greetings())

                @pl.when(edge)
                def _():
                    loop(16, lambda h: send_to(place, *seg_hop(h)))

            for m in range(2):
                lanes = slice(128 * m, 128 * m + 128)
                h = 4 * lax.rem(g + turn, 4) + 2 * m
                kv = swap_halves(k[:, lanes].astype(bf16), v[:, lanes].astype(bf16))
                qq = q[:, lanes].astype(bf16)
                qp = swap_halves(qq[:HT], qq[HT:])
                for e in range(2):
                    stage2[h + e, 0:T] = kv[e]
                    stage2[h + e, T:PACK] = qp[e]
                    send_to(place, *packet_hop(h + e))
        a_hop.start()
        dm_hop.start()

    pl.run_scoped(qkv, pltpu.VMEM((4, 3, D, 256), bf16))

    def out_hop(m):
        return (stage1.at[m], o_in.at[place.head], c_send.at[m], c_recv.at[place.head], place.block_device(m))

    def attention(keys, queries, vt, top, acc, even, odd, even_p, odd_p):
        one = jnp.where(lax.broadcasted_iota(jnp.int32, (16, TILE), 0) == 0, 1.0, 0.0).astype(bf16)

        def forward(n):
            i = place.own_block(n)
            return remote(pk.at[i, 0:T], pk.at[i, 0:T], f_send.at[n], f_recv.at[n], place.partner)

        def seg_forward(k):
            return remote(segs.at[k], segs.at[k], f_send.at[16 + k], f_recv.at[16 + k], place.partner)

        def key_tile(t):
            rows = load_keys(pk, t)
            keys[t, :, 0:128] = rows

            def put(rows, lane, number):
                keys[t, rows, 128:256] = jnp.where(lane == number, 1.0, 0.0).astype(bf16)

            put_marks(segs, t, put)
            turned = transposed(rows)
            kt[t] = turned[:HD]
            vt[t, 0:HD] = turned[HD:]
            vt[t, HD : HD + 16] = one

        def query_tile(j):
            t = place.own_tile(j)
            for b in range(4):
                put_unpacked(pk[t * 4 + b, T : T + HT], False, queries.at[j, b * T : (b + 1) * T, 0:128])

            def put(rows, lane, number):
                other = jnp.logical_and(lane < 2 * MIDDLE + 1, lane != number)
                queries[j, rows, 128:256] = jnp.where(other, NEG, 0.0).astype(bf16)

            put_marks(segs, t, put)

        def keep(j, k_tile, weights, which):
            for half in (slice(0, TILE // 2), slice(TILE // 2, TILE)):
                pltpu.make_async_copy(weights.at[half], probs.at[j, k_tile, half], s_sem.at[which]).start()

        def kept(weights, which):
            pltpu.make_async_copy(weights, probs.at[0, 0], s_sem.at[which]).wait()

        def finish_tile(j):
            total = acc[j, HD : HD + 1]
            out_t = acc[j, 0:HD] / total
            lse[j] = top[j] + jnp.log2(total)
            ot[j] = out_t
            packed = pack_transposed(out_t)
            for b in range(4):
                m = j * 4 + b
                stage1[m] = packed[b]
                send_to(place, *out_hop(m))

        def diagonal(j, weights, which, again):
            for b in range(4):
                n = j * 4 + b
                arrived(pk.at[place.own_block(n)], x_recv.at[n])
                forward(n).start()
            t = place.own_tile(j)
            for k, special in ((0, 0), (1, TILES - 1)):

                @pl.when(t == special)
                def _(k=k):
                    arrived(segs.at[k], y_recv.at[k])
                    seg_forward(k).start()

            key_tile(t)
            query_tile(j)
            scores = causal(dot_nt(keys[t], queries[j]))
            peak = jnp.max(scores, axis=0, keepdims=True)
            top[j] = peak
            peaks[j, t] = peak
            value = jnp.exp2(scores - peak).astype(bf16)

            @pl.when(again)
            def _():
                kept(weights, which)

            weights[...] = value
            keep(j, t, weights, which)
            acc[j] = dot(vt[t], value)

        def diagonals(i):
            diagonal(2 * i, even_p, 0, i > 0)
            diagonal(2 * i + 1, odd_p, 1, i > 0)

        loop(2, diagonals)

        @pl.when(core == 0)
        def _():
            finish_tile(0)

        def others(j):
            for b in range(4):
                forward(j * 4 + b).wait_recv()
            other = place.own_tile(j, 1 - core)
            for k, special in ((0, 0), (1, TILES - 1)):

                @pl.when(other == special)
                def _(k=k):
                    seg_forward(k).wait_recv()

            key_tile(place.own_tile(j, 1 - core))

        loop(4, others)

        def score(n, scores):
            j, k_tile, _ = walk(place, jnp.minimum(n, OFF - 1))
            scores[...] = dot_nt(keys[k_tile], queries[j])

        def body(n, now, later, weights, which):
            j, k_tile, last = walk(place, n)
            kept(weights, which)
            score(n + 1, later)
            scores = now[...]
            peak = jnp.maximum(top[j], jnp.max(scores, axis=0, keepdims=True))
            fade = jnp.exp2(top[j] - peak)
            top[j] = peak
            peaks[j, k_tile] = peak
            value = jnp.exp2(scores - peak).astype(bf16)
            weights[...] = value
            acc[j] = acc[j] * fade + dot(vt[k_tile], value)
            keep(j, k_tile, weights, which)

            @pl.when(last)
            def _():
                finish_tile(j)

        score(0, even)

        def pair(i):
            body(2 * i, even, odd, even_p, 0)
            body(2 * i + 1, odd, even, odd_p, 1)

        loop(OFF // 2, pair)
        kept(even_p, 0)
        kept(odd_p, 1)

        @pl.when(core == 0)
        def _():
            for k in range(2):
                seg_forward(k).wait_send()


        def finish(n):
            sent_to(place, *packet_hop(n))

            @pl.when(edge)
            def _():
                sent_to(place, *seg_hop(n))

            forward(n).wait_send()

        loop(16, finish)

    pl.run_scoped(
        attention,
        pltpu.VMEM((TILES, TILE, 256), bf16),
        pltpu.VMEM((4, TILE, 256), bf16),
        pltpu.VMEM((TILES, HD + 16, TILE), bf16),
        pltpu.VMEM((4, 1, TILE), f32),
        pltpu.VMEM((4, HD + 16, TILE), f32),
        pltpu.VMEM((TILE, TILE), f32),
        pltpu.VMEM((TILE, TILE), f32),
        pltpu.VMEM((TILE, TILE), bf16),
        pltpu.VMEM((TILE, TILE), bf16),
    )

    def da_hop(h):
        return (
            stage1.at[h], da_in.at[place.slot], a_send.at[h], a_recv.at[place.slot], place.head_device(h),
        )

    def feed_forward(wo, wu, wd, b2t, gzt, x1s, ysum, hsum, dgz):
        def up_copy(j):
            at = pl.multiple_of(core * 2048 + j * 512, 512)
            return pltpu.make_async_copy(w_up.at[:, pl.ds(at, 512)], wu.at[j], w_sem.at[1 + j])

        def down_copy(j):
            at = pl.multiple_of(core * 2048 + j * 512, 512)
            return pltpu.make_async_copy(w_down.at[pl.ds(at, 512)], wd.at[j], w_sem.at[5 + j])

        out_copy = pltpu.make_async_copy(w_out, wo, w_sem.at[0])
        for j in range(4):
            down_copy(j).start()
        out_copy.start()
        for j in range(4):
            up_copy(j).start()
        dm_hop.wait_recv()
        for j in range(4):
            down_copy(j).wait()
            dgz[j] = dot_nt(dm2[...], wd[j]).astype(bf16)
        for m in range(8):
            for h in (2 * m, 2 * m + 1):
                arrived(o_in.at[h], c_recv.at[h])
            lo, hi = swap_halves(o_in[2 * m], o_in[2 * m + 1])
            o2[0:HT, 128 * m : 128 * m + 128] = lo
            o2[HT:T, 128 * m : 128 * m + 128] = hi
        o_hop = across(1, o2.at[0:T], o2.at[T : 2 * T])
        o_hop.start()
        out_copy.wait()
        x1 = x_ref[0].astype(f32) + dot(o2[0:T], wo[...])
        x1s[...] = x1
        scale1 = lax.rsqrt(jnp.mean(x1 * x1, axis=-1, keepdims=True) + EPS)
        b2[0:T] = (x1 * scale1 * gain2_ref[...]).astype(bf16)
        b_hop = across(2, b2.at[0:T], b2.at[T : 2 * T])
        b_hop.start()
        b_hop.wait_recv()
        b2t[...] = transposed(b2[...])

        for j in range(4):
            up_copy(j).wait()
            z = dot(b2[...], wu[j])
            zz = z * z
            th = jnp.tanh(ROOT * z * (1.0 + CUBE * zz))
            half = 0.5 * (1.0 + th)
            gz = (z * half).astype(bf16)
            slope = half + 0.5 * z * (1.0 - th * th) * (ROOT * (1.0 + 3.0 * CUBE * zz))
            dz = (dgz[j].astype(f32) * slope).astype(bf16)
            gzt[j * 512 : (j + 1) * 512] = transposed(gz)
            yj = dot(gz, wd[j])
            hj = dot_nt(dz, wu[j])
            if j == 0:
                ysum[...] = yj
                hsum[...] = hj
            else:
                ysum[...] += yj
                hsum[...] += hj
            up = dot(b2t[...], dz).astype(bf16)
            for u in range(2):
                unit = 2 * j + u
                spread(gs, SLOT[unit], LONG[TURN[unit]], up[:, u * 256 : u * 256 + 256])
                first_hop(unit).start()

        y_hop = across(3, ysum.at[T : 2 * T], yside)
        h_hop = across(4, hsum.at[T : 2 * T], hside)
        h_hop.start()
        y_hop.start()

        def down_units(u):
            for y_lo in range(2):
                at = y_lo * 512 + u * 256
                grad = dot(gzt[...], dm2[:, at : at + 256]).astype(bf16)
                for owner in range(32):
                    for group in range(4):
                        unit = 8 + u * 4 + group
                        place_at = position(LONG[TURN[unit]], y_lo, owner // 8, owner // 2 % 4, owner % 2)
                        gs[SLOT[unit], place_at] = grad[owner * 64 + group * 16 : owner * 64 + group * 16 + 16]
            for group in range(4):
                first_hop(8 + u * 4 + group).start()

        down_units(0)
        h_hop.wait_recv()
        x1 = x1s[...]
        scale1 = lax.rsqrt(jnp.mean(x1 * x1, axis=-1, keepdims=True) + EPS)
        dh2 = hsum[0:T] + hside[...]
        gain2_grad[...] = jnp.sum(dh2 * x1 * scale1, axis=0, keepdims=True)
        dn = dh2 * gain2_ref[...]
        back = scale1 * dn - x1 * (scale1 * scale1 * scale1) * jnp.mean(dn * x1, axis=-1, keepdims=True)
        dx1 = dy_ref[0].astype(f32) + back
        hside[...] = dx1
        da = dx1.astype(bf16)
        das[...] = da
        side_hop = across(5, das.at[:, pl.ds(pl.multiple_of((1 - core) * 512, 512), 512)], da_side)
        side_hop.start()
        loop(16, lambda n: sent_to(place, *out_hop(n)))
        for g in range(4):
            group = lax.rem(g + lax.rem(lax.div(place.s, 4), 4), 4)
            dattn = dot_nt(da, wo[pl.ds(pl.multiple_of(group * 256, 256), 256)]).astype(bf16)
            for m in range(2):
                tile = dattn[:, 128 * m : 128 * m + 128]
                packed = swap_halves(tile[:HT], tile[HT:])
                for e in range(2):
                    h = 4 * group + 2 * m + e
                    stage1[h] = packed[e]
                    send_to(place, *da_hop(h))
        down_units(1)
        y_hop.wait_recv()
        y_ref[0] = (x1 + ysum[0:T] + yside[...]).astype(bf16)
        o_hop.wait_recv()
        side_hop.wait_recv()
        o2t = transposed(o2[...])
        mine = das[:, pl.ds(pl.multiple_of(core * 512, 512), 512)]
        out = (dot(o2t[:, 0:T], mine) + dot(o2t[:, T:], da_side[...])).astype(bf16)
        for u in range(2):
            spread(outg, u, LONG[TURN[16 + u]], out[:, u * 256 : u * 256 + 256])
            outs[u].start()
        for hop in (dm_hop, o_hop, b_hop, y_hop, h_hop, side_hop):
            hop.wait_send()

    pl.run_scoped(
        feed_forward,
        pltpu.VMEM((D, D), bf16),
        pltpu.VMEM((4, D, 512), bf16),
        pltpu.VMEM((4, 512, D), bf16),
        pltpu.VMEM((D, 2 * T), bf16),
        pltpu.VMEM((2048, 2 * T), bf16),
        pltpu.VMEM((T, D), f32),
        pltpu.VMEM((2 * T, D), f32),
        pltpu.VMEM((2 * T, D), f32),
        pltpu.VMEM((4, 2 * T, 512), bf16),
    )

    def hook(which):
        if which == 0:
            for sums_of in main:
                sums_of.advance(0)
        elif which == 1:
            for sums_of in outs:
                sums_of.advance(0)
        elif which < 6:
            for sums_of in main + outs:
                sums_of.advance(which - 1)
        elif which == 6:
            for p, sums_of in enumerate(main):
                total = sums_of.last()
                for k in range(COUNTS[p]):
                    mid.store(p + 6 * k, total[k])
            for u, sums_of in enumerate(outs):
                mid.store(16 + u, sums_of.last()[0])
            mid.start()
        else:
            mid.finish()

    def hooks_at(slot):
        for which in range(8):
            if HOOKS[which] == slot:
                hook(which)

    def key_hop(m):
        return (
            stage2.at[m, 0:T], dqkv_in.at[place.head, 0:T], b_send.at[0, m], b_recv.at[0, place.head],
            place.block_device(m),
        )

    def query_hop(m):
        return (
            stage2.at[m, T:PACK], dqkv_in.at[place.head, T:PACK], b_send.at[1, m], b_recv.at[1, place.head],
            place.block_device(m),
        )

    def part_hop(j):
        return remote(part.at[j], landed.at[j], q_send.at[j], q_recv.at[j], place.partner)

    def attention_back(queries, gp, delta, dq, dkv, weights):
        hooks_at(-1)

        def prepare(t):
            dkv[t] = jnp.zeros((TILE, 128), f32)

        loop(TILES, prepare)

        def prepare_query(j):
            for b in range(4):
                m = j * 4 + b
                put_unpacked(pk[place.own_block(m), T : T + HT], False, queries.at[j, b * T : (b + 1) * T])
                arrived(da_in.at[m], a_recv.at[m])
                put_unpacked(da_in[m], True, gp.at[j, b * T : (b + 1) * T])
            delta[j] = jnp.sum(gp[j].astype(f32).T[HD:] * ot[j], axis=0, keepdims=True)
            dq[j] = jnp.zeros((HD, TILE), f32)

        loop(4, prepare_query)
        factor = jnp.where(lax.broadcasted_iota(jnp.int32, (1, 128), 1) < HD, LN2, 1.0)

        def give(j):
            part[j] = (dkv[place.own_tile(j, 1 - core)] * factor).astype(bf16)
            part_hop(j).start()

        def take(j):
            alone = jnp.logical_and(core == 0, j == 3)

            @pl.when(jnp.logical_not(alone))
            def _():
                part_hop(j).wait_recv()

            total = dkv[place.own_tile(j)] * factor
            total = (total + jnp.where(alone, 0.0, landed[j].astype(f32))).astype(bf16)
            for b in range(4):
                m = j * 4 + b
                stage2[m, 0:T] = total[b * T : (b + 1) * T]
                send_to(place, *key_hop(m))

        def fetch(i, at, n):
            which = lax.rem(n, AHEAD)
            j, k_tile = query_of(at, i), key_order(place, i)
            for half in (slice(0, TILE // 2), slice(TILE // 2, TILE)):
                pltpu.make_async_copy(
                    probs.at[j, k_tile, half], weights.at[which, half], s_sem.at[2 + which]
                ).start()

        def fetched(n):
            which = lax.rem(n, AHEAD)
            pltpu.make_async_copy(probs.at[0, 0], weights.at[which], s_sem.at[2 + which]).wait()

        def step(j, k_tile, n, pieces):
            size = TILE // len(pieces)
            which = lax.rem(n, AHEAD)
            shift = jnp.exp2(peaks[j, k_tile] - lse[j])
            for at, begin in pieces:
                ks, qs = slice(at, at + size), slice(begin, TILE)
                value = weights[which, ks, qs].astype(f32) * shift[:, qs]
                rows = load_keys(pk, k_tile)[ks]
                slopes = (value * (dot_nt(rows, gp[j, qs]) - delta[j][:, qs])).astype(bf16)
                value = value.astype(bf16)
                dkv[k_tile, ks] += dot(value, gp[j, qs]) + dot(slopes, queries[j, qs])
                dq[j, :, qs] += dot(kt[k_tile][:, ks], slopes)

        def hooks(n):
            for which in range(8):
                if 0 <= HOOKS[which] < STEPS:

                    @pl.when(n == HOOKS[which])
                    def _(which=which):
                        hook(which)

        def owned(k_tile):
            return lax.rem(lax.div(k_tile + 1, 2), 2) == core

        def skipped(k_tile):
            skip = 0
            for j in range(4):
                skip = skip + jnp.where(place.own_tile(j) < k_tile, 1, 0)
            return skip

        def query_of(at, i):
            return jnp.where(i == 7, lax.rem(at + turn, 4), at)

        def first_of(i):
            i = jnp.where(jnp.logical_and(core == 1, key_order(place, i) == 7), i + 1, i)
            return i, skipped(key_order(place, i))

        def following(i, at):
            next_i, next_at = first_of(jnp.minimum(i + 1, 7))
            return jnp.where(at < 3, i, next_i), jnp.where(at < 3, at + 1, next_at)

        ahead = first_of(0)
        for n in range(AHEAD - 1):
            fetch(*ahead, n)
            ahead = following(*ahead)

        def key_tile(i, carry):
            k_tile = key_order(place, i)

            def query_tile(at, carry):
                n, ahead = carry[0], carry[1:]
                hooks(n)
                j = query_of(at, i)
                fetched(n)

                @pl.when(n + AHEAD - 1 < STEPS)
                def _():
                    fetch(*ahead, n + AHEAD - 1)

                diagonal = place.own_tile(j) == k_tile

                @pl.when(diagonal)
                def _():
                    step(j, k_tile, n, [(at, at) for at in range(0, TILE, 256)])

                @pl.when(jnp.logical_not(diagonal))
                def _():
                    step(j, k_tile, n, [(0, 0)])

                @pl.when(i == 7)
                def _():
                    packed = pack_transposed(dq[j] * SCALE)
                    for b in range(4):
                        m = j * 4 + b
                        stage2[m, T:PACK] = packed[b]
                        send_to(place, *query_hop(m))

                return (n + 1,) + following(*ahead)

            carry = lax.fori_loop(skipped(k_tile), 4, query_tile, carry)
            mine = owned(k_tile)
            before = key_order(place, jnp.maximum(i - 1, 0))

            @pl.when(jnp.logical_and(jnp.logical_not(mine), jnp.logical_not(jnp.logical_and(core == 1, k_tile == 7))))
            def _():
                give(lax.div(k_tile, 2))

            @pl.when(jnp.logical_and(i > 0, owned(before)))
            def _():
                take(lax.div(before, 2))

            return carry

        lax.fori_loop(0, TILES, key_tile, (0,) + ahead)
        take(0)

        hooks_at(STEPS)

    def back(w_scr, a2t):
        weight = pltpu.make_async_copy(w_qkv, w_scr, l_sem.at[0])
        weight.start()
        a_hop.wait_recv()
        a2t[...] = transposed(a2[...])
        pl.run_scoped(
            attention_back,
            pltpu.VMEM((4, TILE, 128), bf16),
            pltpu.VMEM((4, TILE, 128), bf16),
            pltpu.VMEM((4, 1, TILE), f32),
            pltpu.VMEM((4, HD, TILE), f32),
            pltpu.VMEM((TILES, TILE, 128), f32),
            pltpu.VMEM((AHEAD, TILE, TILE), bf16),
        )
        pl.run_scoped(
            functools.partial(last, weight, w_scr, a2t),
            pltpu.VMEM((T, 3 * D), bf16),
            pltpu.VMEM((6, 64, 16, 256), bf16),
        )

    def last(weight, w_scr, a2t, dn, gs3):
        sums = [Part(net, gs3, land3, u, 1, SHORT[u], (t_send, u), (t_recv, u), (), tail3) for u in range(6)]
        d_hops = []
        for k in range(8):
            m = k % 4 + 4 * (1 - core if k < 4 else core)
            for h in (2 * m, 2 * m + 1):
                arrived(dqkv_in.at[h, 0:T], b_recv.at[0, h])
                arrived(dqkv_in.at[h, T:PACK], b_recv.at[1, h])
            lo, hi = swap_halves(dqkv_in[2 * m, T:PACK], dqkv_in[2 * m + 1, T:PACK])
            dk, dv = swap_halves(dqkv_in[2 * m, 0:T], dqkv_in[2 * m + 1, 0:T])
            dn[0:HT, pl.ds(pl.multiple_of(128 * m, 128), 128)] = lo
            dn[HT:T, pl.ds(pl.multiple_of(128 * m, 128), 128)] = hi
            dn[:, pl.ds(pl.multiple_of(D + 128 * m, 128), 128)] = dk
            dn[:, pl.ds(pl.multiple_of(2 * D + 128 * m, 128), 128)] = dv
            if k == 3:
                for section in range(3):
                    at = pl.multiple_of(section * D + (1 - core) * 512, 512)
                    d_hops.append(
                        across(9 + section, dn.at[:, pl.ds(at, 512)], d_side.at[:, section * 512 : section * 512 + 512])
                    )
                    d_hops[section].start()
        for u in range(6):
            section, half = u // 2, u % 2
            if half == 0:
                d_hops[section].wait_recv()
            at = pl.multiple_of(section * D + core * 512 + half * 256, 256)
            grad = dot(a2t[:, 0:T], dn[:, pl.ds(at, 256)]) + dot(a2t[:, T:], d_side[:, u * 256 : u * 256 + 256])
            spread(gs3, u, SHORT[u], grad.astype(bf16))
            sums[u].start()
        weight.wait()
        x = x_ref[0].astype(f32)
        scale = lax.rsqrt(jnp.mean(x * x, axis=-1, keepdims=True) + EPS)
        dh1 = dot_nt(dn[...], w_scr[...])
        gain1_grad = jnp.sum(dh1 * x * scale, axis=0, keepdims=True)
        both = [gain1_grad[:, 128 * k : 128 * k + 128] for k in range(8)]
        both += [gain2_grad[:, 128 * k : 128 * k + 128] for k in range(8)]
        gain_value[0] = jnp.concatenate(both, axis=0)
        gains.start(0)
        dxn = dh1 * gain1_ref[...]
        back = scale * dxn - x * (scale * scale * scale) * jnp.mean(dxn * x, axis=-1, keepdims=True)
        dx_ref[0] = (hside[...] + back).astype(bf16)

        for stage in range(2):
            for sums_of in sums:
                sums_of.advance(stage)
            gains.take(stage)
            gains.start(stage + 1)
            hooks_at(STEPS + 1 + stage)
        for g in range(2):
            for sums_of in sums[3 * g : 3 * g + 3]:
                sums_of.settle()
            ends3[g].start()
        gains.take(2)
        hooks_at(STEPS + 3)
        for g in range(2):
            ends3[g].wait()
            for u in range(3):
                fin3[3 * g + u] = ends3[g].result(u).reshape(2, 8, 256)
        aside = across(8, fin3.at[:, 1 - core], side3)
        aside.start()
        hooks_at(STEPS + 4)
        shard = place.s * 4 + place.r
        turn = lax.rem(128 - lax.rem(shard, 16) * 8, 128)
        for k in range(2):
            row = gain_value[3, pl.ds(8 * k + lax.div(shard, 16), 1)]
            gain_out[k : k + 1] = pltpu.roll(row, turn, 1)
        aside.wait_recv()
        mine, other = core, 1 - core
        for u in range(6):
            at = (u // 2) * D + (u % 2) * 256
            qkv_out[:, pl.ds(at + mine * 512, 256)] = fin3[u, mine]
            qkv_out[:, pl.ds(at + other * 512, 256)] = side3[u]
        for hop in [a_hop, aside] + d_hops:
            hop.wait_send()
        for sums_of in sums:
            sums_of.finish()

    pl.run_scoped(back, pltpu.VMEM((D, 3 * D), bf16), pltpu.VMEM((D, 2 * T), bf16))

    def finish(n):
        sent_to(place, *da_hop(n))
        sent_to(place, *key_hop(n))
        sent_to(place, *query_hop(n))

    loop(16, finish)

    def given(j, carry):
        part_hop(j).wait_send()
        return carry

    lax.fori_loop(0, 4 - core, given, 0)
    for sums_of in main + outs + ends3 + [gains]:
        sums_of.finish()


def block_call(frames, segment_ids, out_grad, gain1, gain2, w_qkv, w_out, w_up, w_down):
    dma = pltpu.SemaphoreType.DMA
    return pl.pallas_call(
        block_kernel,
        name="block",
        out_shape=(
            jax.ShapeDtypeStruct((1, T, D), bf16),
            jax.ShapeDtypeStruct((1, T, D), bf16),
            jax.ShapeDtypeStruct((8, 3 * D), f32),
            jax.ShapeDtypeStruct((8, 128), f32),
            jax.ShapeDtypeStruct((8, FF), f32),
            jax.ShapeDtypeStruct((8, D), f32),
            jax.ShapeDtypeStruct((32, D), f32),
            jax.ShapeDtypeStruct((4, TILES, TILE, TILE), bf16),
        ),
        in_specs=[VM] * 5 + [ANY] * 4,
        out_specs=(VM,) * 7 + (ANY,),
        scratch_shapes=[
            pltpu.VMEM((BLOCKS, PACK, 128), bf16),
            pltpu.VMEM((2, 16, 128), bf16),
            pltpu.VMEM((16, 128), bf16),
            pltpu.VMEM((TILES, HD, TILE), bf16),
            pltpu.VMEM((16, HT, 128), bf16),
            pltpu.VMEM((4, HD, TILE), f32),
            pltpu.VMEM((4, 1, TILE), f32),
            pltpu.VMEM((4, TILES, 1, TILE), f32),
            pltpu.VMEM((2 * T, D), bf16),
            pltpu.VMEM((2 * T, D), bf16),
            pltpu.VMEM((2 * T, D), bf16),
            pltpu.VMEM((T, D), f32),
            pltpu.VMEM((T, D), f32),
            pltpu.VMEM((T, D), bf16),
            pltpu.VMEM((T, 512), bf16),
            pltpu.VMEM((1, D), f32),
            pltpu.VMEM((16, 64, 16, 256), bf16),
            pltpu.VMEM((16, 63, 16, 256), bf16),
            pltpu.VMEM((2, 64, 16, 256), bf16),
            pltpu.VMEM((2, 63, 16, 256), bf16),
            pltpu.VMEM((16, HT, 128), bf16),
            pltpu.VMEM((16, HT, 128), bf16),
            pltpu.VMEM((4, TILE, 128), bf16),
            pltpu.VMEM((4, TILE, 128), bf16),
            pltpu.VMEM((16, PACK, 128), bf16),
            pltpu.VMEM((16, PACK, 128), bf16),
            pltpu.VMEM((18, 2, 8, 256), f32),
            pltpu.VMEM((10, 8, 256), f32),
            pltpu.VMEM((2, 4, 2, 8, 256), f32),
            pltpu.VMEM((2 * T, D), bf16),
            pltpu.VMEM((T, 1536), bf16),
            pltpu.VMEM((6, 56, 16, 256), bf16),
            pltpu.VMEM((6, 8, 16, 256), bf16),
            pltpu.VMEM((2, 7, 3, 16, 256), bf16),
            pltpu.VMEM((4, 16, 128), f32),
            pltpu.VMEM((3, 7, 16, 128), f32),
            pltpu.VMEM((6, 2, 8, 256), f32),
            pltpu.VMEM((6, 8, 256), f32),
            dma((9,)), dma((1,)), dma((12,)), dma((12,)), dma((4,)), dma((4,)), dma((16,)), dma((16,)),
            dma((16,)), dma((16,)), dma((2, 16)), dma((2, 16)), dma((8, 6)), dma((8, 6)), dma((6, 3)), dma((6, 3)),
            dma((2, 7)), dma((2, 7)), dma((3, 7)), dma((3, 7)), dma((6,)),
            dma((4, 3)), dma((16,)), dma((16,)), dma((18,)), dma((18,)), dma((16,)), dma((16,)), dma((2 + AHEAD,)),
            dma((16,)), dma((2,)),
        ],
        compiler_params=params(0),
    )(frames, segment_ids, out_grad, gain1, gain2, w_qkv, w_out, w_up, w_down)


def deliver_kernel(*refs):
    count = len(refs) // 2 - 2
    sources, gains, targets = refs[:count], refs[count], refs[count + 1 : 2 * count + 1]
    gain1, gain2, sem = refs[2 * count + 1 :]
    del sem
    for k in range(count):
        targets[k][...] = sources[k][...]
    gain1[...] = gains[0, 0:8]
    gain2[...] = gains[1, 0:8]


def deliver(arrays, gains):
    count = len(arrays)
    small = jax.ShapeDtypeStruct((8,), f32)
    return pl.pallas_call(
        deliver_kernel,
        name="deliver",
        out_shape=tuple(jax.ShapeDtypeStruct(v.shape, v.dtype) for v in arrays) + (small, small),
        in_specs=[VM] * (count + 1),
        out_specs=(VM,) * (count + 2),
        scratch_shapes=[pltpu.SemaphoreType.DMA((count,))],
    )(*arrays, gains)


def shards(frames, segment_ids, norm1_gain, w_qkv, w_out, norm2_gain, w_up, w_down, out_grad):
    gain1, gain2 = norm1_gain[None], norm2_gain[None]
    y, dx, qkv_sum, gain_sums, up_sum, out_sum, down_sum, _ = block_call(
        frames, segment_ids, out_grad, gain1, gain2, w_qkv, w_out, w_up, w_down
    )
    y, dx, qkv_sum, out_sum, up_sum, down_sum, gain1_sum, gain2_sum = deliver(
        (y, dx, qkv_sum, out_sum, up_sum, down_sum), gain_sums
    )
    return (y, dx, gain1_sum, qkv_sum, out_sum, gain2_sum, up_sum, down_sum)


def solution(mesh):
    return jax.shard_map(
        shards,
        mesh=mesh,
        in_specs=(
            P("row", "seq", None),
            P("row", "seq"),
            P(),
            P(),
            P(),
            P(),
            P(),
            P(),
            P("row", "seq", None),
        ),
        out_specs=(
            P("row", "seq", None),
            P("row", "seq", None),
            P(("seq", "row")),
            P(("seq", "row"), None),
            P(("seq", "row"), None),
            P(("seq", "row")),
            P(("seq", "row"), None),
            P(("seq", "row"), None),
        ),
        check_vma=False,
    )
```
